32 devices in a mesh: slab: 8 (over z, core), obs: 4 (over y, x).
Axes of the slice: x: 2, y: 2, z: 4, core: 2. Of those that a mesh axis runs over, the one named last changes fastest.
Arguments:
- innovation: float32 [32, 75, 256], P('obs'), may hold values from -6 to 6
- obs_precision: float32 [32, 75, 256], P('obs'), may hold values from 0.5 to 4
- seeds: int32 [4], replicated, may hold values from 0 to 999999
- col_sd: float32 [32, 128], P(('slab', 'obs')), may hold values from 0.3 to 3
- vert_factor: float32 [75, 75], replicated, may hold values from -0.75 to 0.75
- h_values: bfloat16 [8, 4, 32, 128, 256], P('slab', 'obs'), may hold values from -0.125 to 0.125
- block_obs: int32 [8, 4, 32], P('slab', 'obs'), may hold values from 0 to 7, as said below
- block_col: int32 [8, 4, 32], P('slab', 'obs'), may hold values from 0 to 3
- entry_count: int32 [8, 4], P('slab', 'obs'), may hold values from 5 to 32, as said below
Outputs:
- analysis_increment: float32 [32, 4, 75, 128], P(('slab', 'obs'))
- residual: float32 [32, 4, 75, 128], P(('slab', 'obs'))
The draws below stay inside these ranges and needn't reach their ends.
Inputs may be any that keep to these rules, and one draw needn't show every extreme that they name: For each slab s and obs index o, the first entry_count[s, o] slots name distinct pairs (block_obs, block_col); later slots are unused. `entry_count`: 32 is reached in every draw.
All inputs are finite; a program needn't handle non-finite values.
Results may differ from the reference program's by a relative error of at most 0.02.
Values may be sent and summed in bfloat16 or wider, within the bound.
No kernel may reach another device: no remote copies, remote signals or barrier semaphores. Data moves between devices by JAX's collectives and lax.ppermute only.
A program may use at most 64 MiB of HBM per device.

```python
import math
import jax
import jax.numpy as jnp
from jax import lax

LEV = 75
PROFILES = 256
BLOCK_COLS = 128
MEM = 4
ITERS = 2
OBSB_DEV = 8
NNZ_DEV = 32
CB_SLAB = 4
NCB = 32
NOBSBLK = 32
N_SLAB = 8
N_OBS = 4


def pattern_pairs(key):
    devices = N_SLAB * N_OBS
    pairs = OBSB_DEV * CB_SLAB
    keys = jax.random.split(jax.random.fold_in(key, 17), devices)
    orders = jax.vmap(lambda single: jax.random.permutation(single, pairs))(keys)[:, :NNZ_DEV]
    return orders.reshape(N_SLAB, N_OBS, NNZ_DEV).astype(jnp.int32)


def draw_block_obs(key, part):
    return pattern_pairs(key) // CB_SLAB


def draw_block_col(key, part):
    return pattern_pairs(key) % CB_SLAB


def draw_entry_count(key, part):
    devices = N_SLAB * N_OBS
    coastal = jax.random.randint(jax.random.fold_in(key, 29), (devices,), 0, 5) == 0
    forced = jax.random.randint(jax.random.fold_in(key, 31), (), 0, devices)
    lower = max(1, NNZ_DEV // 6)
    upper = max(1, NNZ_DEV // 3)
    inland = jax.random.randint(jax.random.fold_in(key, 37), (devices,), lower, upper + 1)
    chosen = coastal | (jnp.arange(devices) == forced)
    counts = jnp.where(chosen, NNZ_DEV, inland)
    return counts.reshape(N_SLAB, N_OBS).astype(jnp.int32)


def touch_ends(array, stream_key, low, high):
    spot = [jax.random.randint(jax.random.fold_in(stream_key, axis), (), 0, length) for axis, length in enumerate(array.shape)]
    main_axis = array.shape.index(max(array.shape))
    neighbour = spot[:main_axis] + [(spot[main_axis] + 1) % array.shape[main_axis]] + spot[main_axis + 1:]
    return array.at[tuple(spot)].set(low).at[tuple(neighbour)].set(high)


def shard_levels(own_key, extent, cuts, smallest, top_value):
    def one(position, shards_of):
        heights = jax.random.uniform(jax.random.fold_in(jax.random.fold_in(own_key, 6), position), (shards_of,), jnp.float32, smallest / len(cuts), top_value / len(cuts))
        return jnp.repeat(jnp.exp(heights), extent[position] // shards_of).reshape((-1,) + (1,) * (len(extent) - position - 1))

    level = one(*cuts[0])
    for cut in cuts[1:]:
        level = level * one(*cut)
    return level


def bell_draw(own_key, shape, scale, reach, cuts=(), kind=jnp.bfloat16):
    loudness = shard_levels(own_key, shape, cuts, -0.22, 0.18) if cuts else 1.0
    result = jax.random.normal(own_key, shape, jnp.float32) * scale * loudness
    return jnp.minimum(jnp.maximum(result, -reach), reach).astype(kind)


def setup_inputs(seed: int = 0) -> dict:
    splits = jax.random.split(jax.random.key(seed), 10)
    return {
        "innovation": bell_draw(splits[0], (NOBSBLK, LEV, PROFILES), 1.0, 6.0, ((0, 4),), jnp.float32),
        "obs_precision": jnp.clip(jnp.exp(math.log(4.0) - 2.0794415 * jax.random.uniform(splits[1], (NOBSBLK, LEV, PROFILES), jnp.float32) ** shard_levels(splits[1], (NOBSBLK, LEV, PROFILES), ((0, 4),), -0.2, 0.2)), 0.5, 4.0),
        "seeds": touch_ends(jax.random.randint(splits[2], (MEM,), 0, 1000000), jax.random.fold_in(splits[2], 1), 0, 999999).astype(jnp.int32),
        "col_sd": jnp.clip(jnp.exp(math.log(3.0) - 2.3025851 * jax.random.uniform(splits[3], (NCB, BLOCK_COLS), jnp.float32) ** shard_levels(splits[3], (NCB, BLOCK_COLS), ((0, 32),), -0.2, 0.2)), 0.3, 3.0),
        "vert_factor": bell_draw(splits[4], (LEV, LEV), LEV ** -0.5, 0.75, (), jnp.float32),
        "h_values": bell_draw(splits[5], (N_SLAB, N_OBS, NNZ_DEV, BLOCK_COLS, PROFILES), (128 * N_SLAB * NNZ_DEV // (2 * OBSB_DEV)) ** -0.5, 0.125, ((0, 8), (1, 4))),
        "block_obs": draw_block_obs(jax.random.fold_in(splits[9], 71), 0),
        "block_col": draw_block_col(jax.random.fold_in(splits[9], 71), 0),
        "entry_count": draw_entry_count(jax.random.fold_in(splits[9], 71), 0),
    }


def perturbed(innovation, precision, seeds, first_block):
    blocks = innovation.shape[0]
    levels = innovation.shape[1]
    width = innovation.shape[2]
    block_index = (first_block + jnp.arange(blocks, dtype=jnp.int32))[:, None, None]
    level_index = jnp.arange(levels, dtype=jnp.int32)[None, :, None]
    profile_index = jnp.arange(width, dtype=jnp.int32)[None, None, :]
    flat_index = (block_index * levels + level_index) * width + profile_index
    hashed = (seeds[None, :, None, None] % 32749 + 7919 * (flat_index[:, None] % 32749)) % 32749
    hashed = (hashed * hashed + 12345) % 32749
    hashed = (hashed * hashed + 2719) % 32749
    noise = hashed.astype(jnp.float32) / 32749.0 - 0.5
    spread = lax.rsqrt(precision)[:, None]
    return innovation[:, None] + 3.4 * noise * spread

def vertical(matrix, field):
    return jnp.einsum('kl,cmlp->cmkp', matrix, field, precision=lax.Precision.HIGHEST)

def vertical_adj(matrix, field):
    return jnp.einsum('lk,cmlp->cmkp', matrix, field, precision=lax.Precision.HIGHEST)

def forward_ref(moved, h_values, block_obs, block_col, entry_count):
    slab_fields = moved.reshape(N_SLAB, CB_SLAB, MEM, LEV, 128)

    def per_slab(carry, inputs):
        panel, h_block, obs_ids, col_ids, counts = inputs
        pieces = panel[col_ids].astype(jnp.float32)
        product = jnp.einsum('onmlc,oncp->onmlp', pieces, h_block.astype(jnp.float32), precision=lax.Precision.HIGHEST)
        live = (jnp.arange(NNZ_DEV, dtype=jnp.int32)[None, :] < counts[:, None]).astype(jnp.float32)
        obs_pick = (obs_ids[:, :, None] == jnp.arange(OBSB_DEV, dtype=jnp.int32)[None, None, :]).astype(jnp.float32) * live[:, :, None]
        partial_value = jnp.einsum('onb,onmlp->obmlp', obs_pick, product, precision=lax.Precision.HIGHEST)
        return (carry + partial_value, None)
    start_sum = jnp.zeros((N_OBS, OBSB_DEV, MEM, LEV, 256), jnp.float32)
    total, unused = lax.scan(per_slab, start_sum, (slab_fields, h_values, block_obs, block_col, entry_count))
    return total.reshape(NOBSBLK, MEM, LEV, 256)

def adjoint_ref(weighted, h_values, block_obs, block_col, entry_count):
    grouped = weighted.reshape(N_OBS, OBSB_DEV, MEM, LEV, 256)
    group_ids = jnp.arange(N_OBS, dtype=jnp.int32)[:, None]

    def per_slab(inputs):
        h_block, obs_ids, col_ids, counts = inputs
        pieces = grouped[group_ids, obs_ids].astype(jnp.float32)
        contrib = jnp.einsum('onmlp,oncp->onmlc', pieces, h_block.astype(jnp.float32), precision=lax.Precision.HIGHEST)
        live = (jnp.arange(NNZ_DEV, dtype=jnp.int32)[None, :] < counts[:, None]).astype(jnp.float32)
        col_pick = (col_ids[:, :, None] == jnp.arange(CB_SLAB, dtype=jnp.int32)[None, None, :]).astype(jnp.float32) * live[:, :, None]
        term = jnp.einsum('onk,onmlc->okmlc', col_pick, contrib, precision=lax.Precision.HIGHEST)
        rounded = lax.optimization_barrier(term.astype(jnp.bfloat16)).astype(jnp.float32)
        return lax.optimization_barrier(jnp.sum(rounded, axis=0))
    stacked = lax.map(per_slab, (h_values, block_obs, block_col, entry_count))
    return stacked.reshape(NCB, MEM, LEV, 128)

def member_sum(left, right):
    return lax.optimization_barrier(jnp.sum(left * right, axis=(0, 2, 3)))

def reference(innovation, obs_precision, seeds, col_sd, vert_factor, h_values, block_obs, block_col, entry_count):
    sigma = col_sd[:, None, None, :]
    target = perturbed(innovation, obs_precision, seeds, 0)
    weighted0 = (obs_precision[:, None] * target).astype(jnp.bfloat16)
    rhs = vertical_adj(vert_factor, sigma * adjoint_ref(weighted0, h_values, block_obs, block_col, entry_count))
    solution = jnp.zeros_like(rhs)
    residual = rhs
    direction = rhs
    norm_now = member_sum(residual, residual)
    for sweep in range(ITERS):
        moved = (sigma * vertical(vert_factor, direction)).astype(jnp.bfloat16)
        obs_image = forward_ref(moved, h_values, block_obs, block_col, entry_count)
        weighted = (obs_precision[:, None] * obs_image).astype(jnp.bfloat16)
        image = direction + vertical_adj(vert_factor, sigma * adjoint_ref(weighted, h_values, block_obs, block_col, entry_count))
        alpha = (norm_now / member_sum(direction, image))[None, :, None, None]
        solution = solution + alpha * direction
        residual = residual - alpha * image
        norm_next = member_sum(residual, residual)
        direction = residual + (norm_next / norm_now)[None, :, None, None] * direction
        norm_now = norm_next
    analysis_increment = sigma * vertical(vert_factor, solution)
    return (analysis_increment, residual)
```

```python
import functools

import jax
import jax.numpy as jnp
from jax import lax
from jax.experimental import pallas as pl
from jax.experimental.pallas import tpu as pltpu
from jax.sharding import PartitionSpec as P

ITERS = 2
GROUPS = 1
LANES = 128
PIECES = 3
PRIME = 32749
VMEM = pl.BlockSpec(memory_space=pltpu.VMEM)
SMEM = pl.BlockSpec(memory_space=pltpu.SMEM)
F32 = jnp.float32
BF16 = jnp.bfloat16
NT = (((1,), (1,)), ((), ()))


def call(kernel, outs, scratch, flops, *args, scalars=0):
    nbytes = sum(a.size * a.dtype.itemsize for a in (*args, *outs))
    return pl.pallas_call(
        kernel,
        out_shape=outs,
        in_specs=[SMEM] * scalars + [VMEM] * (len(args) - scalars),
        out_specs=[VMEM] * len(outs),
        scratch_shapes=scratch,
        compiler_params=pltpu.CompilerParams(vmem_limit_bytes=40 * 1024 * 1024),
        cost_estimate=pl.CostEstimate(flops=flops, bytes_accessed=nbytes, transcendentals=0),
    )(*args)


def struct(shape, dtype):
    return jax.ShapeDtypeStruct(shape, dtype)


def place():
    slab = lax.axis_index("slab")
    return slab // 2, slab % 2, lax.axis_index("obs")


def total(x):
    return jnp.sum(jnp.sum(x, axis=0, keepdims=True), axis=1, keepdims=True)


def with_scalars(body, values):
    rows = lax.broadcasted_iota(jnp.int32, body.shape, 0)
    lanes = lax.broadcasted_iota(jnp.int32, body.shape, 1)
    line = jnp.zeros(body.shape, F32)
    for q, value in enumerate(values):
        rest = value
        for piece in range(PIECES):
            part = rest.astype(BF16).astype(F32)
            rest = rest - part
            line = jnp.where(lanes == q * PIECES + piece, part, line)
    return jnp.where(rows == body.shape[0] - 1, line, body)


def read_scalars(refs, member, count):
    rows = refs[0].shape[1]
    tail = refs[0][member, rows - 16 : rows, 0:LANES].astype(F32)
    for ref in refs[1:]:
        tail = tail + ref[member, rows - 16 : rows, 0:LANES].astype(F32)
    sub = lax.broadcasted_iota(jnp.int32, tail.shape, 0)
    lanes = lax.broadcasted_iota(jnp.int32, tail.shape, 1)
    found = []
    for q in range(count):
        mine = (sub == 15) & (lanes >= q * PIECES) & (lanes < (q + 1) * PIECES)
        found.append(total(jnp.where(mine, tail, 0.0)))
    return found


def remainder(x, factor):
    return x - (x.astype(F32) * factor).astype(jnp.int32) * PRIME


def start_kernel(
    dims, seeds, ids, cols, count, innov, prec, h, own, partner, *rest
):
    chips, n_obs, lev, halves, groups = dims
    outs, (scratch, acc) = rest[:-2], rest[-2:]
    z, core, obs = place()
    blocks, width, profiles = innov.shape[0], own.shape[3], innov.shape[2]
    colblocks = own.shape[1]
    members = seeds.shape[0]
    levp = scratch.shape[1]

    own[...] = jnp.zeros_like(own)
    partner[...] = jnp.zeros_like(partner)

    def put(n, carry):
        b, k = ids[n], cols[n]
        for half in range(halves):
            piece = b * halves + half
            tile = h[n, :, half * width : (half + 1) * width]

            @pl.when(piece % 2 == core)
            def _():
                own[piece // 2, k] = tile

            @pl.when(piece % 2 != core)
            def _():
                partner[piece // 2, k] = tile

        return carry

    lax.fori_loop(0, count[0], put, 0)

    scratch[...] = jnp.zeros_like(scratch)
    shape = (lev, profiles)
    spot = lax.broadcasted_iota(jnp.int32, shape, 0) * profiles + lax.broadcasted_iota(
        jnp.int32, shape, 1
    )
    first = True
    for source in range(2):
        for zz in range(chips):
            piece = 2 * zz + (core if source == 0 else 1 - core)
            b = piece // halves
            flat = spot + (obs * blocks + b) * (lev * profiles)
            base = remainder(7919 * remainder(flat, 1.0 / PRIME), 1.0 / PRIME)
            p = prec[b]
            gain = 3.4 * p * lax.rsqrt(p)
            offset = p * innov[b] - 0.5 * gain
            gain = gain * (1.0 / PRIME)
            for m in range(members):
                k0 = base + lax.rem(seeds[m], PRIME)
                k0 = jnp.where(k0 >= PRIME, k0 - PRIME, k0)
                k1 = remainder(k0 * k0 + 12345, 1.0 / PRIME)
                k2 = remainder(k1 * k1 + 2719, 1.0 / PRIME)
                k2 = jnp.where(k2 < 0, k2 + PRIME, k2)
                k2 = jnp.where(k2 >= PRIME, k2 - PRIME, k2)
                scratch[m, 0:lev, :] = offset + gain * k2.astype(F32)
            if halves == 1:
                w = scratch[...]
            else:
                w = scratch[:, :, pl.ds(pl.multiple_of((piece % halves) * width, LANES), width)]
            w = w.astype(BF16).reshape(members * levp, width)
            tiles = (own if source == 0 else partner)[zz].reshape(colblocks * LANES, width)
            part = lax.dot_general(w, tiles, NT, preferred_element_type=F32)
            for k in range(colblocks):
                piece_k = part[:, k * LANES : (k + 1) * LANES]
                acc[k] = piece_k if first else acc[k] + piece_k
            first = False

    share = members // groups
    for i in range(n_obs):
        value = acc[obs ^ i].astype(BF16).reshape(members, levp, LANES)
        for g in range(groups):
            outs[g * n_obs + i][...] = value[g * share : (g + 1) * share]


def precision_kernel(halves, prec, out):
    z, core, unused = place()
    piece = 2 * z + core
    lev = prec.shape[1]
    width = out.shape[1]
    out[...] = jnp.zeros_like(out)
    if halves == 1:
        out[0:lev, :] = prec[piece]
    else:
        out[0:lev, :] = prec[
            piece // halves, :, pl.ds(pl.multiple_of((piece % halves) * width, LANES), width)
        ]


def dot(a, b):
    return jnp.dot(a, b, preferred_element_type=F32, precision=lax.Precision.HIGHEST)


def first_kernel(parts, *refs):
    pieces, (sd, vert, vert_t), (residual, moved) = refs[:parts], refs[parts : parts + 3], refs[-2:]
    for m in range(residual.shape[0]):
        t = pieces[0][m].astype(F32)
        for ref in pieces[1:]:
            t = t + ref[m].astype(F32)
        r = dot(vert_t[...], sd[...] * t)
        residual[m] = r
        x = sd[...] * dot(vert[...], r)
        moved[m] = with_scalars(x, [total(r * r)]).astype(BF16)


def forward_kernel(dims, *refs):
    chips, n_obs = dims
    xs = refs[: 2 * n_obs]
    own, partner = refs[2 * n_obs : 2 * n_obs + 2]
    outs, panel = refs[-1 - chips : -1], refs[-1]
    z, core, obs = place()
    members, levp, unused = xs[0].shape
    colblocks, width = own.shape[1], own.shape[3]
    rows = members * levp
    for source in range(2):
        for i in range(n_obs):
            at = pl.multiple_of((source * colblocks + (obs ^ i)) * LANES, LANES)
            panel[:, pl.ds(at, LANES)] = xs[source * n_obs + i][...].reshape(rows, LANES)
    scalars = [read_scalars(xs, m, 2) for m in range(members)]
    half = colblocks * LANES
    for i in range(chips):
        zz = z ^ i
        y = jnp.dot(panel[:, 0:half], own[zz].reshape(half, width), preferred_element_type=F32)
        y = y + jnp.dot(
            panel[:, half : 2 * half], partner[zz].reshape(half, width), preferred_element_type=F32
        )
        y = y.reshape(members, levp, width)
        for m in range(members):
            outs[i][m] = with_scalars(y[m], scalars[m]).astype(outs[i].dtype)


def weigh_kernel(chips, later, *refs):
    ys, prec = refs[:chips], refs[chips]
    image, weighted, state = refs[-3:]
    p = prec[...]
    for m in range(image.shape[0]):
        y = ys[0][m]
        for ref in ys[1:]:
            y = y + ref[m].astype(F32)
        norm, cross = read_scalars(ys, m, 2)
        if later:
            old_image, old = refs[chips + 1 : chips + 3]
            old_norm, old_square = old[m, 0:1, 0:1], old[m, 1:2, 0:1]
            beta = norm / old_norm
            square = norm + 2.0 * beta * cross + beta * beta * old_square
            y = y + beta * old_image[m]
        else:
            beta = jnp.zeros_like(norm)
            square = norm
        scaled = p * y
        image[m] = y
        weighted[m] = with_scalars(scaled, [total(scaled * y)]).astype(BF16)
        sub = lax.broadcasted_iota(jnp.int32, (8, LANES), 0)
        state[m] = jnp.where(sub == 0, norm, jnp.where(sub == 1, square, beta))


def adjoint_kernel(dims, *refs):
    chips, n_obs = dims
    ws, own, partner = refs[:chips], refs[chips], refs[chips + 1]
    outs, acc = refs[-1 - 2 * n_obs : -1], refs[-1]
    z, core, obs = place()
    members, levp, width = ws[0].shape
    colblocks = own.shape[1]
    rows = members * levp
    energies = [read_scalars(ws, m, 1) for m in range(members)]
    for source in range(2):
        tiles = own if source == 0 else partner
        for i in range(chips):
            part = lax.dot_general(
                ws[i][...].reshape(rows, width),
                tiles[z ^ i].reshape(colblocks * LANES, width),
                NT,
                preferred_element_type=F32,
            )
            for k in range(colblocks):
                piece = part[:, k * LANES : (k + 1) * LANES]
                at = source * colblocks + k
                acc[at] = piece if i == 0 else acc[at] + piece
    for source in range(2):
        for i in range(n_obs):
            value = acc[source * colblocks + (obs ^ i)].reshape(members, levp, LANES)
            out = outs[source * n_obs + i]
            for m in range(members):
                out[m] = with_scalars(value[m], energies[m]).astype(BF16)


def update_kernel(parts, later, last, lev, *refs):
    pieces, (sd, vert, vert_t, state, residual) = refs[:parts], refs[parts : parts + 5]
    more = refs[parts + 5 :]
    old_direction = old_solution = None
    if later:
        old_direction, old_solution = more[:2]
        more = more[2:]
    for m in range(residual.shape[0]):
        t = pieces[0][m].astype(F32)
        for ref in pieces[1:]:
            t = t + ref[m].astype(F32)
        (energy,) = read_scalars(pieces, m, 1)
        norm, square, beta = state[m, 0:1, 0:1], state[m, 1:2, 0:1], state[m, 2:3, 0:1]
        alpha = norm / (square + energy)
        r = residual[m]
        d = r + beta * old_direction[m] if later else r
        q = d + dot(vert_t[...], sd[...] * t)
        solution = alpha * d
        if later:
            solution = old_solution[m] + solution
        r = r - alpha * q
        if last:
            increment_out, residual_out = more
            increment = sd[...] * dot(vert[...], solution)
            increment_out[0, m] = increment[0:lev]
            residual_out[0, m] = r[0:lev]
        else:
            residual_out, direction_out, solution_out, moved = more
            residual_out[m] = r
            direction_out[m] = d
            solution_out[m] = solution
            x = sd[...] * dot(vert[...], r)
            moved[m] = with_scalars(x, [total(r * r), total(r * d)]).astype(BF16)


def per_device(
    n_slab,
    n_obs,
    innovation,
    obs_precision,
    seeds,
    col_sd,
    vert_factor,
    h_values,
    block_obs,
    block_col,
    entry_count,
):
    blocks, lev, profiles = innovation.shape
    members = seeds.shape[0]
    groups, share = GROUPS, members // GROUPS
    chips = n_slab // 2
    halves = n_slab // blocks
    width = profiles // halves
    colblocks = n_obs
    assert halves * blocks == n_slab and width % LANES == 0 and col_sd.shape[0] == 1
    assert chips & (chips - 1) == 0 and n_obs & (n_obs - 1) == 0
    levp = (lev + 1 + 15) // 16 * 16
    rows = share * levp
    field = (share, levp, LANES)
    panel = (share, levp, width)
    pad = ((0, levp - lev), (0, levp - lev))
    vert = jnp.pad(vert_factor, pad)
    vert_t = jnp.pad(vert_factor.T, pad)
    h_block = h_values.reshape(h_values.shape[2:])
    product = 2 * n_slab * width * colblocks * LANES * rows
    small = 24 * rows * levp * LANES

    def across(x, i):
        return lax.ppermute(x, "slab", [(s, s ^ (2 * i)) for s in range(n_slab)])

    def beside(x, c, i):
        pairs = [
            (s * n_obs + o, (s ^ c) * n_obs + (o ^ i)) for s in range(n_slab) for o in range(n_obs)
        ]
        return lax.ppermute(x, ("slab", "obs"), pairs)

    def spread(outs):
        return [
            x if at == 0 else beside(x, at // n_obs, at % n_obs) for at, x in enumerate(outs)
        ]

    dense = struct((chips, colblocks, LANES, width), BF16)
    own, for_partner, *partials = call(
        functools.partial(start_kernel, (chips, n_obs, lev, halves, groups)),
        [dense, dense] + [struct(field, BF16)] * (groups * n_obs),
        [
            pltpu.VMEM((members, levp, profiles), F32),
            pltpu.VMEM((colblocks, members * levp, LANES), F32),
        ],
        product * groups,
        seeds,
        block_obs.reshape(-1),
        block_col.reshape(-1),
        entry_count.reshape(-1),
        innovation,
        obs_precision,
        h_block,
        scalars=4,
    )
    arrived = [spread(partials[g * n_obs : (g + 1) * n_obs]) for g in range(groups)]
    partner = beside(for_partner, 1, 0)
    (precision,) = call(
        functools.partial(precision_kernel, halves),
        [struct((levp, width), F32)],
        [],
        0,
        obs_precision,
    )
    state = [None] * groups
    direction = [None] * groups
    total_step = [None] * groups
    image = [None] * groups
    residual, moved, outputs = [], [], []
    for g in range(groups):
        r, x = call(
            functools.partial(first_kernel, n_obs),
            [struct(field, F32), struct(field, BF16)],
            [],
            small,
            *arrived[g],
            col_sd,
            vert,
            vert_t,
        )
        residual.append(r)
        moved.append(x)
    for sweep in range(ITERS):
        later, last = sweep > 0, sweep == ITERS - 1
        for g in range(groups):
            columns = spread([moved[g]] * (2 * n_obs))
            ys = call(
                functools.partial(forward_kernel, (chips, n_obs)),
                [struct(panel, F32)] + [struct(panel, BF16)] * (chips - 1),
                [pltpu.VMEM((rows, 2 * colblocks * LANES), BF16)],
                product,
                *columns,
                own,
                partner,
            )
            ys = [y if i == 0 else across(y, i) for i, y in enumerate(ys)]
            image[g], weighted, state[g] = call(
                functools.partial(weigh_kernel, chips, later),
                [struct(panel, F32), struct(panel, BF16), struct((share, 8, LANES), F32)],
                [],
                0,
                *ys,
                precision,
                *([image[g], state[g]] if later else []),
            )
            ws = [weighted if i == 0 else across(weighted, i) for i in range(chips)]
            ps = call(
                functools.partial(adjoint_kernel, (chips, n_obs)),
                [struct(field, BF16)] * (2 * n_obs),
                [pltpu.VMEM((2 * colblocks, rows, LANES), F32)],
                product,
                *ws,
                own,
                partner,
            )
            if last:
                outs = [struct((1, share, lev, LANES), F32)] * 2
            else:
                outs = [struct(field, F32)] * 3 + [struct(field, BF16)]
            results = call(
                functools.partial(update_kernel, 2 * n_obs, later, last, lev),
                outs,
                [],
                small,
                *spread(ps),
                col_sd,
                vert,
                vert_t,
                state[g],
                residual[g],
                *([direction[g], total_step[g]] if later else []),
            )
            if last:
                outputs.append(results)
            else:
                residual[g], direction[g], total_step[g], moved[g] = results
    if groups == 1:
        return tuple(outputs[0])
    return tuple(jnp.concatenate(parts, axis=1) for parts in zip(*outputs))


def solution(mesh):
    return jax.shard_map(
        functools.partial(per_device, mesh.shape["slab"], mesh.shape["obs"]),
        mesh=mesh,
        in_specs=(
            P("obs", None, None),
            P("obs", None, None),
            P(),
            P(("slab", "obs"), None),
            P(),
            P("slab", "obs", None, None, None),
            P("slab", "obs", None),
            P("slab", "obs", None),
            P("slab", "obs"),
        ),
        out_specs=(P(("slab", "obs"), None, None, None), P(("slab", "obs"), None, None, None)),
        check_vma=False,
    )
```

```python
import functools

import jax
import jax.numpy as jnp
from jax import lax
from jax.experimental import pallas as pl
from jax.experimental.pallas import tpu as pltpu
from jax.sharding import PartitionSpec as P

ITERS = 2
GROUPS = 1
PLANE_SUM = "permute"
PLANE_GATHER = "permute"
LINE_SUM = "permute"
LINE_GATHER = "permute"
LANES = 128
PIECES = 3
PRIME = 32749
VMEM = pl.BlockSpec(memory_space=pltpu.VMEM)
SMEM = pl.BlockSpec(memory_space=pltpu.SMEM)
F32 = jnp.float32
BF16 = jnp.bfloat16
NT = (((1,), (1,)), ((), ()))


def call(kernel, outs, scratch, flops, *args, scalars=0):
    nbytes = sum(a.size * a.dtype.itemsize for a in (*args, *outs))
    return pl.pallas_call(
        kernel,
        out_shape=outs,
        in_specs=[SMEM] * scalars + [VMEM] * (len(args) - scalars),
        out_specs=[VMEM] * len(outs),
        scratch_shapes=scratch,
        compiler_params=pltpu.CompilerParams(vmem_limit_bytes=40 * 1024 * 1024),
        cost_estimate=pl.CostEstimate(flops=flops, bytes_accessed=nbytes, transcendentals=0),
    )(*args)


def struct(shape, dtype):
    return jax.ShapeDtypeStruct(shape, dtype)


def place():
    slab = lax.axis_index("slab")
    return slab // 2, slab % 2, lax.axis_index("obs")


def views(refs, count, me):
    if len(refs) == 1:
        return [refs[0].at[me ^ i] for i in range(count)]
    return refs


def total(x):
    return jnp.sum(jnp.sum(x, axis=0, keepdims=True), axis=1, keepdims=True)


def with_scalars(body, values):
    rows = lax.broadcasted_iota(jnp.int32, body.shape, 0)
    lanes = lax.broadcasted_iota(jnp.int32, body.shape, 1)
    line = jnp.zeros(body.shape, F32)
    for q, value in enumerate(values):
        rest = value
        for piece in range(PIECES):
            part = rest.astype(BF16).astype(F32)
            rest = rest - part
            line = jnp.where(lanes == q * PIECES + piece, part, line)
    return jnp.where(rows == body.shape[0] - 1, line, body)


def read_scalars(refs, member, count):
    rows = refs[0].shape[1]
    tail = refs[0][member, rows - 16 : rows, 0:LANES].astype(F32)
    for ref in refs[1:]:
        tail = tail + ref[member, rows - 16 : rows, 0:LANES].astype(F32)
    sub = lax.broadcasted_iota(jnp.int32, tail.shape, 0)
    lanes = lax.broadcasted_iota(jnp.int32, tail.shape, 1)
    found = []
    for q in range(count):
        mine = (sub == 15) & (lanes >= q * PIECES) & (lanes < (q + 1) * PIECES)
        found.append(total(jnp.where(mine, tail, 0.0)))
    return found


def remainder(x, factor):
    return x - (x.astype(F32) * factor).astype(jnp.int32) * PRIME


def start_kernel(dims, seeds, ids, cols, count, innov, prec, h, own, partner, *rest):
    chips, n_obs, halves, groups = dims
    outs, (scratch, acc) = rest[:-2], rest[-2:]
    z, core, obs = place()
    lev, blocks, profiles = innov.shape
    colblocks, width = own.shape[1], own.shape[3]
    members = seeds.shape[0]
    levp = scratch.shape[2] // blocks
    strips = profiles // LANES

    own[...] = jnp.zeros_like(own)
    partner[...] = jnp.zeros_like(partner)

    def put(n, carry):
        b, k = ids[n], cols[n]
        for half in range(halves):
            piece = b * halves + half
            tile = h[n, :, half * width : (half + 1) * width]

            @pl.when(piece % 2 == core)
            def _():
                own[piece // 2, k] = tile

            @pl.when(piece % 2 != core)
            def _():
                partner[piece // 2, k] = tile

        return carry

    lax.fori_loop(0, count[0], put, 0)

    scratch[:, :, lev * blocks :, :] = jnp.zeros(
        (members, strips, (levp - lev) * blocks, LANES), F32
    )
    shape = (blocks, profiles)
    spot = (
        lax.broadcasted_iota(jnp.int32, shape, 0) + obs * blocks
    ) * (lev * profiles) + lax.broadcasted_iota(jnp.int32, shape, 1)
    starts = [lax.rem(seeds[m], PRIME) for m in range(members)]

    def draw(level, carry):
        base = remainder(7919 * remainder(spot + level * profiles, 1.0 / PRIME), 1.0 / PRIME)
        p = prec[level]
        gain = 3.4 * p * lax.rsqrt(p)
        offset = p * innov[level] - 0.5 * gain
        gain = gain * (1.0 / PRIME)
        at = pl.multiple_of(level * blocks, blocks)
        for m in range(members):
            k0 = base + starts[m]
            k0 = jnp.where(k0 >= PRIME, k0 - PRIME, k0)
            k1 = remainder(k0 * k0 + 12345, 1.0 / PRIME)
            k2 = remainder(k1 * k1 + 2719, 1.0 / PRIME)
            k2 = jnp.where(k2 < 0, k2 + PRIME, k2)
            k2 = jnp.where(k2 >= PRIME, k2 - PRIME, k2)
            w = offset + gain * k2.astype(F32)
            for t in range(strips):
                scratch[m, t, pl.ds(at, blocks), :] = w[:, t * LANES : (t + 1) * LANES]
        return carry

    lax.fori_loop(0, lev, draw, 0, unroll=3)

    for source in range(2):
        for zz in range(chips):
            piece = 2 * zz + (core if source == 0 else 1 - core)
            rows = pl.ds(piece // halves, levp, stride=blocks)
            strip = (piece % halves) * (width // LANES)
            w = [
                jnp.concatenate(
                    [scratch[m, strip + t, rows, :].astype(BF16) for t in range(width // LANES)],
                    axis=1,
                )
                for m in range(members)
            ]
            w = jnp.concatenate(w, axis=0)
            tiles = (own if source == 0 else partner)[zz].reshape(colblocks * LANES, width)
            part = lax.dot_general(w, tiles, NT, preferred_element_type=F32)
            for k in range(colblocks):
                piece_k = part[:, k * LANES : (k + 1) * LANES]
                acc[k] = piece_k if source + zz == 0 else acc[k] + piece_k

    share = members // groups
    for g in range(groups):
        for i, out in enumerate(views(outs[g::groups], n_obs, obs)):
            value = acc[obs ^ i].astype(BF16).reshape(members, levp, LANES)
            out[...] = value[g * share : (g + 1) * share]


def precision_kernel(halves, prec, out):
    z, core, unused = place()
    piece = 2 * z + core
    lev, blocks, unused = prec.shape
    width = out.shape[1]
    block = lax.broadcasted_iota(jnp.int32, (lev, blocks, width), 1)
    if halves == 1:
        mine = prec[...]
    else:
        mine = prec[:, :, pl.ds(pl.multiple_of((piece % halves) * width, LANES), width)]
    out[...] = jnp.zeros_like(out)
    out[0:lev, :] = jnp.sum(jnp.where(block == piece // halves, mine, 0.0), axis=1)


def dot(a, b):
    return jnp.dot(a, b, preferred_element_type=F32, precision=lax.Precision.HIGHEST)


def first_kernel(n_obs, *refs):
    (sd, vert, vert_t, residual, moved), pieces = refs[-5:], refs[:-5]
    pieces = views(pieces, n_obs, lax.axis_index("obs"))
    for m in range(residual.shape[0]):
        t = pieces[0][m].astype(F32)
        for ref in pieces[1:]:
            t = t + ref[m].astype(F32)
        r = dot(vert_t[...], sd[...] * t)
        residual[m] = r
        x = sd[...] * dot(vert[...], r)
        put_columns(moved, m, with_scalars(x, [total(r * r)]).astype(BF16))


def put_columns(moved, m, x):
    if len(moved.shape) == 3:
        moved[m] = x
    else:
        for i in range(moved.shape[0]):
            moved[i, m] = x


def forward_kernel(dims, *refs):
    chips, n_obs, n_columns, n_outs = dims
    z, core, obs = place()
    xs = []
    for source in range(2):
        xs += views(refs[source * n_columns : (source + 1) * n_columns], n_obs, obs)
    own, partner = refs[2 * n_columns : 2 * n_columns + 2]
    panel = refs[-1]
    outs = views(refs[-1 - n_outs : -1], chips, z)
    members, levp, unused = xs[0].shape
    colblocks, width = own.shape[1], own.shape[3]
    rows = members * levp
    for source in range(2):
        for i in range(n_obs):
            at = pl.multiple_of((source * colblocks + (obs ^ i)) * LANES, LANES)
            panel[:, pl.ds(at, LANES)] = xs[source * n_obs + i][...].reshape(rows, LANES)
    scalars = [read_scalars(xs, m, 2) for m in range(members)]
    half = colblocks * LANES
    for i in range(chips):
        zz = z ^ i
        y = jnp.dot(panel[:, 0:half], own[zz].reshape(half, width), preferred_element_type=F32)
        y = y + jnp.dot(
            panel[:, half : 2 * half], partner[zz].reshape(half, width), preferred_element_type=F32
        )
        y = y.reshape(members, levp, width)
        for m in range(members):
            outs[i][m] = with_scalars(y[m], scalars[m]).astype(outs[i].dtype)


def weigh_kernel(chips, later, n_ys, *refs):
    ys, prec = views(refs[:n_ys], chips, place()[0]), refs[n_ys]
    image, weighted, state = refs[-3:]
    p = prec[...]
    for m in range(image.shape[0]):
        y = ys[0][m].astype(F32)
        for ref in ys[1:]:
            y = y + ref[m].astype(F32)
        norm, cross = read_scalars(ys, m, 2)
        if later:
            old_image, old = refs[n_ys + 1 : n_ys + 3]
            old_norm, old_square = old[m, 0:1, 0:1], old[m, 1:2, 0:1]
            beta = norm / old_norm
            square = norm + 2.0 * beta * cross + beta * beta * old_square
            y = y + beta * old_image[m]
        else:
            beta = jnp.zeros_like(norm)
            square = norm
        scaled = p * y
        image[m] = y
        put_columns(weighted, m, with_scalars(scaled, [total(scaled * y)]).astype(BF16))
        sub = lax.broadcasted_iota(jnp.int32, (8, LANES), 0)
        state[m] = jnp.where(sub == 0, norm, jnp.where(sub == 1, square, beta))


def adjoint_kernel(dims, *refs):
    chips, n_obs, n_ws, n_outs, added = dims
    z, core, obs = place()
    ws, tiles = views(refs[:n_ws], chips, z), refs[n_ws]
    acc = refs[-1]
    outs = refs[-1 - n_outs : -1]
    members, levp, width = ws[0].shape
    colblocks = tiles.shape[1]
    rows = members * levp
    for i in range(chips):
        part = lax.dot_general(
            ws[i][...].reshape(rows, width),
            tiles[z ^ i].reshape(colblocks * LANES, width),
            NT,
            preferred_element_type=F32,
        )
        for k in range(colblocks):
            piece = part[:, k * LANES : (k + 1) * LANES]
            acc[k] = piece if i == 0 else acc[k] + piece
    if added:
        more = refs[n_ws + 1]
        outs = views(outs, n_obs, obs)
    for m in range(members):
        (energy,) = read_scalars(ws, m, 1)
        if added:
            energy = energy + read_scalars([more.at[0]], m, 1)[0]
        for i in range(n_obs):
            if added:
                value = acc[obs ^ i].reshape(members, levp, LANES)[m]
                value = value + more[obs ^ i, m].astype(F32)
                outs[i][m] = with_scalars(value, [energy]).astype(BF16)
            else:
                value = acc[i].reshape(members, levp, LANES)[m]
                outs[0][i, m] = with_scalars(value, [energy]).astype(BF16)


def update_kernel(n_obs, n_pieces, later, last, lev, *refs):
    pieces = views(refs[:n_pieces], n_obs, lax.axis_index("obs"))
    sd, vert, vert_t, state, residual = refs[n_pieces : n_pieces + 5]
    more = refs[n_pieces + 5 :]
    old_direction = old_solution = None
    if later:
        old_direction, old_solution = more[:2]
        more = more[2:]
    for m in range(residual.shape[0]):
        t = pieces[0][m].astype(F32)
        for ref in pieces[1:]:
            t = t + ref[m].astype(F32)
        (energy,) = read_scalars(pieces, m, 1)
        norm, square, beta = state[m, 0:1, 0:1], state[m, 1:2, 0:1], state[m, 2:3, 0:1]
        alpha = norm / (square + energy)
        r = residual[m]
        d = r + beta * old_direction[m] if later else r
        q = d + dot(vert_t[...], sd[...] * t)
        solution = alpha * d
        if later:
            solution = old_solution[m] + solution
        r = r - alpha * q
        if last:
            increment_out, residual_out = more
            increment = sd[...] * dot(vert[...], solution)
            increment_out[:, m, :] = increment[0:lev]
            residual_out[:, m, :] = r[0:lev]
        else:
            residual_out, direction_out, solution_out, moved = more
            residual_out[m] = r
            direction_out[m] = d
            solution_out[m] = solution
            x = sd[...] * dot(vert[...], r)
            put_columns(moved, m, with_scalars(x, [total(r * r), total(r * d)]).astype(BF16))


def per_device(
    n_slab,
    n_obs,
    innovation,
    obs_precision,
    seeds,
    col_sd,
    vert_factor,
    h_values,
    block_obs,
    block_col,
    entry_count,
):
    blocks, lev, profiles = innovation.shape
    members = seeds.shape[0]
    groups, share = GROUPS, members // GROUPS
    chips = n_slab // 2
    halves = n_slab // blocks
    width = profiles // halves
    colblocks = n_obs
    assert halves * blocks == n_slab and width % LANES == 0 and col_sd.shape[0] == 1
    assert chips & (chips - 1) == 0 and n_obs & (n_obs - 1) == 0
    levp = (lev + 1 + 15) // 16 * 16
    rows = share * levp
    field = (share, levp, LANES)
    panel = (share, levp, width)
    pad = ((0, levp - lev), (0, levp - lev))
    vert = jnp.pad(vert_factor, pad)
    vert_t = jnp.pad(vert_factor.T, pad)
    h_block = h_values.reshape(h_values.shape[2:])
    innovation = jnp.transpose(innovation, (1, 0, 2))
    obs_precision = jnp.transpose(obs_precision, (1, 0, 2))
    product = n_slab * width * colblocks * LANES * rows
    small = 24 * rows * levp * LANES
    cores = [[s for s in range(n_slab) if s % 2 == c] for c in range(2)]

    def along(x, i):
        return lax.ppermute(x, "slab", [(s, s ^ (2 * i)) for s in range(n_slab)])

    def plane(x, i):
        return lax.ppermute(x, "obs", [(o, o ^ i) for o in range(n_obs)])

    def swap(x):
        return lax.ppermute(x, "slab", [(s, s ^ 1) for s in range(n_slab)])

    def spread(mode, outs, move):
        if mode == "permute":
            return [x if i == 0 else move(x, i) for i, x in enumerate(outs)]
        if move is plane:
            return [lax.all_to_all(outs[0], "obs", 0, 0, tiled=True)]
        return [lax.all_to_all(outs[0], "slab", 0, 0, axis_index_groups=cores, tiled=True)]

    def copies(mode, x, count):
        return [x] * count if mode == "permute" else [x]

    def shapes(mode, shape, dtype, count):
        return [struct(shape, dtype)] * count if mode == "permute" else [struct((count, *shape), dtype)]

    dense = struct((chips, colblocks, LANES, width), BF16)
    partial_shapes = shapes(PLANE_SUM, field, BF16, n_obs)
    n_parts = len(partial_shapes)
    own, for_partner, *partials = call(
        functools.partial(start_kernel, (chips, n_obs, halves, groups)),
        [dense, dense] + [x for x in partial_shapes for g in range(groups)],
        [
            pltpu.VMEM((members, profiles // LANES, levp * blocks, LANES), F32),
            pltpu.VMEM((colblocks, members * levp, LANES), F32),
        ],
        2 * product * groups,
        seeds,
        block_obs.reshape(-1),
        block_col.reshape(-1),
        entry_count.reshape(-1),
        innovation,
        obs_precision,
        h_block,
        scalars=4,
    )
    arrived = [spread(PLANE_SUM, partials[g::groups], plane) for g in range(groups)]
    partner = swap(for_partner)
    (precision,) = call(
        functools.partial(precision_kernel, halves),
        [struct((levp, width), F32)],
        [],
        0,
        obs_precision,
    )
    state = [None] * groups
    direction = [None] * groups
    total_step = [None] * groups
    image = [None] * groups
    residual, moved, outputs = [], [], []
    (moved_shape,) = shapes(PLANE_GATHER, field, BF16, n_obs)[:1]
    (weighted_shape,) = shapes(LINE_GATHER, panel, BF16, chips)[:1]
    for g in range(groups):
        r, x = call(
            functools.partial(first_kernel, n_obs),
            [struct(field, F32), moved_shape],
            [],
            small,
            *arrived[g],
            col_sd,
            vert,
            vert_t,
        )
        residual.append(r)
        moved.append(x)
    for sweep in range(ITERS):
        later, last = sweep > 0, sweep == ITERS - 1
        for g in range(groups):
            columns = spread(PLANE_GATHER, copies(PLANE_GATHER, moved[g], n_obs), plane)
            others = [swap(x) for x in columns]
            image_shapes = shapes(LINE_SUM, panel, BF16, chips)
            if len(image_shapes) > 1:
                image_shapes[0] = struct(panel, F32)
            ys = call(
                functools.partial(
                    forward_kernel, (chips, n_obs, len(columns), len(image_shapes))
                ),
                image_shapes,
                [pltpu.VMEM((rows, 2 * colblocks * LANES), BF16)],
                2 * product,
                *columns,
                *others,
                own,
                partner,
            )
            ys = spread(LINE_SUM, ys, along)
            image[g], weighted, state[g] = call(
                functools.partial(weigh_kernel, chips, later, len(ys)),
                [struct(panel, F32), weighted_shape, struct((share, 8, LANES), F32)],
                [],
                0,
                *ys,
                precision,
                *([image[g], state[g]] if later else []),
            )
            ws = spread(LINE_GATHER, copies(LINE_GATHER, weighted, chips), along)
            acc = [pltpu.VMEM((colblocks, rows, LANES), F32)]
            (theirs,) = call(
                functools.partial(adjoint_kernel, (chips, n_obs, len(ws), 1, False)),
                [struct((n_obs, *field), BF16)],
                acc,
                product,
                *ws,
                partner,
            )
            ps = call(
                functools.partial(adjoint_kernel, (chips, n_obs, len(ws), n_parts, True)),
                partial_shapes,
                acc,
                product,
                *ws,
                own,
                swap(theirs),
            )
            ps = spread(PLANE_SUM, ps, plane)
            if last:
                outs = [struct((lev, share, LANES), F32)] * 2
            else:
                outs = [struct(field, F32)] * 3 + [moved_shape]
            results = call(
                functools.partial(update_kernel, n_obs, len(ps), later, last, lev),
                outs,
                [],
                small,
                *ps,
                col_sd,
                vert,
                vert_t,
                state[g],
                residual[g],
                *([direction[g], total_step[g]] if later else []),
            )
            if last:
                outputs.append(results)
            else:
                residual[g], direction[g], total_step[g], moved[g] = results
    outputs = [x[0] if groups == 1 else jnp.concatenate(x, axis=1) for x in zip(*outputs)]
    return tuple(jnp.transpose(x, (1, 0, 2))[None] for x in outputs)


def solution(mesh):
    return jax.shard_map(
        functools.partial(per_device, mesh.shape["slab"], mesh.shape["obs"]),
        mesh=mesh,
        in_specs=(
            P("obs", None, None),
            P("obs", None, None),
            P(),
            P(("slab", "obs"), None),
            P(),
            P("slab", "obs", None, None, None),
            P("slab", "obs", None),
            P("slab", "obs", None),
            P("slab", "obs"),
        ),
        out_specs=(P(("slab", "obs"), None, None, None), P(("slab", "obs"), None, None, None)),
        check_vma=False,
    )
```

```python
import functools

import jax
import jax.numpy as jnp
from jax import lax
from jax.experimental import pallas as pl
from jax.experimental.pallas import tpu as pltpu
from jax.sharding import PartitionSpec as P

ITERS = 2
GROUPS = 1
PLANE_SUM = "whole"
PLANE_GATHER = "whole"
LINE_SUM = "whole"
LINE_GATHER = "permute"
LANES = 128
PIECES = 3
PRIME = 32749
VMEM = pl.BlockSpec(memory_space=pltpu.VMEM)
HBM = pl.BlockSpec(memory_space=pltpu.HBM)
F32 = jnp.float32
BF16 = jnp.bfloat16
NT = (((1,), (1,)), ((), ()))


def call(kernel, outs, scratch, flops, *args, space=VMEM, limit=40):
    nbytes = sum(a.size * a.dtype.itemsize for a in (*args, *outs))
    return pl.pallas_call(
        kernel,
        out_shape=outs,
        in_specs=[space] * len(args),
        out_specs=[VMEM] * len(outs),
        scratch_shapes=scratch,
        compiler_params=pltpu.CompilerParams(vmem_limit_bytes=limit * 1024 * 1024),
        cost_estimate=pl.CostEstimate(flops=flops, bytes_accessed=nbytes, transcendentals=0),
    )(*args)


def struct(shape, dtype):
    return jax.ShapeDtypeStruct(shape, dtype)


def place():
    slab = lax.axis_index("slab")
    return slab // 2, slab % 2, lax.axis_index("obs")


def views(refs, count, me):
    if len(refs) == 1:
        return [refs[0].at[me ^ i] for i in range(count)]
    return refs


def total(x):
    return jnp.sum(jnp.sum(x, axis=0, keepdims=True), axis=1, keepdims=True)


def with_scalars(body, values):
    rows = lax.broadcasted_iota(jnp.int32, body.shape, 0)
    lanes = lax.broadcasted_iota(jnp.int32, body.shape, 1)
    line = jnp.zeros(body.shape, F32)
    for q, value in enumerate(values):
        rest = value
        for piece in range(PIECES):
            part = rest.astype(BF16).astype(F32)
            rest = rest - part
            line = jnp.where(lanes == q * PIECES + piece, part, line)
    return jnp.where(rows == body.shape[0] - 1, line, body)


def read_scalars(refs, member, count):
    rows = refs[0].shape[1]
    tail = refs[0][member, rows - 16 : rows, 0:LANES].astype(F32)
    for ref in refs[1:]:
        tail = tail + ref[member, rows - 16 : rows, 0:LANES].astype(F32)
    sub = lax.broadcasted_iota(jnp.int32, tail.shape, 0)
    lanes = lax.broadcasted_iota(jnp.int32, tail.shape, 1)
    found = []
    for q in range(count):
        mine = (sub == 15) & (lanes >= q * PIECES) & (lanes < (q + 1) * PIECES)
        found.append(total(jnp.where(mine, tail, 0.0)))
    return found


def remainder(x, factor):
    return x - (x.astype(F32) * factor).astype(jnp.int32) * PRIME


def start_kernel(dims, seeds_in, ids_in, cols_in, count_in, innov_in, prec_in, h, own, partner, *rest):
    chips, n_obs, halves, groups = dims
    outs = rest[:-11]
    seeds, ids, cols, count, innov, prec, hashed, scratch, acc, sems, h_sems = rest[-11:]
    z, core, obs = place()
    blocks, lev, profiles = innov.shape
    colblocks, width = own.shape[1], own.shape[3]
    members, levp = scratch.shape[0], scratch.shape[1]

    pairs = [(seeds_in, seeds), (ids_in, ids), (cols_in, cols), (count_in, count)]
    small = [pltpu.make_async_copy(x, y, sems.at[i]) for i, (x, y) in enumerate(pairs)]
    for copy in small:
        copy.start()
    large = []
    for b in range(blocks):
        at = len(pairs) + 2 * b
        large.append(pltpu.make_async_copy(innov_in.at[:, b, :], innov.at[b], sems.at[at]))
        large.append(pltpu.make_async_copy(prec_in.at[:, b, :], prec.at[b], sems.at[at + 1]))
    for copy in large:
        copy.start()
    own[...] = jnp.zeros_like(own)
    partner[...] = jnp.zeros_like(partner)
    scratch[...] = jnp.zeros_like(scratch)
    for copy in small:
        copy.wait()

    def tile_copy(n, half, target):
        lanes = pl.ds(half * width, width)
        return pltpu.make_async_copy(h.at[n, :, lanes], target, h_sems.at[n * halves + half])

    def put(n, carry):
        for half in range(halves):
            piece, k = ids[0, 0, n] * halves + half, cols[0, 0, n]

            @pl.when(piece % 2 == core)
            def _():
                tile_copy(n, half, own.at[piece // 2, k]).start()

            @pl.when(piece % 2 != core)
            def _():
                tile_copy(n, half, partner.at[piece // 2, k]).start()

        return carry

    lax.fori_loop(0, count[0, 0], put, 0)

    starts = [lax.rem(seeds[m], PRIME) for m in range(members)]
    order = [(source, zz) for source in range(2) for zz in range(chips)]
    shape = (levp, width)
    spot = lax.broadcasted_iota(jnp.int32, shape, 0) * profiles
    spot = spot + lax.broadcasted_iota(jnp.int32, shape, 1)
    for at, (source, zz) in enumerate(order):
        piece = 2 * zz + (core if source == 0 else 1 - core)
        first = (obs * blocks + piece // halves) * (lev * profiles) + (piece % halves) * width
        base = remainder(7919 * remainder(spot + first, 1.0 / PRIME), 1.0 / PRIME)
        for m in range(members):
            k0 = base + starts[m]
            k0 = jnp.where(k0 >= PRIME, k0 - PRIME, k0)
            k1 = remainder(k0 * k0 + 12345, 1.0 / PRIME)
            k2 = remainder(k1 * k1 + 2719, 1.0 / PRIME)
            k2 = jnp.where(k2 < 0, k2 + PRIME, k2)
            k2 = jnp.where(k2 >= PRIME, k2 - PRIME, k2)
            hashed[at, m] = k2.astype(F32)

    for copy in large:
        copy.wait()

    def arrive(n, carry):
        for half in range(halves):
            tile_copy(n, half, own.at[0, 0]).wait()
        return carry

    lax.fori_loop(0, count[0, 0], arrive, 0)

    for at, (source, zz) in enumerate(order):
        piece = 2 * zz + (core if source == 0 else 1 - core)
        b = piece // halves
        if halves == 1:
            p, d = prec[b], innov[b]
        else:
            lanes = pl.ds(pl.multiple_of((piece % halves) * width, LANES), width)
            p, d = prec[b, :, lanes], innov[b, :, lanes]
        gain = 3.4 * p * lax.rsqrt(p)
        offset = p * d - 0.5 * gain
        gain = gain * (1.0 / PRIME)
        for m in range(members):
            scratch[m, 0:lev, :] = offset + gain * hashed[at, m, 0:lev, :]
        w = scratch[...].astype(BF16).reshape(members * levp, width)
        tiles = (own if source == 0 else partner)[zz].reshape(colblocks * LANES, width)
        part = lax.dot_general(w, tiles, NT, preferred_element_type=F32)
        for k in range(colblocks):
            piece_k = part[:, k * LANES : (k + 1) * LANES]
            acc[k] = piece_k if at == 0 else acc[k] + piece_k

    share = members // groups
    for g in range(groups):
        for i, out in enumerate(views(outs[g::groups], n_obs, obs)):
            value = acc[obs ^ i].astype(BF16).reshape(members, levp, LANES)
            out[...] = value[g * share : (g + 1) * share]


def precision_kernel(halves, prec, out):
    z, core, unused = place()
    piece = 2 * z + core
    lev, blocks, unused = prec.shape
    width = out.shape[1]
    block = lax.broadcasted_iota(jnp.int32, (lev, blocks, width), 1)
    if halves == 1:
        mine = prec[...]
    else:
        mine = prec[:, :, pl.ds(pl.multiple_of((piece % halves) * width, LANES), width)]
    out[...] = jnp.zeros_like(out)
    out[0:lev, :] = jnp.sum(jnp.where(block == piece // halves, mine, 0.0), axis=1)


def dot(a, b):
    return jnp.dot(a, b, preferred_element_type=F32, precision=lax.Precision.HIGHEST)


def first_kernel(n_obs, *refs):
    (sd, vert, vert_t, residual, moved), pieces = refs[-5:], refs[:-5]
    pieces = views(pieces, n_obs, lax.axis_index("obs"))
    for m in range(residual.shape[0]):
        t = pieces[0][m].astype(F32)
        for ref in pieces[1:]:
            t = t + ref[m].astype(F32)
        r = dot(vert_t[...], sd[...] * t)
        residual[m] = r
        x = sd[...] * dot(vert[...], r)
        put_columns(moved, m, with_scalars(x, [total(r * r)]).astype(BF16))


def put_columns(moved, m, x):
    if len(moved.shape) == 3:
        moved[m] = x
    else:
        for i in range(moved.shape[0]):
            moved[i, m] = x


def forward_kernel(dims, *refs):
    chips, n_obs, n_columns, n_outs = dims
    z, core, obs = place()
    xs = []
    for source in range(2):
        xs += views(refs[source * n_columns : (source + 1) * n_columns], n_obs, obs)
    own, partner = refs[2 * n_columns : 2 * n_columns + 2]
    panel = refs[-1]
    outs = views(refs[-1 - n_outs : -1], chips, z)
    members, levp, unused = xs[0].shape
    colblocks, width = own.shape[1], own.shape[3]
    rows = members * levp
    for source in range(2):
        for i in range(n_obs):
            at = pl.multiple_of((source * colblocks + (obs ^ i)) * LANES, LANES)
            panel[:, pl.ds(at, LANES)] = xs[source * n_obs + i][...].reshape(rows, LANES)
    scalars = [read_scalars(xs, m, 2) for m in range(members)]
    half = colblocks * LANES
    for i in range(chips):
        zz = z ^ i
        y = jnp.dot(panel[:, 0:half], own[zz].reshape(half, width), preferred_element_type=F32)
        y = y + jnp.dot(
            panel[:, half : 2 * half], partner[zz].reshape(half, width), preferred_element_type=F32
        )
        y = y.reshape(members, levp, width)
        for m in range(members):
            outs[i][m] = with_scalars(y[m], scalars[m]).astype(outs[i].dtype)


def weigh_kernel(chips, later, n_ys, *refs):
    ys, prec = views(refs[:n_ys], chips, place()[0]), refs[n_ys]
    image, weighted, state = refs[-3:]
    p = prec[...]
    for m in range(image.shape[0]):
        y = ys[0][m].astype(F32)
        for ref in ys[1:]:
            y = y + ref[m].astype(F32)
        norm, cross = read_scalars(ys, m, 2)
        if later:
            old_image, old = refs[n_ys + 1 : n_ys + 3]
            old_norm, old_square = old[m, 0:1, 0:1], old[m, 1:2, 0:1]
            beta = norm / old_norm
            square = norm + 2.0 * beta * cross + beta * beta * old_square
            y = y + beta * old_image[m]
        else:
            beta = jnp.zeros_like(norm)
            square = norm
        scaled = p * y
        image[m] = y
        put_columns(weighted, m, with_scalars(scaled, [total(scaled * y)]).astype(BF16))
        sub = lax.broadcasted_iota(jnp.int32, (8, LANES), 0)
        state[m] = jnp.where(sub == 0, norm, jnp.where(sub == 1, square, beta))


def adjoint_kernel(dims, *refs):
    chips, n_obs, n_ws, n_outs, added = dims
    z, core, obs = place()
    ws, tiles = views(refs[:n_ws], chips, z), refs[n_ws]
    acc = refs[-1]
    outs = refs[-1 - n_outs : -1]
    members, levp, width = ws[0].shape
    colblocks = tiles.shape[1]
    rows = members * levp
    for i in range(chips):
        part = lax.dot_general(
            ws[i][...].reshape(rows, width),
            tiles[z ^ i].reshape(colblocks * LANES, width),
            NT,
            preferred_element_type=F32,
        )
        for k in range(colblocks):
            piece = part[:, k * LANES : (k + 1) * LANES]
            acc[k] = piece if i == 0 else acc[k] + piece
    if added:
        more = refs[n_ws + 1]
        outs = views(outs, n_obs, obs)
    for m in range(members):
        (energy,) = read_scalars(ws, m, 1)
        if added:
            energy = energy + read_scalars([more.at[0]], m, 1)[0]
        for i in range(n_obs):
            if added:
                value = acc[obs ^ i].reshape(members, levp, LANES)[m]
                value = value + more[obs ^ i, m].astype(F32)
                outs[i][m] = with_scalars(value, [energy]).astype(BF16)
            else:
                value = acc[i].reshape(members, levp, LANES)[m]
                outs[0][i, m] = with_scalars(value, [energy]).astype(BF16)


def update_kernel(n_obs, n_pieces, later, last, lev, *refs):
    pieces = views(refs[:n_pieces], n_obs, lax.axis_index("obs"))
    sd, vert, vert_t, state, residual = refs[n_pieces : n_pieces + 5]
    more = refs[n_pieces + 5 :]
    old_direction = old_solution = None
    if later:
        old_direction, old_solution = more[:2]
        more = more[2:]
    for m in range(residual.shape[0]):
        t = pieces[0][m].astype(F32)
        for ref in pieces[1:]:
            t = t + ref[m].astype(F32)
        (energy,) = read_scalars(pieces, m, 1)
        norm, square, beta = state[m, 0:1, 0:1], state[m, 1:2, 0:1], state[m, 2:3, 0:1]
        alpha = norm / (square + energy)
        r = residual[m]
        d = r + beta * old_direction[m] if later else r
        q = d + dot(vert_t[...], sd[...] * t)
        solution = alpha * d
        if later:
            solution = old_solution[m] + solution
        r = r - alpha * q
        if last:
            increment_out, residual_out = more
            increment = sd[...] * dot(vert[...], solution)
            increment_out[:, m, :] = increment[0:lev]
            residual_out[:, m, :] = r[0:lev]
        else:
            residual_out, direction_out, solution_out, moved = more
            residual_out[m] = r
            direction_out[m] = d
            solution_out[m] = solution
            x = sd[...] * dot(vert[...], r)
            put_columns(moved, m, with_scalars(x, [total(r * r), total(r * d)]).astype(BF16))


def per_device(
    n_slab,
    n_obs,
    innovation,
    obs_precision,
    seeds,
    col_sd,
    vert_factor,
    h_values,
    block_obs,
    block_col,
    entry_count,
):
    blocks, lev, profiles = innovation.shape
    members = seeds.shape[0]
    groups, share = GROUPS, members // GROUPS
    chips = n_slab // 2
    halves = n_slab // blocks
    width = profiles // halves
    colblocks = n_obs
    assert halves * blocks == n_slab and width % LANES == 0 and col_sd.shape[0] == 1
    assert chips & (chips - 1) == 0 and n_obs & (n_obs - 1) == 0
    levp = (lev + 1 + 15) // 16 * 16
    rows = share * levp
    field = (share, levp, LANES)
    panel = (share, levp, width)
    pad = ((0, levp - lev), (0, levp - lev))
    vert = jnp.pad(vert_factor, pad)
    vert_t = jnp.pad(vert_factor.T, pad)
    h_block = h_values.reshape(h_values.shape[2:])
    innovation = jnp.transpose(innovation, (1, 0, 2))
    obs_precision = jnp.transpose(obs_precision, (1, 0, 2))
    product = n_slab * width * colblocks * LANES * rows
    small = 24 * rows * levp * LANES
    cores = [[s for s in range(n_slab) if s % 2 == c] for c in range(2)]

    def along(x, i):
        return lax.ppermute(x, "slab", [(s, s ^ (2 * i)) for s in range(n_slab)])

    def plane(x, i):
        return lax.ppermute(x, "obs", [(o, o ^ i) for o in range(n_obs)])

    def swap(x):
        return lax.ppermute(x, "slab", [(s, s ^ 1) for s in range(n_slab)])

    def spread(mode, outs, move):
        if mode == "permute":
            return [x if i == 0 else move(x, i) for i, x in enumerate(outs)]
        if move is plane:
            return [lax.all_to_all(outs[0], "obs", 0, 0, tiled=True)]
        return [lax.all_to_all(outs[0], "slab", 0, 0, axis_index_groups=cores, tiled=True)]

    def copies(mode, x, count):
        return [x] * count if mode == "permute" else [x]

    def shapes(mode, shape, dtype, count):
        return [struct(shape, dtype)] * count if mode == "permute" else [struct((count, *shape), dtype)]

    dense = struct((chips, colblocks, LANES, width), BF16)
    partial_shapes = shapes(PLANE_SUM, field, BF16, n_obs)
    n_parts = len(partial_shapes)
    own, for_partner, *partials = call(
        functools.partial(start_kernel, (chips, n_obs, halves, groups)),
        [dense, dense] + [x for x in partial_shapes for g in range(groups)],
        [
            pltpu.SMEM(seeds.shape, jnp.int32),
            pltpu.SMEM(block_obs.shape, jnp.int32),
            pltpu.SMEM(block_col.shape, jnp.int32),
            pltpu.SMEM(entry_count.shape, jnp.int32),
            pltpu.VMEM((blocks, lev, profiles), F32),
            pltpu.VMEM((blocks, lev, profiles), F32),
            pltpu.VMEM((n_slab, members, levp, width), F32),
            pltpu.VMEM((members, levp, width), F32),
            pltpu.VMEM((colblocks, members * levp, LANES), F32),
            pltpu.SemaphoreType.DMA((4 + 2 * blocks,)),
            pltpu.SemaphoreType.DMA((h_block.shape[0] * halves,)),
        ],
        2 * product * groups,
        seeds,
        block_obs,
        block_col,
        entry_count,
        innovation,
        obs_precision,
        h_block,
        space=HBM,
        limit=60,
    )
    arrived = [spread(PLANE_SUM, partials[g::groups], plane) for g in range(groups)]
    partner = swap(for_partner)
    (precision,) = call(
        functools.partial(precision_kernel, halves),
        [struct((levp, width), F32)],
        [],
        0,
        obs_precision,
    )
    state = [None] * groups
    direction = [None] * groups
    total_step = [None] * groups
    image = [None] * groups
    residual, moved, outputs = [], [], []
    (moved_shape,) = shapes(PLANE_GATHER, field, BF16, n_obs)[:1]
    (weighted_shape,) = shapes(LINE_GATHER, panel, BF16, chips)[:1]
    for g in range(groups):
        r, x = call(
            functools.partial(first_kernel, n_obs),
            [struct(field, F32), moved_shape],
            [],
            small,
            *arrived[g],
            col_sd,
            vert,
            vert_t,
        )
        residual.append(r)
        moved.append(x)
    for sweep in range(ITERS):
        later, last = sweep > 0, sweep == ITERS - 1
        for g in range(groups):
            columns = spread(PLANE_GATHER, copies(PLANE_GATHER, moved[g], n_obs), plane)
            others = [swap(x) for x in columns]
            image_shapes = shapes(LINE_SUM, panel, BF16, chips)
            if len(image_shapes) > 1:
                image_shapes[0] = struct(panel, F32)
            ys = call(
                functools.partial(
                    forward_kernel, (chips, n_obs, len(columns), len(image_shapes))
                ),
                image_shapes,
                [pltpu.VMEM((rows, 2 * colblocks * LANES), BF16)],
                2 * product,
                *columns,
                *others,
                own,
                partner,
            )
            ys = spread(LINE_SUM, ys, along)
            image[g], weighted, state[g] = call(
                functools.partial(weigh_kernel, chips, later, len(ys)),
                [struct(panel, F32), weighted_shape, struct((share, 8, LANES), F32)],
                [],
                0,
                *ys,
                precision,
                *([image[g], state[g]] if later else []),
            )
            ws = spread(LINE_GATHER, copies(LINE_GATHER, weighted, chips), along)
            acc = [pltpu.VMEM((colblocks, rows, LANES), F32)]
            (theirs,) = call(
                functools.partial(adjoint_kernel, (chips, n_obs, len(ws), 1, False)),
                [struct((n_obs, *field), BF16)],
                acc,
                product,
                *ws,
                partner,
            )
            ps = call(
                functools.partial(adjoint_kernel, (chips, n_obs, len(ws), n_parts, True)),
                partial_shapes,
                acc,
                product,
                *ws,
                own,
                swap(theirs),
            )
            ps = spread(PLANE_SUM, ps, plane)
            if last:
                outs = [struct((lev, share, LANES), F32)] * 2
            else:
                outs = [struct(field, F32)] * 3 + [moved_shape]
            results = call(
                functools.partial(update_kernel, n_obs, len(ps), later, last, lev),
                outs,
                [],
                small,
                *ps,
                col_sd,
                vert,
                vert_t,
                state[g],
                residual[g],
                *([direction[g], total_step[g]] if later else []),
            )
            if last:
                outputs.append(results)
            else:
                residual[g], direction[g], total_step[g], moved[g] = results
    outputs = [x[0] if groups == 1 else jnp.concatenate(x, axis=1) for x in zip(*outputs)]
    return tuple(jnp.transpose(x, (1, 0, 2))[None] for x in outputs)


def solution(mesh):
    return jax.shard_map(
        functools.partial(per_device, mesh.shape["slab"], mesh.shape["obs"]),
        mesh=mesh,
        in_specs=(
            P("obs", None, None),
            P("obs", None, None),
            P(),
            P(("slab", "obs"), None),
            P(),
            P("slab", "obs", None, None, None),
            P("slab", "obs", None),
            P("slab", "obs", None),
            P("slab", "obs"),
        ),
        out_specs=(P(("slab", "obs"), None, None, None), P(("slab", "obs"), None, None, None)),
        check_vma=False,
    )
```

```python
import functools

import jax
import jax.numpy as jnp
from jax import lax
from jax.experimental import pallas as pl
from jax.experimental.pallas import tpu as pltpu
from jax.sharding import PartitionSpec as P

ITERS = 2
GROUPS = 2
PLANE_SUM = "permute"
PLANE_GATHER = "permute"
LINE_SUM = "permute"
LINE_GATHER = "permute"
LANES = 128
PIECES = 3
PRIME = 32749
VMEM = pl.BlockSpec(memory_space=pltpu.VMEM)
HBM = pl.BlockSpec(memory_space=pltpu.HBM)
F32 = jnp.float32
BF16 = jnp.bfloat16
NT = (((1,), (1,)), ((), ()))


def call(kernel, outs, scratch, flops, *args, space=VMEM, limit=40):
    nbytes = sum(a.size * a.dtype.itemsize for a in (*args, *outs))
    return pl.pallas_call(
        kernel,
        out_shape=outs,
        in_specs=[space] * len(args),
        out_specs=[VMEM] * len(outs),
        scratch_shapes=scratch,
        compiler_params=pltpu.CompilerParams(vmem_limit_bytes=limit * 1024 * 1024),
        cost_estimate=pl.CostEstimate(flops=flops, bytes_accessed=nbytes, transcendentals=0),
    )(*args)


def struct(shape, dtype):
    return jax.ShapeDtypeStruct(shape, dtype)


def place():
    slab = lax.axis_index("slab")
    return slab // 2, slab % 2, lax.axis_index("obs")


def views(refs, count, me):
    if len(refs) == 1:
        return [refs[0].at[me ^ i] for i in range(count)]
    return refs


def total(x):
    return jnp.sum(jnp.sum(x, axis=0, keepdims=True), axis=1, keepdims=True)


def with_scalars(body, values):
    rows = lax.broadcasted_iota(jnp.int32, body.shape, 0)
    lanes = lax.broadcasted_iota(jnp.int32, body.shape, 1)
    line = jnp.zeros(body.shape, F32)
    for q, value in enumerate(values):
        rest = value
        for piece in range(PIECES):
            part = rest.astype(BF16).astype(F32)
            rest = rest - part
            line = jnp.where(lanes == q * PIECES + piece, part, line)
    return jnp.where(rows == body.shape[0] - 1, line, body)


def read_scalars(refs, member, count):
    rows = refs[0].shape[1]
    tail = refs[0][member, rows - 16 : rows, 0:LANES].astype(F32)
    for ref in refs[1:]:
        tail = tail + ref[member, rows - 16 : rows, 0:LANES].astype(F32)
    sub = lax.broadcasted_iota(jnp.int32, tail.shape, 0)
    lanes = lax.broadcasted_iota(jnp.int32, tail.shape, 1)
    found = []
    for q in range(count):
        mine = (sub == 15) & (lanes >= q * PIECES) & (lanes < (q + 1) * PIECES)
        found.append(total(jnp.where(mine, tail, 0.0)))
    return found


def remainder(x, factor):
    return x - (x.astype(F32) * factor).astype(jnp.int32) * PRIME


def start_kernel(dims, seeds_in, ids_in, cols_in, count_in, innov_in, prec_in, h, own, partner, *rest):
    chips, n_obs, halves, groups = dims
    outs = rest[:-11]
    seeds, ids, cols, count, innov, prec, hashed, scratch, acc, sems, h_sems = rest[-11:]
    z, core, obs = place()
    blocks, lev, profiles = innov.shape
    colblocks, width = own.shape[1], own.shape[3]
    members, levp = scratch.shape[0], scratch.shape[1]

    pairs = [(seeds_in, seeds), (ids_in, ids), (cols_in, cols), (count_in, count)]
    small = [pltpu.make_async_copy(x, y, sems.at[i]) for i, (x, y) in enumerate(pairs)]
    for copy in small:
        copy.start()
    large = []
    for b in range(blocks):
        at = len(pairs) + 2 * b
        large.append(pltpu.make_async_copy(innov_in.at[:, b, :], innov.at[b], sems.at[at]))
        large.append(pltpu.make_async_copy(prec_in.at[:, b, :], prec.at[b], sems.at[at + 1]))
    for copy in large:
        copy.start()
    own[...] = jnp.zeros_like(own)
    partner[...] = jnp.zeros_like(partner)
    scratch[...] = jnp.zeros_like(scratch)
    for copy in small:
        copy.wait()

    def tile_copy(n, half, target):
        lanes = pl.ds(half * width, width)
        return pltpu.make_async_copy(h.at[n, :, lanes], target, h_sems.at[n * halves + half])

    def put(n, carry):
        for half in range(halves):
            piece, k = ids[0, 0, n] * halves + half, cols[0, 0, n]

            @pl.when(piece % 2 == core)
            def _():
                tile_copy(n, half, own.at[piece // 2, k]).start()

            @pl.when(piece % 2 != core)
            def _():
                tile_copy(n, half, partner.at[piece // 2, k]).start()

        return carry

    lax.fori_loop(0, count[0, 0], put, 0)

    starts = [lax.rem(seeds[m], PRIME) for m in range(members)]
    order = [(source, zz) for source in range(2) for zz in range(chips)]
    shape = (levp, width)
    spot = lax.broadcasted_iota(jnp.int32, shape, 0) * profiles
    spot = spot + lax.broadcasted_iota(jnp.int32, shape, 1)
    for at, (source, zz) in enumerate(order):
        piece = 2 * zz + (core if source == 0 else 1 - core)
        first = (obs * blocks + piece // halves) * (lev * profiles) + (piece % halves) * width
        base = remainder(7919 * remainder(spot + first, 1.0 / PRIME), 1.0 / PRIME)
        for m in range(members):
            k0 = base + starts[m]
            k0 = jnp.where(k0 >= PRIME, k0 - PRIME, k0)
            k1 = remainder(k0 * k0 + 12345, 1.0 / PRIME)
            k2 = remainder(k1 * k1 + 2719, 1.0 / PRIME)
            k2 = jnp.where(k2 < 0, k2 + PRIME, k2)
            k2 = jnp.where(k2 >= PRIME, k2 - PRIME, k2)
            hashed[at, m] = k2.astype(F32)

    for copy in large:
        copy.wait()

    def arrive(n, carry):
        for half in range(halves):
            tile_copy(n, half, own.at[0, 0]).wait()
        return carry

    lax.fori_loop(0, count[0, 0], arrive, 0)

    for at, (source, zz) in enumerate(order):
        piece = 2 * zz + (core if source == 0 else 1 - core)
        b = piece // halves
        if halves == 1:
            p, d = prec[b], innov[b]
        else:
            lanes = pl.ds(pl.multiple_of((piece % halves) * width, LANES), width)
            p, d = prec[b, :, lanes], innov[b, :, lanes]
        gain = 3.4 * p * lax.rsqrt(p)
        offset = p * d - 0.5 * gain
        gain = gain * (1.0 / PRIME)
        for m in range(members):
            scratch[m, 0:lev, :] = offset + gain * hashed[at, m, 0:lev, :]
        w = scratch[...].astype(BF16).reshape(members * levp, width)
        tiles = (own if source == 0 else partner)[zz].reshape(colblocks * LANES, width)
        part = lax.dot_general(w, tiles, NT, preferred_element_type=F32)
        for k in range(colblocks):
            piece_k = part[:, k * LANES : (k + 1) * LANES]
            acc[k] = piece_k if at == 0 else acc[k] + piece_k

    share = members // groups
    for g in range(groups):
        for i, out in enumerate(views(outs[g::groups], n_obs, obs)):
            value = acc[obs ^ i].astype(BF16).reshape(members, levp, LANES)
            out[...] = value[g * share : (g + 1) * share]


def precision_kernel(halves, prec, out):
    z, core, unused = place()
    piece = 2 * z + core
    lev, blocks, unused = prec.shape
    width = out.shape[1]
    block = lax.broadcasted_iota(jnp.int32, (lev, blocks, width), 1)
    if halves == 1:
        mine = prec[...]
    else:
        mine = prec[:, :, pl.ds(pl.multiple_of((piece % halves) * width, LANES), width)]
    out[...] = jnp.zeros_like(out)
    out[0:lev, :] = jnp.sum(jnp.where(block == piece // halves, mine, 0.0), axis=1)


def dot(a, b):
    return jnp.dot(a, b, preferred_element_type=F32, precision=lax.Precision.HIGHEST)


def first_kernel(n_obs, *refs):
    (sd, vert, vert_t, residual, moved), pieces = refs[-5:], refs[:-5]
    pieces = views(pieces, n_obs, lax.axis_index("obs"))
    for m in range(residual.shape[0]):
        t = pieces[0][m].astype(F32)
        for ref in pieces[1:]:
            t = t + ref[m].astype(F32)
        r = dot(vert_t[...], sd[...] * t)
        residual[m] = r
        x = sd[...] * dot(vert[...], r)
        put_columns(moved, m, with_scalars(x, [total(r * r)]).astype(BF16))


def put_columns(moved, m, x):
    if len(moved.shape) == 3:
        moved[m] = x
    else:
        for i in range(moved.shape[0]):
            moved[i, m] = x


def forward_kernel(dims, *refs):
    chips, n_obs, n_columns, n_outs = dims
    z, core, obs = place()
    xs = []
    for source in range(2):
        xs += views(refs[source * n_columns : (source + 1) * n_columns], n_obs, obs)
    own, partner = refs[2 * n_columns : 2 * n_columns + 2]
    panel = refs[-1]
    outs = views(refs[-1 - n_outs : -1], chips, z)
    members, levp, unused = xs[0].shape
    colblocks, width = own.shape[1], own.shape[3]
    rows = members * levp
    for source in range(2):
        for i in range(n_obs):
            at = pl.multiple_of((source * colblocks + (obs ^ i)) * LANES, LANES)
            panel[:, pl.ds(at, LANES)] = xs[source * n_obs + i][...].reshape(rows, LANES)
    scalars = [read_scalars(xs, m, 2) for m in range(members)]
    half = colblocks * LANES
    for i in range(chips):
        zz = z ^ i
        y = jnp.dot(panel[:, 0:half], own[zz].reshape(half, width), preferred_element_type=F32)
        y = y + jnp.dot(
            panel[:, half : 2 * half], partner[zz].reshape(half, width), preferred_element_type=F32
        )
        y = y.reshape(members, levp, width)
        for m in range(members):
            outs[i][m] = with_scalars(y[m], scalars[m]).astype(outs[i].dtype)


def weigh_kernel(chips, later, n_ys, *refs):
    ys, prec = views(refs[:n_ys], chips, place()[0]), refs[n_ys]
    image, weighted, state = refs[-3:]
    p = prec[...]
    for m in range(image.shape[0]):
        y = ys[0][m].astype(F32)
        for ref in ys[1:]:
            y = y + ref[m].astype(F32)
        norm, cross = read_scalars(ys, m, 2)
        if later:
            old_image, old = refs[n_ys + 1 : n_ys + 3]
            old_norm, old_square = old[m, 0:1, 0:1], old[m, 1:2, 0:1]
            beta = norm / old_norm
            square = norm + 2.0 * beta * cross + beta * beta * old_square
            y = y + beta * old_image[m]
        else:
            beta = jnp.zeros_like(norm)
            square = norm
        scaled = p * y
        image[m] = y
        put_columns(weighted, m, with_scalars(scaled, [total(scaled * y)]).astype(BF16))
        sub = lax.broadcasted_iota(jnp.int32, (8, LANES), 0)
        state[m] = jnp.where(sub == 0, norm, jnp.where(sub == 1, square, beta))


def adjoint_kernel(dims, *refs):
    chips, n_obs, n_ws, n_outs, added = dims
    z, core, obs = place()
    ws, tiles = views(refs[:n_ws], chips, z), refs[n_ws]
    acc = refs[-1]
    outs = refs[-1 - n_outs : -1]
    members, levp, width = ws[0].shape
    colblocks = tiles.shape[1]
    rows = members * levp
    for i in range(chips):
        part = lax.dot_general(
            ws[i][...].reshape(rows, width),
            tiles[z ^ i].reshape(colblocks * LANES, width),
            NT,
            preferred_element_type=F32,
        )
        for k in range(colblocks):
            piece = part[:, k * LANES : (k + 1) * LANES]
            acc[k] = piece if i == 0 else acc[k] + piece
    if added:
        more = refs[n_ws + 1]
        outs = views(outs, n_obs, obs)
    for m in range(members):
        (energy,) = read_scalars(ws, m, 1)
        if added:
            energy = energy + read_scalars([more.at[0]], m, 1)[0]
        for i in range(n_obs):
            if added:
                value = acc[obs ^ i].reshape(members, levp, LANES)[m]
                value = value + more[obs ^ i, m].astype(F32)
                outs[i][m] = with_scalars(value, [energy]).astype(BF16)
            else:
                value = acc[i].reshape(members, levp, LANES)[m]
                outs[0][i, m] = with_scalars(value, [energy]).astype(BF16)


def update_kernel(n_obs, n_pieces, later, last, lev, *refs):
    pieces = views(refs[:n_pieces], n_obs, lax.axis_index("obs"))
    sd, vert, vert_t, state, residual = refs[n_pieces : n_pieces + 5]
    more = refs[n_pieces + 5 :]
    old_direction = old_solution = None
    if later:
        old_direction, old_solution = more[:2]
        more = more[2:]
    for m in range(residual.shape[0]):
        t = pieces[0][m].astype(F32)
        for ref in pieces[1:]:
            t = t + ref[m].astype(F32)
        (energy,) = read_scalars(pieces, m, 1)
        norm, square, beta = state[m, 0:1, 0:1], state[m, 1:2, 0:1], state[m, 2:3, 0:1]
        alpha = norm / (square + energy)
        r = residual[m]
        d = r + beta * old_direction[m] if later else r
        q = d + dot(vert_t[...], sd[...] * t)
        solution = alpha * d
        if later:
            solution = old_solution[m] + solution
        r = r - alpha * q
        if last:
            increment_out, residual_out = more
            increment = sd[...] * dot(vert[...], solution)
            increment_out[:, m, :] = increment[0:lev]
            residual_out[:, m, :] = r[0:lev]
        else:
            residual_out, direction_out, solution_out, moved = more
            residual_out[m] = r
            direction_out[m] = d
            solution_out[m] = solution
            x = sd[...] * dot(vert[...], r)
            put_columns(moved, m, with_scalars(x, [total(r * r), total(r * d)]).astype(BF16))


def per_device(
    n_slab,
    n_obs,
    innovation,
    obs_precision,
    seeds,
    col_sd,
    vert_factor,
    h_values,
    block_obs,
    block_col,
    entry_count,
):
    blocks, lev, profiles = innovation.shape
    members = seeds.shape[0]
    groups, share = GROUPS, members // GROUPS
    chips = n_slab // 2
    halves = n_slab // blocks
    width = profiles // halves
    colblocks = n_obs
    assert halves * blocks == n_slab and width % LANES == 0 and col_sd.shape[0] == 1
    assert chips & (chips - 1) == 0 and n_obs & (n_obs - 1) == 0
    levp = (lev + 1 + 15) // 16 * 16
    rows = share * levp
    field = (share, levp, LANES)
    panel = (share, levp, width)
    pad = ((0, levp - lev), (0, levp - lev))
    vert = jnp.pad(vert_factor, pad)
    vert_t = jnp.pad(vert_factor.T, pad)
    h_block = h_values.reshape(h_values.shape[2:])
    innovation = jnp.transpose(innovation, (1, 0, 2))
    obs_precision = jnp.transpose(obs_precision, (1, 0, 2))
    product = n_slab * width * colblocks * LANES * rows
    small = 24 * rows * levp * LANES
    cores = [[s for s in range(n_slab) if s % 2 == c] for c in range(2)]

    def along(x, i):
        return lax.ppermute(x, "slab", [(s, s ^ (2 * i)) for s in range(n_slab)])

    def plane(x, i):
        return lax.ppermute(x, "obs", [(o, o ^ i) for o in range(n_obs)])

    def swap(x):
        return lax.ppermute(x, "slab", [(s, s ^ 1) for s in range(n_slab)])

    def spread(mode, outs, move):
        if mode == "permute":
            return [x if i == 0 else move(x, i) for i, x in enumerate(outs)]
        if move is plane:
            return [lax.all_to_all(outs[0], "obs", 0, 0, tiled=True)]
        return [lax.all_to_all(outs[0], "slab", 0, 0, axis_index_groups=cores, tiled=True)]

    def copies(mode, x, count):
        return [x] * count if mode == "permute" else [x]

    def shapes(mode, shape, dtype, count):
        return [struct(shape, dtype)] * count if mode == "permute" else [struct((count, *shape), dtype)]

    dense = struct((chips, colblocks, LANES, width), BF16)
    partial_shapes = shapes(PLANE_SUM, field, BF16, n_obs)
    n_parts = len(partial_shapes)
    own, for_partner, *partials = call(
        functools.partial(start_kernel, (chips, n_obs, halves, groups)),
        [dense, dense] + [x for x in partial_shapes for g in range(groups)],
        [
            pltpu.SMEM(seeds.shape, jnp.int32),
            pltpu.SMEM(block_obs.shape, jnp.int32),
            pltpu.SMEM(block_col.shape, jnp.int32),
            pltpu.SMEM(entry_count.shape, jnp.int32),
            pltpu.VMEM((blocks, lev, profiles), F32),
            pltpu.VMEM((blocks, lev, profiles), F32),
            pltpu.VMEM((n_slab, members, levp, width), F32),
            pltpu.VMEM((members, levp, width), F32),
            pltpu.VMEM((colblocks, members * levp, LANES), F32),
            pltpu.SemaphoreType.DMA((4 + 2 * blocks,)),
            pltpu.SemaphoreType.DMA((h_block.shape[0] * halves,)),
        ],
        2 * product * groups,
        seeds,
        block_obs,
        block_col,
        entry_count,
        innovation,
        obs_precision,
        h_block,
        space=HBM,
        limit=60,
    )
    arrived = [spread(PLANE_SUM, partials[g::groups], plane) for g in range(groups)]
    partner = swap(for_partner)
    (precision,) = call(
        functools.partial(precision_kernel, halves),
        [struct((levp, width), F32)],
        [],
        0,
        obs_precision,
    )
    state = [None] * groups
    direction = [None] * groups
    total_step = [None] * groups
    image = [None] * groups
    residual, moved, outputs = [], [], []
    (moved_shape,) = shapes(PLANE_GATHER, field, BF16, n_obs)[:1]
    (weighted_shape,) = shapes(LINE_GATHER, panel, BF16, chips)[:1]
    for g in range(groups):
        r, x = call(
            functools.partial(first_kernel, n_obs),
            [struct(field, F32), moved_shape],
            [],
            small,
            *arrived[g],
            col_sd,
            vert,
            vert_t,
        )
        residual.append(r)
        moved.append(x)
    for sweep in range(ITERS):
        later, last = sweep > 0, sweep == ITERS - 1
        for g in range(groups):
            columns = spread(PLANE_GATHER, copies(PLANE_GATHER, moved[g], n_obs), plane)
            others = [swap(x) for x in columns]
            image_shapes = shapes(LINE_SUM, panel, BF16, chips)
            if len(image_shapes) > 1:
                image_shapes[0] = struct(panel, F32)
            ys = call(
                functools.partial(
                    forward_kernel, (chips, n_obs, len(columns), len(image_shapes))
                ),
                image_shapes,
                [pltpu.VMEM((rows, 2 * colblocks * LANES), BF16)],
                2 * product,
                *columns,
                *others,
                own,
                partner,
            )
            ys = spread(LINE_SUM, ys, along)
            image[g], weighted, state[g] = call(
                functools.partial(weigh_kernel, chips, later, len(ys)),
                [struct(panel, F32), weighted_shape, struct((share, 8, LANES), F32)],
                [],
                0,
                *ys,
                precision,
                *([image[g], state[g]] if later else []),
            )
            ws = spread(LINE_GATHER, copies(LINE_GATHER, weighted, chips), along)
            acc = [pltpu.VMEM((colblocks, rows, LANES), F32)]
            (theirs,) = call(
                functools.partial(adjoint_kernel, (chips, n_obs, len(ws), 1, False)),
                [struct((n_obs, *field), BF16)],
                acc,
                product,
                *ws,
                partner,
            )
            ps = call(
                functools.partial(adjoint_kernel, (chips, n_obs, len(ws), n_parts, True)),
                partial_shapes,
                acc,
                product,
                *ws,
                own,
                swap(theirs),
            )
            ps = spread(PLANE_SUM, ps, plane)
            if last:
                outs = [struct((lev, share, LANES), F32)] * 2
            else:
                outs = [struct(field, F32)] * 3 + [moved_shape]
            results = call(
                functools.partial(update_kernel, n_obs, len(ps), later, last, lev),
                outs,
                [],
                small,
                *ps,
                col_sd,
                vert,
                vert_t,
                state[g],
                residual[g],
                *([direction[g], total_step[g]] if later else []),
            )
            if last:
                outputs.append(results)
            else:
                residual[g], direction[g], total_step[g], moved[g] = results
    outputs = [x[0] if groups == 1 else jnp.concatenate(x, axis=1) for x in zip(*outputs)]
    return tuple(jnp.transpose(x, (1, 0, 2))[None] for x in outputs)


def solution(mesh):
    return jax.shard_map(
        functools.partial(per_device, mesh.shape["slab"], mesh.shape["obs"]),
        mesh=mesh,
        in_specs=(
            P("obs", None, None),
            P("obs", None, None),
            P(),
            P(("slab", "obs"), None),
            P(),
            P("slab", "obs", None, None, None),
            P("slab", "obs", None),
            P("slab", "obs", None),
            P("slab", "obs"),
        ),
        out_specs=(P(("slab", "obs"), None, None, None), P(("slab", "obs"), None, None, None)),
        check_vma=False,
    )
```

```python
import functools

import jax
import jax.numpy as jnp
from jax import lax
from jax.experimental import pallas as pl
from jax.experimental.pallas import tpu as pltpu
from jax.sharding import PartitionSpec as P

ITERS = 2
GROUPS = 1
LANES = 128
PIECES = 3
PRIME = 32749
VMEM = pl.BlockSpec(memory_space=pltpu.VMEM)
HBM = pl.BlockSpec(memory_space=pltpu.HBM)
F32 = jnp.float32
BF16 = jnp.bfloat16
NT = (((1,), (1,)), ((), ()))


def call(kernel, outs, scratch, flops, *args, space=VMEM, limit=40):
    nbytes = sum(a.size * a.dtype.itemsize for a in (*args, *outs))
    return pl.pallas_call(
        kernel,
        out_shape=outs,
        in_specs=[space] * len(args),
        out_specs=[VMEM] * len(outs),
        scratch_shapes=scratch,
        compiler_params=pltpu.CompilerParams(vmem_limit_bytes=limit * 1024 * 1024),
        cost_estimate=pl.CostEstimate(flops=flops, bytes_accessed=nbytes, transcendentals=0),
    )(*args)


def struct(shape, dtype):
    return jax.ShapeDtypeStruct(shape, dtype)


def place():
    slab = lax.axis_index("slab")
    return slab // 2, slab % 2, lax.axis_index("obs")


def add(parts):
    value = parts[0].astype(F32)
    for part in parts[1:]:
        value = value + part.astype(F32)
    return value


def split(x):
    high = x.astype(BF16)
    return high, (x - high.astype(F32)).astype(BF16)


def dot(a, b):
    (a, a_rest), (b, b_rest) = split(a), split(b)
    one = functools.partial(jnp.dot, preferred_element_type=F32)
    return one(a, b) + (one(a, b_rest) + one(a_rest, b))


def total(x):
    return jnp.sum(jnp.sum(x, axis=0, keepdims=True), axis=1, keepdims=True)


def with_scalars(body, values):
    rows = lax.broadcasted_iota(jnp.int32, body.shape, 0)
    lanes = lax.broadcasted_iota(jnp.int32, body.shape, 1)
    line = jnp.zeros(body.shape, F32)
    for q, value in enumerate(values):
        rest = value
        for piece in range(PIECES):
            part = rest.astype(BF16).astype(F32)
            rest = rest - part
            line = jnp.where(lanes == q * PIECES + piece, part, line)
    return jnp.where(rows == body.shape[0] - 1, line, body)


def read_scalars(refs, member, count):
    rows = refs[0].shape[1]
    tail = add([ref[member, rows - 16 : rows, 0:LANES] for ref in refs])
    sub = lax.broadcasted_iota(jnp.int32, tail.shape, 0)
    lanes = lax.broadcasted_iota(jnp.int32, tail.shape, 1)
    found = []
    for q in range(count):
        mine = (sub == 15) & (lanes >= q * PIECES) & (lanes < (q + 1) * PIECES)
        found.append(total(jnp.where(mine, tail, 0.0)))
    return found


def remainder(x, factor):
    return x - (x.astype(F32) * factor).astype(jnp.int32) * PRIME


def start_kernel(
    dims, seeds_in, ids_in, cols_in, count_in, sd_in, innov_in, prec_in, h, own, partner, *rest
):
    chips, halves, groups = dims
    outs = rest[:-12]
    seeds, ids, cols, count, sd, innov, prec, hashed, scratch, acc, sems, h_sems = rest[-12:]
    z, core, obs = place()
    blocks, lev, profiles = innov.shape
    colblocks, width = own.shape[1], own.shape[3]
    members, levp = scratch.shape[0], scratch.shape[1]

    pairs = [(seeds_in, seeds), (ids_in, ids), (cols_in, cols), (count_in, count), (sd_in, sd)]
    small = [pltpu.make_async_copy(x, y, sems.at[i]) for i, (x, y) in enumerate(pairs)]
    for copy in small:
        copy.start()
    large = []
    for b in range(blocks):
        at = len(pairs) + 2 * b
        large.append(pltpu.make_async_copy(innov_in.at[:, b, :], innov.at[b], sems.at[at]))
        large.append(pltpu.make_async_copy(prec_in.at[:, b, :], prec.at[b], sems.at[at + 1]))
    for copy in large:
        copy.start()
    own[...] = jnp.zeros_like(own)
    partner[...] = jnp.zeros_like(partner)
    scratch[...] = jnp.zeros_like(scratch)
    for copy in small:
        copy.wait()

    def tile_copy(n, half, target):
        lanes = pl.ds(half * width, width)
        return pltpu.make_async_copy(h.at[n, :, lanes], target, h_sems.at[n * halves + half])

    def put(n, carry):
        for half in range(halves):
            piece, k = ids[0, 0, n] * halves + half, cols[0, 0, n]

            @pl.when(piece % 2 == core)
            def _():
                tile_copy(n, half, own.at[piece // 2, k]).start()

            @pl.when(piece % 2 != core)
            def _():
                tile_copy(n, half, partner.at[piece // 2, k]).start()

        return carry

    lax.fori_loop(0, count[0, 0], put, 0)

    starts = [lax.rem(seeds[m], PRIME) for m in range(members)]
    order = [(source, zz) for source in range(2) for zz in range(chips)]
    shape = (levp, width)
    spot = lax.broadcasted_iota(jnp.int32, shape, 0) * profiles
    spot = spot + lax.broadcasted_iota(jnp.int32, shape, 1)
    for at, (source, zz) in enumerate(order):
        piece = 2 * zz + (core if source == 0 else 1 - core)
        first = (obs * blocks + piece // halves) * (lev * profiles) + (piece % halves) * width
        base = remainder(7919 * remainder(spot + first, 1.0 / PRIME), 1.0 / PRIME)
        for m in range(members):
            k0 = base + starts[m]
            k0 = jnp.where(k0 >= PRIME, k0 - PRIME, k0)
            k1 = remainder(k0 * k0 + 12345, 1.0 / PRIME)
            k2 = remainder(k1 * k1 + 2719, 1.0 / PRIME)
            k2 = jnp.where(k2 < 0, k2 + PRIME, k2)
            k2 = jnp.where(k2 >= PRIME, k2 - PRIME, k2)
            hashed[at, m] = k2.astype(F32)

    for copy in large:
        copy.wait()

    def arrive(n, carry):
        for half in range(halves):
            tile_copy(n, half, own.at[0, 0]).wait()
        return carry

    lax.fori_loop(0, count[0, 0], arrive, 0)

    for at, (source, zz) in enumerate(order):
        piece = 2 * zz + (core if source == 0 else 1 - core)
        b = piece // halves
        if halves == 1:
            p, d = prec[b], innov[b]
        else:
            lanes = pl.ds(pl.multiple_of((piece % halves) * width, LANES), width)
            p, d = prec[b, :, lanes], innov[b, :, lanes]
        gain = 3.4 * p * lax.rsqrt(p)
        offset = p * d - 0.5 * gain
        gain = gain * (1.0 / PRIME)
        for m in range(members):
            scratch[m, 0:lev, :] = offset + gain * hashed[at, m, 0:lev, :]
        w = scratch[...].astype(BF16).reshape(members * levp, width)
        tiles = (own if source == 0 else partner)[zz].reshape(colblocks * LANES, width)
        part = lax.dot_general(w, tiles, NT, preferred_element_type=F32)
        if at == 0:
            acc[...] = part
        else:
            acc[...] += part

    share = members // groups
    half = colblocks * LANES // 2
    for g in range(groups):
        for m in range(share):
            first = (g * share + m) * levp
            value = acc[first : first + levp, :]
            if m == 0:
                value = with_columns(value, jnp.concatenate([sd[...]] * colblocks, axis=1), obs)
            outs[2 * g][m] = value[:, :half].astype(BF16)
            outs[2 * g + 1][m] = value[:, half:].astype(BF16)


def with_columns(body, line, obs):
    rows = lax.broadcasted_iota(jnp.int32, body.shape, 0)
    mine = lax.broadcasted_iota(jnp.int32, body.shape, 1) // LANES == obs
    rest = line
    for piece in range(PIECES):
        part = rest.astype(BF16).astype(F32)
        rest = rest - part
        body = jnp.where((rows == body.shape[0] - 1 - PIECES + piece) & mine, part, body)
    return body


def read_columns(body):
    tail = body[body.shape[0] - 8 :]
    sub = lax.broadcasted_iota(jnp.int32, tail.shape, 0)
    mine = (sub >= 7 - PIECES) & (sub < 7)
    return jnp.sum(jnp.where(mine, tail, 0.0), axis=0, keepdims=True)


def precision_kernel(halves, prec, out):
    z, core, unused = place()
    piece = 2 * z + core
    lev, blocks, unused = prec.shape
    width = out.shape[1]
    block = lax.broadcasted_iota(jnp.int32, (lev, blocks, width), 1)
    if halves == 1:
        mine = prec[...]
    else:
        mine = prec[:, :, pl.ds(pl.multiple_of((piece % halves) * width, LANES), width)]
    out[...] = jnp.zeros_like(out)
    out[0:lev, :] = jnp.sum(jnp.where(block == piece // halves, mine, 0.0), axis=1)


def joined(refs, m):
    one, two = refs[: len(refs) // 2], refs[len(refs) // 2 :]
    return jnp.concatenate([add([x[m] for x in one]), add([x[m] for x in two])], axis=1)


def first_kernel(parts, *refs):
    pieces = refs[:parts]
    vert, vert_t, sd_out, residual, moved = refs[parts:]
    for m in range(residual.shape[0]):
        t = joined(pieces, m)
        if m == 0:
            sd = read_columns(t)
            sd_out[...] = sd
        r = dot(vert_t[...], sd * t)
        residual[m] = r
        x = sd * dot(vert[...], r)
        moved[m] = with_scalars(x, [total(r * r)]).astype(BF16)


def add_kernel(scalars, *refs):
    parts, out = refs[:-1], refs[-1]
    for m in range(out.shape[0]):
        value = add([x[m] for x in parts])
        if scalars:
            value = with_scalars(value, read_scalars(parts, m, scalars))
        out[m] = value.astype(BF16)


def add_halves_kernel(scalars, one, one_more, two, two_more, one_out, two_out):
    add_kernel(scalars, one, one_more, one_out)
    add_kernel(0, two, two_more, two_out)


def forward_kernel(mine, other, own, partner, *outs):
    z, core, obs = place()
    members, levp, lanes = mine.shape
    chips, width = own.shape[0], own.shape[3]
    rows = members * levp
    scalars = [read_scalars([mine, other], m, 2) for m in range(members)]
    order = [i for i in range(chips) if i % 2] + [i for i in range(chips) if i % 2 == 0]
    for i in order:
        zz = z ^ i
        y = jnp.dot(
            mine[...].reshape(rows, lanes),
            own[zz].reshape(lanes, width),
            preferred_element_type=F32,
        )
        y = y + jnp.dot(
            other[...].reshape(rows, lanes),
            partner[zz].reshape(lanes, width),
            preferred_element_type=F32,
        )
        y = y.reshape(members, levp, width)
        for m in range(members):
            outs[i][m] = with_scalars(y[m], scalars[m]).astype(outs[i].dtype)


def weigh_kernel(later, n_ys, *refs):
    ys, prec = refs[:n_ys], refs[n_ys]
    image, weighted, state = refs[-3:]
    p = prec[...]
    for m in range(image.shape[0]):
        y = add([x[m] for x in ys])
        norm, cross = read_scalars(ys, m, 2)
        if later:
            old_image, old = refs[n_ys + 1 : n_ys + 3]
            old_norm, old_square = old[m, 0:1, 0:1], old[m, 1:2, 0:1]
            beta = norm / old_norm
            square = norm + 2.0 * beta * cross + beta * beta * old_square
            y = y + beta * old_image[m]
        else:
            beta = jnp.zeros_like(norm)
            square = norm
        scaled = p * y
        image[m] = y
        weighted[m] = with_scalars(scaled, [total(scaled * y)]).astype(BF16)
        sub = lax.broadcasted_iota(jnp.int32, (8, LANES), 0)
        state[m] = jnp.where(sub == 0, norm, jnp.where(sub == 1, square, beta))


def adjoint_kernel(chips, kind, *refs):
    z, core, obs = place()
    ws, tiles = refs[:chips], refs[chips]
    members, levp, width = ws[0].shape
    lanes = tiles.shape[1] * LANES
    rows = members * levp
    acc = None
    for i in range(chips):
        part = lax.dot_general(
            ws[i][...].reshape(rows, width),
            tiles[z ^ i].reshape(lanes, width),
            NT,
            preferred_element_type=F32,
        )
        acc = part if i == 0 else acc + part
    acc = acc.reshape(members, levp, lanes)
    if kind == "theirs":
        (out,) = refs[chips + 1 :]
        for m in range(members):
            out[m] = with_scalars(acc[m], read_scalars(ws, m, 1)).astype(BF16)
        return
    more = refs[chips + 1]
    for m in range(members):
        (energy,) = read_scalars(ws, m, 1)
        energy = energy + read_scalars([more], m, 1)[0]
        value = acc[m] + more[m].astype(F32)
        if kind == "halves":
            one, two = refs[chips + 2 :]
            one[m] = with_scalars(value[:, : lanes // 2], [energy]).astype(BF16)
            two[m] = value[:, lanes // 2 :].astype(BF16)
        else:
            outs, scratch = refs[chips + 2 : -1], refs[-1]
            scratch[m] = value
            for i, out in enumerate(outs):
                lane = pl.ds(pl.multiple_of((obs ^ i) * LANES, LANES), LANES)
                out[m] = with_scalars(scratch[m, :, lane], [energy]).astype(BF16)


def update_kernel(parts, later, *refs):
    pieces, refs = refs[:parts], refs[parts:]
    sd, vert, vert_t, state, residual = refs[:5]
    if later:
        old_direction, old_solution, residual_out, solution_out, moved, direction_out = refs[5:]
    else:
        residual_out, solution_out, moved = refs[5:]
    obs = lax.axis_index("obs")
    mine = pl.ds(pl.multiple_of(obs * LANES, LANES), LANES)
    for m in range(residual.shape[0]):
        t = joined(pieces, m)
        (energy,) = read_scalars(pieces[: parts // 2], m, 1)
        norm, square, beta = state[m, 0:1, 0:1], state[m, 1:2, 0:1], state[m, 2:3, 0:1]
        alpha = norm / (square + energy)
        r = residual[m]
        if later:
            d = r + beta * old_direction[m]
            direction_out[m] = d
            step = direction_out[m, :, mine]
            solution_out[m] = old_solution[m] + alpha * step
        else:
            d = r
            solution_out[m] = alpha * residual[m, :, mine]
        r = r - alpha * (d + dot(vert_t[...], sd[...] * t))
        residual_out[m] = r
        x = sd[...] * dot(vert[...], r)
        moved[m] = with_scalars(x, [total(r * r), total(r * d)]).astype(BF16)


def last_kernel(parts, later, lev, *refs):
    pieces, refs = refs[:parts], refs[parts:]
    sd, vert, vert_t, state, residual = refs[:5]
    increment_out, residual_out = refs[-2:]
    obs = lax.axis_index("obs")
    mine = pl.ds(pl.multiple_of(obs * LANES, LANES), LANES)
    for m in range(residual.shape[0]):
        t = add([x[m] for x in pieces])
        (energy,) = read_scalars(pieces, m, 1)
        norm, square, beta = state[m, 0:1, 0:1], state[m, 1:2, 0:1], state[m, 2:3, 0:1]
        alpha = norm / (square + energy)
        d = r = residual[m, :, mine]
        if later:
            old_direction, old_solution = refs[5:7]
            d = r + beta * old_direction[m, :, mine]
        solution = alpha * d
        if later:
            solution = old_solution[m] + solution
        r = r - alpha * (d + dot(vert_t[...], sd[...] * t))
        increment = sd[...] * dot(vert[...], solution)
        increment_out[:, m, :] = increment[0:lev]
        residual_out[:, m, :] = r[0:lev]


def per_device(
    n_slab,
    n_obs,
    innovation,
    obs_precision,
    seeds,
    col_sd,
    vert_factor,
    h_values,
    block_obs,
    block_col,
    entry_count,
):
    blocks, lev, profiles = innovation.shape
    members = seeds.shape[0]
    groups, share = GROUPS, members // GROUPS
    chips = n_slab // 2
    halves = n_slab // blocks
    width = profiles // halves
    colblocks = n_obs
    assert halves * blocks == n_slab and width % LANES == 0 and col_sd.shape[0] == 1
    assert chips & (chips - 1) == 0 and n_obs & (n_obs - 1) == 0
    levp = (lev + 1 + 15) // 16 * 16
    rows = share * levp
    lanes = colblocks * LANES
    field = (share, levp, LANES)
    half_field = (share, levp, lanes // 2)
    slab_field = (share, levp, lanes)
    panel = (share, levp, width)
    pad = ((0, levp - lev), (0, levp - lev))
    vert = jnp.pad(vert_factor, pad)
    vert_t = jnp.pad(vert_factor.T, pad)
    h_block = h_values.reshape(h_values.shape[2:])
    innovation = jnp.transpose(innovation, (1, 0, 2))
    obs_precision = jnp.transpose(obs_precision, (1, 0, 2))
    product = n_slab * width * lanes * rows
    small = 12 * rows * levp * LANES
    line_bits = [1 << k for k in range(chips.bit_length() - 1)]
    plane_bits = [1 << k for k in range(n_obs.bit_length() - 1)]

    def along(x, i):
        return lax.ppermute(x, "slab", [(s, s ^ (2 * i)) for s in range(n_slab)])

    def plane(x, i):
        return lax.ppermute(x, "obs", [(o, o ^ i) for o in range(n_obs)])

    def swap(x):
        return lax.ppermute(x, "slab", [(s, s ^ 1) for s in range(n_slab)])

    def plane_sum(one, two, scalars):
        for step, bit in enumerate(plane_bits):
            far = plane_bits[len(plane_bits) - 1 - step]
            parts = [one, plane(one, bit), two, plane(two, far)]
            if step < len(plane_bits) - 1:
                one, two = call(
                    functools.partial(add_halves_kernel, scalars),
                    [struct(half_field, BF16)] * 2,
                    [],
                    0,
                    *parts,
                )
        return parts

    def line_sum(ys):
        parts = {i: [y] for i, y in enumerate(ys)}
        for bit in line_bits:
            sent = [i for i in parts if i & bit]
            for i in sorted(sent, reverse=True):
                y = parts.pop(i)
                if len(y) > 1:
                    y = call(
                        functools.partial(add_kernel, 2), [struct(panel, BF16)], [], 0, *y
                    )
                parts[i ^ bit].append(along(y[0], bit))
        return parts[0]

    def line_gather(w):
        held = {0: w}
        for bit in reversed(line_bits):
            held.update({i ^ bit: along(x, bit) for i, x in held.items()})
        return [held[i] for i in range(chips)]

    dense = struct((chips, colblocks, LANES, width), BF16)
    own, for_partner, *partials = call(
        functools.partial(start_kernel, (chips, halves, groups)),
        [dense, dense] + [struct(half_field, BF16)] * (2 * groups),
        [
            pltpu.SMEM(seeds.shape, jnp.int32),
            pltpu.SMEM(block_obs.shape, jnp.int32),
            pltpu.SMEM(block_col.shape, jnp.int32),
            pltpu.SMEM(entry_count.shape, jnp.int32),
            pltpu.VMEM(col_sd.shape, F32),
            pltpu.VMEM((blocks, lev, profiles), F32),
            pltpu.VMEM((blocks, lev, profiles), F32),
            pltpu.VMEM((n_slab, members, levp, width), F32),
            pltpu.VMEM((members, levp, width), F32),
            pltpu.VMEM((members * levp, lanes), F32),
            pltpu.SemaphoreType.DMA((5 + 2 * blocks,)),
            pltpu.SemaphoreType.DMA((h_block.shape[0] * halves,)),
        ],
        2 * product * groups,
        seeds,
        block_obs,
        block_col,
        entry_count,
        col_sd,
        innovation,
        obs_precision,
        h_block,
        space=HBM,
        limit=60,
    )
    arrived = [plane_sum(*partials[2 * g : 2 * g + 2], 0) for g in range(groups)]
    partner = swap(for_partner)
    (precision,) = call(
        functools.partial(precision_kernel, halves),
        [struct((levp, width), F32)],
        [],
        0,
        obs_precision,
    )
    state = [None] * groups
    direction = [None] * groups
    total_step = [None] * groups
    image = [None] * groups
    residual, moved, slab_sd, outputs = [], [], [], []
    for g in range(groups):
        sd, r, x = call(
            functools.partial(first_kernel, len(arrived[g])),
            [struct((1, lanes), F32), struct(slab_field, F32), struct(slab_field, BF16)],
            [],
            small * colblocks,
            *arrived[g],
            vert,
            vert_t,
        )
        slab_sd.append(sd)
        residual.append(r)
        moved.append(x)
    for sweep in range(ITERS):
        later, last = sweep > 0, sweep == ITERS - 1
        for g in range(groups):
            ys = call(
                forward_kernel,
                [struct(panel, BF16 if i % 2 else F32) for i in range(chips)],
                [],
                2 * product,
                moved[g],
                swap(moved[g]),
                own,
                partner,
            )
            ys = line_sum(ys)
            image[g], weighted, state[g] = call(
                functools.partial(weigh_kernel, later, len(ys)),
                [struct(panel, F32), struct(panel, BF16), struct((share, 8, LANES), F32)],
                [],
                0,
                *ys,
                precision,
                *([image[g], state[g]] if later else []),
            )
            ws = line_gather(weighted)
            (theirs,) = call(
                functools.partial(adjoint_kernel, chips, "theirs"),
                [struct(slab_field, BF16)],
                [],
                product,
                *ws,
                partner,
            )
            theirs = swap(theirs)
            old = [direction[g], total_step[g]] if later else []
            known = [vert, vert_t, state[g], residual[g], *old]
            if last:
                ps = call(
                    functools.partial(adjoint_kernel, chips, "columns"),
                    [struct(field, BF16)] * n_obs,
                    [pltpu.VMEM(slab_field, F32)],
                    product,
                    *ws,
                    own,
                    theirs,
                )
                ps = [x if i == 0 else plane(x, i) for i, x in enumerate(ps)]
                outputs.append(
                    call(
                        functools.partial(last_kernel, len(ps), later, lev),
                        [struct((lev, share, LANES), F32)] * 2,
                        [],
                        small,
                        *ps,
                        col_sd,
                        *known,
                    )
                )
                continue
            ps = call(
                functools.partial(adjoint_kernel, chips, "halves"),
                [struct(half_field, BF16)] * 2,
                [],
                product,
                *ws,
                own,
                theirs,
            )
            ps = plane_sum(*ps, 1)
            outs = [struct(slab_field, F32), struct(field, F32), struct(slab_field, BF16)]
            if later:
                outs.append(struct(slab_field, F32))
            r, total_step[g], moved[g], *d = call(
                functools.partial(update_kernel, len(ps), later),
                outs,
                [],
                small * colblocks,
                *ps,
                slab_sd[g],
                *known,
            )
            direction[g] = d[0] if later else residual[g]
            residual[g] = r
    outputs = [x[0] if groups == 1 else jnp.concatenate(x, axis=1) for x in zip(*outputs)]
    return tuple(jnp.transpose(x, (1, 0, 2))[None] for x in outputs)


def solution(mesh):
    return jax.shard_map(
        functools.partial(per_device, mesh.shape["slab"], mesh.shape["obs"]),
        mesh=mesh,
        in_specs=(
            P("obs", None, None),
            P("obs", None, None),
            P(),
            P(("slab", "obs"), None),
            P(),
            P("slab", "obs", None, None, None),
            P("slab", "obs", None),
            P("slab", "obs", None),
            P("slab", "obs"),
        ),
        out_specs=(P(("slab", "obs"), None, None, None), P(("slab", "obs"), None, None, None)),
        check_vma=False,
    )
```

```python
import functools

import jax
import jax.numpy as jnp
from jax import lax
from jax.experimental import pallas as pl
from jax.experimental.pallas import tpu as pltpu
from jax.sharding import PartitionSpec as P

ITERS = 2
GROUPS = 2
LANES = 128
PIECES = 3
PRIME = 32749
VMEM = pl.BlockSpec(memory_space=pltpu.VMEM)
HBM = pl.BlockSpec(memory_space=pltpu.HBM)
F32 = jnp.float32
BF16 = jnp.bfloat16
NT = (((1,), (1,)), ((), ()))


class Caller:
    def __init__(self):
        self.previous = None

    def __call__(self, kernel, outs, scratch, flops, *args, space=VMEM, limit=40):
        nbytes = sum(a.size * a.dtype.itemsize for a in (*args, *outs))
        count = len(args)
        specs = [space] * count
        body = kernel
        if self.previous is not None:
            args = (*args, self.previous)
            specs = specs + [pl.BlockSpec(memory_space=pl.ANY)]

            def body(*refs):
                kernel(*refs[:count], *refs[count + 1 :])

        results = pl.pallas_call(
            body,
            out_shape=outs,
            in_specs=specs,
            out_specs=[VMEM] * len(outs),
            scratch_shapes=scratch,
            compiler_params=pltpu.CompilerParams(vmem_limit_bytes=limit * 1024 * 1024),
            cost_estimate=pl.CostEstimate(flops=flops, bytes_accessed=nbytes, transcendentals=0),
        )(*args)
        self.previous = results[-1]
        return results


def struct(shape, dtype):
    return jax.ShapeDtypeStruct(shape, dtype)


def place():
    slab = lax.axis_index("slab")
    return slab // 2, slab % 2, lax.axis_index("obs")


def add(parts):
    value = parts[0].astype(F32)
    for part in parts[1:]:
        value = value + part.astype(F32)
    return value


def split(x):
    high = x.astype(BF16)
    return high, (x - high.astype(F32)).astype(BF16)


def dot(a, b):
    (a, a_rest), (b, b_rest) = split(a), split(b)
    one = functools.partial(jnp.dot, preferred_element_type=F32)
    return one(a, b) + (one(a, b_rest) + one(a_rest, b))


def total(x):
    return jnp.sum(jnp.sum(x, axis=0, keepdims=True), axis=1, keepdims=True)


def with_scalars(body, values):
    rows = lax.broadcasted_iota(jnp.int32, body.shape, 0)
    lanes = lax.broadcasted_iota(jnp.int32, body.shape, 1)
    line = jnp.zeros(body.shape, F32)
    for q, value in enumerate(values):
        rest = value
        for piece in range(PIECES):
            part = rest.astype(BF16).astype(F32)
            rest = rest - part
            line = jnp.where(lanes == q * PIECES + piece, part, line)
    return jnp.where(rows == body.shape[0] - 1, line, body)


def read_scalars(refs, member, count):
    rows = refs[0].shape[1]
    tail = add([ref[member, rows - 16 : rows, 0:LANES] for ref in refs])
    sub = lax.broadcasted_iota(jnp.int32, tail.shape, 0)
    lanes = lax.broadcasted_iota(jnp.int32, tail.shape, 1)
    found = []
    for q in range(count):
        mine = (sub == 15) & (lanes >= q * PIECES) & (lanes < (q + 1) * PIECES)
        found.append(total(jnp.where(mine, tail, 0.0)))
    return found


def remainder(x, factor):
    return x - (x.astype(F32) * factor).astype(jnp.int32) * PRIME


def start_kernel(
    dims, seeds_in, ids_in, cols_in, count_in, sd_in, innov_in, prec_in, h, own, partner, *rest
):
    chips, halves, groups = dims
    outs = rest[:-12]
    seeds, ids, cols, count, sd, innov, prec, hashed, scratch, acc, sems, h_sems = rest[-12:]
    z, core, obs = place()
    blocks, lev, profiles = innov.shape
    colblocks, width = own.shape[1], own.shape[3]
    members, levp = scratch.shape[0], scratch.shape[1]

    pairs = [(seeds_in, seeds), (ids_in, ids), (cols_in, cols), (count_in, count), (sd_in, sd)]
    small = [pltpu.make_async_copy(x, y, sems.at[i]) for i, (x, y) in enumerate(pairs)]
    for copy in small:
        copy.start()
    large = []
    for b in range(blocks):
        at = len(pairs) + 2 * b
        large.append(pltpu.make_async_copy(innov_in.at[:, b, :], innov.at[b], sems.at[at]))
        large.append(pltpu.make_async_copy(prec_in.at[:, b, :], prec.at[b], sems.at[at + 1]))
    for copy in large:
        copy.start()
    own[...] = jnp.zeros_like(own)
    partner[...] = jnp.zeros_like(partner)
    scratch[...] = jnp.zeros_like(scratch)
    for copy in small:
        copy.wait()

    def tile_copy(n, half, target):
        lanes = pl.ds(half * width, width)
        return pltpu.make_async_copy(h.at[n, :, lanes], target, h_sems.at[n * halves + half])

    def put(n, carry):
        for half in range(halves):
            piece, k = ids[0, 0, n] * halves + half, cols[0, 0, n]

            @pl.when(piece % 2 == core)
            def _():
                tile_copy(n, half, own.at[piece // 2, k]).start()

            @pl.when(piece % 2 != core)
            def _():
                tile_copy(n, half, partner.at[piece // 2, k]).start()

        return carry

    lax.fori_loop(0, count[0, 0], put, 0)

    starts = [lax.rem(seeds[m], PRIME) for m in range(members)]
    order = [(source, zz) for source in range(2) for zz in range(chips)]
    shape = (levp, width)
    spot = lax.broadcasted_iota(jnp.int32, shape, 0) * profiles
    spot = spot + lax.broadcasted_iota(jnp.int32, shape, 1)
    for at, (source, zz) in enumerate(order):
        piece = 2 * zz + (core if source == 0 else 1 - core)
        first = (obs * blocks + piece // halves) * (lev * profiles) + (piece % halves) * width
        base = remainder(7919 * remainder(spot + first, 1.0 / PRIME), 1.0 / PRIME)
        for m in range(members):
            k0 = base + starts[m]
            k0 = jnp.where(k0 >= PRIME, k0 - PRIME, k0)
            k1 = remainder(k0 * k0 + 12345, 1.0 / PRIME)
            k2 = remainder(k1 * k1 + 2719, 1.0 / PRIME)
            k2 = jnp.where(k2 < 0, k2 + PRIME, k2)
            k2 = jnp.where(k2 >= PRIME, k2 - PRIME, k2)
            hashed[at, m] = k2.astype(F32)

    for copy in large:
        copy.wait()

    def arrive(n, carry):
        for half in range(halves):
            tile_copy(n, half, own.at[0, 0]).wait()
        return carry

    lax.fori_loop(0, count[0, 0], arrive, 0)

    for at, (source, zz) in enumerate(order):
        piece = 2 * zz + (core if source == 0 else 1 - core)
        b = piece // halves
        if halves == 1:
            p, d = prec[b], innov[b]
        else:
            lanes = pl.ds(pl.multiple_of((piece % halves) * width, LANES), width)
            p, d = prec[b, :, lanes], innov[b, :, lanes]
        gain = 3.4 * p * lax.rsqrt(p)
        offset = p * d - 0.5 * gain
        gain = gain * (1.0 / PRIME)
        for m in range(members):
            scratch[m, 0:lev, :] = offset + gain * hashed[at, m, 0:lev, :]
        w = scratch[...].astype(BF16).reshape(members * levp, width)
        tiles = (own if source == 0 else partner)[zz].reshape(colblocks * LANES, width)
        part = lax.dot_general(w, tiles, NT, preferred_element_type=F32)
        if at == 0:
            acc[...] = part
        else:
            acc[...] += part

    share = members // groups
    half = colblocks * LANES // 2
    for g in range(groups):
        for m in range(share):
            first = (g * share + m) * levp
            value = acc[first : first + levp, :]
            if m == 0:
                value = with_columns(value, jnp.concatenate([sd[...]] * colblocks, axis=1), obs)
            outs[2 * g][m] = value[:, :half].astype(BF16)
            outs[2 * g + 1][m] = value[:, half:].astype(BF16)


def with_columns(body, line, obs):
    rows = lax.broadcasted_iota(jnp.int32, body.shape, 0)
    mine = lax.broadcasted_iota(jnp.int32, body.shape, 1) // LANES == obs
    rest = line
    for piece in range(PIECES):
        part = rest.astype(BF16).astype(F32)
        rest = rest - part
        body = jnp.where((rows == body.shape[0] - 1 - PIECES + piece) & mine, part, body)
    return body


def read_columns(body):
    tail = body[body.shape[0] - 8 :]
    sub = lax.broadcasted_iota(jnp.int32, tail.shape, 0)
    mine = (sub >= 7 - PIECES) & (sub < 7)
    return jnp.sum(jnp.where(mine, tail, 0.0), axis=0, keepdims=True)


def precision_kernel(halves, prec, out):
    z, core, unused = place()
    piece = 2 * z + core
    lev, blocks, unused = prec.shape
    width = out.shape[1]
    block = lax.broadcasted_iota(jnp.int32, (lev, blocks, width), 1)
    if halves == 1:
        mine = prec[...]
    else:
        mine = prec[:, :, pl.ds(pl.multiple_of((piece % halves) * width, LANES), width)]
    out[...] = jnp.zeros_like(out)
    out[0:lev, :] = jnp.sum(jnp.where(block == piece // halves, mine, 0.0), axis=1)


def joined(refs, m):
    one, two = refs[: len(refs) // 2], refs[len(refs) // 2 :]
    return jnp.concatenate([add([x[m] for x in one]), add([x[m] for x in two])], axis=1)


def first_kernel(parts, *refs):
    pieces = refs[:parts]
    vert, vert_t, sd_out, residual, moved = refs[parts:]
    for m in range(residual.shape[0]):
        t = joined(pieces, m)
        if m == 0:
            sd = read_columns(t)
            sd_out[...] = sd
        r = dot(vert_t[...], sd * t)
        residual[m] = r
        x = sd * dot(vert[...], r)
        moved[m] = with_scalars(x, [total(r * r)]).astype(BF16)


def add_kernel(scalars, *refs):
    parts, out = refs[:-1], refs[-1]
    for m in range(out.shape[0]):
        value = add([x[m] for x in parts])
        if scalars:
            value = with_scalars(value, read_scalars(parts, m, scalars))
        out[m] = value.astype(BF16)


def add_halves_kernel(scalars, one, one_more, two, two_more, one_out, two_out):
    add_kernel(scalars, one, one_more, one_out)
    add_kernel(0, two, two_more, two_out)


def forward_kernel(mine, other, own, partner, *outs):
    z, core, obs = place()
    members, levp, lanes = mine.shape
    chips, width = own.shape[0], own.shape[3]
    rows = members * levp
    scalars = [read_scalars([mine, other], m, 2) for m in range(members)]
    for i in reversed(range(chips)):
        zz = z ^ i
        y = jnp.dot(
            mine[...].reshape(rows, lanes),
            own[zz].reshape(lanes, width),
            preferred_element_type=F32,
        )
        y = y + jnp.dot(
            other[...].reshape(rows, lanes),
            partner[zz].reshape(lanes, width),
            preferred_element_type=F32,
        )
        y = y.reshape(members, levp, width)
        for m in range(members):
            outs[i][m] = with_scalars(y[m], scalars[m]).astype(outs[i].dtype)


def weigh_kernel(later, n_ys, *refs):
    ys, prec = refs[:n_ys], refs[n_ys]
    image, weighted, state = refs[-3:]
    p = prec[...]
    for m in range(image.shape[0]):
        y = add([x[m] for x in ys])
        norm, cross = read_scalars(ys, m, 2)
        if later:
            old_image, old = refs[n_ys + 1 : n_ys + 3]
            old_norm, old_square = old[m, 0:1, 0:1], old[m, 1:2, 0:1]
            beta = norm / old_norm
            square = norm + 2.0 * beta * cross + beta * beta * old_square
            y = y + beta * old_image[m]
        else:
            beta = jnp.zeros_like(norm)
            square = norm
        scaled = p * y
        image[m] = y
        weighted[m] = with_scalars(scaled, [total(scaled * y)]).astype(BF16)
        sub = lax.broadcasted_iota(jnp.int32, (8, LANES), 0)
        state[m] = jnp.where(sub == 0, norm, jnp.where(sub == 1, square, beta))


def adjoint_kernel(chips, kind, *refs):
    z, core, obs = place()
    ws, tiles = refs[:chips], refs[chips]
    members, levp, width = ws[0].shape
    lanes = tiles.shape[1] * LANES
    rows = members * levp
    acc = None
    for i in range(chips):
        part = lax.dot_general(
            ws[i][...].reshape(rows, width),
            tiles[z ^ i].reshape(lanes, width),
            NT,
            preferred_element_type=F32,
        )
        acc = part if i == 0 else acc + part
    acc = acc.reshape(members, levp, lanes)
    if kind == "theirs":
        (out,) = refs[chips + 1 :]
        for m in range(members):
            out[m] = with_scalars(acc[m], read_scalars(ws, m, 1)).astype(BF16)
        return
    more = refs[chips + 1]
    for m in range(members):
        (energy,) = read_scalars(ws, m, 1)
        energy = energy + read_scalars([more], m, 1)[0]
        value = acc[m] + more[m].astype(F32)
        if kind == "halves":
            one, two = refs[chips + 2 :]
            one[m] = with_scalars(value[:, : lanes // 2], [energy]).astype(BF16)
            two[m] = value[:, lanes // 2 :].astype(BF16)
        else:
            outs, scratch = refs[chips + 2 : -1], refs[-1]
            scratch[m] = value
            for i, out in enumerate(outs):
                lane = pl.ds(pl.multiple_of((obs ^ i) * LANES, LANES), LANES)
                out[m] = with_scalars(scratch[m, :, lane], [energy]).astype(BF16)


def update_kernel(parts, later, *refs):
    pieces, refs = refs[:parts], refs[parts:]
    sd, vert, vert_t, state, residual = refs[:5]
    if later:
        old_direction, old_solution, residual_out, solution_out, moved, direction_out = refs[5:]
    else:
        residual_out, solution_out, moved = refs[5:]
    obs = lax.axis_index("obs")
    mine = pl.ds(pl.multiple_of(obs * LANES, LANES), LANES)
    for m in range(residual.shape[0]):
        t = joined(pieces, m)
        (energy,) = read_scalars(pieces[: parts // 2], m, 1)
        norm, square, beta = state[m, 0:1, 0:1], state[m, 1:2, 0:1], state[m, 2:3, 0:1]
        alpha = norm / (square + energy)
        r = residual[m]
        if later:
            d = r + beta * old_direction[m]
            direction_out[m] = d
            step = direction_out[m, :, mine]
            solution_out[m] = old_solution[m] + alpha * step
        else:
            d = r
            solution_out[m] = alpha * residual[m, :, mine]
        r = r - alpha * (d + dot(vert_t[...], sd[...] * t))
        residual_out[m] = r
        x = sd[...] * dot(vert[...], r)
        moved[m] = with_scalars(x, [total(r * r), total(r * d)]).astype(BF16)


def last_kernel(parts, later, lev, first, *refs):
    pieces, refs = refs[:parts], refs[parts:]
    sd, vert, vert_t, state, residual = refs[:5]
    increment_out, residual_out = refs[-2:]
    if first:
        increment_out[:, 0:first, :] = refs[-4][...]
        residual_out[:, 0:first, :] = refs[-3][...]
    obs = lax.axis_index("obs")
    mine = pl.ds(pl.multiple_of(obs * LANES, LANES), LANES)
    for m in range(residual.shape[0]):
        t = add([x[m] for x in pieces])
        (energy,) = read_scalars(pieces, m, 1)
        norm, square, beta = state[m, 0:1, 0:1], state[m, 1:2, 0:1], state[m, 2:3, 0:1]
        alpha = norm / (square + energy)
        d = r = residual[m, :, mine]
        if later:
            old_direction, old_solution = refs[5:7]
            d = r + beta * old_direction[m, :, mine]
        solution = alpha * d
        if later:
            solution = old_solution[m] + solution
        r = r - alpha * (d + dot(vert_t[...], sd[...] * t))
        increment = sd[...] * dot(vert[...], solution)
        increment_out[:, first + m, :] = increment[0:lev]
        residual_out[:, first + m, :] = r[0:lev]


def per_device(
    n_slab,
    n_obs,
    innovation,
    obs_precision,
    seeds,
    col_sd,
    vert_factor,
    h_values,
    block_obs,
    block_col,
    entry_count,
):
    blocks, lev, profiles = innovation.shape
    members = seeds.shape[0]
    groups, share = GROUPS, members // GROUPS
    chips = n_slab // 2
    halves = n_slab // blocks
    width = profiles // halves
    colblocks = n_obs
    assert halves * blocks == n_slab and width % LANES == 0 and col_sd.shape[0] == 1
    assert chips & (chips - 1) == 0 and n_obs & (n_obs - 1) == 0
    levp = (lev + 1 + 15) // 16 * 16
    rows = share * levp
    lanes = colblocks * LANES
    field = (share, levp, LANES)
    half_field = (share, levp, lanes // 2)
    slab_field = (share, levp, lanes)
    panel = (share, levp, width)
    pad = ((0, levp - lev), (0, levp - lev))
    vert = jnp.pad(vert_factor, pad)
    vert_t = jnp.pad(vert_factor.T, pad)
    h_block = h_values.reshape(h_values.shape[2:])
    innovation = jnp.transpose(innovation, (1, 0, 2))
    obs_precision = jnp.transpose(obs_precision, (1, 0, 2))
    product = n_slab * width * lanes * rows
    small = 12 * rows * levp * LANES
    plane_bits = [1 << k for k in range(n_obs.bit_length() - 1)]

    def along(x, i):
        return lax.ppermute(x, "slab", [(s, s ^ (2 * i)) for s in range(n_slab)])

    def plane(x, i):
        return lax.ppermute(x, "obs", [(o, o ^ i) for o in range(n_obs)])

    def swap(x):
        return lax.ppermute(x, "slab", [(s, s ^ 1) for s in range(n_slab)])

    def plane_sum(one, two, scalars):
        for step, bit in enumerate(plane_bits):
            far = plane_bits[len(plane_bits) - 1 - step]
            parts = [one, plane(one, bit), two, plane(two, far)]
            if step < len(plane_bits) - 1:
                yield
                one, two = call(
                    functools.partial(add_halves_kernel, scalars),
                    [struct(half_field, BF16)] * 2,
                    [],
                    0,
                    *parts,
                )
        yield
        return parts

    def line_sum(ys):
        return [y if i == 0 else along(y, i) for i, y in enumerate(ys)]

    def line_gather(w):
        return [w if i == 0 else along(w, i) for i in range(chips)]

    call = Caller()
    dense = struct((chips, colblocks, LANES, width), BF16)
    own, for_partner, *partials = call(
        functools.partial(start_kernel, (chips, halves, groups)),
        [dense, dense] + [struct(half_field, BF16)] * (2 * groups),
        [
            pltpu.SMEM(seeds.shape, jnp.int32),
            pltpu.SMEM(block_obs.shape, jnp.int32),
            pltpu.SMEM(block_col.shape, jnp.int32),
            pltpu.SMEM(entry_count.shape, jnp.int32),
            pltpu.VMEM(col_sd.shape, F32),
            pltpu.VMEM((blocks, lev, profiles), F32),
            pltpu.VMEM((blocks, lev, profiles), F32),
            pltpu.VMEM((n_slab, members, levp, width), F32),
            pltpu.VMEM((members, levp, width), F32),
            pltpu.VMEM((members * levp, lanes), F32),
            pltpu.SemaphoreType.DMA((5 + 2 * blocks,)),
            pltpu.SemaphoreType.DMA((h_block.shape[0] * halves,)),
        ],
        2 * product * groups,
        seeds,
        block_obs,
        block_col,
        entry_count,
        col_sd,
        innovation,
        obs_precision,
        h_block,
        space=HBM,
        limit=60,
    )
    partner = swap(for_partner)
    (precision,) = Caller()(
        functools.partial(precision_kernel, halves),
        [struct((levp, width), F32)],
        [],
        0,
        obs_precision,
    )
    outputs = []

    def group(partials):
        ps = yield from plane_sum(*partials, 0)
        slab_sd, residual, moved = call(
            functools.partial(first_kernel, len(ps)),
            [struct((1, lanes), F32), struct(slab_field, F32), struct(slab_field, BF16)],
            [],
            small * colblocks,
            *ps,
            vert,
            vert_t,
        )
        direction = total_step = image = state = None
        for sweep in range(ITERS):
            later, last = sweep > 0, sweep == ITERS - 1
            other = swap(moved)
            yield
            ys = call(
                forward_kernel,
                [struct(panel, BF16 if i else F32) for i in range(chips)],
                [],
                2 * product,
                moved,
                other,
                own,
                partner,
            )
            ys = line_sum(ys)
            yield
            image, weighted, state = call(
                functools.partial(weigh_kernel, later, len(ys)),
                [struct(panel, F32), struct(panel, BF16), struct((share, 8, LANES), F32)],
                [],
                0,
                *ys,
                precision,
                *([image, state] if later else []),
            )
            ws = line_gather(weighted)
            yield
            (theirs,) = call(
                functools.partial(adjoint_kernel, chips, "theirs"),
                [struct(slab_field, BF16)],
                [],
                product,
                *ws,
                partner,
            )
            theirs = swap(theirs)
            known = [vert, vert_t, state, residual]
            if later:
                known += [direction, total_step]
            yield
            if last:
                ps = call(
                    functools.partial(adjoint_kernel, chips, "columns"),
                    [struct(field, BF16)] * n_obs,
                    [pltpu.VMEM(slab_field, F32)],
                    product,
                    *ws,
                    own,
                    theirs,
                )
                ps = [x if i == 0 else plane(x, i) for i, x in enumerate(ps)]
                yield
                before = outputs[-1] if outputs else []
                done = before[0].shape[1] if before else 0
                outputs.append(
                    call(
                        functools.partial(last_kernel, len(ps), later, lev, done),
                        [struct((lev, done + share, LANES), F32)] * 2,
                        [],
                        small,
                        *ps,
                        col_sd,
                        *known,
                        *before,
                    )
                )
                return
            ps = call(
                functools.partial(adjoint_kernel, chips, "halves"),
                [struct(half_field, BF16)] * 2,
                [],
                product,
                *ws,
                own,
                theirs,
            )
            ps = yield from plane_sum(*ps, 1)
            outs = [struct(slab_field, F32), struct(field, F32), struct(slab_field, BF16)]
            if later:
                outs.append(struct(slab_field, F32))
            r, total_step, moved, *d = call(
                functools.partial(update_kernel, len(ps), later),
                outs,
                [],
                small * colblocks,
                *ps,
                slab_sd,
                *known,
            )
            direction, residual = (d[0] if later else residual), r

    steps = [group(partials[2 * g : 2 * g + 2]) for g in range(groups)]
    for g in range(groups):
        next(steps[g])
    if groups == 2:
        adds = len(plane_bits) - 1
        order = [0] * adds + [0, 0] + [1] * adds + [0, 1]
        for sweep in range(ITERS - 1):
            order += [1, 0, 0, 1] + [0] * adds + [0]
            order += [0, 1, 1, 0] + [1] * adds + [1]
        order += [1, 0, 0, 1, 0, 1, 1, 1]
    else:
        order = [g for g in range(groups) for step in range(ITERS * (6 + len(plane_bits)))]
    for g in order:
        next(steps[g], None)
    return tuple(jnp.transpose(x, (1, 0, 2))[None] for x in outputs[-1])


def solution(mesh):
    return jax.shard_map(
        functools.partial(per_device, mesh.shape["slab"], mesh.shape["obs"]),
        mesh=mesh,
        in_specs=(
            P("obs", None, None),
            P("obs", None, None),
            P(),
            P(("slab", "obs"), None),
            P(),
            P("slab", "obs", None, None, None),
            P("slab", "obs", None),
            P("slab", "obs", None),
            P("slab", "obs"),
        ),
        out_specs=(P(("slab", "obs"), None, None, None), P(("slab", "obs"), None, None, None)),
        check_vma=False,
    )
```

```python
import functools

import jax
import jax.numpy as jnp
from jax import lax
from jax.experimental import pallas as pl
from jax.experimental.pallas import tpu as pltpu
from jax.sharding import PartitionSpec as P

ITERS = 2
LANES = 128
PIECES = 3
PRIME = 32749
VMEM = pl.BlockSpec(memory_space=pltpu.VMEM)
HBM = pl.BlockSpec(memory_space=pltpu.HBM)
F32 = jnp.float32
BF16 = jnp.bfloat16
NT = (((1,), (1,)), ((), ()))


def call(kernel, outs, scratch, flops, *args, space=VMEM, limit=24):
    nbytes = sum(a.size * a.dtype.itemsize for a in (*args, *outs))
    return pl.pallas_call(
        kernel,
        out_shape=outs,
        in_specs=[space] * len(args),
        out_specs=[VMEM] * len(outs),
        scratch_shapes=scratch,
        compiler_params=pltpu.CompilerParams(vmem_limit_bytes=limit * 1024 * 1024),
        cost_estimate=pl.CostEstimate(flops=flops, bytes_accessed=nbytes, transcendentals=0),
    )(*args)


def struct(shape, dtype):
    return jax.ShapeDtypeStruct(shape, dtype)


def place():
    slab = lax.axis_index("slab")
    return slab // 2, slab % 2, lax.axis_index("obs")


def add(parts):
    value = parts[0].astype(F32)
    for part in parts[1:]:
        value = value + part.astype(F32)
    return value


def split(x):
    high = x.astype(BF16)
    return high, (x - high.astype(F32)).astype(BF16)


def dot(a, b):
    (a, a_rest), (b, b_rest) = split(a), split(b)
    one = functools.partial(jnp.dot, preferred_element_type=F32)
    return one(a, b) + (one(a, b_rest) + one(a_rest, b))


def total(x):
    return jnp.sum(jnp.sum(x, axis=0, keepdims=True), axis=1, keepdims=True)


def with_scalars(body, values):
    rows = lax.broadcasted_iota(jnp.int32, body.shape, 0)
    lanes = lax.broadcasted_iota(jnp.int32, body.shape, 1)
    line = jnp.zeros(body.shape, F32)
    for q, value in enumerate(values):
        rest = value
        for piece in range(PIECES):
            part = rest.astype(BF16).astype(F32)
            rest = rest - part
            line = jnp.where(lanes == q * PIECES + piece, part, line)
    return jnp.where(rows == body.shape[0] - 1, line, body)


def read_scalars(refs, count):
    rows = refs[0].shape[0]
    tail = add([ref[rows - 16 : rows, 0:LANES] for ref in refs])
    sub = lax.broadcasted_iota(jnp.int32, tail.shape, 0)
    lanes = lax.broadcasted_iota(jnp.int32, tail.shape, 1)
    found = []
    for q in range(count):
        mine = (sub == 15) & (lanes >= q * PIECES) & (lanes < (q + 1) * PIECES)
        found.append(total(jnp.where(mine, tail, 0.0)))
    return found


def of_member(refs, spans, m):
    return [
        ref.at[m - first] for ref, (first, count) in zip(refs, spans) if first <= m < first + count
    ]


def remainder(x, factor):
    return x - (x.astype(F32) * factor).astype(jnp.int32) * PRIME


def start_kernel(
    dims, seeds_in, ids_in, cols_in, count_in, sd_in, innov_in, prec_in, h, own, partner, *rest
):
    chips, halves = dims
    outs = rest[:-12]
    seeds, ids, cols, count, sd, innov, prec, hashed, scratch, acc, sems, h_sems = rest[-12:]
    z, core, obs = place()
    blocks, lev, profiles = innov.shape
    colblocks, width = own.shape[1], own.shape[3]
    members, levp = scratch.shape[1], scratch.shape[2]

    pairs = [(seeds_in, seeds), (ids_in, ids), (cols_in, cols), (count_in, count), (sd_in, sd)]
    small = [pltpu.make_async_copy(x, y, sems.at[i]) for i, (x, y) in enumerate(pairs)]
    for copy in small:
        copy.start()
    large = []
    for b in range(blocks):
        at = len(pairs) + 2 * b
        large.append(pltpu.make_async_copy(innov_in.at[:, b, :], innov.at[b], sems.at[at]))
        large.append(pltpu.make_async_copy(prec_in.at[:, b, :], prec.at[b], sems.at[at + 1]))
    for copy in large:
        copy.start()
    own[...] = jnp.zeros_like(own)
    partner[...] = jnp.zeros_like(partner)
    scratch[...] = jnp.zeros_like(scratch)
    for copy in small:
        copy.wait()

    def tile_copy(n, half, target):
        lanes = pl.ds(half * width, width)
        return pltpu.make_async_copy(h.at[n, :, lanes], target, h_sems.at[n * halves + half])

    def put(n, carry):
        for half in range(halves):
            piece, k = ids[0, 0, n] * halves + half, cols[0, 0, n]

            @pl.when(piece % 2 == core)
            def _():
                tile_copy(n, half, own.at[piece // 2, k]).start()

            @pl.when(piece % 2 != core)
            def _():
                tile_copy(n, half, partner.at[piece // 2, k]).start()

        return carry

    lax.fori_loop(0, count[0, 0], put, 0)

    starts = [lax.rem(seeds[m], PRIME) - PRIME for m in range(members)]
    order = [(source, zz) for source in range(2) for zz in range(chips)]
    shape = (levp, width)
    spot = lax.broadcasted_iota(jnp.int32, shape, 0) * profiles
    spot = spot + lax.broadcasted_iota(jnp.int32, shape, 1)
    low = (1.0 - 2.0**-21) / PRIME

    def piece_at(at):
        source, zz = order[at]
        return 2 * zz + (core if source == 0 else 1 - core)

    def draw(at):
        piece = piece_at(at)
        first = (obs * blocks + piece // halves) * (lev * profiles) + (piece % halves) * width
        base = remainder(7919 * remainder(spot + first, 1.0 / PRIME), 1.0 / PRIME)
        for m in range(members):
            k0 = base + starts[m]
            k1 = remainder(k0 * k0 + 12345, 1.0 / PRIME)
            k2 = remainder(k1 * k1 + 2719, low)
            k2 = jnp.where(k2 >= PRIME, k2 - PRIME, k2)
            hashed[at, m] = k2.astype(F32)

    def adjoint(at):
        source, zz = order[at]
        piece = piece_at(at)
        b = piece // halves
        if halves == 1:
            p, d = prec[b], innov[b]
        else:
            lanes = pl.ds(pl.multiple_of((piece % halves) * width, LANES), width)
            p, d = prec[b, :, lanes], innov[b, :, lanes]
        gain = 3.4 * p * lax.rsqrt(p)
        offset = p * d - 0.5 * gain
        gain = gain * (1.0 / PRIME)
        for m in range(members):
            scratch[at % 2, m, 0:lev, :] = offset + gain * hashed[at, m, 0:lev, :]
        w = scratch[at % 2].astype(BF16).reshape(members * levp, width)
        tiles = (own if source == 0 else partner)[zz].reshape(colblocks * LANES, width)
        part = lax.dot_general(w, tiles, NT, preferred_element_type=F32)
        if at == 0:
            acc[...] = part
        else:
            acc[...] += part

    early = len(order) // 2
    for at in range(early):
        draw(at)
    for copy in large:
        copy.wait()

    def arrive(n, carry):
        for half in range(halves):
            tile_copy(n, half, own.at[0, 0]).wait()
        return carry

    lax.fori_loop(0, count[0, 0], arrive, 0)

    for at in range(len(order)):
        if at + early < len(order):
            draw(at + early)
        adjoint(at)

    half = colblocks * LANES // 2
    for m in range(members):
        value = acc[m * levp : (m + 1) * levp, :]
        if m == 0:
            value = with_columns(value, jnp.concatenate([sd[...]] * colblocks, axis=1), obs)
        outs[0][m] = value[:, :half].astype(BF16)
        outs[1][m] = value[:, half:].astype(BF16)


def with_columns(body, line, obs):
    rows = lax.broadcasted_iota(jnp.int32, body.shape, 0)
    mine = lax.broadcasted_iota(jnp.int32, body.shape, 1) // LANES == obs
    rest = line
    for piece in range(PIECES):
        part = rest.astype(BF16).astype(F32)
        rest = rest - part
        body = jnp.where((rows == body.shape[0] - 1 - PIECES + piece) & mine, part, body)
    return body


def read_columns(body):
    tail = body[body.shape[0] - 8 :]
    sub = lax.broadcasted_iota(jnp.int32, tail.shape, 0)
    mine = (sub >= 7 - PIECES) & (sub < 7)
    return jnp.sum(jnp.where(mine, tail, 0.0), axis=0, keepdims=True)


def precision_kernel(halves, prec, out):
    z, core, unused = place()
    piece = 2 * z + core
    lev, blocks, unused = prec.shape
    width = out.shape[1]
    block = lax.broadcasted_iota(jnp.int32, (lev, blocks, width), 1)
    if halves == 1:
        mine = prec[...]
    else:
        mine = prec[:, :, pl.ds(pl.multiple_of((piece % halves) * width, LANES), width)]
    out[...] = jnp.zeros_like(out)
    out[0:lev, :] = jnp.sum(jnp.where(block == piece // halves, mine, 0.0), axis=1)


def joined(refs, m):
    one, two = refs[: len(refs) // 2], refs[len(refs) // 2 :]
    return jnp.concatenate([add([x[m] for x in one]), add([x[m] for x in two])], axis=1)


def first_kernel(parts, *refs):
    pieces = refs[:parts]
    vert, vert_t, sd_out, residual, moved = refs[parts:]
    for m in range(residual.shape[0]):
        t = joined(pieces, m)
        if m == 0:
            sd = read_columns(t)
            sd_out[...] = sd
        r = dot(vert_t[...], sd * t)
        residual[m] = r
        x = sd * dot(vert[...], r)
        moved[m] = with_scalars(x, [total(r * r)]).astype(BF16)


def add_kernel(scalars, *refs):
    parts, out = refs[:-1], refs[-1]
    for m in range(out.shape[0]):
        value = add([x[m] for x in parts])
        if scalars:
            value = with_scalars(value, read_scalars([x.at[m] for x in parts], scalars))
        out[m] = value.astype(BF16)


def add_halves_kernel(scalars, one, one_more, two, two_more, one_out, two_out):
    add_kernel(scalars, one, one_more, one_out)
    add_kernel(0, two, two_more, two_out)


def stage_kernel(one, two, one_out, two_out, sems):
    copies = [
        pltpu.make_async_copy(x, y, sems.at[i])
        for i, (x, y) in enumerate([(one, one_out), (two, two_out)])
    ]
    for copy in copies:
        copy.start()
    for copy in copies:
        copy.wait()


def forward_kernel(plan, mine, other, own, partner, *outs):
    z, core, obs = place()
    members, levp, lanes = mine.shape
    chips, width = own.shape[0], own.shape[3]
    rows = members * levp
    scalars = [read_scalars([mine.at[m], other.at[m]], 2) for m in range(members)]
    for i in reversed(range(chips)):
        zz = z ^ i
        y = jnp.dot(
            mine[...].reshape(rows, lanes),
            own[zz].reshape(lanes, width),
            preferred_element_type=F32,
        )
        y = y + jnp.dot(
            other[...].reshape(rows, lanes),
            partner[zz].reshape(lanes, width),
            preferred_element_type=F32,
        )
        y = y.reshape(members, levp, width)
        for out, (chip, first, count) in zip(outs, plan):
            if chip == i:
                for m in range(count):
                    value = with_scalars(y[first + m], scalars[first + m])
                    out[m] = value.astype(out.dtype)


def weigh_kernel(later, spans, *refs):
    ys, refs = refs[: len(spans)], refs[len(spans) :]
    prec = refs[0]
    image, state, weighted, *parts = refs[3 if later else 1 :]
    p = prec[...]
    for m in range(image.shape[0]):
        mine = of_member(ys, spans, m)
        y = add([x[...] for x in mine])
        norm, cross = read_scalars(mine, 2)
        if later:
            old_image, old = refs[1:3]
            old_norm, old_square = old[m, 0:1, 0:1], old[m, 1:2, 0:1]
            beta = norm / old_norm
            square = norm + 2.0 * beta * cross + beta * beta * old_square
            y = y + beta * old_image[m]
        else:
            beta = jnp.zeros_like(norm)
            square = norm
        scaled = p * y
        image[m] = y
        value = with_scalars(scaled, [total(scaled * y)]).astype(BF16)
        weighted[m] = value
        first = 0
        for part in parts:
            if first <= m < first + part.shape[0]:
                part[m - first] = value
            first += part.shape[0]
        sub = lax.broadcasted_iota(jnp.int32, (8, LANES), 0)
        state[m] = jnp.where(sub == 0, norm, jnp.where(sub == 1, square, beta))


def adjoint_kernel(plan, *refs):
    z, core, obs = place()
    ws, tiles, out = refs[: len(plan)], refs[len(plan)], refs[len(plan) + 1]
    members, levp, lanes = out.shape
    width = ws[0].shape[2]
    acc = None
    for i in range(tiles.shape[0]):
        w = [ref[...].reshape(-1, width) for ref, (chip, *span) in zip(ws, plan) if chip == i]
        w = w[0] if len(w) == 1 else jnp.concatenate(w, axis=0)
        part = lax.dot_general(
            w, tiles[z ^ i].reshape(lanes, width), NT, preferred_element_type=F32
        )
        acc = part if i == 0 else acc + part
    acc = acc.reshape(members, levp, lanes)
    spans = [span for chip, *span in plan]
    for m in range(members):
        energy = read_scalars(of_member(ws, spans, m), 1)
        out[m] = with_scalars(acc[m], energy).astype(out.dtype)


def combine_kernel(mine, theirs, one, two):
    half = one.shape[2]
    for m in range(one.shape[0]):
        energy = read_scalars([mine.at[m], theirs.at[m]], 1)
        value = mine[m] + theirs[m].astype(F32)
        one[m] = with_scalars(value[:, :half], energy).astype(BF16)
        two[m] = value[:, half:].astype(BF16)


def combine_columns_kernel(mine, theirs, *outs):
    obs = lax.axis_index("obs")
    for m in range(mine.shape[0]):
        energy = read_scalars([mine.at[m], theirs.at[m]], 1)
        for i, out in enumerate(outs):
            lane = pl.ds(pl.multiple_of((obs ^ i) * LANES, LANES), LANES)
            value = mine[m, :, lane] + theirs[m, :, lane].astype(F32)
            out[m] = with_scalars(value, energy).astype(BF16)


def update_kernel(parts, later, *refs):
    pieces, refs = refs[:parts], refs[parts:]
    sd, vert, vert_t, state, residual = refs[:5]
    if later:
        old_direction, old_solution, residual_out, solution_out, moved, direction_out = refs[5:]
    else:
        residual_out, solution_out, moved = refs[5:]
    obs = lax.axis_index("obs")
    mine = pl.ds(pl.multiple_of(obs * LANES, LANES), LANES)
    for m in range(residual.shape[0]):
        t = joined(pieces, m)
        (energy,) = read_scalars([x.at[m] for x in pieces[: parts // 2]], 1)
        norm, square, beta = state[m, 0:1, 0:1], state[m, 1:2, 0:1], state[m, 2:3, 0:1]
        alpha = norm / (square + energy)
        r = residual[m]
        if later:
            d = r + beta * old_direction[m]
            direction_out[m] = d
            step = direction_out[m, :, mine]
            solution_out[m] = old_solution[m] + alpha * step
        else:
            d = r
            solution_out[m] = alpha * residual[m, :, mine]
        r = r - alpha * (d + dot(vert_t[...], sd[...] * t))
        residual_out[m] = r
        x = sd[...] * dot(vert[...], r)
        moved[m] = with_scalars(x, [total(r * r), total(r * d)]).astype(BF16)


def last_kernel(parts, later, lev, *refs):
    pieces, refs = refs[:parts], refs[parts:]
    sd, vert, vert_t, state, residual = refs[:5]
    increment_out, residual_out = refs[-2:]
    obs = lax.axis_index("obs")
    mine = pl.ds(pl.multiple_of(obs * LANES, LANES), LANES)
    for m in range(residual.shape[0]):
        t = add([x[m] for x in pieces])
        (energy,) = read_scalars([x.at[m] for x in pieces], 1)
        norm, square, beta = state[m, 0:1, 0:1], state[m, 1:2, 0:1], state[m, 2:3, 0:1]
        alpha = norm / (square + energy)
        d = r = residual[m, :, mine]
        if later:
            old_direction, old_solution = refs[5:7]
            d = r + beta * old_direction[m, :, mine]
        solution = alpha * d
        if later:
            solution = old_solution[m] + solution
        r = r - alpha * (d + dot(vert_t[...], sd[...] * t))
        increment = sd[...] * dot(vert[...], solution)
        increment_out[:, m, :] = increment[0:lev]
        residual_out[:, m, :] = r[0:lev]


def per_device(
    n_slab,
    n_obs,
    innovation,
    obs_precision,
    seeds,
    col_sd,
    vert_factor,
    h_values,
    block_obs,
    block_col,
    entry_count,
):
    blocks, lev, profiles = innovation.shape
    members = seeds.shape[0]
    chips = n_slab // 2
    halves = n_slab // blocks
    width = profiles // halves
    colblocks = n_obs
    assert halves * blocks == n_slab and width % LANES == 0 and col_sd.shape[0] == 1
    assert chips & (chips - 1) == 0 and n_obs & (n_obs - 1) == 0
    levp = (lev + 1 + 15) // 16 * 16
    rows = members * levp
    lanes = colblocks * LANES
    field = (members, levp, LANES)
    half_field = (members, levp, lanes // 2)
    slab_field = (members, levp, lanes)
    panel = (members, levp, width)
    some, rest = members // 2, members - members // 2
    via = chips == 4 and some > 0
    if via:
        plan = [(0, 0, members), (1, 0, members)]
        plan += [(i, *span) for i in (2, 3) for span in ((0, some), (some, rest))]
    else:
        plan = [(i, 0, members) for i in range(chips)]
    pad = ((0, levp - lev), (0, levp - lev))
    vert = jnp.pad(vert_factor, pad)
    vert_t = jnp.pad(vert_factor.T, pad)
    h_block = h_values.reshape(h_values.shape[2:])
    innovation = jnp.transpose(innovation, (1, 0, 2))
    obs_precision = jnp.transpose(obs_precision, (1, 0, 2))
    product = n_slab * width * lanes * rows
    small = 12 * rows * levp * LANES
    plane_bits = [1 << k for k in range(n_obs.bit_length() - 1)]

    def along(x, i):
        return lax.ppermute(x, "slab", [(s, s ^ (2 * i)) for s in range(n_slab)])

    def plane(x, i):
        return lax.ppermute(x, "obs", [(o, o ^ i) for o in range(n_obs)])

    def swap(x):
        return lax.ppermute(x, "slab", [(s, s ^ 1) for s in range(n_slab)])

    def plane_sum(one, two, scalars):
        for step, bit in enumerate(plane_bits):
            far = plane_bits[len(plane_bits) - 1 - step]
            one_more, two_more = plane(one, bit), plane(two, far)
            if step == 0 and not scalars:
                one, two = call(
                    stage_kernel,
                    [struct(half_field, BF16)] * 2,
                    [pltpu.SemaphoreType.DMA((2,))],
                    0,
                    one,
                    two,
                    space=HBM,
                )
            parts = [one, one_more, two, two_more]
            if step < len(plane_bits) - 1:
                one, two = call(
                    functools.partial(add_halves_kernel, scalars),
                    [struct(half_field, BF16)] * 2,
                    [],
                    0,
                    *parts,
                )
        return parts

    def line_sum(ys):
        if not via:
            return [y if i == 0 else along(y, i) for i, y in enumerate(ys)], [
                (0, members) for y in ys
            ]
        near, next_, far, far_rest, last_, last_rest = ys
        passed = along(last_, 1)
        far_rest, last_rest, next_ = along(far_rest, 2), along(last_rest, 3), along(next_, 1)
        (far,) = call(
            functools.partial(add_kernel, 2),
            [struct((some, levp, width), BF16)],
            [],
            0,
            far,
            passed,
        )
        spans = [(0, members), (0, members), (0, some), (some, rest), (some, rest)]
        return [near, next_, along(far, 2), far_rest, last_rest], spans

    def line_gather(w, *parts):
        if not via:
            return [w if i == 0 else along(w, i) for i in range(chips)]
        one, two = parts
        far = along(one, 2)
        far_rest, last_rest, next_ = along(two, 2), along(two, 3), along(w, 1)
        return [w, next_, far, far_rest, along(far, 1), last_rest]

    dense = struct((chips, colblocks, LANES, width), BF16)
    own, for_partner, *partials = call(
        functools.partial(start_kernel, (chips, halves)),
        [dense, dense] + [struct(half_field, BF16)] * 2,
        [
            pltpu.SMEM(seeds.shape, jnp.int32),
            pltpu.SMEM(block_obs.shape, jnp.int32),
            pltpu.SMEM(block_col.shape, jnp.int32),
            pltpu.SMEM(entry_count.shape, jnp.int32),
            pltpu.VMEM(col_sd.shape, F32),
            pltpu.VMEM((blocks, lev, profiles), F32),
            pltpu.VMEM((blocks, lev, profiles), F32),
            pltpu.VMEM((n_slab, members, levp, width), F32),
            pltpu.VMEM((2, members, levp, width), F32),
            pltpu.VMEM((rows, lanes), F32),
            pltpu.SemaphoreType.DMA((5 + 2 * blocks,)),
            pltpu.SemaphoreType.DMA((h_block.shape[0] * halves,)),
        ],
        2 * product,
        seeds,
        block_obs,
        block_col,
        entry_count,
        col_sd,
        innovation,
        obs_precision,
        h_block,
        space=HBM,
        limit=60,
    )
    ps = plane_sum(*partials, 0)
    partner = swap(for_partner)
    (precision,) = call(
        functools.partial(precision_kernel, halves),
        [struct((levp, width), F32)],
        [],
        0,
        obs_precision,
    )
    slab_sd, residual, moved = call(
        functools.partial(first_kernel, len(ps)),
        [struct((1, lanes), F32), struct(slab_field, F32), struct(slab_field, BF16)],
        [],
        small * colblocks,
        *ps,
        vert,
        vert_t,
    )
    direction = total_step = image = state = None
    for sweep in range(ITERS):
        later, last = sweep > 0, sweep == ITERS - 1
        ys = call(
            functools.partial(forward_kernel, plan),
            [
                struct((count, levp, width), F32 if at == 0 or (via and at == 2) else BF16)
                for at, (unused, unused, count) in enumerate(plan)
            ],
            [],
            2 * product,
            moved,
            swap(moved),
            own,
            partner,
        )
        ys, spans = line_sum(ys)
        image, state, *weighted = call(
            functools.partial(weigh_kernel, later, spans),
            [struct(panel, F32), struct((members, 8, LANES), F32), struct(panel, BF16)]
            + ([struct((n, levp, width), BF16) for n in (some, rest)] if via else []),
            [],
            0,
            *ys,
            precision,
            *([image, state] if later else []),
        )
        ws = line_gather(*weighted)
        (theirs,) = call(
            functools.partial(adjoint_kernel, plan),
            [struct(slab_field, BF16)],
            [],
            product,
            *ws,
            partner,
        )
        theirs = swap(theirs)
        (mine,) = call(
            functools.partial(adjoint_kernel, plan),
            [struct(slab_field, F32)],
            [],
            product,
            *ws,
            own,
        )
        known = [vert, vert_t, state, residual]
        if later:
            known += [direction, total_step]
        if last:
            ps = call(
                combine_columns_kernel, [struct(field, BF16)] * n_obs, [], 0, mine, theirs
            )
            ps = [x if i == 0 else plane(x, i) for i, x in enumerate(ps)]
            outputs = call(
                functools.partial(last_kernel, len(ps), later, lev),
                [struct((lev, members, LANES), F32)] * 2,
                [],
                small,
                *ps,
                col_sd,
                *known,
            )
            break
        ps = call(combine_kernel, [struct(half_field, BF16)] * 2, [], 0, mine, theirs)
        ps = plane_sum(*ps, 1)
        outs = [struct(slab_field, F32), struct(field, F32), struct(slab_field, BF16)]
        if later:
            outs.append(struct(slab_field, F32))
        r, total_step, moved, *d = call(
            functools.partial(update_kernel, len(ps), later),
            outs,
            [],
            small * colblocks,
            *ps,
            slab_sd,
            *known,
        )
        direction, residual = (d[0] if later else residual), r
    return tuple(jnp.transpose(x, (1, 0, 2))[None] for x in outputs)


def solution(mesh):
    return jax.shard_map(
        functools.partial(per_device, mesh.shape["slab"], mesh.shape["obs"]),
        mesh=mesh,
        in_specs=(
            P("obs", None, None),
            P("obs", None, None),
            P(),
            P(("slab", "obs"), None),
            P(),
            P("slab", "obs", None, None, None),
            P("slab", "obs", None),
            P("slab", "obs", None),
            P("slab", "obs"),
        ),
        out_specs=(P(("slab", "obs"), None, None, None), P(("slab", "obs"), None, None, None)),
        check_vma=False,
    )
```

```python
import functools

import jax
import jax.numpy as jnp
from jax import lax
from jax.experimental import pallas as pl
from jax.experimental.pallas import tpu as pltpu
from jax.sharding import PartitionSpec as P

ITERS = 2
LANES = 128
PIECES = 3
PRIME = 32749
VMEM = pl.BlockSpec(memory_space=pltpu.VMEM)
HBM = pl.BlockSpec(memory_space=pltpu.HBM)
F32 = jnp.float32
BF16 = jnp.bfloat16
NT = (((1,), (1,)), ((), ()))


def call(kernel, outs, scratch, flops, *args, space=VMEM, limit=24):
    nbytes = sum(a.size * a.dtype.itemsize for a in (*args, *outs))
    return pl.pallas_call(
        kernel,
        out_shape=outs,
        in_specs=[space] * len(args),
        out_specs=[VMEM] * len(outs),
        scratch_shapes=scratch,
        compiler_params=pltpu.CompilerParams(vmem_limit_bytes=limit * 1024 * 1024),
        cost_estimate=pl.CostEstimate(flops=flops, bytes_accessed=nbytes, transcendentals=0),
    )(*args)


def struct(shape, dtype):
    return jax.ShapeDtypeStruct(shape, dtype)


def place():
    slab = lax.axis_index("slab")
    return slab // 2, slab % 2, lax.axis_index("obs")


def add(parts):
    value = parts[0].astype(F32)
    for part in parts[1:]:
        value = value + part.astype(F32)
    return value


def dot(matrix, x):
    high = x.astype(BF16)
    rest = (x - high.astype(F32)).astype(BF16)
    x = jnp.concatenate([high, rest, high], axis=0)
    return jnp.dot(matrix, x, preferred_element_type=F32)


def total(x):
    return jnp.sum(jnp.sum(x, axis=0, keepdims=True), axis=1, keepdims=True)


def with_scalars(body, values):
    rows = lax.broadcasted_iota(jnp.int32, body.shape, 0)
    lanes = lax.broadcasted_iota(jnp.int32, body.shape, 1)
    line = jnp.zeros(body.shape, F32)
    for q, value in enumerate(values):
        rest = value
        for piece in range(PIECES):
            part = rest.astype(BF16).astype(F32)
            rest = rest - part
            line = jnp.where(lanes == q * PIECES + piece, part, line)
    return jnp.where(rows == body.shape[0] - 1, line, body)


def read_scalars(refs, count):
    rows = refs[0].shape[0]
    tail = add([ref[rows - 16 : rows, 0:LANES] for ref in refs])
    sub = lax.broadcasted_iota(jnp.int32, tail.shape, 0)
    lanes = lax.broadcasted_iota(jnp.int32, tail.shape, 1)
    found = []
    for q in range(count):
        mine = (sub == 15) & (lanes >= q * PIECES) & (lanes < (q + 1) * PIECES)
        found.append(total(jnp.where(mine, tail, 0.0)))
    return found


def of_member(refs, spans, m):
    return [
        ref.at[m - first + skip]
        for ref, (first, count, skip) in zip(refs, spans)
        if first <= m < first + count
    ]


def remainder(x, factor):
    return x - (x.astype(F32) * factor).astype(jnp.int32) * PRIME


def start_kernel(
    dims, seeds_in, ids_in, cols_in, count_in, sd_in, innov_in, prec_in, h, own, partner, *rest
):
    chips, halves = dims
    outs = rest[:-12]
    seeds, ids, cols, count, sd, innov, prec, hashed, scratch, acc, sems, h_sems = rest[-12:]
    z, core, obs = place()
    blocks, lev, profiles = innov.shape
    colblocks, width = own.shape[1], own.shape[3]
    members, levp = scratch.shape[1], scratch.shape[2]

    pairs = [(seeds_in, seeds), (ids_in, ids), (cols_in, cols), (count_in, count), (sd_in, sd)]
    small = [pltpu.make_async_copy(x, y, sems.at[i]) for i, (x, y) in enumerate(pairs)]
    for copy in small:
        copy.start()
    large = []
    for b in range(blocks):
        at = len(pairs) + 2 * b
        large.append(pltpu.make_async_copy(innov_in.at[:, b, :], innov.at[b], sems.at[at]))
        large.append(pltpu.make_async_copy(prec_in.at[:, b, :], prec.at[b], sems.at[at + 1]))
    for copy in large:
        copy.start()
    own[...] = jnp.zeros_like(own)
    partner[...] = jnp.zeros_like(partner)
    scratch[...] = jnp.zeros_like(scratch)
    for copy in small:
        copy.wait()

    def tile_copy(n, half, target):
        lanes = pl.ds(half * width, width)
        return pltpu.make_async_copy(h.at[n, :, lanes], target, h_sems.at[n * halves + half])

    def put(n, carry):
        for half in range(halves):
            piece, k = ids[0, 0, n] * halves + half, cols[0, 0, n]

            @pl.when(piece % 2 == core)
            def _():
                tile_copy(n, half, own.at[piece // 2, k]).start()

            @pl.when(piece % 2 != core)
            def _():
                tile_copy(n, half, partner.at[piece // 2, k]).start()

        return carry

    lax.fori_loop(0, count[0, 0], put, 0)

    starts = [lax.rem(seeds[m], PRIME) - PRIME for m in range(members)]
    order = [(source, zz) for source in range(2) for zz in range(chips)]
    shape = (levp, width)
    spot = lax.broadcasted_iota(jnp.int32, shape, 0) * profiles
    spot = spot + lax.broadcasted_iota(jnp.int32, shape, 1)
    low = (1.0 - 2.0**-21) / PRIME

    def piece_at(at):
        source, zz = order[at]
        return 2 * zz + (core if source == 0 else 1 - core)

    def draw(at):
        piece = piece_at(at)
        first = (obs * blocks + piece // halves) * (lev * profiles) + (piece % halves) * width
        base = remainder(7919 * remainder(spot + first, 1.0 / PRIME), 1.0 / PRIME)
        for m in range(members):
            k0 = base + starts[m]
            k1 = remainder(k0 * k0 + 12345, 1.0 / PRIME)
            k2 = remainder(k1 * k1 + 2719, low)
            k2 = jnp.where(k2 >= PRIME, k2 - PRIME, k2)
            hashed[at, m] = k2.astype(F32)

    def adjoint(at):
        source, zz = order[at]
        piece = piece_at(at)
        b = piece // halves
        if halves == 1:
            p, d = prec[b], innov[b]
        else:
            lanes = pl.ds(pl.multiple_of((piece % halves) * width, LANES), width)
            p, d = prec[b, :, lanes], innov[b, :, lanes]
        gain = 3.4 * p * lax.rsqrt(p)
        offset = p * d - 0.5 * gain
        gain = gain * (1.0 / PRIME)
        for m in range(members):
            scratch[at % 2, m, 0:lev, :] = offset + gain * hashed[at, m, 0:lev, :]
        w = scratch[at % 2].astype(BF16).reshape(members * levp, width)
        tiles = (own if source == 0 else partner)[zz].reshape(colblocks * LANES, width)
        part = lax.dot_general(w, tiles, NT, preferred_element_type=F32)
        if at == 0:
            acc[...] = part
        else:
            acc[...] += part

    early = len(order) // 2
    for at in range(early):
        draw(at)
    for copy in large:
        copy.wait()

    def arrive(n, carry):
        for half in range(halves):
            tile_copy(n, half, own.at[0, 0]).wait()
        return carry

    lax.fori_loop(0, count[0, 0], arrive, 0)

    for at in range(len(order)):
        if at + early < len(order):
            draw(at + early)
        adjoint(at)

    for m in range(members):
        value = acc[m * levp : (m + 1) * levp, :]
        if m == 0:
            value = with_columns(value, jnp.concatenate([sd[...]] * colblocks, axis=1), obs)
        put_halves(outs, m, value)


def put_halves(outs, m, value):
    half = value.shape[1] // 2
    for one, two in zip(outs[::2], outs[1::2]):
        if 0 <= m < one.shape[0]:
            one[m] = value[:, :half].astype(BF16)
            two[m] = value[:, half:].astype(BF16)
        m -= one.shape[0]


def with_columns(body, line, obs):
    rows = lax.broadcasted_iota(jnp.int32, body.shape, 0)
    mine = lax.broadcasted_iota(jnp.int32, body.shape, 1) // LANES == obs
    rest = line
    for piece in range(PIECES):
        part = rest.astype(BF16).astype(F32)
        rest = rest - part
        body = jnp.where((rows == body.shape[0] - 1 - PIECES + piece) & mine, part, body)
    return body


def read_columns(body):
    tail = body[body.shape[0] - 8 :]
    sub = lax.broadcasted_iota(jnp.int32, tail.shape, 0)
    mine = (sub >= 7 - PIECES) & (sub < 7)
    return jnp.sum(jnp.where(mine, tail, 0.0), axis=0, keepdims=True)


def precision_kernel(halves, prec, out):
    z, core, unused = place()
    piece = 2 * z + core
    lev, blocks, unused = prec.shape
    width = out.shape[1]
    block = lax.broadcasted_iota(jnp.int32, (lev, blocks, width), 1)
    if halves == 1:
        mine = prec[...]
    else:
        mine = prec[:, :, pl.ds(pl.multiple_of((piece % halves) * width, LANES), width)]
    out[...] = jnp.zeros_like(out)
    out[0:lev, :] = jnp.sum(jnp.where(block == piece // halves, mine, 0.0), axis=1)


def joined(pieces, m):
    for at in range(0, len(pieces), 4):
        one, one_more, two, two_more = pieces[at : at + 4]
        if m < one.shape[0]:
            halves = [add([one[m], one_more[m]]), add([two[m], two_more[m]])]
            return jnp.concatenate(halves, axis=1), [one.at[m], one_more.at[m]]
        m -= one.shape[0]


def first_kernel(parts, *refs):
    pieces = refs[:parts]
    vert, vert_t, sd_out, residual, moved = refs[parts:]
    for m in range(residual.shape[0]):
        t, unused = joined(pieces, m)
        if m == 0:
            sd = read_columns(t)
            sd_out[...] = sd
        r = dot(vert_t[...], sd * t)
        residual[m] = r
        x = sd * dot(vert[...], r)
        moved[m] = with_scalars(x, [total(r * r)]).astype(BF16)


def add_kernel(scalars, *refs):
    parts, out = refs[:-1], refs[-1]
    for m in range(out.shape[0]):
        value = add([x[m] for x in parts])
        if scalars:
            value = with_scalars(value, read_scalars([x.at[m] for x in parts], scalars))
        out[m] = value.astype(BF16)


def add_halves_kernel(scalars, one, one_more, two, two_more, one_out, two_out):
    add_kernel(scalars, one, one_more, one_out)
    add_kernel(0, two, two_more, two_out)


def stage_kernel(*refs):
    sems = refs[-1]
    count = len(refs) // 2
    copies = [
        pltpu.make_async_copy(refs[i], refs[count + i], sems.at[i]) for i in range(count)
    ]
    for copy in copies:
        copy.start()
    for copy in copies:
        copy.wait()


def forward_kernel(sends, mine, other, own, partner, *outs):
    z, core, obs = place()
    members, levp, lanes = mine.shape
    chips, width = own.shape[0], own.shape[3]
    rows = members * levp
    scalars = [read_scalars([mine.at[m], other.at[m]], 2) for m in range(members)]
    for i in reversed(range(chips)):
        zz = z ^ i
        y = jnp.dot(
            mine[...].reshape(rows, lanes),
            own[zz].reshape(lanes, width),
            preferred_element_type=F32,
        )
        y = y + jnp.dot(
            other[...].reshape(rows, lanes),
            partner[zz].reshape(lanes, width),
            preferred_element_type=F32,
        )
        y = y.reshape(members, levp, width)
        for out, parts in zip(outs, sends):
            at = 0
            for chip, first, count in parts:
                for m in range(first, first + count if chip == i else first):
                    out[at + m - first] = with_scalars(y[m], scalars[m]).astype(out.dtype)
                at += count


def weigh_kernel(later, last, spans, *refs):
    ys, refs = refs[: len(spans)], refs[len(spans) :]
    prec = refs[0]
    state, weighted, *parts = refs[3 if later else 1 :]
    if not last:
        *parts, image = parts
    p = prec[...]
    for m in range(weighted.shape[0]):
        mine = of_member(ys, spans, m)
        y = add([x[...] for x in mine])
        norm, cross = read_scalars(mine, 2)
        if later:
            old_image, old = refs[1:3]
            old_norm, old_square = old[m, 0:1, 0:1], old[m, 1:2, 0:1]
            beta = norm / old_norm
            square = norm + 2.0 * beta * cross + beta * beta * old_square
            y = y + beta * old_image[m]
        else:
            beta = jnp.zeros_like(norm)
            square = norm
        scaled = p * y
        if not last:
            image[m] = y
        value = with_scalars(scaled, [total(scaled * y)]).astype(BF16)
        weighted[m] = value
        first = 0
        for part in parts:
            if first <= m < first + part.shape[0]:
                part[m - first] = value
            first += part.shape[0]
        sub = lax.broadcasted_iota(jnp.int32, (8, LANES), 0)
        state[m] = jnp.where(sub == 0, norm, jnp.where(sub == 1, square, beta))


def adjoint_kernel(plan, *refs):
    z, core, obs = place()
    ws, tiles, out = refs[: len(plan)], refs[len(plan)], refs[len(plan) + 1]
    members, levp, lanes = out.shape
    width = ws[0].shape[2]
    acc = None
    for i in range(tiles.shape[0]):
        w = [ref[...].reshape(-1, width) for ref, (chip, *span) in zip(ws, plan) if chip == i]
        w = w[0] if len(w) == 1 else jnp.concatenate(w, axis=0)
        part = lax.dot_general(
            w, tiles[z ^ i].reshape(lanes, width), NT, preferred_element_type=F32
        )
        acc = part if i == 0 else acc + part
    acc = acc.reshape(members, levp, lanes)
    spans = [(*span, 0) for chip, *span in plan]
    for m in range(members):
        energy = read_scalars(of_member(ws, spans, m), 1)
        out[m] = with_scalars(acc[m], energy).astype(out.dtype)


def combine_kernel(mine, theirs, *outs):
    for m in range(mine.shape[0]):
        energy = read_scalars([mine.at[m], theirs.at[m]], 1)
        put_halves(outs, m, with_scalars(mine[m] + theirs[m].astype(F32), energy))


def combine_columns_kernel(mine, theirs, *outs):
    obs = lax.axis_index("obs")
    for m in range(mine.shape[0]):
        energy = read_scalars([mine.at[m], theirs.at[m]], 1)
        for i, out in enumerate(outs):
            lane = pl.ds(pl.multiple_of((obs ^ i) * LANES, LANES), LANES)
            value = mine[m, :, lane] + theirs[m, :, lane].astype(F32)
            out[m] = with_scalars(value, energy).astype(BF16)


def update_kernel(parts, later, *refs):
    pieces, refs = refs[:parts], refs[parts:]
    sd, vert, vert_t, state, residual = refs[:5]
    if later:
        old_direction, old_solution, residual_out, solution_out, moved, direction_out = refs[5:]
    else:
        residual_out, solution_out, moved = refs[5:]
    obs = lax.axis_index("obs")
    mine = pl.ds(pl.multiple_of(obs * LANES, LANES), LANES)
    for m in range(residual.shape[0]):
        t, places = joined(pieces, m)
        (energy,) = read_scalars(places, 1)
        norm, square, beta = state[m, 0:1, 0:1], state[m, 1:2, 0:1], state[m, 2:3, 0:1]
        alpha = norm / (square + energy)
        r = residual[m]
        if later:
            d = r + beta * old_direction[m]
            direction_out[m] = d
            step = direction_out[m, :, mine]
            solution_out[m] = old_solution[m] + alpha * step
        else:
            d = r
            solution_out[m] = alpha * residual[m, :, mine]
        r = r - alpha * (d + dot(vert_t[...], sd[...] * t))
        residual_out[m] = r
        x = sd[...] * dot(vert[...], r)
        moved[m] = with_scalars(x, [total(r * r), total(r * d)]).astype(BF16)


def last_kernel(parts, later, lev, *refs):
    pieces, refs = refs[:parts], refs[parts:]
    sd, vert, vert_t, state, residual = refs[:5]
    increment_out, residual_out = refs[-2:]
    obs = lax.axis_index("obs")
    mine = pl.ds(pl.multiple_of(obs * LANES, LANES), LANES)
    for m in range(residual.shape[0]):
        t = add([x[m] for x in pieces])
        (energy,) = read_scalars([x.at[m] for x in pieces], 1)
        norm, square, beta = state[m, 0:1, 0:1], state[m, 1:2, 0:1], state[m, 2:3, 0:1]
        alpha = norm / (square + energy)
        d = r = residual[m, :, mine]
        if later:
            old_direction, old_solution = refs[5:7]
            d = r + beta * old_direction[m, :, mine]
        solution = alpha * d
        if later:
            solution = old_solution[m] + solution
        r = r - alpha * (d + dot(vert_t[...], sd[...] * t))
        increment = sd[...] * dot(vert[...], solution)
        increment_out[:, m, :] = increment[0:lev]
        residual_out[:, m, :] = r[0:lev]


def per_device(
    n_slab,
    n_obs,
    innovation,
    obs_precision,
    seeds,
    col_sd,
    vert_factor,
    h_values,
    block_obs,
    block_col,
    entry_count,
):
    blocks, lev, profiles = innovation.shape
    members = seeds.shape[0]
    chips = n_slab // 2
    halves = n_slab // blocks
    width = profiles // halves
    colblocks = n_obs
    assert halves * blocks == n_slab and width % LANES == 0 and col_sd.shape[0] == 1
    assert chips & (chips - 1) == 0 and n_obs & (n_obs - 1) == 0
    levp = (lev + 1 + 15) // 16 * 16
    rows = members * levp
    lanes = colblocks * LANES
    field = (members, levp, LANES)
    slab_field = (members, levp, lanes)
    panel = (members, levp, width)
    some, rest = members // 2, members - members // 2
    half_fields = [
        struct((n, levp, lanes // 2), BF16) for n in (some, rest) if n for half in range(2)
    ]
    via = chips == 4 and some > 0
    if via:
        plan = [(0, 0, members), (1, 0, members)]
        plan += [(i, *span) for i in (2, 3) for span in ((0, some), (some, rest))]
        sends = [[plan[0]], [plan[4], plan[1]], [plan[2]], [plan[3]], [plan[5]]]
    else:
        plan = [(i, 0, members) for i in range(chips)]
        sends = [[part] for part in plan]
    pad = ((0, levp - lev), (0, levp - lev))
    high = lax.reduce_precision(vert_factor, 8, 7)
    low = vert_factor - high
    vert, vert_t = [
        jnp.concatenate([jnp.pad(x, pad).astype(BF16) for x in parts], axis=1)
        for parts in ((high, high, low), (high.T, high.T, low.T))
    ]
    h_block = h_values.reshape(h_values.shape[2:])
    innovation = jnp.transpose(innovation, (1, 0, 2))
    obs_precision = jnp.transpose(obs_precision, (1, 0, 2))
    product = n_slab * width * lanes * rows
    small = 12 * rows * levp * LANES
    plane_bits = [1 << k for k in range(n_obs.bit_length() - 1)]

    def along(x, i):
        return lax.ppermute(x, "slab", [(s, s ^ (2 * i)) for s in range(n_slab)])

    def plane(x, i):
        return lax.ppermute(x, "obs", [(o, o ^ i) for o in range(n_obs)])

    def swap(x):
        return lax.ppermute(x, "slab", [(s, s ^ 1) for s in range(n_slab)])

    def plane_sum(halves, staged):
        halves = list(halves)
        moved_halves = [None] * len(halves)
        for step, bit in enumerate(plane_bits):
            bits = [bit, plane_bits[len(plane_bits) - 1 - step]]
            for at in range(0, len(halves), 2):
                if step > 0:
                    one, two = halves[at : at + 2]
                    one_more, two_more = moved_halves[at : at + 2]
                    halves[at : at + 2] = call(
                        functools.partial(add_halves_kernel, 0 if staged else 1),
                        [struct(one.shape, BF16)] * 2,
                        [],
                        0,
                        one,
                        one_more,
                        two,
                        two_more,
                    )
                for half in range(2):
                    moved_halves[at + half] = plane(halves[at + half], bits[half])
            if step == 0 and staged:
                halves[:] = call(
                    stage_kernel,
                    [struct(x.shape, BF16) for x in halves],
                    [pltpu.SemaphoreType.DMA((len(halves),))],
                    0,
                    *halves,
                    space=HBM,
                )
        return [x for pair in zip(halves, moved_halves) for x in pair]

    def line_sum(ys):
        if not via:
            return [y if i == 0 else along(y, i) for i, y in enumerate(ys)], [
                (0, members, 0) for y in ys
            ]
        near, next_, far, far_rest, last_rest = ys
        next_ = along(next_, 1)
        far_rest, last_rest = along(far_rest, 2), along(last_rest, 3)
        (far,) = call(
            functools.partial(add_kernel, 2),
            [struct((some, levp, width), BF16)],
            [],
            0,
            far,
            next_,
        )
        spans = [(0, members, 0), (0, members, some), (0, some, 0)]
        spans += [(some, rest, 0), (some, rest, 0)]
        return [near, next_, along(far, 2), far_rest, last_rest], spans

    def line_gather(w, *parts):
        if not via:
            return [w if i == 0 else along(w, i) for i in range(chips)]
        one, two = parts
        far = along(one, 2)
        far_rest, last_rest, next_ = along(two, 2), along(two, 3), along(w, 1)
        return [w, next_, far, far_rest, along(far, 1), last_rest]

    dense = struct((chips, colblocks, LANES, width), BF16)
    own, for_partner, *partials = call(
        functools.partial(start_kernel, (chips, halves)),
        [dense, dense] + half_fields,
        [
            pltpu.SMEM(seeds.shape, jnp.int32),
            pltpu.SMEM(block_obs.shape, jnp.int32),
            pltpu.SMEM(block_col.shape, jnp.int32),
            pltpu.SMEM(entry_count.shape, jnp.int32),
            pltpu.VMEM(col_sd.shape, F32),
            pltpu.VMEM((blocks, lev, profiles), F32),
            pltpu.VMEM((blocks, lev, profiles), F32),
            pltpu.VMEM((n_slab, members, levp, width), F32),
            pltpu.VMEM((2, members, levp, width), F32),
            pltpu.VMEM((rows, lanes), F32),
            pltpu.SemaphoreType.DMA((5 + 2 * blocks,)),
            pltpu.SemaphoreType.DMA((h_block.shape[0] * halves,)),
        ],
        2 * product,
        seeds,
        block_obs,
        block_col,
        entry_count,
        col_sd,
        innovation,
        obs_precision,
        h_block,
        space=HBM,
        limit=60,
    )
    ps = plane_sum(partials, True)
    partner = swap(for_partner)
    (precision,) = call(
        functools.partial(precision_kernel, halves),
        [struct((levp, width), F32)],
        [],
        0,
        obs_precision,
    )
    slab_sd, residual, moved = call(
        functools.partial(first_kernel, len(ps)),
        [struct((1, lanes), F32), struct(slab_field, F32), struct(slab_field, BF16)],
        [],
        small * colblocks,
        *ps,
        vert,
        vert_t,
    )
    direction = total_step = image = state = None
    for sweep in range(ITERS):
        later, last = sweep > 0, sweep == ITERS - 1
        ys = call(
            functools.partial(forward_kernel, sends),
            [
                struct(
                    (sum(count for *unused, count in parts), levp, width),
                    F32 if at == 0 or (via and at == 2) else BF16,
                )
                for at, parts in enumerate(sends)
            ],
            [],
            2 * product,
            moved,
            swap(moved),
            own,
            partner,
        )
        ys, spans = line_sum(ys)
        state, *weighted = call(
            functools.partial(weigh_kernel, later, last, spans),
            [struct((members, 8, LANES), F32), struct(panel, BF16)]
            + ([struct((n, levp, width), BF16) for n in (some, rest)] if via else [])
            + ([] if last else [struct(panel, F32)]),
            [],
            0,
            *ys,
            precision,
            *([image, state] if later else []),
        )
        if not last:
            *weighted, image = weighted
        ws = line_gather(*weighted)
        (theirs,) = call(
            functools.partial(adjoint_kernel, plan),
            [struct(slab_field, BF16)],
            [],
            product,
            *ws,
            partner,
        )
        theirs = swap(theirs)
        (mine,) = call(
            functools.partial(adjoint_kernel, plan),
            [struct(slab_field, F32)],
            [],
            product,
            *ws,
            own,
        )
        known = [vert, vert_t, state, residual]
        if later:
            known += [direction, total_step]
        if last:
            ps = call(
                combine_columns_kernel, [struct(field, BF16)] * n_obs, [], 0, mine, theirs
            )
            ps = [x if i == 0 else plane(x, i) for i, x in enumerate(ps)]
            outputs = call(
                functools.partial(last_kernel, len(ps), later, lev),
                [struct((lev, members, LANES), F32)] * 2,
                [],
                small,
                *ps,
                col_sd,
                *known,
            )
            break
        ps = call(combine_kernel, half_fields, [], 0, mine, theirs)
        ps = plane_sum(ps, False)
        outs = [struct(slab_field, F32), struct(field, F32), struct(slab_field, BF16)]
        if later:
            outs.append(struct(slab_field, F32))
        r, total_step, moved, *d = call(
            functools.partial(update_kernel, len(ps), later),
            outs,
            [],
            small * colblocks,
            *ps,
            slab_sd,
            *known,
        )
        direction, residual = (d[0] if later else residual), r
    return tuple(jnp.transpose(x, (1, 0, 2))[None] for x in outputs)


def solution(mesh):
    return jax.shard_map(
        functools.partial(per_device, mesh.shape["slab"], mesh.shape["obs"]),
        mesh=mesh,
        in_specs=(
            P("obs", None, None),
            P("obs", None, None),
            P(),
            P(("slab", "obs"), None),
            P(),
            P("slab", "obs", None, None, None),
            P("slab", "obs", None),
            P("slab", "obs", None),
            P("slab", "obs"),
        ),
        out_specs=(P(("slab", "obs"), None, None, None), P(("slab", "obs"), None, None, None)),
        check_vma=False,
    )
```

```python
import functools

import jax
import jax.numpy as jnp
from jax import lax
from jax.experimental import pallas as pl
from jax.experimental.pallas import tpu as pltpu
from jax.sharding import PartitionSpec as P

ITERS = 2
LANES = 128
PIECES = 3
PRIME = 32749
VMEM = pl.BlockSpec(memory_space=pltpu.VMEM)
HBM = pl.BlockSpec(memory_space=pltpu.HBM)
F32 = jnp.float32
BF16 = jnp.bfloat16
NT = (((1,), (1,)), ((), ()))


def call(kernel, outs, scratch, flops, *args, space=VMEM, limit=24):
    nbytes = sum(a.size * a.dtype.itemsize for a in (*args, *outs))
    return pl.pallas_call(
        kernel,
        out_shape=outs,
        in_specs=[space] * len(args),
        out_specs=[VMEM] * len(outs),
        scratch_shapes=scratch,
        compiler_params=pltpu.CompilerParams(vmem_limit_bytes=limit * 1024 * 1024),
        cost_estimate=pl.CostEstimate(flops=flops, bytes_accessed=nbytes, transcendentals=0),
    )(*args)


def struct(shape, dtype):
    return jax.ShapeDtypeStruct(shape, dtype)


def place():
    slab = lax.axis_index("slab")
    return slab // 2, slab % 2, lax.axis_index("obs")


def add(parts):
    value = parts[0].astype(F32)
    for part in parts[1:]:
        value = value + part.astype(F32)
    return value


def dot(matrix, x):
    high = x.astype(BF16)
    rest = (x - high.astype(F32)).astype(BF16)
    x = jnp.concatenate([high, rest, high], axis=0)
    return jnp.dot(matrix, x, preferred_element_type=F32)


def total(x):
    return jnp.sum(jnp.sum(x, axis=0, keepdims=True), axis=1, keepdims=True)


def with_scalars(body, values):
    rows = lax.broadcasted_iota(jnp.int32, body.shape, 0)
    lanes = lax.broadcasted_iota(jnp.int32, body.shape, 1)
    line = jnp.zeros(body.shape, F32)
    for q, value in enumerate(values):
        rest = value
        for piece in range(PIECES):
            part = rest.astype(BF16).astype(F32)
            rest = rest - part
            line = jnp.where(lanes == q * PIECES + piece, part, line)
    return jnp.where(rows == body.shape[0] - 1, line, body)


def read_scalars(refs, count):
    rows = refs[0].shape[0]
    tail = add([ref[rows - 16 : rows, 0:LANES] for ref in refs])
    sub = lax.broadcasted_iota(jnp.int32, tail.shape, 0)
    lanes = lax.broadcasted_iota(jnp.int32, tail.shape, 1)
    found = []
    for q in range(count):
        mine = (sub == 15) & (lanes >= q * PIECES) & (lanes < (q + 1) * PIECES)
        found.append(total(jnp.where(mine, tail, 0.0)))
    return found


def of_member(refs, spans, m):
    return [
        ref.at[m - first + skip]
        for ref, (first, count, skip) in zip(refs, spans)
        if first <= m < first + count
    ]


def remainder(x, factor):
    return x - (x.astype(F32) * factor).astype(jnp.int32) * PRIME


def start_kernel(
    dims, seeds_in, ids_in, cols_in, count_in, sd_in, innov_in, prec_in, h, own, partner, *rest
):
    chips, halves = dims
    outs = rest[:-12]
    seeds, ids, cols, count, sd, innov, prec, hashed, scratch, acc, sems, h_sems = rest[-12:]
    z, core, obs = place()
    blocks, lev, profiles = innov.shape
    colblocks, width = own.shape[1], own.shape[3]
    members, levp = scratch.shape[1], scratch.shape[2]

    pairs = [(seeds_in, seeds), (ids_in, ids), (cols_in, cols), (count_in, count), (sd_in, sd)]
    small = [pltpu.make_async_copy(x, y, sems.at[i]) for i, (x, y) in enumerate(pairs)]
    for copy in small:
        copy.start()
    large = []
    for b in range(blocks):
        at = len(pairs) + 2 * b
        large.append(pltpu.make_async_copy(innov_in.at[:, b, :], innov.at[b], sems.at[at]))
        large.append(pltpu.make_async_copy(prec_in.at[:, b, :], prec.at[b], sems.at[at + 1]))
    for copy in large:
        copy.start()
    own[...] = jnp.zeros_like(own)
    partner[...] = jnp.zeros_like(partner)
    scratch[...] = jnp.zeros_like(scratch)
    for copy in small:
        copy.wait()

    def tile_copy(n, half, target):
        lanes = pl.ds(half * width, width)
        return pltpu.make_async_copy(h.at[n, :, lanes], target, h_sems.at[n * halves + half])

    def put(n, carry):
        for half in range(halves):
            piece, k = ids[0, 0, n] * halves + half, cols[0, 0, n]

            @pl.when(piece % 2 == core)
            def _():
                tile_copy(n, half, own.at[piece // 2, k]).start()

            @pl.when(piece % 2 != core)
            def _():
                tile_copy(n, half, partner.at[piece // 2, k]).start()

        return carry

    lax.fori_loop(0, count[0, 0], put, 0)

    starts = [lax.rem(seeds[m], PRIME) - PRIME for m in range(members)]
    order = [(source, zz) for source in range(2) for zz in range(chips)]
    shape = (levp, width)
    spot = lax.broadcasted_iota(jnp.int32, shape, 0) * profiles
    spot = spot + lax.broadcasted_iota(jnp.int32, shape, 1)
    low = (1.0 - 2.0**-21) / PRIME

    def piece_at(at):
        source, zz = order[at]
        return 2 * zz + (core if source == 0 else 1 - core)

    def draw(at):
        piece = piece_at(at)
        first = (obs * blocks + piece // halves) * (lev * profiles) + (piece % halves) * width
        base = remainder(7919 * remainder(spot + first, 1.0 / PRIME), 1.0 / PRIME)
        for m in range(members):
            k0 = base + starts[m]
            k1 = remainder(k0 * k0 + 12345, 1.0 / PRIME)
            k2 = remainder(k1 * k1 + 2719, low)
            k2 = jnp.where(k2 >= PRIME, k2 - PRIME, k2)
            hashed[at, m] = k2.astype(F32)

    def adjoint(at):
        source, zz = order[at]
        piece = piece_at(at)
        b = piece // halves
        if halves == 1:
            p, d = prec[b], innov[b]
        else:
            lanes = pl.ds(pl.multiple_of((piece % halves) * width, LANES), width)
            p, d = prec[b, :, lanes], innov[b, :, lanes]
        gain = 3.4 * p * lax.rsqrt(p)
        offset = p * d - 0.5 * gain
        gain = gain * (1.0 / PRIME)
        for m in range(members):
            scratch[at % 2, m, 0:lev, :] = offset + gain * hashed[at, m, 0:lev, :]
        w = scratch[at % 2].astype(BF16).reshape(members * levp, width)
        tiles = (own if source == 0 else partner)[zz].reshape(colblocks * LANES, width)
        part = lax.dot_general(w, tiles, NT, preferred_element_type=F32)
        if at == 0:
            acc[...] = part
        else:
            acc[...] += part

    early = len(order) // 2
    for at in range(early):
        draw(at)
    for copy in large:
        copy.wait()

    def arrive(n, carry):
        for half in range(halves):
            tile_copy(n, half, own.at[0, 0]).wait()
        return carry

    lax.fori_loop(0, count[0, 0], arrive, 0)

    for at in range(len(order)):
        if at + early < len(order):
            draw(at + early)
        adjoint(at)

    for m in range(members):
        value = acc[m * levp : (m + 1) * levp, :]
        if m == 0:
            value = with_columns(value, jnp.concatenate([sd[...]] * colblocks, axis=1), obs)
        put_halves(outs, m, value)


def put_halves(outs, m, value):
    half = value.shape[1] // 2
    for one, two in zip(outs[::2], outs[1::2]):
        if 0 <= m < one.shape[0]:
            one[m] = value[:, :half].astype(BF16)
            two[m] = value[:, half:].astype(BF16)
        m -= one.shape[0]


def with_columns(body, line, obs):
    rows = lax.broadcasted_iota(jnp.int32, body.shape, 0)
    mine = lax.broadcasted_iota(jnp.int32, body.shape, 1) // LANES == obs
    rest = line
    for piece in range(PIECES):
        part = rest.astype(BF16).astype(F32)
        rest = rest - part
        body = jnp.where((rows == body.shape[0] - 1 - PIECES + piece) & mine, part, body)
    return body


def read_columns(body):
    tail = body[body.shape[0] - 8 :]
    sub = lax.broadcasted_iota(jnp.int32, tail.shape, 0)
    mine = (sub >= 7 - PIECES) & (sub < 7)
    return jnp.sum(jnp.where(mine, tail, 0.0), axis=0, keepdims=True)


def precision_kernel(halves, prec, out):
    z, core, unused = place()
    piece = 2 * z + core
    lev, blocks, unused = prec.shape
    width = out.shape[1]
    block = lax.broadcasted_iota(jnp.int32, (lev, blocks, width), 1)
    if halves == 1:
        mine = prec[...]
    else:
        mine = prec[:, :, pl.ds(pl.multiple_of((piece % halves) * width, LANES), width)]
    out[...] = jnp.zeros_like(out)
    out[0:lev, :] = jnp.sum(jnp.where(block == piece // halves, mine, 0.0), axis=1)


def joined(pieces, m):
    for at in range(0, len(pieces), 4):
        one, one_more, two, two_more = pieces[at : at + 4]
        if m < one.shape[0]:
            halves = [add([one[m], one_more[m]]), add([two[m], two_more[m]])]
            return jnp.concatenate(halves, axis=1), [one.at[m], one_more.at[m]]
        m -= one.shape[0]


def first_kernel(parts, *refs):
    pieces = refs[:parts]
    vert, vert_t, sd_out, residual, moved = refs[parts:]
    for m in range(residual.shape[0]):
        t, unused = joined(pieces, m)
        if m == 0:
            sd = read_columns(t)
            sd_out[...] = sd
        r = dot(vert_t[...], sd * t)
        residual[m] = r
        x = sd * dot(vert[...], r)
        moved[m] = with_scalars(x, [total(r * r)]).astype(BF16)


def add_kernel(scalars, *refs):
    parts, out = refs[:-1], refs[-1]
    for m in range(out.shape[0]):
        value = add([x[m] for x in parts])
        if scalars:
            value = with_scalars(value, read_scalars([x.at[m] for x in parts], scalars))
        out[m] = value.astype(BF16)


def add_halves_kernel(scalars, one, one_more, two, two_more, one_out, two_out):
    add_kernel(scalars, one, one_more, one_out)
    add_kernel(0, two, two_more, two_out)


def stage_kernel(*refs):
    sems = refs[-1]
    count = len(refs) // 2
    copies = [
        pltpu.make_async_copy(refs[i], refs[count + i], sems.at[i]) for i in range(count)
    ]
    for copy in copies:
        copy.start()
    for copy in copies:
        copy.wait()


def forward_kernel(sends, mine, other, own, partner, *outs):
    z, core, obs = place()
    members, levp, lanes = mine.shape
    width = own.shape[3]
    scalars = [read_scalars([mine.at[m], other.at[m]], 2) for m in range(members)]
    for out, (chip, first, count) in zip(outs, sends):
        zz = z ^ chip
        y = [
            jnp.dot(
                x[first : first + count].reshape(count * levp, lanes),
                tiles[zz].reshape(lanes, width),
                preferred_element_type=F32,
            )
            for x, tiles in ((mine, own), (other, partner))
        ]
        y = (y[0] + y[1]).reshape(count, levp, width)
        for m in range(count):
            out[m] = with_scalars(y[m], scalars[first + m]).astype(out.dtype)


def weigh_kernel(later, last, spans, *refs):
    ys, refs = refs[: len(spans)], refs[len(spans) :]
    prec = refs[0]
    state, *parts = refs[3 if later else 1 :]
    if not last:
        *parts, image = parts
    p = prec[...]
    for m in range(state.shape[0]):
        mine = of_member(ys, spans, m)
        y = add([x[...] for x in mine])
        norm, cross = read_scalars(mine, 2)
        if later:
            old_image, old = refs[1:3]
            old_norm, old_square = old[m, 0:1, 0:1], old[m, 1:2, 0:1]
            beta = norm / old_norm
            square = norm + 2.0 * beta * cross + beta * beta * old_square
            y = y + beta * old_image[m]
        else:
            beta = jnp.zeros_like(norm)
            square = norm
        scaled = p * y
        if not last:
            image[m] = y
        value = with_scalars(scaled, [total(scaled * y)]).astype(BF16)
        first = 0
        for part in parts:
            if first <= m < first + part.shape[0]:
                part[m - first] = value
            first += part.shape[0]
        sub = lax.broadcasted_iota(jnp.int32, (8, LANES), 0)
        state[m] = jnp.where(sub == 0, norm, jnp.where(sub == 1, square, beta))


def adjoint_kernel(plan, *refs):
    z, core, obs = place()
    ws, tiles, out = refs[: len(plan)], refs[len(plan)], refs[len(plan) + 1]
    members, levp, lanes = out.shape
    width = ws[0].shape[2]
    acc = None
    for i in range(tiles.shape[0]):
        w = {span[0]: ref for ref, (chip, *span) in zip(ws, plan) if chip == i}
        w = [w[first][...].reshape(-1, width) for first in sorted(w)]
        w = w[0] if len(w) == 1 else jnp.concatenate(w, axis=0)
        part = lax.dot_general(
            w, tiles[z ^ i].reshape(lanes, width), NT, preferred_element_type=F32
        )
        acc = part if i == 0 else acc + part
    acc = acc.reshape(members, levp, lanes)
    spans = [(*span, 0) for chip, *span in plan]
    for m in range(members):
        energy = read_scalars(of_member(ws, spans, m), 1)
        out[m] = with_scalars(acc[m], energy).astype(out.dtype)


def combine_kernel(mine, theirs, *outs):
    for m in range(mine.shape[0]):
        energy = read_scalars([mine.at[m], theirs.at[m]], 1)
        put_halves(outs, m, with_scalars(mine[m] + theirs[m].astype(F32), energy))


def combine_columns_kernel(mine, theirs, *outs):
    obs = lax.axis_index("obs")
    for m in range(mine.shape[0]):
        energy = read_scalars([mine.at[m], theirs.at[m]], 1)
        for i, out in enumerate(outs):
            lane = pl.ds(pl.multiple_of((obs ^ i) * LANES, LANES), LANES)
            value = mine[m, :, lane] + theirs[m, :, lane].astype(F32)
            out[m] = with_scalars(value, energy).astype(BF16)


def update_kernel(parts, later, *refs):
    pieces, refs = refs[:parts], refs[parts:]
    sd, vert, vert_t, state, residual = refs[:5]
    if later:
        old_direction, old_solution, residual_out, solution_out, moved, direction_out = refs[5:]
    else:
        residual_out, solution_out, moved = refs[5:]
    obs = lax.axis_index("obs")
    mine = pl.ds(pl.multiple_of(obs * LANES, LANES), LANES)
    for m in range(residual.shape[0]):
        t, places = joined(pieces, m)
        (energy,) = read_scalars(places, 1)
        norm, square, beta = state[m, 0:1, 0:1], state[m, 1:2, 0:1], state[m, 2:3, 0:1]
        alpha = norm / (square + energy)
        r = residual[m]
        if later:
            d = r + beta * old_direction[m]
            direction_out[m] = d
            step = direction_out[m, :, mine]
            solution_out[m] = old_solution[m] + alpha * step
        else:
            d = r
            solution_out[m] = alpha * residual[m, :, mine]
        r = r - alpha * (d + dot(vert_t[...], sd[...] * t))
        residual_out[m] = r
        x = sd[...] * dot(vert[...], r)
        moved[m] = with_scalars(x, [total(r * r), total(r * d)]).astype(BF16)


def last_kernel(parts, later, lev, *refs):
    pieces, refs = refs[:parts], refs[parts:]
    sd, vert, vert_t, state, residual = refs[:5]
    increment_out, residual_out = refs[-2:]
    obs = lax.axis_index("obs")
    mine = pl.ds(pl.multiple_of(obs * LANES, LANES), LANES)
    for m in range(residual.shape[0]):
        t = add([x[m] for x in pieces])
        (energy,) = read_scalars([x.at[m] for x in pieces], 1)
        norm, square, beta = state[m, 0:1, 0:1], state[m, 1:2, 0:1], state[m, 2:3, 0:1]
        alpha = norm / (square + energy)
        d = r = residual[m, :, mine]
        if later:
            old_direction, old_solution = refs[5:7]
            d = r + beta * old_direction[m, :, mine]
        solution = alpha * d
        if later:
            solution = old_solution[m] + solution
        r = r - alpha * (d + dot(vert_t[...], sd[...] * t))
        increment = sd[...] * dot(vert[...], solution)
        increment_out[:, m, :] = increment[0:lev]
        residual_out[:, m, :] = r[0:lev]


def per_device(
    n_slab,
    n_obs,
    innovation,
    obs_precision,
    seeds,
    col_sd,
    vert_factor,
    h_values,
    block_obs,
    block_col,
    entry_count,
):
    blocks, lev, profiles = innovation.shape
    members = seeds.shape[0]
    chips = n_slab // 2
    halves = n_slab // blocks
    width = profiles // halves
    colblocks = n_obs
    assert halves * blocks == n_slab and width % LANES == 0 and col_sd.shape[0] == 1
    assert chips & (chips - 1) == 0 and n_obs & (n_obs - 1) == 0
    levp = (lev + 1 + 15) // 16 * 16
    rows = members * levp
    lanes = colblocks * LANES
    field = (members, levp, LANES)
    slab_field = (members, levp, lanes)
    panel = (members, levp, width)
    some, rest = members // 2, members - members // 2
    half_fields = [struct((members, levp, lanes // 2), BF16)] * 2
    via = chips == 4 and some > 0
    if via:
        plan = [(i, *span) for i in range(chips) for span in ((0, some), (some, rest))]
        sends = [plan[6], plan[5], plan[7], *plan[2:4], (0, 0, members), plan[4]]
        plan = [*plan[0:2], plan[5], plan[7], *plan[2:4], plan[4], plan[6]]
    else:
        plan = [(i, 0, members) for i in range(chips)]
        sends = plan
    pad = ((0, levp - lev), (0, levp - lev))
    high = lax.reduce_precision(vert_factor, 8, 7)
    low = vert_factor - high
    vert, vert_t = [
        jnp.concatenate([jnp.pad(x, pad).astype(BF16) for x in parts], axis=1)
        for parts in ((high, high, low), (high.T, high.T, low.T))
    ]
    h_block = h_values.reshape(h_values.shape[2:])
    innovation = jnp.transpose(innovation, (1, 0, 2))
    obs_precision = jnp.transpose(obs_precision, (1, 0, 2))
    product = n_slab * width * lanes * rows
    small = 12 * rows * levp * LANES
    plane_bits = [1 << k for k in range(n_obs.bit_length() - 1)]

    def along(x, i):
        return lax.ppermute(x, "slab", [(s, s ^ (2 * i)) for s in range(n_slab)])

    def plane(x, i):
        return lax.ppermute(x, "obs", [(o, o ^ i) for o in range(n_obs)])

    def swap(x):
        return lax.ppermute(x, "slab", [(s, s ^ 1) for s in range(n_slab)])

    def plane_sum(halves, staged):
        halves = list(halves)
        moved_halves = [None] * len(halves)
        for step, bit in enumerate(plane_bits):
            bits = [bit, plane_bits[len(plane_bits) - 1 - step]]
            for at in range(0, len(halves), 2):
                if step > 0:
                    one, two = halves[at : at + 2]
                    one_more, two_more = moved_halves[at : at + 2]
                    halves[at : at + 2] = call(
                        functools.partial(add_halves_kernel, 0 if staged else 1),
                        [struct(one.shape, BF16)] * 2,
                        [],
                        0,
                        one,
                        one_more,
                        two,
                        two_more,
                    )
                for half in range(2):
                    moved_halves[at + half] = plane(halves[at + half], bits[half])
            if step == 0 and staged:
                halves[:] = call(
                    stage_kernel,
                    [struct(x.shape, BF16) for x in halves],
                    [pltpu.SemaphoreType.DMA((len(halves),))],
                    0,
                    *halves,
                    space=HBM,
                )
        return [x for pair in zip(halves, moved_halves) for x in pair]

    def line_sum(moved, other):
        ys = call(
            functools.partial(forward_kernel, sends),
            [
                struct((count, levp, width), F32 if i == 0 or (via and at == 6) else BF16)
                for at, (i, unused, count) in enumerate(sends)
            ],
            [],
            2 * product,
            moved,
            other,
            own,
            partner,
        )
        if not via:
            return [y if i == 0 else along(y, i) for i, y in enumerate(ys)], [
                (0, members, 0) for y in ys
            ]
        passed, far_rest, last_rest, next_some, next_rest, near, far = ys
        passed = along(passed, 1)
        far_rest, last_rest = along(far_rest, 2), along(last_rest, 3)
        next_some, next_rest = along(next_some, 1), along(next_rest, 1)
        (far,) = call(
            functools.partial(add_kernel, 2),
            [struct((some, levp, width), BF16)],
            [],
            0,
            far,
            passed,
        )
        ys = [near, far_rest, last_rest, next_some, next_rest, along(far, 2)]
        spans = [(0, members, 0)] + [(some, rest, 0)] * 2 + [(0, some, 0), (some, rest, 0)]
        return ys, spans + [(0, some, 0)]

    def line_gather(*parts):
        if not via:
            return [parts[0] if i == 0 else along(parts[0], i) for i in range(chips)]
        one, two = parts
        far = along(one, 2)
        far_rest, last_rest = along(two, 2), along(two, 3)
        return [one, two, far_rest, last_rest, along(one, 1), along(two, 1), far, along(far, 1)]

    dense = struct((chips, colblocks, LANES, width), BF16)
    own, for_partner, *partials = call(
        functools.partial(start_kernel, (chips, halves)),
        [dense, dense] + half_fields,
        [
            pltpu.SMEM(seeds.shape, jnp.int32),
            pltpu.SMEM(block_obs.shape, jnp.int32),
            pltpu.SMEM(block_col.shape, jnp.int32),
            pltpu.SMEM(entry_count.shape, jnp.int32),
            pltpu.VMEM(col_sd.shape, F32),
            pltpu.VMEM((blocks, lev, profiles), F32),
            pltpu.VMEM((blocks, lev, profiles), F32),
            pltpu.VMEM((n_slab, members, levp, width), F32),
            pltpu.VMEM((2, members, levp, width), F32),
            pltpu.VMEM((rows, lanes), F32),
            pltpu.SemaphoreType.DMA((5 + 2 * blocks,)),
            pltpu.SemaphoreType.DMA((h_block.shape[0] * halves,)),
        ],
        2 * product,
        seeds,
        block_obs,
        block_col,
        entry_count,
        col_sd,
        innovation,
        obs_precision,
        h_block,
        space=HBM,
        limit=60,
    )
    ps = plane_sum(partials, True)
    partner = swap(for_partner)
    (precision,) = call(
        functools.partial(precision_kernel, halves),
        [struct((levp, width), F32)],
        [],
        0,
        obs_precision,
    )
    slab_sd, residual, moved = call(
        functools.partial(first_kernel, len(ps)),
        [struct((1, lanes), F32), struct(slab_field, F32), struct(slab_field, BF16)],
        [],
        small * colblocks,
        *ps,
        vert,
        vert_t,
    )
    direction = total_step = image = state = None
    for sweep in range(ITERS):
        later, last = sweep > 0, sweep == ITERS - 1
        ys, spans = line_sum(moved, swap(moved))
        state, *weighted = call(
            functools.partial(weigh_kernel, later, last, spans),
            [struct((members, 8, LANES), F32)]
            + [struct((n, levp, width), BF16) for n in ((some, rest) if via else (members,))]
            + ([] if last else [struct(panel, F32)]),
            [],
            0,
            *ys,
            precision,
            *([image, state] if later else []),
        )
        if not last:
            *weighted, image = weighted
        ws = line_gather(*weighted)
        (theirs,) = call(
            functools.partial(adjoint_kernel, plan),
            [struct(slab_field, BF16)],
            [],
            product,
            *ws,
            partner,
        )
        theirs = swap(theirs)
        (mine,) = call(
            functools.partial(adjoint_kernel, plan),
            [struct(slab_field, F32)],
            [],
            product,
            *ws,
            own,
        )
        known = [vert, vert_t, state, residual]
        if later:
            known += [direction, total_step]
        if last:
            ps = call(
                combine_columns_kernel, [struct(field, BF16)] * n_obs, [], 0, mine, theirs
            )
            ps = [ps[0]] + [plane(ps[i], i) for i in reversed(range(1, n_obs))]
            outputs = call(
                functools.partial(last_kernel, len(ps), later, lev),
                [struct((lev, members, LANES), F32)] * 2,
                [],
                small,
                *ps,
                col_sd,
                *known,
            )
            break
        ps = call(combine_kernel, half_fields, [], 0, mine, theirs)
        ps = plane_sum(ps, False)
        outs = [struct(slab_field, F32), struct(field, F32), struct(slab_field, BF16)]
        if later:
            outs.append(struct(slab_field, F32))
        r, total_step, moved, *d = call(
            functools.partial(update_kernel, len(ps), later),
            outs,
            [],
            small * colblocks,
            *ps,
            slab_sd,
            *known,
        )
        direction, residual = (d[0] if later else residual), r
    return tuple(jnp.transpose(x, (1, 0, 2))[None] for x in outputs)


def solution(mesh):
    return jax.shard_map(
        functools.partial(per_device, mesh.shape["slab"], mesh.shape["obs"]),
        mesh=mesh,
        in_specs=(
            P("obs", None, None),
            P("obs", None, None),
            P(),
            P(("slab", "obs"), None),
            P(),
            P("slab", "obs", None, None, None),
            P("slab", "obs", None),
            P("slab", "obs", None),
            P("slab", "obs"),
        ),
        out_specs=(P(("slab", "obs"), None, None, None), P(("slab", "obs"), None, None, None)),
        check_vma=False,
    )
```

```python
import functools

import jax
import jax.numpy as jnp
from jax import lax
from jax.experimental import pallas as pl
from jax.experimental.pallas import tpu as pltpu
from jax.sharding import PartitionSpec as P

ITERS = 2
LANES = 128
PIECES = 3
PRIME = 32749
VMEM = pl.BlockSpec(memory_space=pltpu.VMEM)
HBM = pl.BlockSpec(memory_space=pltpu.HBM)
F32 = jnp.float32
BF16 = jnp.bfloat16
NT = (((1,), (1,)), ((), ()))


def call(kernel, outs, scratch, flops, *args, space=VMEM, limit=24):
    nbytes = sum(a.size * a.dtype.itemsize for a in (*args, *outs))
    return pl.pallas_call(
        kernel,
        out_shape=outs,
        in_specs=[space] * len(args),
        out_specs=[VMEM] * len(outs),
        scratch_shapes=scratch,
        compiler_params=pltpu.CompilerParams(vmem_limit_bytes=limit * 1024 * 1024),
        cost_estimate=pl.CostEstimate(flops=flops, bytes_accessed=nbytes, transcendentals=0),
    )(*args)


def struct(shape, dtype):
    return jax.ShapeDtypeStruct(shape, dtype)


def place():
    slab = lax.axis_index("slab")
    return slab // 2, slab % 2, lax.axis_index("obs")


def add(parts):
    value = parts[0].astype(F32)
    for part in parts[1:]:
        value = value + part.astype(F32)
    return value


def dot(matrix, x):
    high = x.astype(BF16)
    rest = (x - high.astype(F32)).astype(BF16)
    x = jnp.concatenate([high, rest, high], axis=0)
    return jnp.dot(matrix, x, preferred_element_type=F32)


def total(x):
    return jnp.sum(jnp.sum(x, axis=0, keepdims=True), axis=1, keepdims=True)


def with_scalars(body, values):
    count = body.shape[0]
    tail = body[count - 16 :]
    sub = lax.broadcasted_iota(jnp.int32, tail.shape, 0) - (16 - len(values))
    lanes = lax.broadcasted_iota(jnp.int32, tail.shape, 1)
    line = jnp.zeros(tail.shape, F32)
    for m, member in enumerate(values):
        for q, value in enumerate(member):
            rest = value
            for piece in range(PIECES):
                part = rest.astype(BF16).astype(F32)
                rest = rest - part
                line = jnp.where((sub == m) & (lanes == q * PIECES + piece), part, line)
    return jnp.concatenate([body[: count - 16], jnp.where(sub >= 0, line, tail)], axis=0)


def read_scalars(refs, members, count):
    tail = add([ref[ref.shape[0] - 16 :, 0:LANES] for ref in refs])
    sub = lax.broadcasted_iota(jnp.int32, tail.shape, 0) - (16 - members)
    lanes = lax.broadcasted_iota(jnp.int32, tail.shape, 1)
    return [
        [
            total(
                jnp.where(
                    (sub == m) & (lanes >= q * PIECES) & (lanes < (q + 1) * PIECES), tail, 0.0
                )
            )
            for q in range(count)
        ]
        for m in range(members)
    ]


def by_member(values, shape, lev):
    rows = lax.broadcasted_iota(jnp.int32, shape, 0)
    out = jnp.zeros(shape, F32)
    for m, value in enumerate(values):
        out = jnp.where((rows >= m * lev) & (rows < (m + 1) * lev), value, out)
    return out


def member_sums(x, members, lev):
    lines = jnp.sum(x, axis=1, keepdims=True)
    rows = lax.broadcasted_iota(jnp.int32, lines.shape, 0)
    return [
        jnp.sum(
            jnp.where((rows >= m * lev) & (rows < (m + 1) * lev), lines, 0.0),
            axis=0,
            keepdims=True,
        )
        for m in range(members)
    ]


def remainder(x, factor):
    return x - (x.astype(F32) * factor).astype(jnp.int32) * PRIME


def start_kernel(
    dims, seeds_in, ids_in, cols_in, count_in, sd_in, innov_in, prec_in, h, own, partner, *rest
):
    chips, halves = dims
    outs = rest[:-12]
    seeds, ids, cols, count, sd, innov, prec, hashed, scratch, acc, sems, h_sems = rest[-12:]
    z, core, obs = place()
    blocks, lev, profiles = innov.shape
    colblocks, width = own.shape[1], own.shape[3]
    members, levp = hashed.shape[1], hashed.shape[2]
    rows = acc.shape[0]

    pairs = [(seeds_in, seeds), (ids_in, ids), (cols_in, cols), (count_in, count), (sd_in, sd)]
    small = [pltpu.make_async_copy(x, y, sems.at[i]) for i, (x, y) in enumerate(pairs)]
    for copy in small:
        copy.start()
    large = []
    for b in range(blocks):
        at = len(pairs) + 2 * b
        large.append(pltpu.make_async_copy(innov_in.at[:, b, :], innov.at[b], sems.at[at]))
        large.append(pltpu.make_async_copy(prec_in.at[:, b, :], prec.at[b], sems.at[at + 1]))
    for copy in large:
        copy.start()
    own[...] = jnp.zeros_like(own)
    partner[...] = jnp.zeros_like(partner)
    scratch[...] = jnp.zeros_like(scratch)
    for copy in small:
        copy.wait()

    def tile_copy(n, half, target):
        lanes = pl.ds(half * width, width)
        return pltpu.make_async_copy(h.at[n, :, lanes], target, h_sems.at[n * halves + half])

    def put(n, carry):
        for half in range(halves):
            piece, k = ids[0, 0, n] * halves + half, cols[0, 0, n]

            @pl.when(piece % 2 == core)
            def _():
                tile_copy(n, half, own.at[piece // 2, k]).start()

            @pl.when(piece % 2 != core)
            def _():
                tile_copy(n, half, partner.at[piece // 2, k]).start()

        return carry

    lax.fori_loop(0, count[0, 0], put, 0)

    starts = [lax.rem(seeds[m], PRIME) - PRIME for m in range(members)]
    order = [(source, zz) for source in range(2) for zz in range(chips)]
    shape = (levp, width)
    spot = lax.broadcasted_iota(jnp.int32, shape, 0) * profiles
    spot = spot + lax.broadcasted_iota(jnp.int32, shape, 1)
    low = (1.0 - 2.0**-21) / PRIME

    def piece_at(at):
        source, zz = order[at]
        return 2 * zz + (core if source == 0 else 1 - core)

    def draw(at):
        piece = piece_at(at)
        first = (obs * blocks + piece // halves) * (lev * profiles) + (piece % halves) * width
        base = remainder(7919 * remainder(spot + first, 1.0 / PRIME), 1.0 / PRIME)
        for m in range(members):
            k0 = base + starts[m]
            k1 = remainder(k0 * k0 + 12345, 1.0 / PRIME)
            k2 = remainder(k1 * k1 + 2719, low)
            k2 = jnp.where(k2 >= PRIME, k2 - PRIME, k2)
            hashed[at, m] = k2.astype(F32)

    def adjoint(at):
        source, zz = order[at]
        piece = piece_at(at)
        b = piece // halves
        if halves == 1:
            p, d = prec[b], innov[b]
        else:
            lanes = pl.ds(pl.multiple_of((piece % halves) * width, LANES), width)
            p, d = prec[b, :, lanes], innov[b, :, lanes]
        gain = 3.4 * p * lax.rsqrt(p)
        offset = p * d - 0.5 * gain
        gain = gain * (1.0 / PRIME)
        for m in range(members):
            w = offset + gain * hashed[at, m, 0:lev, :]
            scratch[at % 2, m * lev : (m + 1) * lev, :] = w
        w = scratch[at % 2].astype(BF16)
        tiles = (own if source == 0 else partner)[zz].reshape(colblocks * LANES, width)
        part = lax.dot_general(w, tiles, NT, preferred_element_type=F32)
        if at == 0:
            acc[...] = part
        else:
            acc[...] += part

    early = len(order) // 2
    for at in range(early):
        draw(at)
    for copy in large:
        copy.wait()

    def arrive(n, carry):
        for half in range(halves):
            tile_copy(n, half, own.at[0, 0]).wait()
        return carry

    lax.fori_loop(0, count[0, 0], arrive, 0)

    for at in range(len(order)):
        if at + early < len(order):
            draw(at + early)
        adjoint(at)

    line = jnp.concatenate([sd[...]] * colblocks, axis=1)
    put_halves(outs, with_columns(acc[...], line, obs, members))


def put_halves(outs, value):
    half = value.shape[1] // 2
    outs[0][...] = value[:, :half].astype(BF16)
    outs[1][...] = value[:, half:].astype(BF16)


def with_columns(body, line, obs, members):
    tail = body[body.shape[0] - 16 :]
    sub = lax.broadcasted_iota(jnp.int32, tail.shape, 0)
    mine = lax.broadcasted_iota(jnp.int32, tail.shape, 1) // LANES == obs
    rest = line
    for piece in range(PIECES):
        part = rest.astype(BF16).astype(F32)
        rest = rest - part
        tail = jnp.where((sub == 16 - PIECES + piece) & mine, part, tail)
    return jnp.concatenate([body[: body.shape[0] - 16], tail], axis=0)


def read_columns(body):
    tail = body[body.shape[0] - 16 :]
    sub = lax.broadcasted_iota(jnp.int32, tail.shape, 0)
    return jnp.sum(jnp.where(sub >= 16 - PIECES, tail, 0.0), axis=0, keepdims=True)


def precision_kernel(halves, members, prec, out):
    z, core, unused = place()
    piece = 2 * z + core
    lev, blocks, unused = prec.shape
    width = out.shape[1]
    block = lax.broadcasted_iota(jnp.int32, (lev, blocks, width), 1)
    if halves == 1:
        mine = prec[...]
    else:
        mine = prec[:, :, pl.ds(pl.multiple_of((piece % halves) * width, LANES), width)]
    out[...] = jnp.zeros_like(out)
    mine = jnp.sum(jnp.where(block == piece // halves, mine, 0.0), axis=1)
    for m in range(members):
        out[m * lev : (m + 1) * lev, :] = mine


def joined(pieces):
    one, one_more, two, two_more = [x[...] for x in pieces]
    return jnp.concatenate([add([one, one_more]), add([two, two_more])], axis=1)


def unpack(spread, value):
    count = value.shape[0]
    spread[0:count, :] = value
    spread[count:, :] = jnp.zeros((spread.shape[0] - count, value.shape[1]), F32)


def first_kernel(lev, *refs):
    vert, vert_t, sd_out, residual, moved, spread, packed = refs[4:]
    members, levp, unused = residual.shape
    t = joined(refs[:4])
    sd = read_columns(t)
    sd_out[...] = sd
    unpack(spread, t)
    scalars = []
    for m in range(members):
        at = slice(m * lev, m * lev + levp)
        r = dot(vert_t[...], sd * spread[at, :])
        residual[m] = r
        packed[at, :] = sd * dot(vert[...], r)
        scalars.append([total(r * r)])
    moved[...] = with_scalars(packed[0 : moved.shape[0], :], scalars).astype(BF16)


def add_kernel(members, scalars, *refs):
    parts, out = refs[:-1], refs[-1]
    value = add([x[...] for x in parts])
    if scalars:
        value = with_scalars(value, read_scalars(parts, members, scalars))
    out[...] = value.astype(BF16)


def add_halves_kernel(members, scalars, one, one_more, two, two_more, one_out, two_out):
    add_kernel(members, scalars, one, one_more, one_out)
    add_kernel(members, 0, two, two_more, two_out)


def stage_kernel(*refs):
    sems = refs[-1]
    count = len(refs) // 2
    copies = [
        pltpu.make_async_copy(refs[i], refs[count + i], sems.at[i]) for i in range(count)
    ]
    for copy in copies:
        copy.start()
    for copy in copies:
        copy.wait()


def forward_kernel(sends, members, mine, other, own, partner, *outs):
    z, core, obs = place()
    rows, lanes = mine.shape
    width = own.shape[3]
    scalars = read_scalars([mine, other], members, 2)
    for out, (chip, first, count) in zip(outs, sends):
        zz = z ^ chip
        y = [
            jnp.dot(
                x[first : first + count, :],
                tiles[zz].reshape(lanes, width),
                preferred_element_type=F32,
            )
            for x, tiles in ((mine, own), (other, partner))
        ]
        y = y[0] + y[1]
        if first + count == rows:
            y = with_scalars(y, scalars)
        out[...] = y.astype(out.dtype)


def weigh_kernel(later, last, members, lev, spans, *refs):
    ys, refs = refs[: len(spans)], refs[len(spans) :]
    prec, old_image, old = refs[0], *(refs[1:3] if later else (None, None))
    state, *outs = refs[3 if later else 1 :]
    if not last:
        *outs, image = outs
    rows = prec.shape[0]
    cuts = sorted({first for first, count in spans}) + [rows]
    parts = []
    for low, high in zip(cuts, cuts[1:]):
        held = [
            ref[low - first : high - first, :]
            for ref, (first, count) in zip(ys, spans)
            if first <= low < first + count
        ]
        parts.append(add(held))
    y = parts[0] if len(parts) == 1 else jnp.concatenate(parts, axis=0)
    ends = [ref for ref, (first, count) in zip(ys, spans) if first + count == rows]
    sub = lax.broadcasted_iota(jnp.int32, (8, LANES), 0)
    betas = []
    for m, (norm, cross) in enumerate(read_scalars(ends, members, 2)):
        if later:
            old_norm, old_square = old[m, 0:1, 0:1], old[m, 1:2, 0:1]
            beta = norm / old_norm
            square = norm + 2.0 * beta * cross + beta * beta * old_square
        else:
            beta = jnp.zeros_like(norm)
            square = norm
        betas.append(beta)
        state[m] = jnp.where(sub == 0, norm, jnp.where(sub == 1, square, beta))
    if later:
        y = y + by_member(betas, (rows, 1), lev) * old_image[...]
    if not last:
        image[...] = y
    scaled = prec[...] * y
    energies = [[x] for x in member_sums(scaled * y, members, lev)]
    weighted = with_scalars(scaled, energies).astype(BF16)
    first = 0
    outs[0][...] = weighted
    for out in outs[1:]:
        out[...] = weighted[first : first + out.shape[0]]
        first += out.shape[0]


def adjoint_kernel(plan, members, *refs):
    z, core, obs = place()
    ws, tiles, out = refs[: len(plan)], refs[len(plan)], refs[len(plan) + 1]
    rows, lanes = out.shape
    width = ws[0].shape[1]
    acc = None
    for i in range(tiles.shape[0]):
        w = [ref[...] for ref, (chip, *span) in zip(ws, plan) if chip == i]
        w = w[0] if len(w) == 1 else jnp.concatenate(w, axis=0)
        part = lax.dot_general(
            w, tiles[z ^ i].reshape(lanes, width), NT, preferred_element_type=F32
        )
        acc = part if i == 0 else acc + part
    ends = [ref for ref, (chip, first, count) in zip(ws, plan) if first + count == rows]
    out[...] = with_scalars(acc, read_scalars(ends, members, 1)).astype(out.dtype)


def combine_kernel(members, mine, theirs, *outs):
    value = mine[...] + theirs[...].astype(F32)
    put_halves(outs, with_scalars(value, read_scalars([mine, theirs], members, 1)))


def combine_columns_kernel(members, mine, theirs, *outs):
    obs = lax.axis_index("obs")
    energies = read_scalars([mine, theirs], members, 1)
    for i, out in enumerate(outs):
        lane = pl.ds(pl.multiple_of((obs ^ i) * LANES, LANES), LANES)
        value = mine[:, lane] + theirs[:, lane].astype(F32)
        out[...] = with_scalars(value, energies).astype(BF16)


def update_kernel(later, lev, *refs):
    pieces, refs = refs[:4], refs[4:]
    sd, vert, vert_t, state, residual = refs[:5]
    spread, packed = refs[-2:]
    if later:
        old_direction, old_solution, residual_out, solution_out, moved, direction_out = refs[5:-2]
    else:
        residual_out, solution_out, moved = refs[5:-2]
    members, levp, unused = residual.shape
    obs = lax.axis_index("obs")
    mine = pl.ds(pl.multiple_of(obs * LANES, LANES), LANES)
    unpack(spread, joined(pieces))
    energies = read_scalars(pieces[:2], members, 1)
    scalars = []
    for m in range(members):
        at = slice(m * lev, m * lev + levp)
        norm, square, beta = state[m, 0:1, 0:1], state[m, 1:2, 0:1], state[m, 2:3, 0:1]
        alpha = norm / (square + energies[m][0])
        r = residual[m]
        if later:
            d = r + beta * old_direction[m]
            direction_out[m] = d
            step = direction_out[m, :, mine]
            solution_out[m] = old_solution[m] + alpha * step
        else:
            d = r
            solution_out[m] = alpha * residual[m, :, mine]
        r = r - alpha * (d + dot(vert_t[...], sd[...] * spread[at, :]))
        residual_out[m] = r
        packed[at, :] = sd[...] * dot(vert[...], r)
        scalars.append([total(r * r), total(r * d)])
    moved[...] = with_scalars(packed[0 : moved.shape[0], :], scalars).astype(BF16)


def last_kernel(parts, later, lev, *refs):
    pieces, refs = refs[:parts], refs[parts:]
    sd, vert, vert_t, state, residual = refs[:5]
    increment_out, residual_out, spread = refs[-3:]
    members, levp, unused = residual.shape
    obs = lax.axis_index("obs")
    mine = pl.ds(pl.multiple_of(obs * LANES, LANES), LANES)
    unpack(spread, add([x[...] for x in pieces]))
    energies = read_scalars(pieces, members, 1)
    for m in range(members):
        t = spread[m * lev : m * lev + levp, :]
        norm, square, beta = state[m, 0:1, 0:1], state[m, 1:2, 0:1], state[m, 2:3, 0:1]
        alpha = norm / (square + energies[m][0])
        d = r = residual[m, :, mine]
        if later:
            old_direction, old_solution = refs[5:7]
            d = r + beta * old_direction[m, :, mine]
        solution = alpha * d
        if later:
            solution = old_solution[m] + solution
        r = r - alpha * (d + dot(vert_t[...], sd[...] * t))
        increment = sd[...] * dot(vert[...], solution)
        increment_out[:, m, :] = increment[0:lev]
        residual_out[:, m, :] = r[0:lev]


def per_device(
    n_slab,
    n_obs,
    innovation,
    obs_precision,
    seeds,
    col_sd,
    vert_factor,
    h_values,
    block_obs,
    block_col,
    entry_count,
):
    blocks, lev, profiles = innovation.shape
    members = seeds.shape[0]
    chips = n_slab // 2
    halves = n_slab // blocks
    width = profiles // halves
    colblocks = n_obs
    assert halves * blocks == n_slab and width % LANES == 0 and col_sd.shape[0] == 1
    assert chips & (chips - 1) == 0 and n_obs & (n_obs - 1) == 0
    levp = (lev + 1 + 15) // 16 * 16
    assert members <= 16 and members >= PIECES
    rows = (members * (lev + 1) + 15) // 16 * 16
    lanes = colblocks * LANES
    slab_field = (members, levp, lanes)
    slab_rows = (rows, lanes)
    half_rows = [struct((rows, lanes // 2), BF16)] * 2
    wide = rows + levp - lev + 7
    spread = pltpu.VMEM((wide // 8 * 8, lanes), F32)
    some = rows // 32 * 16
    some, rest = rows - some, some
    via = chips == 4
    if via:
        one, two = (0, some), (some, rest)
        plan = [(0, 0, rows), (1, 0, rows), (2, *one), (2, *two), (3, *one), (3, *two)]
        sends = [(3, *one), (2, *two), (3, *two), (1, *one), (1, *two), (0, 0, rows), (2, *one)]
    else:
        sends = plan = [(i, 0, rows) for i in range(chips)]
    pad = ((0, levp - lev), (0, levp - lev))
    high = lax.reduce_precision(vert_factor, 8, 7)
    low = vert_factor - high
    vert, vert_t = [
        jnp.concatenate([jnp.pad(x, pad).astype(BF16) for x in parts], axis=1)
        for parts in ((high, high, low), (high.T, high.T, low.T))
    ]
    h_block = h_values.reshape(h_values.shape[2:])
    innovation = jnp.transpose(innovation, (1, 0, 2))
    obs_precision = jnp.transpose(obs_precision, (1, 0, 2))
    product = n_slab * width * lanes * rows
    small = 12 * rows * levp * LANES
    plane_bits = [1 << k for k in range(n_obs.bit_length() - 1)]

    def along(x, i):
        return lax.ppermute(x, "slab", [(s, s ^ (2 * i)) for s in range(n_slab)])

    def plane(x, i):
        return lax.ppermute(x, "obs", [(o, o ^ i) for o in range(n_obs)])

    def swap(x):
        return lax.ppermute(x, "slab", [(s, s ^ 1) for s in range(n_slab)])

    def plane_sum(halves, staged):
        halves = list(halves)
        moved_halves = [None] * len(halves)
        for step, bit in enumerate(plane_bits):
            bits = [bit, plane_bits[len(plane_bits) - 1 - step]]
            for at in range(0, len(halves), 2):
                if step > 0:
                    one, two = halves[at : at + 2]
                    one_more, two_more = moved_halves[at : at + 2]
                    halves[at : at + 2] = call(
                        functools.partial(add_halves_kernel, members, 0 if staged else 1),
                        [struct(one.shape, BF16)] * 2,
                        [],
                        0,
                        one,
                        one_more,
                        two,
                        two_more,
                    )
                for half in range(2):
                    moved_halves[at + half] = plane(halves[at + half], bits[half])
            if step == 0 and staged:
                halves[:] = call(
                    stage_kernel,
                    [struct(x.shape, BF16) for x in halves],
                    [pltpu.SemaphoreType.DMA((len(halves),))],
                    0,
                    *halves,
                    space=HBM,
                )
        return [x for pair in zip(halves, moved_halves) for x in pair]

    def line_sum(moved, other):
        ys = call(
            functools.partial(forward_kernel, sends, members),
            [
                struct((count, width), F32 if i == 0 or (via and at == 6) else BF16)
                for at, (i, unused, count) in enumerate(sends)
            ],
            [],
            2 * product,
            moved,
            other,
            own,
            partner,
        )
        if not via:
            return [y if i == 0 else along(y, i) for i, y in enumerate(ys)], [(0, rows)] * chips
        passed, far_rest, last_rest, next_some, next_rest, near, far = ys
        passed = along(passed, 1)
        far_rest, last_rest = along(far_rest, 2), along(last_rest, 3)
        next_some, next_rest = along(next_some, 1), along(next_rest, 1)
        (far,) = call(
            functools.partial(add_kernel, members, 0),
            [struct((some, width), BF16)],
            [],
            0,
            far,
            passed,
        )
        ys = [near, far_rest, last_rest, next_some, next_rest, along(far, 2)]
        return ys, [(0, rows), two, two, one, two, one]

    def line_gather(w, *parts):
        if not via:
            return [w if i == 0 else along(w, i) for i in range(chips)]
        some_w, rest_w = parts
        far = along(some_w, 2)
        far_rest, last_rest, next_ = along(rest_w, 2), along(rest_w, 3), along(w, 1)
        return [w, next_, far, far_rest, along(far, 1), last_rest]

    dense = struct((chips, colblocks, LANES, width), BF16)
    own, for_partner, *partials = call(
        functools.partial(start_kernel, (chips, halves)),
        [dense, dense] + half_rows,
        [
            pltpu.SMEM(seeds.shape, jnp.int32),
            pltpu.SMEM(block_obs.shape, jnp.int32),
            pltpu.SMEM(block_col.shape, jnp.int32),
            pltpu.SMEM(entry_count.shape, jnp.int32),
            pltpu.VMEM(col_sd.shape, F32),
            pltpu.VMEM((blocks, lev, profiles), F32),
            pltpu.VMEM((blocks, lev, profiles), F32),
            pltpu.VMEM((n_slab, members, levp, width), F32),
            pltpu.VMEM((2, rows, width), F32),
            pltpu.VMEM((rows, lanes), F32),
            pltpu.SemaphoreType.DMA((5 + 2 * blocks,)),
            pltpu.SemaphoreType.DMA((h_block.shape[0] * halves,)),
        ],
        2 * product,
        seeds,
        block_obs,
        block_col,
        entry_count,
        col_sd,
        innovation,
        obs_precision,
        h_block,
        space=HBM,
        limit=60,
    )
    ps = plane_sum(partials, True)
    partner = swap(for_partner)
    (precision,) = call(
        functools.partial(precision_kernel, halves, members),
        [struct((rows, width), F32)],
        [],
        0,
        obs_precision,
    )
    slab_sd, residual, moved = call(
        functools.partial(first_kernel, lev),
        [struct((1, lanes), F32), struct(slab_field, F32), struct(slab_rows, BF16)],
        [spread, spread],
        small * colblocks,
        *ps,
        vert,
        vert_t,
    )
    direction = total_step = image = state = None
    for sweep in range(ITERS):
        later, last = sweep > 0, sweep == ITERS - 1
        ys, spans = line_sum(moved, swap(moved))
        state, *weighted = call(
            functools.partial(weigh_kernel, later, last, members, lev, spans),
            [struct((members, 8, LANES), F32)]
            + [struct((n, width), BF16) for n in ((rows, some, rest) if via else (rows,))]
            + ([] if last else [struct((rows, width), F32)]),
            [],
            0,
            *ys,
            precision,
            *([image, state] if later else []),
        )
        if not last:
            *weighted, image = weighted
        ws = line_gather(*weighted)
        (theirs,) = call(
            functools.partial(adjoint_kernel, plan, members),
            [struct(slab_rows, BF16)],
            [],
            product,
            *ws,
            partner,
        )
        theirs = swap(theirs)
        (mine,) = call(
            functools.partial(adjoint_kernel, plan, members),
            [struct(slab_rows, F32)],
            [],
            product,
            *ws,
            own,
        )
        known = [vert, vert_t, state, residual]
        if later:
            known += [direction, total_step]
        if last:
            ps = call(
                functools.partial(combine_columns_kernel, members),
                [struct((rows, LANES), BF16)] * n_obs,
                [],
                0,
                mine,
                theirs,
            )
            ps = [ps[0]] + [plane(ps[i], i) for i in reversed(range(1, n_obs))]
            outputs = call(
                functools.partial(last_kernel, len(ps), later, lev),
                [struct((lev, members, LANES), F32)] * 2,
                [pltpu.VMEM((wide // 8 * 8, LANES), F32)],
                small,
                *ps,
                col_sd,
                *known,
            )
            break
        ps = call(
            functools.partial(combine_kernel, members), half_rows, [], 0, mine, theirs
        )
        ps = plane_sum(ps, False)
        outs = [
            struct(slab_field, F32),
            struct((members, levp, LANES), F32),
            struct(slab_rows, BF16),
        ]
        if later:
            outs.append(struct(slab_field, F32))
        r, total_step, moved, *d = call(
            functools.partial(update_kernel, later, lev),
            outs,
            [spread, spread],
            small * colblocks,
            *ps,
            slab_sd,
            *known,
        )
        direction, residual = (d[0] if later else residual), r
    return tuple(jnp.transpose(x, (1, 0, 2))[None] for x in outputs)


def solution(mesh):
    return jax.shard_map(
        functools.partial(per_device, mesh.shape["slab"], mesh.shape["obs"]),
        mesh=mesh,
        in_specs=(
            P("obs", None, None),
            P("obs", None, None),
            P(),
            P(("slab", "obs"), None),
            P(),
            P("slab", "obs", None, None, None),
            P("slab", "obs", None),
            P("slab", "obs", None),
            P("slab", "obs"),
        ),
        out_specs=(P(("slab", "obs"), None, None, None), P(("slab", "obs"), None, None, None)),
        check_vma=False,
    )
```

```python
import functools

import jax
import jax.numpy as jnp
from jax import lax
from jax.experimental import pallas as pl
from jax.experimental.pallas import tpu as pltpu
from jax.sharding import PartitionSpec as P

ITERS = 2
LANES = 128
PIECES = 3
PRIME = 32749
VMEM = pl.BlockSpec(memory_space=pltpu.VMEM)
HBM = pl.BlockSpec(memory_space=pltpu.HBM)
F32 = jnp.float32
BF16 = jnp.bfloat16
NT = (((1,), (1,)), ((), ()))


def call(kernel, outs, scratch, flops, *args, space=VMEM, limit=24):
    nbytes = sum(a.size * a.dtype.itemsize for a in (*args, *outs))
    return pl.pallas_call(
        kernel,
        out_shape=outs,
        in_specs=[space] * len(args),
        out_specs=[VMEM] * len(outs),
        scratch_shapes=scratch,
        compiler_params=pltpu.CompilerParams(vmem_limit_bytes=limit * 1024 * 1024),
        cost_estimate=pl.CostEstimate(flops=flops, bytes_accessed=nbytes, transcendentals=0),
    )(*args)


def struct(shape, dtype):
    return jax.ShapeDtypeStruct(shape, dtype)


def place():
    slab = lax.axis_index("slab")
    return slab // 2, slab % 2, lax.axis_index("obs")


def add(parts):
    value = parts[0].astype(F32)
    for part in parts[1:]:
        value = value + part.astype(F32)
    return value


def dot(matrix, x):
    high = x.astype(BF16)
    rest = (x - high.astype(F32)).astype(BF16)
    x = jnp.concatenate([high, rest, high], axis=0)
    return jnp.dot(matrix, x, preferred_element_type=F32)


def total(x):
    return jnp.sum(jnp.sum(x, axis=0, keepdims=True), axis=1, keepdims=True)


def with_scalars(body, values):
    count = body.shape[0]
    tail = body[count - 16 :]
    sub = lax.broadcasted_iota(jnp.int32, tail.shape, 0) - (16 - len(values))
    lanes = lax.broadcasted_iota(jnp.int32, tail.shape, 1)
    line = jnp.zeros(tail.shape, F32)
    for m, member in enumerate(values):
        for q, value in enumerate(member):
            rest = value
            for piece in range(PIECES):
                part = rest.astype(BF16).astype(F32)
                rest = rest - part
                line = jnp.where((sub == m) & (lanes == q * PIECES + piece), part, line)
    return jnp.concatenate([body[: count - 16], jnp.where(sub >= 0, line, tail)], axis=0)


def read_scalars(refs, members, count):
    tail = add([ref[ref.shape[0] - 16 :, 0:LANES] for ref in refs])
    sub = lax.broadcasted_iota(jnp.int32, tail.shape, 0) - (16 - members)
    lanes = lax.broadcasted_iota(jnp.int32, tail.shape, 1)
    return [
        [
            total(
                jnp.where(
                    (sub == m) & (lanes >= q * PIECES) & (lanes < (q + 1) * PIECES), tail, 0.0
                )
            )
            for q in range(count)
        ]
        for m in range(members)
    ]


def by_member(values, shape, lev):
    rows = lax.broadcasted_iota(jnp.int32, shape, 0)
    out = jnp.zeros(shape, F32)
    for m, value in enumerate(values):
        out = jnp.where((rows >= m * lev) & (rows < (m + 1) * lev), value, out)
    return out


def member_sums(x, members, lev):
    lines = jnp.sum(x, axis=1, keepdims=True)
    rows = lax.broadcasted_iota(jnp.int32, lines.shape, 0)
    return [
        jnp.sum(
            jnp.where((rows >= m * lev) & (rows < (m + 1) * lev), lines, 0.0),
            axis=0,
            keepdims=True,
        )
        for m in range(members)
    ]


def remainder(x, factor):
    return x - (x.astype(F32) * factor).astype(jnp.int32) * PRIME


def start_kernel(
    dims, seeds_in, ids_in, cols_in, count_in, sd_in, innov_in, prec_in, h, own, partner, *rest
):
    chips, halves = dims
    outs = rest[:-12]
    seeds, ids, cols, count, sd, innov, prec, hashed, scratch, acc, sems, h_sems = rest[-12:]
    z, core, obs = place()
    blocks, lev, profiles = innov.shape
    colblocks, width = own.shape[1], own.shape[3]
    members, levp = hashed.shape[1], hashed.shape[2]
    rows = acc.shape[0]

    pairs = [(seeds_in, seeds), (ids_in, ids), (cols_in, cols), (count_in, count), (sd_in, sd)]
    small = [pltpu.make_async_copy(x, y, sems.at[i]) for i, (x, y) in enumerate(pairs)]
    for copy in small:
        copy.start()
    large = []
    for b in range(blocks):
        at = len(pairs) + 2 * b
        large.append(pltpu.make_async_copy(innov_in.at[:, b, :], innov.at[b], sems.at[at]))
        large.append(pltpu.make_async_copy(prec_in.at[:, b, :], prec.at[b], sems.at[at + 1]))
    for copy in large:
        copy.start()
    own[...] = jnp.zeros_like(own)
    partner[...] = jnp.zeros_like(partner)
    scratch[...] = jnp.zeros_like(scratch)
    for copy in small:
        copy.wait()

    def tile_copy(n, half, target):
        lanes = pl.ds(half * width, width)
        return pltpu.make_async_copy(h.at[n, :, lanes], target, h_sems.at[n * halves + half])

    def put(n, carry):
        for half in range(halves):
            piece, k = ids[0, 0, n] * halves + half, cols[0, 0, n]

            @pl.when(piece % 2 == core)
            def _():
                tile_copy(n, half, own.at[piece // 2, k]).start()

            @pl.when(piece % 2 != core)
            def _():
                tile_copy(n, half, partner.at[piece // 2, k]).start()

        return carry

    lax.fori_loop(0, count[0, 0], put, 0)

    starts = [lax.rem(seeds[m], PRIME) - PRIME for m in range(members)]
    order = [(source, zz) for source in range(2) for zz in range(chips)]
    shape = (levp, width)
    spot = lax.broadcasted_iota(jnp.int32, shape, 0) * profiles
    spot = spot + lax.broadcasted_iota(jnp.int32, shape, 1)
    low = (1.0 - 2.0**-21) / PRIME

    def piece_at(at):
        source, zz = order[at]
        return 2 * zz + (core if source == 0 else 1 - core)

    def draw(at):
        piece = piece_at(at)
        first = (obs * blocks + piece // halves) * (lev * profiles) + (piece % halves) * width
        base = remainder(7919 * remainder(spot + first, 1.0 / PRIME), 1.0 / PRIME)
        for m in range(members):
            k0 = base + starts[m]
            k1 = remainder(k0 * k0 + 12345, 1.0 / PRIME)
            k2 = remainder(k1 * k1 + 2719, low)
            k2 = jnp.where(k2 >= PRIME, k2 - PRIME, k2)
            hashed[at, m] = k2.astype(F32)

    def adjoint(at):
        source, zz = order[at]
        piece = piece_at(at)
        b = piece // halves
        if halves == 1:
            p, d = prec[b], innov[b]
        else:
            lanes = pl.ds(pl.multiple_of((piece % halves) * width, LANES), width)
            p, d = prec[b, :, lanes], innov[b, :, lanes]
        gain = 3.4 * p * lax.rsqrt(p)
        offset = p * d - 0.5 * gain
        gain = gain * (1.0 / PRIME)
        for m in range(members):
            w = offset + gain * hashed[at, m, 0:lev, :]
            scratch[at % 2, m * lev : (m + 1) * lev, :] = w
        w = scratch[at % 2].astype(BF16)
        tiles = (own if source == 0 else partner)[zz].reshape(colblocks * LANES, width)
        part = lax.dot_general(w, tiles, NT, preferred_element_type=F32)
        if at == 0:
            acc[...] = part
        else:
            acc[...] += part

    early = len(order) // 2
    for at in range(early):
        draw(at)
    for copy in large:
        copy.wait()

    def arrive(n, carry):
        for half in range(halves):
            tile_copy(n, half, own.at[0, 0]).wait()
        return carry

    lax.fori_loop(0, count[0, 0], arrive, 0)

    for at in range(len(order)):
        if at + early < len(order):
            draw(at + early)
        adjoint(at)

    line = jnp.concatenate([sd[...]] * colblocks, axis=1)
    put_halves(outs, with_columns(acc[...], line, obs, members))


def put_halves(outs, value):
    half = value.shape[1] // 2
    outs[0][...] = value[:, :half].astype(BF16)
    outs[1][...] = value[:, half:].astype(BF16)


def with_columns(body, line, obs, members):
    tail = body[body.shape[0] - 16 :]
    sub = lax.broadcasted_iota(jnp.int32, tail.shape, 0)
    mine = lax.broadcasted_iota(jnp.int32, tail.shape, 1) // LANES == obs
    rest = line
    for piece in range(PIECES):
        part = rest.astype(BF16).astype(F32)
        rest = rest - part
        tail = jnp.where((sub == 16 - PIECES + piece) & mine, part, tail)
    return jnp.concatenate([body[: body.shape[0] - 16], tail], axis=0)


def read_columns(body):
    tail = body[body.shape[0] - 16 :]
    sub = lax.broadcasted_iota(jnp.int32, tail.shape, 0)
    return jnp.sum(jnp.where(sub >= 16 - PIECES, tail, 0.0), axis=0, keepdims=True)


def precision_kernel(halves, members, prec, out):
    z, core, unused = place()
    piece = 2 * z + core
    lev, blocks, unused = prec.shape
    width = out.shape[1]
    block = lax.broadcasted_iota(jnp.int32, (lev, blocks, width), 1)
    if halves == 1:
        mine = prec[...]
    else:
        mine = prec[:, :, pl.ds(pl.multiple_of((piece % halves) * width, LANES), width)]
    out[...] = jnp.zeros_like(out)
    mine = jnp.sum(jnp.where(block == piece // halves, mine, 0.0), axis=1)
    for m in range(members):
        out[m * lev : (m + 1) * lev, :] = mine


def joined(pieces):
    one, one_more, two, two_more = [x[...] for x in pieces]
    return jnp.concatenate([add([one, one_more]), add([two, two_more])], axis=1)


def unpack(spread, value):
    count = value.shape[0]
    spread[0:count, :] = value
    spread[count:, :] = jnp.zeros((spread.shape[0] - count, value.shape[1]), F32)


def first_kernel(lev, *refs):
    vert, vert_t, sd_out, residual, moved, spread, packed = refs[4:]
    members, levp, unused = residual.shape
    t = joined(refs[:4])
    sd = read_columns(t)
    sd_out[...] = sd
    unpack(spread, t)
    scalars = []
    for m in range(members):
        at = slice(m * lev, m * lev + levp)
        r = dot(vert_t[...], sd * spread[at, :])
        residual[m] = r
        packed[at, :] = sd * dot(vert[...], r)
        scalars.append([total(r * r)])
    moved[...] = with_scalars(packed[0 : moved.shape[0], :], scalars).astype(BF16)


def add_kernel(members, scalars, *refs):
    parts, out = refs[:-1], refs[-1]
    value = add([x[...] for x in parts])
    if scalars:
        value = with_scalars(value, read_scalars(parts, members, scalars))
    out[...] = value.astype(BF16)


def add_halves_kernel(members, scalars, one, one_more, two, two_more, one_out, two_out):
    add_kernel(members, scalars, one, one_more, one_out)
    add_kernel(members, 0, two, two_more, two_out)


def stage_kernel(*refs):
    sems = refs[-1]
    count = len(refs) // 2
    copies = [
        pltpu.make_async_copy(refs[i], refs[count + i], sems.at[i]) for i in range(count)
    ]
    for copy in copies:
        copy.start()
    for copy in copies:
        copy.wait()


def forward_kernel(sends, members, mine, other, own, partner, *outs):
    z, core, obs = place()
    rows, lanes = mine.shape
    width = own.shape[3]
    scalars = read_scalars([mine, other], members, 2)
    for out, (chip, first, count) in zip(outs, sends):
        zz = z ^ chip
        y = [
            jnp.dot(
                x[first : first + count, :],
                tiles[zz].reshape(lanes, width),
                preferred_element_type=F32,
            )
            for x, tiles in ((mine, own), (other, partner))
        ]
        y = y[0] + y[1]
        if first + count == rows:
            y = with_scalars(y, scalars)
        out[...] = y.astype(out.dtype)


def weigh_kernel(later, last, members, lev, spans, *refs):
    ys, refs = refs[: len(spans)], refs[len(spans) :]
    prec, old_image, old = refs[0], *(refs[1:3] if later else (None, None))
    state, *outs = refs[3 if later else 1 :]
    if not last:
        *outs, image = outs
    rows = prec.shape[0]
    cuts = sorted({first for first, count in spans}) + [rows]
    parts = []
    for low, high in zip(cuts, cuts[1:]):
        held = [
            ref[low - first : high - first, :]
            for ref, (first, count) in zip(ys, spans)
            if first <= low < first + count
        ]
        parts.append(add(held))
    y = parts[0] if len(parts) == 1 else jnp.concatenate(parts, axis=0)
    ends = [ref for ref, (first, count) in zip(ys, spans) if first + count == rows]
    sub = lax.broadcasted_iota(jnp.int32, (8, LANES), 0)
    betas = []
    for m, (norm, cross) in enumerate(read_scalars(ends, members, 2)):
        if later:
            old_norm, old_square = old[m, 0:1, 0:1], old[m, 1:2, 0:1]
            beta = norm / old_norm
            square = norm + 2.0 * beta * cross + beta * beta * old_square
        else:
            beta = jnp.zeros_like(norm)
            square = norm
        betas.append(beta)
        state[m] = jnp.where(sub == 0, norm, jnp.where(sub == 1, square, beta))
    if later:
        y = y + by_member(betas, (rows, 1), lev) * old_image[...]
    if not last:
        image[...] = y
    scaled = prec[...] * y
    energies = [[x] for x in member_sums(scaled * y, members, lev)]
    weighted = with_scalars(scaled, energies).astype(BF16)
    first = 0
    outs[0][...] = weighted
    for out in outs[1:]:
        out[...] = weighted[first : first + out.shape[0]]
        first += out.shape[0]


def adjoint_kernel(plan, members, *refs):
    z, core, obs = place()
    ws, tiles, out = refs[: len(plan)], refs[len(plan)], refs[len(plan) + 1]
    rows, lanes = out.shape
    width = ws[0].shape[1]
    acc = None
    for i in range(tiles.shape[0]):
        w = {first: ref for ref, (chip, first, count) in zip(ws, plan) if chip == i}
        w = [w[first][...] for first in sorted(w)]
        w = w[0] if len(w) == 1 else jnp.concatenate(w, axis=0)
        part = lax.dot_general(
            w, tiles[z ^ i].reshape(lanes, width), NT, preferred_element_type=F32
        )
        acc = part if i == 0 else acc + part
    ends = [ref for ref, (chip, first, count) in zip(ws, plan) if first + count == rows]
    out[...] = with_scalars(acc, read_scalars(ends, members, 1)).astype(out.dtype)


def combine_kernel(members, mine, theirs, *outs):
    value = mine[...] + theirs[...].astype(F32)
    put_halves(outs, with_scalars(value, read_scalars([mine, theirs], members, 1)))


def combine_columns_kernel(members, mine, theirs, *outs):
    obs = lax.axis_index("obs")
    energies = read_scalars([mine, theirs], members, 1)
    for i, out in enumerate(outs):
        lane = pl.ds(pl.multiple_of((obs ^ i) * LANES, LANES), LANES)
        value = mine[:, lane] + theirs[:, lane].astype(F32)
        out[...] = with_scalars(value, energies).astype(BF16)


def update_kernel(later, lev, *refs):
    pieces, refs = refs[:4], refs[4:]
    sd, vert, vert_t, state, residual = refs[:5]
    spread, packed = refs[-2:]
    if later:
        old_direction, old_solution, residual_out, solution_out, moved, direction_out = refs[5:-2]
    else:
        residual_out, solution_out, moved = refs[5:-2]
    members, levp, unused = residual.shape
    obs = lax.axis_index("obs")
    mine = pl.ds(pl.multiple_of(obs * LANES, LANES), LANES)
    unpack(spread, joined(pieces))
    energies = read_scalars(pieces[:2], members, 1)
    scalars = []
    for m in range(members):
        at = slice(m * lev, m * lev + levp)
        norm, square, beta = state[m, 0:1, 0:1], state[m, 1:2, 0:1], state[m, 2:3, 0:1]
        alpha = norm / (square + energies[m][0])
        r = residual[m]
        if later:
            d = r + beta * old_direction[m]
            direction_out[m] = d
            step = direction_out[m, :, mine]
            solution_out[m] = old_solution[m] + alpha * step
        else:
            d = r
            solution_out[m] = alpha * residual[m, :, mine]
        r = r - alpha * (d + dot(vert_t[...], sd[...] * spread[at, :]))
        residual_out[m] = r
        packed[at, :] = sd[...] * dot(vert[...], r)
        scalars.append([total(r * r), total(r * d)])
    moved[...] = with_scalars(packed[0 : moved.shape[0], :], scalars).astype(BF16)


def last_kernel(parts, later, lev, *refs):
    pieces, refs = refs[:parts], refs[parts:]
    sd, vert, vert_t, state, residual = refs[:5]
    increment_out, residual_out, spread = refs[-3:]
    members, levp, unused = residual.shape
    obs = lax.axis_index("obs")
    mine = pl.ds(pl.multiple_of(obs * LANES, LANES), LANES)
    unpack(spread, add([x[...] for x in pieces]))
    energies = read_scalars(pieces, members, 1)
    for m in range(members):
        t = spread[m * lev : m * lev + levp, :]
        norm, square, beta = state[m, 0:1, 0:1], state[m, 1:2, 0:1], state[m, 2:3, 0:1]
        alpha = norm / (square + energies[m][0])
        d = r = residual[m, :, mine]
        if later:
            old_direction, old_solution = refs[5:7]
            d = r + beta * old_direction[m, :, mine]
        solution = alpha * d
        if later:
            solution = old_solution[m] + solution
        r = r - alpha * (d + dot(vert_t[...], sd[...] * t))
        increment = sd[...] * dot(vert[...], solution)
        increment_out[:, m, :] = increment[0:lev]
        residual_out[:, m, :] = r[0:lev]


def per_device(
    n_slab,
    n_obs,
    innovation,
    obs_precision,
    seeds,
    col_sd,
    vert_factor,
    h_values,
    block_obs,
    block_col,
    entry_count,
):
    blocks, lev, profiles = innovation.shape
    members = seeds.shape[0]
    chips = n_slab // 2
    halves = n_slab // blocks
    width = profiles // halves
    colblocks = n_obs
    assert halves * blocks == n_slab and width % LANES == 0 and col_sd.shape[0] == 1
    assert chips & (chips - 1) == 0 and n_obs & (n_obs - 1) == 0
    levp = (lev + 1 + 15) // 16 * 16
    assert members <= 16 and members >= PIECES
    rows = (members * (lev + 1) + 15) // 16 * 16
    lanes = colblocks * LANES
    slab_field = (members, levp, lanes)
    slab_rows = (rows, lanes)
    half_rows = [struct((rows, lanes // 2), BF16)] * 2
    wide = rows + levp - lev + 7
    spread = pltpu.VMEM((wide // 8 * 8, lanes), F32)
    some = rows // 32 * 16
    rest = rows - some
    via = chips == 4
    if via:
        one, two = (0, some), (some, rest)
        plan = [(0, 0, rows), *((i, *two) for i in (1, 3, 2)), *((i, *one) for i in (1, 2, 3))]
        sends = [(3, *one), (2, *two), (3, *two), (1, *one), (1, *two), (0, 0, rows), (2, *one)]
    else:
        sends = plan = [(i, 0, rows) for i in range(chips)]
    pad = ((0, levp - lev), (0, levp - lev))
    high = lax.reduce_precision(vert_factor, 8, 7)
    low = vert_factor - high
    vert, vert_t = [
        jnp.concatenate([jnp.pad(x, pad).astype(BF16) for x in parts], axis=1)
        for parts in ((high, high, low), (high.T, high.T, low.T))
    ]
    h_block = h_values.reshape(h_values.shape[2:])
    innovation = jnp.transpose(innovation, (1, 0, 2))
    obs_precision = jnp.transpose(obs_precision, (1, 0, 2))
    product = n_slab * width * lanes * rows
    small = 12 * rows * levp * LANES
    plane_bits = [1 << k for k in range(n_obs.bit_length() - 1)]

    def along(x, i):
        return lax.ppermute(x, "slab", [(s, s ^ (2 * i)) for s in range(n_slab)])

    def plane(x, i):
        return lax.ppermute(x, "obs", [(o, o ^ i) for o in range(n_obs)])

    def swap(x):
        return lax.ppermute(x, "slab", [(s, s ^ 1) for s in range(n_slab)])

    def plane_sum(halves, staged):
        halves = list(halves)
        moved_halves = [None] * len(halves)
        for step, bit in enumerate(plane_bits):
            bits = [bit, plane_bits[len(plane_bits) - 1 - step]]
            for at in range(0, len(halves), 2):
                if step > 0:
                    one, two = halves[at : at + 2]
                    one_more, two_more = moved_halves[at : at + 2]
                    halves[at : at + 2] = call(
                        functools.partial(add_halves_kernel, members, 0 if staged else 1),
                        [struct(one.shape, BF16)] * 2,
                        [],
                        0,
                        one,
                        one_more,
                        two,
                        two_more,
                    )
                for half in range(2):
                    moved_halves[at + half] = plane(halves[at + half], bits[half])
            if step == 0 and staged:
                halves[:] = call(
                    stage_kernel,
                    [struct(x.shape, BF16) for x in halves],
                    [pltpu.SemaphoreType.DMA((len(halves),))],
                    0,
                    *halves,
                    space=HBM,
                )
        return [x for pair in zip(halves, moved_halves) for x in pair]

    def line_sum(moved, other):
        ys = call(
            functools.partial(forward_kernel, sends, members),
            [
                struct((count, width), F32 if i == 0 or (via and at == 6) else BF16)
                for at, (i, unused, count) in enumerate(sends)
            ],
            [],
            2 * product,
            moved,
            other,
            own,
            partner,
        )
        if not via:
            return [y if i == 0 else along(y, i) for i, y in enumerate(ys)], [(0, rows)] * chips
        passed, far_rest, last_rest, next_some, next_rest, near, far = ys
        passed = along(passed, 1)
        far_rest, last_rest = along(far_rest, 2), along(last_rest, 3)
        next_some, next_rest = along(next_some, 1), along(next_rest, 1)
        (far,) = call(
            functools.partial(add_kernel, members, 0),
            [struct((some, width), BF16)],
            [],
            0,
            far,
            passed,
        )
        ys = [near, far_rest, last_rest, next_some, next_rest, along(far, 2)]
        return ys, [(0, rows), two, two, one, two, one]

    def line_gather(w, *parts):
        if not via:
            return [w if i == 0 else along(w, i) for i in range(chips)]
        some_w, rest_w = parts
        far, next_ = along(some_w, 2), along(some_w, 1)
        rest_ws = [along(rest_w, i) for i in (1, 3, 2)]
        return [w, *rest_ws, next_, far, along(far, 1)]

    dense = struct((chips, colblocks, LANES, width), BF16)
    own, for_partner, *partials = call(
        functools.partial(start_kernel, (chips, halves)),
        [dense, dense] + half_rows,
        [
            pltpu.SMEM(seeds.shape, jnp.int32),
            pltpu.SMEM(block_obs.shape, jnp.int32),
            pltpu.SMEM(block_col.shape, jnp.int32),
            pltpu.SMEM(entry_count.shape, jnp.int32),
            pltpu.VMEM(col_sd.shape, F32),
            pltpu.VMEM((blocks, lev, profiles), F32),
            pltpu.VMEM((blocks, lev, profiles), F32),
            pltpu.VMEM((n_slab, members, levp, width), F32),
            pltpu.VMEM((2, rows, width), F32),
            pltpu.VMEM((rows, lanes), F32),
            pltpu.SemaphoreType.DMA((5 + 2 * blocks,)),
            pltpu.SemaphoreType.DMA((h_block.shape[0] * halves,)),
        ],
        2 * product,
        seeds,
        block_obs,
        block_col,
        entry_count,
        col_sd,
        innovation,
        obs_precision,
        h_block,
        space=HBM,
        limit=60,
    )
    ps = plane_sum(partials, True)
    partner = swap(for_partner)
    (precision,) = call(
        functools.partial(precision_kernel, halves, members),
        [struct((rows, width), F32)],
        [],
        0,
        obs_precision,
    )
    slab_sd, residual, moved = call(
        functools.partial(first_kernel, lev),
        [struct((1, lanes), F32), struct(slab_field, F32), struct(slab_rows, BF16)],
        [spread, spread],
        small * colblocks,
        *ps,
        vert,
        vert_t,
    )
    direction = total_step = image = state = None
    for sweep in range(ITERS):
        later, last = sweep > 0, sweep == ITERS - 1
        ys, spans = line_sum(moved, swap(moved))
        state, *weighted = call(
            functools.partial(weigh_kernel, later, last, members, lev, spans),
            [struct((members, 8, LANES), F32)]
            + [struct((n, width), BF16) for n in ((rows, some, rest) if via else (rows,))]
            + ([] if last else [struct((rows, width), F32)]),
            [],
            0,
            *ys,
            precision,
            *([image, state] if later else []),
        )
        if not last:
            *weighted, image = weighted
        ws = line_gather(*weighted)
        (theirs,) = call(
            functools.partial(adjoint_kernel, plan, members),
            [struct(slab_rows, BF16)],
            [],
            product,
            *ws,
            partner,
        )
        theirs = swap(theirs)
        (mine,) = call(
            functools.partial(adjoint_kernel, plan, members),
            [struct(slab_rows, F32)],
            [],
            product,
            *ws,
            own,
        )
        known = [vert, vert_t, state, residual]
        if later:
            known += [direction, total_step]
        if last:
            ps = call(
                functools.partial(combine_columns_kernel, members),
                [struct((rows, LANES), BF16)] * n_obs,
                [],
                0,
                mine,
                theirs,
            )
            ps = [ps[0]] + [plane(ps[i], i) for i in reversed(range(1, n_obs))]
            outputs = call(
                functools.partial(last_kernel, len(ps), later, lev),
                [struct((lev, members, LANES), F32)] * 2,
                [pltpu.VMEM((wide // 8 * 8, LANES), F32)],
                small,
                *ps,
                col_sd,
                *known,
            )
            break
        ps = call(
            functools.partial(combine_kernel, members), half_rows, [], 0, mine, theirs
        )
        ps = plane_sum(ps, False)
        outs = [
            struct(slab_field, F32),
            struct((members, levp, LANES), F32),
            struct(slab_rows, BF16),
        ]
        if later:
            outs.append(struct(slab_field, F32))
        r, total_step, moved, *d = call(
            functools.partial(update_kernel, later, lev),
            outs,
            [spread, spread],
            small * colblocks,
            *ps,
            slab_sd,
            *known,
        )
        direction, residual = (d[0] if later else residual), r
    return tuple(jnp.transpose(x, (1, 0, 2))[None] for x in outputs)


def solution(mesh):
    return jax.shard_map(
        functools.partial(per_device, mesh.shape["slab"], mesh.shape["obs"]),
        mesh=mesh,
        in_specs=(
            P("obs", None, None),
            P("obs", None, None),
            P(),
            P(("slab", "obs"), None),
            P(),
            P("slab", "obs", None, None, None),
            P("slab", "obs", None),
            P("slab", "obs", None),
            P("slab", "obs"),
        ),
        out_specs=(P(("slab", "obs"), None, None, None), P(("slab", "obs"), None, None, None)),
        check_vma=False,
    )
```

```python
import functools

import jax
import jax.numpy as jnp
from jax import lax
from jax.experimental import pallas as pl
from jax.experimental.pallas import tpu as pltpu
from jax.sharding import PartitionSpec as P

ITERS = 2
LANES = 128
PIECES = 3
PRIME = 32749
VMEM = pl.BlockSpec(memory_space=pltpu.VMEM)
HBM = pl.BlockSpec(memory_space=pltpu.HBM)
F32 = jnp.float32
BF16 = jnp.bfloat16
NT = (((1,), (1,)), ((), ()))


def call(kernel, outs, scratch, flops, *args, space=VMEM, limit=24):
    nbytes = sum(a.size * a.dtype.itemsize for a in (*args, *outs))
    return pl.pallas_call(
        kernel,
        out_shape=outs,
        in_specs=[space] * len(args),
        out_specs=[VMEM] * len(outs),
        scratch_shapes=scratch,
        compiler_params=pltpu.CompilerParams(vmem_limit_bytes=limit * 1024 * 1024),
        cost_estimate=pl.CostEstimate(flops=flops, bytes_accessed=nbytes, transcendentals=0),
    )(*args)


def struct(shape, dtype):
    return jax.ShapeDtypeStruct(shape, dtype)


def place():
    slab = lax.axis_index("slab")
    return slab // 2, slab % 2, lax.axis_index("obs")


def add(parts):
    value = parts[0].astype(F32)
    for part in parts[1:]:
        value = value + part.astype(F32)
    return value


def dot(matrix, x):
    high = x.astype(BF16)
    rest = (x - high.astype(F32)).astype(BF16)
    x = jnp.concatenate([high, rest, high], axis=0)
    return jnp.dot(matrix, x, preferred_element_type=F32)


def total(x):
    return jnp.sum(jnp.sum(x, axis=0, keepdims=True), axis=1, keepdims=True)


def with_scalars(body, values):
    count = body.shape[0]
    tail = body[count - 16 :]
    sub = lax.broadcasted_iota(jnp.int32, tail.shape, 0) - (16 - len(values))
    lanes = lax.broadcasted_iota(jnp.int32, tail.shape, 1)
    line = jnp.zeros(tail.shape, F32)
    for m, member in enumerate(values):
        for q, value in enumerate(member):
            rest = value
            for piece in range(PIECES):
                part = rest.astype(BF16).astype(F32)
                rest = rest - part
                line = jnp.where((sub == m) & (lanes == q * PIECES + piece), part, line)
    return jnp.concatenate([body[: count - 16], jnp.where(sub >= 0, line, tail)], axis=0)


def read_scalars(refs, members, count):
    tail = add([ref[ref.shape[0] - 16 :, 0:LANES] for ref in refs])
    sub = lax.broadcasted_iota(jnp.int32, tail.shape, 0) - (16 - members)
    lanes = lax.broadcasted_iota(jnp.int32, tail.shape, 1)
    return [
        [
            total(
                jnp.where(
                    (sub == m) & (lanes >= q * PIECES) & (lanes < (q + 1) * PIECES), tail, 0.0
                )
            )
            for q in range(count)
        ]
        for m in range(members)
    ]


def by_member(values, shape, lev):
    rows = lax.broadcasted_iota(jnp.int32, shape, 0)
    out = jnp.zeros(shape, F32)
    for m, value in enumerate(values):
        out = jnp.where((rows >= m * lev) & (rows < (m + 1) * lev), value, out)
    return out


def member_sums(x, members, lev):
    lines = jnp.sum(x, axis=1, keepdims=True)
    rows = lax.broadcasted_iota(jnp.int32, lines.shape, 0)
    return [
        jnp.sum(
            jnp.where((rows >= m * lev) & (rows < (m + 1) * lev), lines, 0.0),
            axis=0,
            keepdims=True,
        )
        for m in range(members)
    ]


def remainder(x, factor):
    return x - (x.astype(F32) * factor).astype(jnp.int32) * PRIME


def start_kernel(
    dims, seeds_in, ids_in, cols_in, count_in, sd_in, innov_in, prec_in, h, own, partner, *rest
):
    chips, halves = dims
    outs = rest[:-12]
    seeds, ids, cols, count, sd, innov, prec, hashed, scratch, acc, sems, h_sems = rest[-12:]
    z, core, obs = place()
    blocks, lev, profiles = innov.shape
    colblocks, width = own.shape[1], own.shape[3]
    members, levp = hashed.shape[1], hashed.shape[2]
    rows = acc.shape[0]

    pairs = [(seeds_in, seeds), (ids_in, ids), (cols_in, cols), (count_in, count), (sd_in, sd)]
    small = [pltpu.make_async_copy(x, y, sems.at[i]) for i, (x, y) in enumerate(pairs)]
    for copy in small:
        copy.start()
    large = []
    for b in range(blocks):
        at = len(pairs) + 2 * b
        large.append(pltpu.make_async_copy(innov_in.at[:, b, :], innov.at[b], sems.at[at]))
        large.append(pltpu.make_async_copy(prec_in.at[:, b, :], prec.at[b], sems.at[at + 1]))
    for copy in large:
        copy.start()
    own[...] = jnp.zeros_like(own)
    partner[...] = jnp.zeros_like(partner)
    scratch[...] = jnp.zeros_like(scratch)
    for copy in small:
        copy.wait()

    def tile_copy(n, half, target):
        lanes = pl.ds(half * width, width)
        return pltpu.make_async_copy(h.at[n, :, lanes], target, h_sems.at[n * halves + half])

    def put(n, carry):
        for half in range(halves):
            piece, k = ids[0, 0, n] * halves + half, cols[0, 0, n]

            @pl.when(piece % 2 == core)
            def _():
                tile_copy(n, half, own.at[piece // 2, k]).start()

            @pl.when(piece % 2 != core)
            def _():
                tile_copy(n, half, partner.at[piece // 2, k]).start()

        return carry

    lax.fori_loop(0, count[0, 0], put, 0)

    starts = [lax.rem(seeds[m], PRIME) - PRIME for m in range(members)]
    order = [(source, zz) for source in range(2) for zz in range(chips)]
    shape = (levp, width)
    spot = lax.broadcasted_iota(jnp.int32, shape, 0) * profiles
    spot = spot + lax.broadcasted_iota(jnp.int32, shape, 1)
    low = (1.0 - 2.0**-21) / PRIME

    def piece_at(at):
        source, zz = order[at]
        return 2 * zz + (core if source == 0 else 1 - core)

    def draw(at):
        piece = piece_at(at)
        first = (obs * blocks + piece // halves) * (lev * profiles) + (piece % halves) * width
        base = remainder(7919 * remainder(spot + first, 1.0 / PRIME), 1.0 / PRIME)
        for m in range(members):
            k0 = base + starts[m]
            k1 = remainder(k0 * k0 + 12345, 1.0 / PRIME)
            k2 = remainder(k1 * k1 + 2719, low)
            k2 = jnp.where(k2 >= PRIME, k2 - PRIME, k2)
            hashed[at, m] = k2.astype(F32)

    def adjoint(at):
        source, zz = order[at]
        piece = piece_at(at)
        b = piece // halves
        if halves == 1:
            p, d = prec[b], innov[b]
        else:
            lanes = pl.ds(pl.multiple_of((piece % halves) * width, LANES), width)
            p, d = prec[b, :, lanes], innov[b, :, lanes]
        gain = 3.4 * p * lax.rsqrt(p)
        offset = p * d - 0.5 * gain
        gain = gain * (1.0 / PRIME)
        for m in range(members):
            w = offset + gain * hashed[at, m, 0:lev, :]
            scratch[at % 2, m * lev : (m + 1) * lev, :] = w
        w = scratch[at % 2].astype(BF16)
        tiles = (own if source == 0 else partner)[zz].reshape(colblocks * LANES, width)
        part = lax.dot_general(w, tiles, NT, preferred_element_type=F32)
        if at == 0:
            acc[...] = part
        else:
            acc[...] += part

    early = len(order) // 2
    for at in range(early):
        draw(at)
    for copy in large:
        copy.wait()

    def arrive(n, carry):
        for half in range(halves):
            tile_copy(n, half, own.at[0, 0]).wait()
        return carry

    lax.fori_loop(0, count[0, 0], arrive, 0)

    for at in range(len(order)):
        if at + early < len(order):
            draw(at + early)
        adjoint(at)

    line = jnp.concatenate([sd[...]] * colblocks, axis=1)
    put_halves(outs, with_columns(acc[...], line, obs, members))


def put_halves(outs, value):
    half = value.shape[1] // 2
    outs[0][...] = value[:, :half].astype(BF16)
    outs[1][...] = value[:, half:].astype(BF16)


def with_columns(body, line, obs, members):
    tail = body[body.shape[0] - 16 :]
    sub = lax.broadcasted_iota(jnp.int32, tail.shape, 0)
    mine = lax.broadcasted_iota(jnp.int32, tail.shape, 1) // LANES == obs
    rest = line
    for piece in range(PIECES):
        part = rest.astype(BF16).astype(F32)
        rest = rest - part
        tail = jnp.where((sub == 16 - PIECES + piece) & mine, part, tail)
    return jnp.concatenate([body[: body.shape[0] - 16], tail], axis=0)


def read_columns(body):
    tail = body[body.shape[0] - 16 :]
    sub = lax.broadcasted_iota(jnp.int32, tail.shape, 0)
    return jnp.sum(jnp.where(sub >= 16 - PIECES, tail, 0.0), axis=0, keepdims=True)


def precision_kernel(halves, members, prec, out):
    z, core, unused = place()
    piece = 2 * z + core
    lev, blocks, unused = prec.shape
    width = out.shape[1]
    block = lax.broadcasted_iota(jnp.int32, (lev, blocks, width), 1)
    if halves == 1:
        mine = prec[...]
    else:
        mine = prec[:, :, pl.ds(pl.multiple_of((piece % halves) * width, LANES), width)]
    out[...] = jnp.zeros_like(out)
    mine = jnp.sum(jnp.where(block == piece // halves, mine, 0.0), axis=1)
    for m in range(members):
        out[m * lev : (m + 1) * lev, :] = mine


def joined(pieces):
    one, one_more, two, two_more = [x[...] for x in pieces]
    return jnp.concatenate([add([one, one_more]), add([two, two_more])], axis=1)


def unpack(spread, value):
    count = value.shape[0]
    spread[0:count, :] = value
    spread[count:, :] = jnp.zeros((spread.shape[0] - count, value.shape[1]), F32)


def first_kernel(lev, *refs):
    vert, vert_t, sd_out, residual, moved, spread, packed = refs[4:]
    members, levp, unused = residual.shape
    t = joined(refs[:4])
    sd = read_columns(t)
    sd_out[...] = sd
    unpack(spread, t)
    scalars = []
    for m in range(members):
        at = slice(m * lev, m * lev + levp)
        r = dot(vert_t[...], sd * spread[at, :])
        residual[m] = r
        packed[at, :] = sd * dot(vert[...], r)
        scalars.append([total(r * r)])
    moved[...] = with_scalars(packed[0 : moved.shape[0], :], scalars).astype(BF16)


def add_kernel(members, scalars, *refs):
    parts, out = refs[:-1], refs[-1]
    value = add([x[...] for x in parts])
    if scalars:
        value = with_scalars(value, read_scalars(parts, members, scalars))
    out[...] = value.astype(BF16)


def add_halves_kernel(members, scalars, one, one_more, two, two_more, one_out, two_out):
    add_kernel(members, scalars, one, one_more, one_out)
    add_kernel(members, 0, two, two_more, two_out)


def stage_kernel(*refs):
    sems = refs[-1]
    count = len(refs) // 2
    copies = [
        pltpu.make_async_copy(refs[i], refs[count + i], sems.at[i]) for i in range(count)
    ]
    for copy in copies:
        copy.start()
    for copy in copies:
        copy.wait()


def forward_kernel(sends, members, x, tiles, *refs):
    z, core, obs = place()
    outs = refs[-len(sends) :]
    rows, lanes = x.shape
    width = tiles.shape[3]
    added = refs[1 : 1 + len(sends)] if len(refs) > len(sends) else [None] * len(sends)
    if added[0] is not None:
        scalars = read_scalars([refs[0], x], members, 2)
    for out, before, (chip, first, count) in zip(outs, added, sends):
        y = jnp.dot(
            x[first : first + count, :],
            tiles[z ^ chip].reshape(lanes, width),
            preferred_element_type=F32,
        )
        if before is not None:
            y = before[...] + y
            if first + count == rows:
                y = with_scalars(y, scalars)
        out[...] = y.astype(out.dtype)


def weigh_kernel(later, last, members, lev, spans, *refs):
    ys, refs = refs[: len(spans)], refs[len(spans) :]
    prec, old_image, old = refs[0], *(refs[1:3] if later else (None, None))
    state, *outs = refs[3 if later else 1 :]
    if not last:
        *outs, image = outs
    rows = prec.shape[0]
    cuts = sorted({first for first, count in spans}) + [rows]
    parts = []
    for low, high in zip(cuts, cuts[1:]):
        held = [
            ref[low - first : high - first, :]
            for ref, (first, count) in zip(ys, spans)
            if first <= low < first + count
        ]
        parts.append(add(held))
    y = parts[0] if len(parts) == 1 else jnp.concatenate(parts, axis=0)
    ends = [ref for ref, (first, count) in zip(ys, spans) if first + count == rows]
    sub = lax.broadcasted_iota(jnp.int32, (8, LANES), 0)
    betas = []
    for m, (norm, cross) in enumerate(read_scalars(ends, members, 2)):
        if later:
            old_norm, old_square = old[m, 0:1, 0:1], old[m, 1:2, 0:1]
            beta = norm / old_norm
            square = norm + 2.0 * beta * cross + beta * beta * old_square
        else:
            beta = jnp.zeros_like(norm)
            square = norm
        betas.append(beta)
        state[m] = jnp.where(sub == 0, norm, jnp.where(sub == 1, square, beta))
    if later:
        y = y + by_member(betas, (rows, 1), lev) * old_image[...]
    if not last:
        image[...] = y
    scaled = prec[...] * y
    energies = [[x] for x in member_sums(scaled * y, members, lev)]
    weighted = with_scalars(scaled, energies).astype(BF16)
    first = 0
    outs[0][...] = weighted
    for out in outs[1:]:
        out[...] = weighted[first : first + out.shape[0]]
        first += out.shape[0]


def adjoint_kernel(plan, members, *refs):
    z, core, obs = place()
    ws, tiles, out = refs[: len(plan)], refs[len(plan)], refs[len(plan) + 1]
    rows, lanes = out.shape
    width = ws[0].shape[1]
    acc = None
    for i in range(tiles.shape[0]):
        w = {first: ref for ref, (chip, first, count) in zip(ws, plan) if chip == i}
        w = [w[first][...] for first in sorted(w)]
        w = w[0] if len(w) == 1 else jnp.concatenate(w, axis=0)
        part = lax.dot_general(
            w, tiles[z ^ i].reshape(lanes, width), NT, preferred_element_type=F32
        )
        acc = part if i == 0 else acc + part
    ends = [ref for ref, (chip, first, count) in zip(ws, plan) if first + count == rows]
    out[...] = with_scalars(acc, read_scalars(ends, members, 1)).astype(out.dtype)


def combine_kernel(members, mine, theirs, *outs):
    value = mine[...] + theirs[...].astype(F32)
    put_halves(outs, with_scalars(value, read_scalars([mine, theirs], members, 1)))


def combine_columns_kernel(members, mine, theirs, *outs):
    obs = lax.axis_index("obs")
    energies = read_scalars([mine, theirs], members, 1)
    for i, out in enumerate(outs):
        lane = pl.ds(pl.multiple_of((obs ^ i) * LANES, LANES), LANES)
        value = mine[:, lane] + theirs[:, lane].astype(F32)
        out[...] = with_scalars(value, energies).astype(BF16)


def update_kernel(later, lev, *refs):
    pieces, refs = refs[:4], refs[4:]
    sd, vert, vert_t, state, residual = refs[:5]
    spread, packed = refs[-2:]
    if later:
        old_direction, old_solution, residual_out, solution_out, moved, direction_out = refs[5:-2]
    else:
        residual_out, solution_out, moved = refs[5:-2]
    members, levp, unused = residual.shape
    obs = lax.axis_index("obs")
    mine = pl.ds(pl.multiple_of(obs * LANES, LANES), LANES)
    unpack(spread, joined(pieces))
    energies = read_scalars(pieces[:2], members, 1)
    scalars = []
    for m in range(members):
        at = slice(m * lev, m * lev + levp)
        norm, square, beta = state[m, 0:1, 0:1], state[m, 1:2, 0:1], state[m, 2:3, 0:1]
        alpha = norm / (square + energies[m][0])
        r = residual[m]
        if later:
            d = r + beta * old_direction[m]
            direction_out[m] = d
            step = direction_out[m, :, mine]
            solution_out[m] = old_solution[m] + alpha * step
        else:
            d = r
            solution_out[m] = alpha * residual[m, :, mine]
        r = r - alpha * (d + dot(vert_t[...], sd[...] * spread[at, :]))
        residual_out[m] = r
        packed[at, :] = sd[...] * dot(vert[...], r)
        scalars.append([total(r * r), total(r * d)])
    moved[...] = with_scalars(packed[0 : moved.shape[0], :], scalars).astype(BF16)


def last_kernel(parts, later, lev, *refs):
    pieces, refs = refs[:parts], refs[parts:]
    sd, vert, vert_t, state, residual = refs[:5]
    increment_out, residual_out, spread = refs[-3:]
    members, levp, unused = residual.shape
    obs = lax.axis_index("obs")
    mine = pl.ds(pl.multiple_of(obs * LANES, LANES), LANES)
    unpack(spread, add([x[...] for x in pieces]))
    energies = read_scalars(pieces, members, 1)
    for m in range(members):
        t = spread[m * lev : m * lev + levp, :]
        norm, square, beta = state[m, 0:1, 0:1], state[m, 1:2, 0:1], state[m, 2:3, 0:1]
        alpha = norm / (square + energies[m][0])
        d = r = residual[m, :, mine]
        if later:
            old_direction, old_solution = refs[5:7]
            d = r + beta * old_direction[m, :, mine]
        solution = alpha * d
        if later:
            solution = old_solution[m] + solution
        r = r - alpha * (d + dot(vert_t[...], sd[...] * t))
        increment = sd[...] * dot(vert[...], solution)
        increment_out[:, m, :] = increment[0:lev]
        residual_out[:, m, :] = r[0:lev]


def per_device(
    n_slab,
    n_obs,
    innovation,
    obs_precision,
    seeds,
    col_sd,
    vert_factor,
    h_values,
    block_obs,
    block_col,
    entry_count,
):
    blocks, lev, profiles = innovation.shape
    members = seeds.shape[0]
    chips = n_slab // 2
    halves = n_slab // blocks
    width = profiles // halves
    colblocks = n_obs
    assert halves * blocks == n_slab and width % LANES == 0 and col_sd.shape[0] == 1
    assert chips & (chips - 1) == 0 and n_obs & (n_obs - 1) == 0
    levp = (lev + 1 + 15) // 16 * 16
    assert members <= 16 and members >= PIECES
    rows = (members * (lev + 1) + 15) // 16 * 16
    lanes = colblocks * LANES
    slab_field = (members, levp, lanes)
    slab_rows = (rows, lanes)
    half_rows = [struct((rows, lanes // 2), BF16)] * 2
    wide = rows + levp - lev + 7
    spread = pltpu.VMEM((wide // 8 * 8, lanes), F32)
    some = rows // 32 * 16
    rest = rows - some
    via = chips == 4
    if via:
        one, two = (0, some), (some, rest)
        plan = [(0, 0, rows), (1, 0, rows), (2, *one), (2, *two), (3, *one), (3, *two)]
        sends = [(3, *one), (2, *two), (3, *two), (1, *one), (1, *two), (0, 0, rows), (2, *one)]
    else:
        sends = plan = [(i, 0, rows) for i in range(chips)]
    pad = ((0, levp - lev), (0, levp - lev))
    high = lax.reduce_precision(vert_factor, 8, 7)
    low = vert_factor - high
    vert, vert_t = [
        jnp.concatenate([jnp.pad(x, pad).astype(BF16) for x in parts], axis=1)
        for parts in ((high, high, low), (high.T, high.T, low.T))
    ]
    h_block = h_values.reshape(h_values.shape[2:])
    innovation = jnp.transpose(innovation, (1, 0, 2))
    obs_precision = jnp.transpose(obs_precision, (1, 0, 2))
    product = n_slab * width * lanes * rows
    small = 12 * rows * levp * LANES
    plane_bits = [1 << k for k in range(n_obs.bit_length() - 1)]

    def along(x, i):
        return lax.ppermute(x, "slab", [(s, s ^ (2 * i)) for s in range(n_slab)])

    def plane(x, i):
        return lax.ppermute(x, "obs", [(o, o ^ i) for o in range(n_obs)])

    def swap(x):
        return lax.ppermute(x, "slab", [(s, s ^ 1) for s in range(n_slab)])

    def plane_sum(halves, staged):
        halves = list(halves)
        moved_halves = [None] * len(halves)
        for step, bit in enumerate(plane_bits):
            bits = [bit, plane_bits[len(plane_bits) - 1 - step]]
            for at in range(0, len(halves), 2):
                if step > 0:
                    one, two = halves[at : at + 2]
                    one_more, two_more = moved_halves[at : at + 2]
                    halves[at : at + 2] = call(
                        functools.partial(add_halves_kernel, members, 0 if staged else 1),
                        [struct(one.shape, BF16)] * 2,
                        [],
                        0,
                        one,
                        one_more,
                        two,
                        two_more,
                    )
                for half in range(2):
                    moved_halves[at + half] = plane(halves[at + half], bits[half])
            if step == 0 and staged:
                halves[:] = call(
                    stage_kernel,
                    [struct(x.shape, BF16) for x in halves],
                    [pltpu.SemaphoreType.DMA((len(halves),))],
                    0,
                    *halves,
                    space=HBM,
                )
        return [x for pair in zip(halves, moved_halves) for x in pair]

    def line_sum(moved, other):
        shapes = [(count, width) for i, unused, count in sends]
        mine = call(
            functools.partial(forward_kernel, sends, members),
            [struct(shape, F32) for shape in shapes],
            [],
            product,
            moved,
            own,
        )
        ys = call(
            functools.partial(forward_kernel, sends, members),
            [
                struct(shape, F32 if i == 0 or (via and at == 6) else BF16)
                for at, ((i, *unused), shape) in enumerate(zip(sends, shapes))
            ],
            [],
            product,
            other,
            partner,
            moved,
            *mine,
        )
        if not via:
            return [y if i == 0 else along(y, i) for i, y in enumerate(ys)], [(0, rows)] * chips
        passed, far_rest, last_rest, next_some, next_rest, near, far = ys
        passed = along(passed, 1)
        far_rest, last_rest = along(far_rest, 2), along(last_rest, 3)
        next_some, next_rest = along(next_some, 1), along(next_rest, 1)
        (far,) = call(
            functools.partial(add_kernel, members, 0),
            [struct((some, width), BF16)],
            [],
            0,
            far,
            passed,
        )
        ys = [near, far_rest, last_rest, next_some, next_rest, along(far, 2)]
        return ys, [(0, rows), two, two, one, two, one]

    def line_gather(w, *parts):
        if not via:
            return [w if i == 0 else along(w, i) for i in range(chips)]
        some_w, rest_w = parts
        far = along(some_w, 2)
        far_rest, last_rest, next_ = along(rest_w, 2), along(rest_w, 3), along(w, 1)
        return [w, next_, far, far_rest, along(far, 1), last_rest]

    dense = struct((chips, colblocks, LANES, width), BF16)
    own, for_partner, *partials = call(
        functools.partial(start_kernel, (chips, halves)),
        [dense, dense] + half_rows,
        [
            pltpu.SMEM(seeds.shape, jnp.int32),
            pltpu.SMEM(block_obs.shape, jnp.int32),
            pltpu.SMEM(block_col.shape, jnp.int32),
            pltpu.SMEM(entry_count.shape, jnp.int32),
            pltpu.VMEM(col_sd.shape, F32),
            pltpu.VMEM((blocks, lev, profiles), F32),
            pltpu.VMEM((blocks, lev, profiles), F32),
            pltpu.VMEM((n_slab, members, levp, width), F32),
            pltpu.VMEM((2, rows, width), F32),
            pltpu.VMEM((rows, lanes), F32),
            pltpu.SemaphoreType.DMA((5 + 2 * blocks,)),
            pltpu.SemaphoreType.DMA((h_block.shape[0] * halves,)),
        ],
        2 * product,
        seeds,
        block_obs,
        block_col,
        entry_count,
        col_sd,
        innovation,
        obs_precision,
        h_block,
        space=HBM,
        limit=60,
    )
    ps = plane_sum(partials, True)
    partner = swap(for_partner)
    (precision,) = call(
        functools.partial(precision_kernel, halves, members),
        [struct((rows, width), F32)],
        [],
        0,
        obs_precision,
    )
    slab_sd, residual, moved = call(
        functools.partial(first_kernel, lev),
        [struct((1, lanes), F32), struct(slab_field, F32), struct(slab_rows, BF16)],
        [spread, spread],
        small * colblocks,
        *ps,
        vert,
        vert_t,
    )
    direction = total_step = image = state = None
    for sweep in range(ITERS):
        later, last = sweep > 0, sweep == ITERS - 1
        ys, spans = line_sum(moved, swap(moved))
        state, *weighted = call(
            functools.partial(weigh_kernel, later, last, members, lev, spans),
            [struct((members, 8, LANES), F32)]
            + [struct((n, width), BF16) for n in ((rows, some, rest) if via else (rows,))]
            + ([] if last else [struct((rows, width), F32)]),
            [],
            0,
            *ys,
            precision,
            *([image, state] if later else []),
        )
        if not last:
            *weighted, image = weighted
        ws = line_gather(*weighted)
        (theirs,) = call(
            functools.partial(adjoint_kernel, plan, members),
            [struct(slab_rows, BF16)],
            [],
            product,
            *ws,
            partner,
        )
        theirs = swap(theirs)
        (mine,) = call(
            functools.partial(adjoint_kernel, plan, members),
            [struct(slab_rows, F32)],
            [],
            product,
            *ws,
            own,
        )
        known = [vert, vert_t, state, residual]
        if later:
            known += [direction, total_step]
        if last:
            ps = call(
                functools.partial(combine_columns_kernel, members),
                [struct((rows, LANES), BF16)] * n_obs,
                [],
                0,
                mine,
                theirs,
            )
            ps = [ps[0]] + [plane(ps[i], i) for i in reversed(range(1, n_obs))]
            outputs = call(
                functools.partial(last_kernel, len(ps), later, lev),
                [struct((lev, members, LANES), F32)] * 2,
                [pltpu.VMEM((wide // 8 * 8, LANES), F32)],
                small,
                *ps,
                col_sd,
                *known,
            )
            break
        ps = call(
            functools.partial(combine_kernel, members), half_rows, [], 0, mine, theirs
        )
        ps = plane_sum(ps, False)
        outs = [
            struct(slab_field, F32),
            struct((members, levp, LANES), F32),
            struct(slab_rows, BF16),
        ]
        if later:
            outs.append(struct(slab_field, F32))
        r, total_step, moved, *d = call(
            functools.partial(update_kernel, later, lev),
            outs,
            [spread, spread],
            small * colblocks,
            *ps,
            slab_sd,
            *known,
        )
        direction, residual = (d[0] if later else residual), r
    return tuple(jnp.transpose(x, (1, 0, 2))[None] for x in outputs)


def solution(mesh):
    return jax.shard_map(
        functools.partial(per_device, mesh.shape["slab"], mesh.shape["obs"]),
        mesh=mesh,
        in_specs=(
            P("obs", None, None),
            P("obs", None, None),
            P(),
            P(("slab", "obs"), None),
            P(),
            P("slab", "obs", None, None, None),
            P("slab", "obs", None),
            P("slab", "obs", None),
            P("slab", "obs"),
        ),
        out_specs=(P(("slab", "obs"), None, None, None), P(("slab", "obs"), None, None, None)),
        check_vma=False,
    )
```

```python
import functools

import jax
import jax.numpy as jnp
from jax import lax
from jax.experimental import pallas as pl
from jax.experimental.pallas import tpu as pltpu
from jax.sharding import PartitionSpec as P

ITERS = 2
LANES = 128
PIECES = 3
PRIME = 32749
VMEM = pl.BlockSpec(memory_space=pltpu.VMEM)
HBM = pl.BlockSpec(memory_space=pltpu.HBM)
F32 = jnp.float32
BF16 = jnp.bfloat16
NT = (((1,), (1,)), ((), ()))


def call(kernel, outs, scratch, flops, *args, space=VMEM, limit=24):
    nbytes = sum(a.size * a.dtype.itemsize for a in (*args, *outs))
    return pl.pallas_call(
        kernel,
        out_shape=outs,
        in_specs=[space] * len(args),
        out_specs=[VMEM] * len(outs),
        scratch_shapes=scratch,
        compiler_params=pltpu.CompilerParams(vmem_limit_bytes=limit * 1024 * 1024),
        cost_estimate=pl.CostEstimate(flops=flops, bytes_accessed=nbytes, transcendentals=0),
    )(*args)


def struct(shape, dtype):
    return jax.ShapeDtypeStruct(shape, dtype)


def place():
    slab = lax.axis_index("slab")
    return slab // 2, slab % 2, lax.axis_index("obs")


def add(parts):
    value = parts[0].astype(F32)
    for part in parts[1:]:
        value = value + part.astype(F32)
    return value


def dot(matrix, x):
    high = x.astype(BF16)
    rest = (x - high.astype(F32)).astype(BF16)
    x = jnp.concatenate([high, rest, high], axis=0)
    return jnp.dot(matrix, x, preferred_element_type=F32)


def total(x):
    return jnp.sum(jnp.sum(x, axis=0, keepdims=True), axis=1, keepdims=True)


def with_scalars(body, values):
    rows = lax.broadcasted_iota(jnp.int32, body.shape, 0)
    lanes = lax.broadcasted_iota(jnp.int32, body.shape, 1)
    line = jnp.zeros(body.shape, F32)
    for q, value in enumerate(values):
        rest = value
        for piece in range(PIECES):
            part = rest.astype(BF16).astype(F32)
            rest = rest - part
            line = jnp.where(lanes == q * PIECES + piece, part, line)
    return jnp.where(rows == body.shape[0] - 1, line, body)


def read_scalars(refs, count):
    rows = refs[0].shape[0]
    tail = add([ref[rows - 16 : rows, 0:LANES] for ref in refs])
    sub = lax.broadcasted_iota(jnp.int32, tail.shape, 0)
    lanes = lax.broadcasted_iota(jnp.int32, tail.shape, 1)
    found = []
    for q in range(count):
        mine = (sub == 15) & (lanes >= q * PIECES) & (lanes < (q + 1) * PIECES)
        found.append(total(jnp.where(mine, tail, 0.0)))
    return found


def of_member(refs, spans, m):
    return [
        ref.at[m - first + skip]
        for ref, (first, count, skip) in zip(refs, spans)
        if first <= m < first + count
    ]


def remainder(x, factor):
    return x - (x.astype(F32) * factor).astype(jnp.int32) * PRIME


def start_kernel(
    dims, seeds_in, ids_in, cols_in, count_in, sd_in, innov_in, prec_in, h, own, partner, *rest
):
    chips, halves = dims
    outs = rest[:-12]
    seeds, ids, cols, count, sd, innov, prec, hashed, scratch, acc, sems, h_sems = rest[-12:]
    z, core, obs = place()
    blocks, lev, profiles = innov.shape
    colblocks, width = own.shape[1], own.shape[3]
    members, levp = scratch.shape[1], scratch.shape[2]

    pairs = [(seeds_in, seeds), (ids_in, ids), (cols_in, cols), (count_in, count), (sd_in, sd)]
    small = [pltpu.make_async_copy(x, y, sems.at[i]) for i, (x, y) in enumerate(pairs)]
    for copy in small:
        copy.start()
    large = []
    for b in range(blocks):
        at = len(pairs) + 2 * b
        large.append(pltpu.make_async_copy(innov_in.at[:, b, :], innov.at[b], sems.at[at]))
        large.append(pltpu.make_async_copy(prec_in.at[:, b, :], prec.at[b], sems.at[at + 1]))
    for copy in large:
        copy.start()
    own[...] = jnp.zeros_like(own)
    partner[...] = jnp.zeros_like(partner)
    scratch[...] = jnp.zeros_like(scratch)
    for copy in small:
        copy.wait()

    def tile_copy(n, half, target):
        lanes = pl.ds(half * width, width)
        return pltpu.make_async_copy(h.at[n, :, lanes], target, h_sems.at[n * halves + half])

    def put(n, carry):
        for half in range(halves):
            piece, k = ids[0, 0, n] * halves + half, cols[0, 0, n]

            @pl.when(piece % 2 == core)
            def _():
                tile_copy(n, half, own.at[piece // 2, k]).start()

            @pl.when(piece % 2 != core)
            def _():
                tile_copy(n, half, partner.at[piece // 2, k]).start()

        return carry

    lax.fori_loop(0, count[0, 0], put, 0)

    starts = [lax.rem(seeds[m], PRIME) - PRIME for m in range(members)]
    order = [(source, zz) for source in range(2) for zz in range(chips)]
    shape = (levp, width)
    spot = lax.broadcasted_iota(jnp.int32, shape, 0) * profiles
    spot = spot + lax.broadcasted_iota(jnp.int32, shape, 1)
    low = (1.0 - 2.0**-21) / PRIME

    def piece_at(at):
        source, zz = order[at]
        return 2 * zz + (core if source == 0 else 1 - core)

    def draw(at):
        piece = piece_at(at)
        first = (obs * blocks + piece // halves) * (lev * profiles) + (piece % halves) * width
        base = remainder(7919 * remainder(spot + first, 1.0 / PRIME), 1.0 / PRIME)
        for m in range(members):
            k0 = base + starts[m]
            k1 = remainder(k0 * k0 + 12345, 1.0 / PRIME)
            k2 = remainder(k1 * k1 + 2719, low)
            k2 = jnp.where(k2 >= PRIME, k2 - PRIME, k2)
            hashed[at, m] = k2.astype(F32)

    def adjoint(at):
        source, zz = order[at]
        piece = piece_at(at)
        b = piece // halves
        if halves == 1:
            p, d = prec[b], innov[b]
        else:
            lanes = pl.ds(pl.multiple_of((piece % halves) * width, LANES), width)
            p, d = prec[b, :, lanes], innov[b, :, lanes]
        gain = 3.4 * p * lax.rsqrt(p)
        offset = p * d - 0.5 * gain
        gain = gain * (1.0 / PRIME)
        for m in range(members):
            scratch[at % 2, m, 0:lev, :] = offset + gain * hashed[at, m, 0:lev, :]
        w = scratch[at % 2].astype(BF16).reshape(members * levp, width)
        tiles = (own if source == 0 else partner)[zz].reshape(colblocks * LANES, width)
        part = lax.dot_general(w, tiles, NT, preferred_element_type=F32)
        if at == 0:
            acc[...] = part
        else:
            acc[...] += part

    early = len(order) // 2
    for at in range(early):
        draw(at)
    for copy in large:
        copy.wait()

    def arrive(n, carry):
        for half in range(halves):
            tile_copy(n, half, own.at[0, 0]).wait()
        return carry

    lax.fori_loop(0, count[0, 0], arrive, 0)

    for at in range(len(order)):
        if at + early < len(order):
            draw(at + early)
        adjoint(at)

    for m in range(members):
        value = acc[m * levp : (m + 1) * levp, :]
        if m == 0:
            value = with_columns(value, jnp.concatenate([sd[...]] * colblocks, axis=1), obs)
        put_halves(outs, m, value)


def put_halves(outs, m, value):
    half = value.shape[1] // 2
    for one, two in zip(outs[::2], outs[1::2]):
        if 0 <= m < one.shape[0]:
            one[m] = value[:, :half].astype(BF16)
            two[m] = value[:, half:].astype(BF16)
        m -= one.shape[0]


def with_columns(body, line, obs):
    rows = lax.broadcasted_iota(jnp.int32, body.shape, 0)
    mine = lax.broadcasted_iota(jnp.int32, body.shape, 1) // LANES == obs
    rest = line
    for piece in range(PIECES):
        part = rest.astype(BF16).astype(F32)
        rest = rest - part
        body = jnp.where((rows == body.shape[0] - 1 - PIECES + piece) & mine, part, body)
    return body


def read_columns(body):
    tail = body[body.shape[0] - 8 :]
    sub = lax.broadcasted_iota(jnp.int32, tail.shape, 0)
    mine = (sub >= 7 - PIECES) & (sub < 7)
    return jnp.sum(jnp.where(mine, tail, 0.0), axis=0, keepdims=True)


def precision_kernel(halves, prec, out):
    z, core, unused = place()
    piece = 2 * z + core
    lev, blocks, unused = prec.shape
    width = out.shape[1]
    block = lax.broadcasted_iota(jnp.int32, (lev, blocks, width), 1)
    if halves == 1:
        mine = prec[...]
    else:
        mine = prec[:, :, pl.ds(pl.multiple_of((piece % halves) * width, LANES), width)]
    out[...] = jnp.zeros_like(out)
    out[0:lev, :] = jnp.sum(jnp.where(block == piece // halves, mine, 0.0), axis=1)


def joined(pieces, m):
    for at in range(0, len(pieces), 4):
        one, one_more, two, two_more = pieces[at : at + 4]
        if m < one.shape[0]:
            halves = [add([one[m], one_more[m]]), add([two[m], two_more[m]])]
            return jnp.concatenate(halves, axis=1), [one.at[m], one_more.at[m]]
        m -= one.shape[0]


def first_kernel(parts, *refs):
    pieces = refs[:parts]
    vert, vert_t, sd_out, residual, moved = refs[parts:]
    for m in range(residual.shape[0]):
        t, unused = joined(pieces, m)
        if m == 0:
            sd = read_columns(t)
            sd_out[...] = sd
        r = dot(vert_t[...], sd * t)
        residual[m] = r
        x = sd * dot(vert[...], r)
        moved[m] = with_scalars(x, [total(r * r)]).astype(BF16)


def add_kernel(scalars, *refs):
    parts, out = refs[:-1], refs[-1]
    for m in range(out.shape[0]):
        value = add([x[m] for x in parts])
        if scalars:
            value = with_scalars(value, read_scalars([x.at[m] for x in parts], scalars))
        out[m] = value.astype(BF16)


def add_halves_kernel(scalars, one, one_more, two, two_more, one_out, two_out):
    add_kernel(scalars, one, one_more, one_out)
    add_kernel(0, two, two_more, two_out)


def stage_kernel(*refs):
    sems = refs[-1]
    count = len(refs) // 2
    copies = [
        pltpu.make_async_copy(refs[i], refs[count + i], sems.at[i]) for i in range(count)
    ]
    for copy in copies:
        copy.start()
    for copy in copies:
        copy.wait()


def forward_kernel(sends, x, tiles, *refs):
    z, core, obs = place()
    outs = refs[-len(sends) :]
    members, levp, lanes = x.shape
    width = tiles.shape[3]
    added = refs[1 : 1 + len(sends)] if len(refs) > len(sends) else [None] * len(sends)
    if added[0] is not None:
        scalars = [read_scalars([refs[0].at[m], x.at[m]], 2) for m in range(members)]
    for out, before, (chip, first, count) in zip(outs, added, sends):
        y = jnp.dot(
            x[first : first + count].reshape(count * levp, lanes),
            tiles[z ^ chip].reshape(lanes, width),
            preferred_element_type=F32,
        ).reshape(count, levp, width)
        if before is None:
            out[...] = y
        else:
            for m in range(count):
                value = with_scalars(before[m] + y[m], scalars[first + m])
                out[m] = value.astype(out.dtype)


def weigh_kernel(later, last, n_ys, *refs):
    ys, prec, refs = refs[:n_ys], refs[n_ys], refs[n_ys + 1 :]
    if later:
        (old_image, old), refs = refs[:2], refs[2:]
    weighted, state = refs[:2]
    p = prec[...]
    for m in range(state.shape[0]):
        mine = [y.at[m] for y in ys]
        y = add([x[...] for x in mine])
        norm, cross = read_scalars(mine, 2)
        if later:
            old_norm, old_square = old[m, 0:1, 0:1], old[m, 1:2, 0:1]
            beta = norm / old_norm
            square = norm + 2.0 * beta * cross + beta * beta * old_square
            y = y + beta * old_image[m]
        else:
            beta = jnp.zeros_like(norm)
            square = norm
        scaled = p * y
        if not last:
            refs[2][m] = y
        weighted[m] = with_scalars(scaled, [total(scaled * y)]).astype(BF16)
        sub = lax.broadcasted_iota(jnp.int32, (8, LANES), 0)
        state[m] = jnp.where(sub == 0, norm, jnp.where(sub == 1, square, beta))


def adjoint_kernel(plan, *refs):
    z, core, obs = place()
    ws, tiles, out = refs[: len(plan)], refs[len(plan)], refs[len(plan) + 1]
    members, levp, lanes = out.shape
    width = ws[0].shape[2]
    acc = None
    for i in range(tiles.shape[0]):
        w = {span[0]: ref for ref, (chip, *span) in zip(ws, plan) if chip == i}
        w = [w[first][...].reshape(-1, width) for first in sorted(w)]
        w = w[0] if len(w) == 1 else jnp.concatenate(w, axis=0)
        part = lax.dot_general(
            w, tiles[z ^ i].reshape(lanes, width), NT, preferred_element_type=F32
        )
        acc = part if i == 0 else acc + part
    acc = acc.reshape(members, levp, lanes)
    spans = [(*span, 0) for chip, *span in plan]
    for m in range(members):
        energy = read_scalars(of_member(ws, spans, m), 1)
        out[m] = with_scalars(acc[m], energy).astype(out.dtype)


def combine_kernel(mine, theirs, *outs):
    for m in range(mine.shape[0]):
        energy = read_scalars([mine.at[m], theirs.at[m]], 1)
        put_halves(outs, m, with_scalars(mine[m] + theirs[m].astype(F32), energy))


def combine_columns_kernel(mine, theirs, *outs):
    obs = lax.axis_index("obs")
    for m in range(mine.shape[0]):
        energy = read_scalars([mine.at[m], theirs.at[m]], 1)
        for i, out in enumerate(outs):
            lane = pl.ds(pl.multiple_of((obs ^ i) * LANES, LANES), LANES)
            value = mine[m, :, lane] + theirs[m, :, lane].astype(F32)
            out[m] = with_scalars(value, energy).astype(BF16)


def update_kernel(parts, later, parts_of, *refs):
    pieces, refs = refs[:parts], refs[parts:]
    n_states = len(parts_of)
    sd, vert, vert_t, *states, residual = refs[: 4 + n_states]
    refs = refs[n_states - 1 :]
    if later:
        old_direction, old_solution, residual_out, solution_out, moved, direction_out = refs[5:]
    else:
        residual_out, solution_out, moved = refs[5:]
    obs = lax.axis_index("obs")
    mine = pl.ds(pl.multiple_of(obs * LANES, LANES), LANES)
    for m in range(residual.shape[0]):
        t, places = joined(pieces, m)
        (energy,) = read_scalars(places, 1)
        state = of_member(states, parts_of, m)[0]
        norm, square, beta = state[0:1, 0:1], state[1:2, 0:1], state[2:3, 0:1]
        alpha = norm / (square + energy)
        r = residual[m]
        if later:
            d = r + beta * old_direction[m]
            direction_out[m] = d
            step = direction_out[m, :, mine]
            solution_out[m] = old_solution[m] + alpha * step
        else:
            d = r
            solution_out[m] = alpha * residual[m, :, mine]
        r = r - alpha * (d + dot(vert_t[...], sd[...] * t))
        residual_out[m] = r
        x = sd[...] * dot(vert[...], r)
        moved[m] = with_scalars(x, [total(r * r), total(r * d)]).astype(BF16)


def last_kernel(parts, later, lev, parts_of, *refs):
    pieces, refs = refs[:parts], refs[parts:]
    n_states = len(parts_of)
    sd, vert, vert_t, *states, residual = refs[: 4 + n_states]
    refs = refs[n_states - 1 :]
    increment_out, residual_out = refs[-2:]
    obs = lax.axis_index("obs")
    mine = pl.ds(pl.multiple_of(obs * LANES, LANES), LANES)
    for m in range(residual.shape[0]):
        t = add([x[m] for x in pieces])
        (energy,) = read_scalars([x.at[m] for x in pieces], 1)
        state = of_member(states, parts_of, m)[0]
        norm, square, beta = state[0:1, 0:1], state[1:2, 0:1], state[2:3, 0:1]
        alpha = norm / (square + energy)
        d = r = residual[m, :, mine]
        if later:
            old_direction, old_solution = refs[5:7]
            d = r + beta * old_direction[m, :, mine]
        solution = alpha * d
        if later:
            solution = old_solution[m] + solution
        r = r - alpha * (d + dot(vert_t[...], sd[...] * t))
        increment = sd[...] * dot(vert[...], solution)
        increment_out[:, m, :] = increment[0:lev]
        residual_out[:, m, :] = r[0:lev]


def per_device(
    n_slab,
    n_obs,
    innovation,
    obs_precision,
    seeds,
    col_sd,
    vert_factor,
    h_values,
    block_obs,
    block_col,
    entry_count,
):
    blocks, lev, profiles = innovation.shape
    members = seeds.shape[0]
    chips = n_slab // 2
    halves = n_slab // blocks
    width = profiles // halves
    colblocks = n_obs
    assert halves * blocks == n_slab and width % LANES == 0 and col_sd.shape[0] == 1
    assert chips & (chips - 1) == 0 and n_obs & (n_obs - 1) == 0
    levp = (lev + 1 + 15) // 16 * 16
    rows = members * levp
    lanes = colblocks * LANES
    field = (members, levp, LANES)
    slab_field = (members, levp, lanes)
    panel = (members, levp, width)
    some, rest = members // 4, members - members // 4
    half_fields = [struct((members, levp, lanes // 2), BF16)] * 2
    via = chips == 4 and some > 0
    if via:
        one, two = (0, some), (some, rest)
        parts_of = [(*one, 0), (*two, 0)]
        plan = [(i, *two) for i in range(chips)] + [(i, *one) for i in range(chips)]
        sends = [(3, *one), (2, *two), (3, *two), (1, *two), (0, *two), (1, *one), (0, *one), (2, *one)]
    else:
        parts_of = [(0, members, 0)]
        sends = plan = [(i, 0, members) for i in range(chips)]
    pad = ((0, levp - lev), (0, levp - lev))
    high = lax.reduce_precision(vert_factor, 8, 7)
    low = vert_factor - high
    vert, vert_t = [
        jnp.concatenate([jnp.pad(x, pad).astype(BF16) for x in parts], axis=1)
        for parts in ((high, high, low), (high.T, high.T, low.T))
    ]
    h_block = h_values.reshape(h_values.shape[2:])
    innovation = jnp.transpose(innovation, (1, 0, 2))
    obs_precision = jnp.transpose(obs_precision, (1, 0, 2))
    product = n_slab * width * lanes * rows
    small = 12 * rows * levp * LANES
    plane_bits = [1 << k for k in range(n_obs.bit_length() - 1)]

    def along(x, i):
        return lax.ppermute(x, "slab", [(s, s ^ (2 * i)) for s in range(n_slab)])

    def plane(x, i):
        return lax.ppermute(x, "obs", [(o, o ^ i) for o in range(n_obs)])

    def swap(x):
        return lax.ppermute(x, "slab", [(s, s ^ 1) for s in range(n_slab)])

    def plane_sum(halves, staged):
        halves = list(halves)
        moved_halves = [None] * len(halves)
        for step, bit in enumerate(plane_bits):
            bits = [bit, plane_bits[len(plane_bits) - 1 - step]]
            for at in range(0, len(halves), 2):
                if step > 0:
                    one, two = halves[at : at + 2]
                    one_more, two_more = moved_halves[at : at + 2]
                    halves[at : at + 2] = call(
                        functools.partial(add_halves_kernel, 0 if staged else 1),
                        [struct(one.shape, BF16)] * 2,
                        [],
                        0,
                        one,
                        one_more,
                        two,
                        two_more,
                    )
                for half in range(2):
                    moved_halves[at + half] = plane(halves[at + half], bits[half])
            if step == 0 and staged:
                halves[:] = call(
                    stage_kernel,
                    [struct(x.shape, BF16) for x in halves],
                    [pltpu.SemaphoreType.DMA((len(halves),))],
                    0,
                    *halves,
                    space=HBM,
                )
        return [x for pair in zip(halves, moved_halves) for x in pair]

    def line_sum(moved, other):
        shapes = [(count, levp, width) for i, unused, count in sends]
        mine = call(
            functools.partial(forward_kernel, sends),
            [struct(shape, F32) for shape in shapes],
            [],
            product,
            moved,
            own,
        )
        ys = call(
            functools.partial(forward_kernel, sends),
            [
                struct(shape, F32 if i == 0 or (via and at == 7) else BF16)
                for at, ((i, *unused), shape) in enumerate(zip(sends, shapes))
            ],
            [],
            product,
            other,
            partner,
            moved,
            *mine,
        )
        if not via:
            return [[y if i == 0 else along(y, i) for i, y in enumerate(ys)]]
        passed, far_rest, last_rest, next_rest, near_rest, next_some, near_some, far = ys
        passed = along(passed, 1)
        rest_ys = [near_rest, along(far_rest, 2), along(last_rest, 3), along(next_rest, 1)]
        next_some = along(next_some, 1)
        (far,) = call(
            functools.partial(add_kernel, 2),
            [struct((some, levp, width), BF16)],
            [],
            0,
            far,
            passed,
        )
        return [[near_some, next_some, along(far, 2)], rest_ys]

    def line_gather(*parts):
        if not via:
            return [parts[0] if i == 0 else along(parts[0], i) for i in range(chips)]
        one, two = parts
        far = along(one, 2)
        return [two, *(along(two, i) for i in (1, 2, 3)), one, along(one, 1), far, along(far, 1)]

    dense = struct((chips, colblocks, LANES, width), BF16)
    own, for_partner, *partials = call(
        functools.partial(start_kernel, (chips, halves)),
        [dense, dense] + half_fields,
        [
            pltpu.SMEM(seeds.shape, jnp.int32),
            pltpu.SMEM(block_obs.shape, jnp.int32),
            pltpu.SMEM(block_col.shape, jnp.int32),
            pltpu.SMEM(entry_count.shape, jnp.int32),
            pltpu.VMEM(col_sd.shape, F32),
            pltpu.VMEM((blocks, lev, profiles), F32),
            pltpu.VMEM((blocks, lev, profiles), F32),
            pltpu.VMEM((n_slab, members, levp, width), F32),
            pltpu.VMEM((2, members, levp, width), F32),
            pltpu.VMEM((rows, lanes), F32),
            pltpu.SemaphoreType.DMA((5 + 2 * blocks,)),
            pltpu.SemaphoreType.DMA((h_block.shape[0] * halves,)),
        ],
        2 * product,
        seeds,
        block_obs,
        block_col,
        entry_count,
        col_sd,
        innovation,
        obs_precision,
        h_block,
        space=HBM,
        limit=60,
    )
    ps = plane_sum(partials, True)
    partner = swap(for_partner)
    (precision,) = call(
        functools.partial(precision_kernel, halves),
        [struct((levp, width), F32)],
        [],
        0,
        obs_precision,
    )
    slab_sd, residual, moved = call(
        functools.partial(first_kernel, len(ps)),
        [struct((1, lanes), F32), struct(slab_field, F32), struct(slab_field, BF16)],
        [],
        small * colblocks,
        *ps,
        vert,
        vert_t,
    )
    direction = total_step = None
    image, state = [None] * len(parts_of), [None] * len(parts_of)
    for sweep in range(ITERS):
        later, last = sweep > 0, sweep == ITERS - 1
        weighted = []
        for part, ys in reversed(list(enumerate(line_sum(moved, swap(moved))))):
            count = parts_of[part][1]
            shape = (count, levp, width)
            w, state[part], *y = call(
                functools.partial(weigh_kernel, later, last, len(ys)),
                [struct(shape, BF16), struct((count, 8, LANES), F32)]
                + ([] if last else [struct(shape, F32)]),
                [],
                0,
                *ys,
                precision,
                *([image[part], state[part]] if later else []),
            )
            weighted.insert(0, w)
            image[part] = None if last else y[0]
        ws = line_gather(*weighted)
        (theirs,) = call(
            functools.partial(adjoint_kernel, plan),
            [struct(slab_field, BF16)],
            [],
            product,
            *ws,
            partner,
        )
        theirs = swap(theirs)
        (mine,) = call(
            functools.partial(adjoint_kernel, plan),
            [struct(slab_field, F32)],
            [],
            product,
            *ws,
            own,
        )
        known = [vert, vert_t, *state, residual]
        if later:
            known += [direction, total_step]
        if last:
            ps = call(
                combine_columns_kernel, [struct(field, BF16)] * n_obs, [], 0, mine, theirs
            )
            ps = [ps[0]] + [plane(ps[i], i) for i in reversed(range(1, n_obs))]
            outputs = call(
                functools.partial(last_kernel, len(ps), later, lev, parts_of),
                [struct((lev, members, LANES), F32)] * 2,
                [],
                small,
                *ps,
                col_sd,
                *known,
            )
            break
        ps = call(combine_kernel, half_fields, [], 0, mine, theirs)
        ps = plane_sum(ps, False)
        outs = [struct(slab_field, F32), struct(field, F32), struct(slab_field, BF16)]
        if later:
            outs.append(struct(slab_field, F32))
        r, total_step, moved, *d = call(
            functools.partial(update_kernel, len(ps), later, parts_of),
            outs,
            [],
            small * colblocks,
            *ps,
            slab_sd,
            *known,
        )
        direction, residual = (d[0] if later else residual), r
    return tuple(jnp.transpose(x, (1, 0, 2))[None] for x in outputs)


def solution(mesh):
    return jax.shard_map(
        functools.partial(per_device, mesh.shape["slab"], mesh.shape["obs"]),
        mesh=mesh,
        in_specs=(
            P("obs", None, None),
            P("obs", None, None),
            P(),
            P(("slab", "obs"), None),
            P(),
            P("slab", "obs", None, None, None),
            P("slab", "obs", None),
            P("slab", "obs", None),
            P("slab", "obs"),
        ),
        out_specs=(P(("slab", "obs"), None, None, None), P(("slab", "obs"), None, None, None)),
        check_vma=False,
    )
```

```python
import functools

import jax
import jax.numpy as jnp
from jax import lax
from jax.experimental import pallas as pl
from jax.experimental.pallas import tpu as pltpu
from jax.sharding import PartitionSpec as P

ITERS = 2
LANES = 128
PIECES = 3
PRIME = 32749
VMEM = pl.BlockSpec(memory_space=pltpu.VMEM)
HBM = pl.BlockSpec(memory_space=pltpu.HBM)
F32 = jnp.float32
BF16 = jnp.bfloat16
NT = (((1,), (1,)), ((), ()))


def call(kernel, outs, scratch, flops, *args, space=VMEM, limit=24):
    nbytes = sum(a.size * a.dtype.itemsize for a in (*args, *outs))
    return pl.pallas_call(
        kernel,
        out_shape=outs,
        in_specs=[space] * len(args),
        out_specs=[VMEM] * len(outs),
        scratch_shapes=scratch,
        compiler_params=pltpu.CompilerParams(vmem_limit_bytes=limit * 1024 * 1024),
        cost_estimate=pl.CostEstimate(flops=flops, bytes_accessed=nbytes, transcendentals=0),
    )(*args)


def struct(shape, dtype):
    return jax.ShapeDtypeStruct(shape, dtype)


def place():
    slab = lax.axis_index("slab")
    return slab // 2, slab % 2, lax.axis_index("obs")


def add(parts):
    value = parts[0].astype(F32)
    for part in parts[1:]:
        value = value + part.astype(F32)
    return value


def dot(matrix, x):
    high = x.astype(BF16)
    rest = (x - high.astype(F32)).astype(BF16)
    x = jnp.concatenate([high, rest, high], axis=0)
    return jnp.dot(matrix, x, preferred_element_type=F32)


def total(x):
    return jnp.sum(jnp.sum(x, axis=0, keepdims=True), axis=1, keepdims=True)


def with_scalars(body, values):
    rows = lax.broadcasted_iota(jnp.int32, body.shape, 0)
    lanes = lax.broadcasted_iota(jnp.int32, body.shape, 1)
    line = jnp.zeros(body.shape, F32)
    for q, value in enumerate(values):
        rest = value
        for piece in range(PIECES):
            part = rest.astype(BF16).astype(F32)
            rest = rest - part
            line = jnp.where(lanes == q * PIECES + piece, part, line)
    return jnp.where(rows == body.shape[0] - 1, line, body)


def read_scalars(refs, count):
    rows = refs[0].shape[0]
    tail = add([ref[rows - 16 : rows, 0:LANES] for ref in refs])
    sub = lax.broadcasted_iota(jnp.int32, tail.shape, 0)
    lanes = lax.broadcasted_iota(jnp.int32, tail.shape, 1)
    found = []
    for q in range(count):
        mine = (sub == 15) & (lanes >= q * PIECES) & (lanes < (q + 1) * PIECES)
        found.append(total(jnp.where(mine, tail, 0.0)))
    return found


def of_member(refs, spans, m):
    return [
        ref.at[m - first + skip]
        for ref, (first, count, skip) in zip(refs, spans)
        if first <= m < first + count
    ]


def remainder(x, factor):
    return x - (x.astype(F32) * factor).astype(jnp.int32) * PRIME


def start_kernel(
    dims, seeds_in, ids_in, cols_in, count_in, sd_in, innov_in, prec_in, h, own, partner, *rest
):
    chips, halves = dims
    outs = rest[:-12]
    seeds, ids, cols, count, sd, innov, prec, hashed, scratch, acc, sems, h_sems = rest[-12:]
    z, core, obs = place()
    blocks, lev, profiles = innov.shape
    colblocks, width = own.shape[1], own.shape[3]
    members, levp = scratch.shape[1], scratch.shape[2]

    pairs = [(seeds_in, seeds), (ids_in, ids), (cols_in, cols), (count_in, count), (sd_in, sd)]
    small = [pltpu.make_async_copy(x, y, sems.at[i]) for i, (x, y) in enumerate(pairs)]
    for copy in small:
        copy.start()
    large = []
    for b in range(blocks):
        at = len(pairs) + 2 * b
        large.append(pltpu.make_async_copy(innov_in.at[:, b, :], innov.at[b], sems.at[at]))
        large.append(pltpu.make_async_copy(prec_in.at[:, b, :], prec.at[b], sems.at[at + 1]))
    for copy in large:
        copy.start()
    own[...] = jnp.zeros_like(own)
    partner[...] = jnp.zeros_like(partner)
    scratch[...] = jnp.zeros_like(scratch)
    for copy in small:
        copy.wait()

    def tile_copy(n, half, target):
        lanes = pl.ds(half * width, width)
        return pltpu.make_async_copy(h.at[n, :, lanes], target, h_sems.at[n * halves + half])

    def put(n, carry):
        for half in range(halves):
            piece, k = ids[0, 0, n] * halves + half, cols[0, 0, n]

            @pl.when(piece % 2 == core)
            def _():
                tile_copy(n, half, own.at[piece // 2, k]).start()

            @pl.when(piece % 2 != core)
            def _():
                tile_copy(n, half, partner.at[piece // 2, k]).start()

        return carry

    lax.fori_loop(0, count[0, 0], put, 0)

    starts = [lax.rem(seeds[m], PRIME) - PRIME for m in range(members)]
    order = [(source, zz) for source in range(2) for zz in range(chips)]
    shape = (levp, width)
    spot = lax.broadcasted_iota(jnp.int32, shape, 0) * profiles
    spot = spot + lax.broadcasted_iota(jnp.int32, shape, 1)
    low = (1.0 - 2.0**-21) / PRIME

    def piece_at(at):
        source, zz = order[at]
        return 2 * zz + (core if source == 0 else 1 - core)

    def draw(at):
        piece = piece_at(at)
        first = (obs * blocks + piece // halves) * (lev * profiles) + (piece % halves) * width
        base = remainder(7919 * remainder(spot + first, 1.0 / PRIME), 1.0 / PRIME)
        for m in range(members):
            k0 = base + starts[m]
            k1 = remainder(k0 * k0 + 12345, 1.0 / PRIME)
            k2 = remainder(k1 * k1 + 2719, low)
            k2 = jnp.where(k2 >= PRIME, k2 - PRIME, k2)
            hashed[at, m] = k2.astype(F32)

    def adjoint(at):
        source, zz = order[at]
        piece = piece_at(at)
        b = piece // halves
        if halves == 1:
            p, d = prec[b], innov[b]
        else:
            lanes = pl.ds(pl.multiple_of((piece % halves) * width, LANES), width)
            p, d = prec[b, :, lanes], innov[b, :, lanes]
        gain = 3.4 * p * lax.rsqrt(p)
        offset = p * d - 0.5 * gain
        gain = gain * (1.0 / PRIME)
        for m in range(members):
            scratch[at % 2, m, 0:lev, :] = offset + gain * hashed[at, m, 0:lev, :]
        w = scratch[at % 2].astype(BF16).reshape(members * levp, width)
        tiles = (own if source == 0 else partner)[zz].reshape(colblocks * LANES, width)
        part = lax.dot_general(w, tiles, NT, preferred_element_type=F32)
        if at == 0:
            acc[...] = part
        else:
            acc[...] += part

    early = len(order) // 2
    for at in range(early):
        draw(at)
    for copy in large:
        copy.wait()

    def arrive(n, carry):
        for half in range(halves):
            tile_copy(n, half, own.at[0, 0]).wait()
        return carry

    lax.fori_loop(0, count[0, 0], arrive, 0)

    for at in range(len(order)):
        if at + early < len(order):
            draw(at + early)
        adjoint(at)

    for m in range(members):
        value = acc[m * levp : (m + 1) * levp, :]
        if m == 0:
            value = with_columns(value, jnp.concatenate([sd[...]] * colblocks, axis=1), obs)
        put_halves(outs, m, value)


def put_halves(outs, m, value):
    half = value.shape[1] // 2
    for one, two in zip(outs[::2], outs[1::2]):
        if 0 <= m < one.shape[0]:
            one[m] = value[:, :half].astype(BF16)
            two[m] = value[:, half:].astype(BF16)
        m -= one.shape[0]


def with_columns(body, line, obs):
    rows = lax.broadcasted_iota(jnp.int32, body.shape, 0)
    mine = lax.broadcasted_iota(jnp.int32, body.shape, 1) // LANES == obs
    rest = line
    for piece in range(PIECES):
        part = rest.astype(BF16).astype(F32)
        rest = rest - part
        body = jnp.where((rows == body.shape[0] - 1 - PIECES + piece) & mine, part, body)
    return body


def read_columns(body):
    tail = body[body.shape[0] - 8 :]
    sub = lax.broadcasted_iota(jnp.int32, tail.shape, 0)
    mine = (sub >= 7 - PIECES) & (sub < 7)
    return jnp.sum(jnp.where(mine, tail, 0.0), axis=0, keepdims=True)


def precision_kernel(halves, prec, out):
    z, core, unused = place()
    piece = 2 * z + core
    lev, blocks, unused = prec.shape
    width = out.shape[1]
    block = lax.broadcasted_iota(jnp.int32, (lev, blocks, width), 1)
    if halves == 1:
        mine = prec[...]
    else:
        mine = prec[:, :, pl.ds(pl.multiple_of((piece % halves) * width, LANES), width)]
    out[...] = jnp.zeros_like(out)
    out[0:lev, :] = jnp.sum(jnp.where(block == piece // halves, mine, 0.0), axis=1)


def joined(pieces, m):
    for at in range(0, len(pieces), 4):
        one, one_more, two, two_more = pieces[at : at + 4]
        if m < one.shape[0]:
            halves = [add([one[m], one_more[m]]), add([two[m], two_more[m]])]
            return jnp.concatenate(halves, axis=1), [one.at[m], one_more.at[m]]
        m -= one.shape[0]


def first_kernel(parts, *refs):
    pieces = refs[:parts]
    vert, vert_t, sd_out, residual, moved = refs[parts:]
    for m in range(residual.shape[0]):
        t, unused = joined(pieces, m)
        if m == 0:
            sd = read_columns(t)
            sd_out[...] = sd
        r = dot(vert_t[...], sd * t)
        residual[m] = r
        x = sd * dot(vert[...], r)
        moved[m] = with_scalars(x, [total(r * r)]).astype(BF16)


def add_kernel(scalars, *refs):
    parts, out = refs[:-1], refs[-1]
    for m in range(out.shape[0]):
        value = add([x[m] for x in parts])
        if scalars:
            value = with_scalars(value, read_scalars([x.at[m] for x in parts], scalars))
        out[m] = value.astype(BF16)


def add_halves_kernel(scalars, one, one_more, two, two_more, one_out, two_out):
    add_kernel(scalars, one, one_more, one_out)
    add_kernel(0, two, two_more, two_out)


def stage_kernel(*refs):
    sems = refs[-1]
    count = len(refs) // 2
    copies = [
        pltpu.make_async_copy(refs[i], refs[count + i], sems.at[i]) for i in range(count)
    ]
    for copy in copies:
        copy.start()
    for copy in copies:
        copy.wait()


def forward_kernel(sends, x, tiles, *refs):
    z, core, obs = place()
    outs = refs[-len(sends) :]
    members, levp, lanes = x.shape
    width = tiles.shape[3]
    added = refs[1 : 1 + len(sends)] if len(refs) > len(sends) else [None] * len(sends)
    if added[0] is not None:
        scalars = [read_scalars([refs[0].at[m], x.at[m]], 2) for m in range(members)]
    for out, before, (chip, first, count) in zip(outs, added, sends):
        y = jnp.dot(
            x[first : first + count].reshape(count * levp, lanes),
            tiles[z ^ chip].reshape(lanes, width),
            preferred_element_type=F32,
        ).reshape(count, levp, width)
        if before is None:
            out[...] = y
        else:
            for m in range(count):
                value = with_scalars(before[m] + y[m], scalars[first + m])
                out[m] = value.astype(out.dtype)


def weigh_kernel(later, last, n_ys, *refs):
    ys, prec, refs = refs[:n_ys], refs[n_ys], refs[n_ys + 1 :]
    if later:
        (old_image, old), refs = refs[:2], refs[2:]
    weighted, state = refs[:2]
    p = prec[...]
    for m in range(state.shape[0]):
        mine = [y.at[m] for y in ys]
        y = add([x[...] for x in mine])
        norm, cross = read_scalars(mine, 2)
        if later:
            old_norm, old_square = old[m, 0:1, 0:1], old[m, 1:2, 0:1]
            beta = norm / old_norm
            square = norm + 2.0 * beta * cross + beta * beta * old_square
            y = y + beta * old_image[m]
        else:
            beta = jnp.zeros_like(norm)
            square = norm
        scaled = p * y
        if not last:
            refs[2][m] = y
        weighted[m] = with_scalars(scaled, [total(scaled * y)]).astype(BF16)
        sub = lax.broadcasted_iota(jnp.int32, (8, LANES), 0)
        state[m] = jnp.where(sub == 0, norm, jnp.where(sub == 1, square, beta))


def adjoint_kernel(plan, *refs):
    z, core, obs = place()
    ws, tiles, out = refs[: len(plan)], refs[len(plan)], refs[len(plan) + 1]
    members, levp, lanes = out.shape
    width = ws[0].shape[2]
    acc = None
    for i in range(tiles.shape[0]):
        w = {span[0]: ref for ref, (chip, *span) in zip(ws, plan) if chip == i}
        w = [w[first][...].reshape(-1, width) for first in sorted(w)]
        w = w[0] if len(w) == 1 else jnp.concatenate(w, axis=0)
        part = lax.dot_general(
            w, tiles[z ^ i].reshape(lanes, width), NT, preferred_element_type=F32
        )
        acc = part if i == 0 else acc + part
    acc = acc.reshape(members, levp, lanes)
    spans = [(*span, 0) for chip, *span in plan]
    for m in range(members):
        energy = read_scalars(of_member(ws, spans, m), 1)
        out[m] = with_scalars(acc[m], energy).astype(out.dtype)


def combine_kernel(mine, theirs, *outs):
    for m in range(mine.shape[0]):
        energy = read_scalars([mine.at[m], theirs.at[m]], 1)
        put_halves(outs, m, with_scalars(mine[m] + theirs[m].astype(F32), energy))


def combine_columns_kernel(mine, theirs, *outs):
    obs = lax.axis_index("obs")
    for m in range(mine.shape[0]):
        energy = read_scalars([mine.at[m], theirs.at[m]], 1)
        for i, out in enumerate(outs):
            lane = pl.ds(pl.multiple_of((obs ^ i) * LANES, LANES), LANES)
            value = mine[m, :, lane] + theirs[m, :, lane].astype(F32)
            out[m] = with_scalars(value, energy).astype(BF16)


def update_kernel(parts, later, parts_of, *refs):
    pieces, refs = refs[:parts], refs[parts:]
    n_states = len(parts_of)
    sd, vert, vert_t, *states, residual = refs[: 4 + n_states]
    refs = refs[n_states - 1 :]
    if later:
        old_direction, old_solution, residual_out, solution_out, moved, direction_out = refs[5:]
    else:
        residual_out, solution_out, moved = refs[5:]
    obs = lax.axis_index("obs")
    mine = pl.ds(pl.multiple_of(obs * LANES, LANES), LANES)
    for m in range(residual.shape[0]):
        t, places = joined(pieces, m)
        (energy,) = read_scalars(places, 1)
        state = of_member(states, parts_of, m)[0]
        norm, square, beta = state[0:1, 0:1], state[1:2, 0:1], state[2:3, 0:1]
        alpha = norm / (square + energy)
        r = residual[m]
        if later:
            d = r + beta * old_direction[m]
            direction_out[m] = d
            step = direction_out[m, :, mine]
            solution_out[m] = old_solution[m] + alpha * step
        else:
            d = r
            solution_out[m] = alpha * residual[m, :, mine]
        r = r - alpha * (d + dot(vert_t[...], sd[...] * t))
        residual_out[m] = r
        x = sd[...] * dot(vert[...], r)
        moved[m] = with_scalars(x, [total(r * r), total(r * d)]).astype(BF16)


def last_kernel(parts, later, lev, parts_of, *refs):
    pieces, refs = refs[:parts], refs[parts:]
    n_states = len(parts_of)
    sd, vert, vert_t, *states, residual = refs[: 4 + n_states]
    refs = refs[n_states - 1 :]
    increment_out, residual_out = refs[-2:]
    obs = lax.axis_index("obs")
    mine = pl.ds(pl.multiple_of(obs * LANES, LANES), LANES)
    for m in range(residual.shape[0]):
        t = add([x[m] for x in pieces])
        (energy,) = read_scalars([x.at[m] for x in pieces], 1)
        state = of_member(states, parts_of, m)[0]
        norm, square, beta = state[0:1, 0:1], state[1:2, 0:1], state[2:3, 0:1]
        alpha = norm / (square + energy)
        d = r = residual[m, :, mine]
        if later:
            old_direction, old_solution = refs[5:7]
            d = r + beta * old_direction[m, :, mine]
        solution = alpha * d
        if later:
            solution = old_solution[m] + solution
        r = r - alpha * (d + dot(vert_t[...], sd[...] * t))
        increment = sd[...] * dot(vert[...], solution)
        increment_out[:, m, :] = increment[0:lev]
        residual_out[:, m, :] = r[0:lev]


def per_device(
    n_slab,
    n_obs,
    innovation,
    obs_precision,
    seeds,
    col_sd,
    vert_factor,
    h_values,
    block_obs,
    block_col,
    entry_count,
):
    blocks, lev, profiles = innovation.shape
    members = seeds.shape[0]
    chips = n_slab // 2
    halves = n_slab // blocks
    width = profiles // halves
    colblocks = n_obs
    assert halves * blocks == n_slab and width % LANES == 0 and col_sd.shape[0] == 1
    assert chips & (chips - 1) == 0 and n_obs & (n_obs - 1) == 0
    levp = (lev + 1 + 15) // 16 * 16
    rows = members * levp
    lanes = colblocks * LANES
    field = (members, levp, LANES)
    slab_field = (members, levp, lanes)
    panel = (members, levp, width)
    some, rest = members // 2, members - members // 2
    half_fields = [struct((members, levp, lanes // 2), BF16)] * 2
    via = chips == 4 and some > 0
    if via:
        one, two = (0, some), (some, rest)
        parts_of = [(*one, 0), (*two, 0)]
        plan = [(i, *two) for i in range(chips)] + [(i, *one) for i in range(chips)]
        sends = [(3, *one), (2, *two), (3, *two), (1, *two), (0, *two), (1, *one), (0, *one), (2, *one)]
    else:
        parts_of = [(0, members, 0)]
        sends = plan = [(i, 0, members) for i in range(chips)]
    pad = ((0, levp - lev), (0, levp - lev))
    high = lax.reduce_precision(vert_factor, 8, 7)
    low = vert_factor - high
    vert, vert_t = [
        jnp.concatenate([jnp.pad(x, pad).astype(BF16) for x in parts], axis=1)
        for parts in ((high, high, low), (high.T, high.T, low.T))
    ]
    h_block = h_values.reshape(h_values.shape[2:])
    innovation = jnp.transpose(innovation, (1, 0, 2))
    obs_precision = jnp.transpose(obs_precision, (1, 0, 2))
    product = n_slab * width * lanes * rows
    small = 12 * rows * levp * LANES
    plane_bits = [1 << k for k in range(n_obs.bit_length() - 1)]

    def along(x, i):
        return lax.ppermute(x, "slab", [(s, s ^ (2 * i)) for s in range(n_slab)])

    def plane(x, i):
        return lax.ppermute(x, "obs", [(o, o ^ i) for o in range(n_obs)])

    def swap(x):
        return lax.ppermute(x, "slab", [(s, s ^ 1) for s in range(n_slab)])

    def plane_sum(halves, staged):
        halves = list(halves)
        moved_halves = [None] * len(halves)
        for step, bit in enumerate(plane_bits):
            bits = [bit, plane_bits[len(plane_bits) - 1 - step]]
            for at in range(0, len(halves), 2):
                if step > 0:
                    one, two = halves[at : at + 2]
                    one_more, two_more = moved_halves[at : at + 2]
                    halves[at : at + 2] = call(
                        functools.partial(add_halves_kernel, 0 if staged else 1),
                        [struct(one.shape, BF16)] * 2,
                        [],
                        0,
                        one,
                        one_more,
                        two,
                        two_more,
                    )
                for half in range(2):
                    moved_halves[at + half] = plane(halves[at + half], bits[half])
            if step == 0 and staged:
                halves[:] = call(
                    stage_kernel,
                    [struct(x.shape, BF16) for x in halves],
                    [pltpu.SemaphoreType.DMA((len(halves),))],
                    0,
                    *halves,
                    space=HBM,
                )
        return [x for pair in zip(halves, moved_halves) for x in pair]

    def line_sum(moved, other):
        shapes = [(count, levp, width) for i, unused, count in sends]
        mine = call(
            functools.partial(forward_kernel, sends),
            [struct(shape, F32) for shape in shapes],
            [],
            product,
            moved,
            own,
        )
        ys = call(
            functools.partial(forward_kernel, sends),
            [
                struct(shape, F32 if i == 0 or (via and at == 7) else BF16)
                for at, ((i, *unused), shape) in enumerate(zip(sends, shapes))
            ],
            [],
            product,
            other,
            partner,
            moved,
            *mine,
        )
        if not via:
            return [[y if i == 0 else along(y, i) for i, y in enumerate(ys)]]
        passed, far_rest, last_rest, next_rest, near_rest, next_some, near_some, far = ys
        passed = along(passed, 1)
        rest_ys = [near_rest, along(far_rest, 2), along(last_rest, 3), along(next_rest, 1)]
        next_some = along(next_some, 1)
        (far,) = call(
            functools.partial(add_kernel, 2),
            [struct((some, levp, width), BF16)],
            [],
            0,
            far,
            passed,
        )
        return [[near_some, next_some, along(far, 2)], rest_ys]

    def line_gather(*parts):
        if not via:
            return [parts[0] if i == 0 else along(parts[0], i) for i in range(chips)]
        one, two = parts
        far = along(one, 2)
        return [two, *(along(two, i) for i in (1, 2, 3)), one, along(one, 1), far, along(far, 1)]

    dense = struct((chips, colblocks, LANES, width), BF16)
    own, for_partner, *partials = call(
        functools.partial(start_kernel, (chips, halves)),
        [dense, dense] + half_fields,
        [
            pltpu.SMEM(seeds.shape, jnp.int32),
            pltpu.SMEM(block_obs.shape, jnp.int32),
            pltpu.SMEM(block_col.shape, jnp.int32),
            pltpu.SMEM(entry_count.shape, jnp.int32),
            pltpu.VMEM(col_sd.shape, F32),
            pltpu.VMEM((blocks, lev, profiles), F32),
            pltpu.VMEM((blocks, lev, profiles), F32),
            pltpu.VMEM((n_slab, members, levp, width), F32),
            pltpu.VMEM((2, members, levp, width), F32),
            pltpu.VMEM((rows, lanes), F32),
            pltpu.SemaphoreType.DMA((5 + 2 * blocks,)),
            pltpu.SemaphoreType.DMA((h_block.shape[0] * halves,)),
        ],
        2 * product,
        seeds,
        block_obs,
        block_col,
        entry_count,
        col_sd,
        innovation,
        obs_precision,
        h_block,
        space=HBM,
        limit=60,
    )
    ps = plane_sum(partials, True)
    partner = swap(for_partner)
    (precision,) = call(
        functools.partial(precision_kernel, halves),
        [struct((levp, width), F32)],
        [],
        0,
        obs_precision,
    )
    slab_sd, residual, moved = call(
        functools.partial(first_kernel, len(ps)),
        [struct((1, lanes), F32), struct(slab_field, F32), struct(slab_field, BF16)],
        [],
        small * colblocks,
        *ps,
        vert,
        vert_t,
    )
    direction = total_step = None
    image, state = [None] * len(parts_of), [None] * len(parts_of)
    for sweep in range(ITERS):
        later, last = sweep > 0, sweep == ITERS - 1
        weighted = []
        for part, ys in reversed(list(enumerate(line_sum(moved, swap(moved))))):
            count = parts_of[part][1]
            shape = (count, levp, width)
            w, state[part], *y = call(
                functools.partial(weigh_kernel, later, last, len(ys)),
                [struct(shape, BF16), struct((count, 8, LANES), F32)]
                + ([] if last else [struct(shape, F32)]),
                [],
                0,
                *ys,
                precision,
                *([image[part], state[part]] if later else []),
            )
            weighted.insert(0, w)
            image[part] = None if last else y[0]
        ws = line_gather(*weighted)
        (theirs,) = call(
            functools.partial(adjoint_kernel, plan),
            [struct(slab_field, BF16)],
            [],
            product,
            *ws,
            partner,
        )
        theirs = swap(theirs)
        (mine,) = call(
            functools.partial(adjoint_kernel, plan),
            [struct(slab_field, F32)],
            [],
            product,
            *ws,
            own,
        )
        known = [vert, vert_t, *state, residual]
        if later:
            known += [direction, total_step]
        if last:
            ps = call(
                combine_columns_kernel, [struct(field, BF16)] * n_obs, [], 0, mine, theirs
            )
            ps = [ps[0]] + [plane(ps[i], i) for i in reversed(range(1, n_obs))]
            outputs = call(
                functools.partial(last_kernel, len(ps), later, lev, parts_of),
                [struct((lev, members, LANES), F32)] * 2,
                [],
                small,
                *ps,
                col_sd,
                *known,
            )
            break
        ps = call(combine_kernel, half_fields, [], 0, mine, theirs)
        ps = plane_sum(ps, False)
        outs = [struct(slab_field, F32), struct(field, F32), struct(slab_field, BF16)]
        if later:
            outs.append(struct(slab_field, F32))
        r, total_step, moved, *d = call(
            functools.partial(update_kernel, len(ps), later, parts_of),
            outs,
            [],
            small * colblocks,
            *ps,
            slab_sd,
            *known,
        )
        direction, residual = (d[0] if later else residual), r
    return tuple(jnp.transpose(x, (1, 0, 2))[None] for x in outputs)


def solution(mesh):
    return jax.shard_map(
        functools.partial(per_device, mesh.shape["slab"], mesh.shape["obs"]),
        mesh=mesh,
        in_specs=(
            P("obs", None, None),
            P("obs", None, None),
            P(),
            P(("slab", "obs"), None),
            P(),
            P("slab", "obs", None, None, None),
            P("slab", "obs", None),
            P("slab", "obs", None),
            P("slab", "obs"),
        ),
        out_specs=(P(("slab", "obs"), None, None, None), P(("slab", "obs"), None, None, None)),
        check_vma=False,
    )
```

```python
import functools

import jax
import jax.numpy as jnp
from jax import lax
from jax.experimental import pallas as pl
from jax.experimental.pallas import tpu as pltpu
from jax.sharding import PartitionSpec as P

ITERS = 2
LANES = 128
PIECES = 3
PRIME = 32749
VMEM = pl.BlockSpec(memory_space=pltpu.VMEM)
HBM = pl.BlockSpec(memory_space=pltpu.HBM)
F32 = jnp.float32
BF16 = jnp.bfloat16
NT = (((1,), (1,)), ((), ()))


def call(kernel, outs, scratch, flops, *args, space=VMEM, limit=24):
    nbytes = sum(a.size * a.dtype.itemsize for a in (*args, *outs))
    return pl.pallas_call(
        kernel,
        out_shape=outs,
        in_specs=[space] * len(args),
        out_specs=[VMEM] * len(outs),
        scratch_shapes=scratch,
        compiler_params=pltpu.CompilerParams(vmem_limit_bytes=limit * 1024 * 1024),
        cost_estimate=pl.CostEstimate(flops=flops, bytes_accessed=nbytes, transcendentals=0),
    )(*args)


def struct(shape, dtype):
    return jax.ShapeDtypeStruct(shape, dtype)


def place():
    slab = lax.axis_index("slab")
    return slab // 2, slab % 2, lax.axis_index("obs")


def add(parts):
    value = parts[0].astype(F32)
    for part in parts[1:]:
        value = value + part.astype(F32)
    return value


def dot(matrix, x):
    high = x.astype(BF16)
    rest = (x - high.astype(F32)).astype(BF16)
    x = jnp.concatenate([high, rest, high], axis=0)
    return jnp.dot(matrix, x, preferred_element_type=F32)


def total(x):
    return jnp.sum(jnp.sum(x, axis=0, keepdims=True), axis=1, keepdims=True)


def with_scalars(body, values):
    count = body.shape[0]
    tail = body[count - 16 :]
    sub = lax.broadcasted_iota(jnp.int32, tail.shape, 0) - (16 - len(values))
    lanes = lax.broadcasted_iota(jnp.int32, tail.shape, 1)
    line = jnp.zeros(tail.shape, F32)
    for m, member in enumerate(values):
        for q, value in enumerate(member):
            rest = value
            for piece in range(PIECES):
                part = rest.astype(BF16).astype(F32)
                rest = rest - part
                line = jnp.where((sub == m) & (lanes == q * PIECES + piece), part, line)
    return jnp.concatenate([body[: count - 16], jnp.where(sub >= 0, line, tail)], axis=0)


def read_scalars(refs, members, count):
    tail = add([ref[ref.shape[0] - 16 :, 0:LANES] for ref in refs])
    sub = lax.broadcasted_iota(jnp.int32, tail.shape, 0) - (16 - members)
    lanes = lax.broadcasted_iota(jnp.int32, tail.shape, 1)
    return [
        [
            total(
                jnp.where(
                    (sub == m) & (lanes >= q * PIECES) & (lanes < (q + 1) * PIECES), tail, 0.0
                )
            )
            for q in range(count)
        ]
        for m in range(members)
    ]


def by_member(values, shape, lev):
    rows = lax.broadcasted_iota(jnp.int32, shape, 0)
    out = jnp.zeros(shape, F32)
    for m, value in enumerate(values):
        out = jnp.where((rows >= m * lev) & (rows < (m + 1) * lev), value, out)
    return out


def member_sums(x, members, lev):
    lines = jnp.sum(x, axis=1, keepdims=True)
    rows = lax.broadcasted_iota(jnp.int32, lines.shape, 0)
    return [
        jnp.sum(
            jnp.where((rows >= m * lev) & (rows < (m + 1) * lev), lines, 0.0),
            axis=0,
            keepdims=True,
        )
        for m in range(members)
    ]


def remainder(x, factor):
    return x - (x.astype(F32) * factor).astype(jnp.int32) * PRIME


def start_kernel(
    dims, seeds_in, ids_in, cols_in, count_in, sd_in, innov_in, prec_in, h, own, partner, *rest
):
    chips, halves = dims
    outs = rest[:-12]
    seeds, ids, cols, count, sd, innov, prec, hashed, scratch, acc, sems, h_sems = rest[-12:]
    z, core, obs = place()
    blocks, lev, profiles = innov.shape
    colblocks, width = own.shape[1], own.shape[3]
    members, levp = hashed.shape[1], hashed.shape[2]
    rows = acc.shape[0]

    pairs = [(seeds_in, seeds), (ids_in, ids), (cols_in, cols), (count_in, count), (sd_in, sd)]
    small = [pltpu.make_async_copy(x, y, sems.at[i]) for i, (x, y) in enumerate(pairs)]
    for copy in small:
        copy.start()
    large = []
    for b in range(blocks):
        at = len(pairs) + 2 * b
        large.append(pltpu.make_async_copy(innov_in.at[:, b, :], innov.at[b], sems.at[at]))
        large.append(pltpu.make_async_copy(prec_in.at[:, b, :], prec.at[b], sems.at[at + 1]))
    for copy in large:
        copy.start()
    own[...] = jnp.zeros_like(own)
    partner[...] = jnp.zeros_like(partner)
    scratch[...] = jnp.zeros_like(scratch)
    for copy in small:
        copy.wait()

    def tile_copy(n, half, target):
        lanes = pl.ds(half * width, width)
        return pltpu.make_async_copy(h.at[n, :, lanes], target, h_sems.at[n * halves + half])

    def put(n, carry):
        for half in range(halves):
            piece, k = ids[0, 0, n] * halves + half, cols[0, 0, n]

            @pl.when(piece % 2 == core)
            def _():
                tile_copy(n, half, own.at[piece // 2, k]).start()

            @pl.when(piece % 2 != core)
            def _():
                tile_copy(n, half, partner.at[piece // 2, k]).start()

        return carry

    lax.fori_loop(0, count[0, 0], put, 0)

    starts = [lax.rem(seeds[m], PRIME) - PRIME for m in range(members)]
    order = [(source, zz) for source in range(2) for zz in range(chips)]
    shape = (levp, width)
    spot = lax.broadcasted_iota(jnp.int32, shape, 0) * profiles
    spot = spot + lax.broadcasted_iota(jnp.int32, shape, 1)
    low = (1.0 - 2.0**-21) / PRIME

    def piece_at(at):
        source, zz = order[at]
        return 2 * zz + (core if source == 0 else 1 - core)

    def draw(at):
        piece = piece_at(at)
        first = (obs * blocks + piece // halves) * (lev * profiles) + (piece % halves) * width
        base = remainder(7919 * remainder(spot + first, 1.0 / PRIME), 1.0 / PRIME)
        for m in range(members):
            k0 = base + starts[m]
            k1 = remainder(k0 * k0 + 12345, 1.0 / PRIME)
            k2 = remainder(k1 * k1 + 2719, low)
            k2 = jnp.where(k2 >= PRIME, k2 - PRIME, k2)
            hashed[at, m] = k2.astype(F32)

    def adjoint(at):
        source, zz = order[at]
        piece = piece_at(at)
        b = piece // halves
        if halves == 1:
            p, d = prec[b], innov[b]
        else:
            lanes = pl.ds(pl.multiple_of((piece % halves) * width, LANES), width)
            p, d = prec[b, :, lanes], innov[b, :, lanes]
        gain = 3.4 * p * lax.rsqrt(p)
        offset = p * d - 0.5 * gain
        gain = gain * (1.0 / PRIME)
        for m in range(members):
            w = offset + gain * hashed[at, m, 0:lev, :]
            scratch[at % 2, m * lev : (m + 1) * lev, :] = w
        w = scratch[at % 2].astype(BF16)
        tiles = (own if source == 0 else partner)[zz].reshape(colblocks * LANES, width)
        part = lax.dot_general(w, tiles, NT, preferred_element_type=F32)
        if at == 0:
            acc[...] = part
        else:
            acc[...] += part

    early = len(order) // 2
    for at in range(early):
        draw(at)
    for copy in large:
        copy.wait()

    def arrive(n, carry):
        for half in range(halves):
            tile_copy(n, half, own.at[0, 0]).wait()
        return carry

    lax.fori_loop(0, count[0, 0], arrive, 0)

    for at in range(len(order)):
        if at + early < len(order):
            draw(at + early)
        adjoint(at)

    line = jnp.concatenate([sd[...]] * colblocks, axis=1)
    put_halves(outs, with_columns(acc[...], line, obs, members))


def put_halves(outs, value):
    half = value.shape[1] // 2
    outs[0][...] = value[:, :half].astype(BF16)
    outs[1][...] = value[:, half:].astype(BF16)


def with_columns(body, line, obs, members):
    tail = body[body.shape[0] - 16 :]
    sub = lax.broadcasted_iota(jnp.int32, tail.shape, 0)
    mine = lax.broadcasted_iota(jnp.int32, tail.shape, 1) // LANES == obs
    rest = line
    for piece in range(PIECES):
        part = rest.astype(BF16).astype(F32)
        rest = rest - part
        tail = jnp.where((sub == 16 - PIECES + piece) & mine, part, tail)
    return jnp.concatenate([body[: body.shape[0] - 16], tail], axis=0)


def read_columns(body):
    tail = body[body.shape[0] - 16 :]
    sub = lax.broadcasted_iota(jnp.int32, tail.shape, 0)
    return jnp.sum(jnp.where(sub >= 16 - PIECES, tail, 0.0), axis=0, keepdims=True)


def precision_kernel(halves, members, prec, out):
    z, core, unused = place()
    piece = 2 * z + core
    lev, blocks, unused = prec.shape
    width = out.shape[1]
    block = lax.broadcasted_iota(jnp.int32, (lev, blocks, width), 1)
    if halves == 1:
        mine = prec[...]
    else:
        mine = prec[:, :, pl.ds(pl.multiple_of((piece % halves) * width, LANES), width)]
    out[...] = jnp.zeros_like(out)
    mine = jnp.sum(jnp.where(block == piece // halves, mine, 0.0), axis=1)
    for m in range(members):
        out[m * lev : (m + 1) * lev, :] = mine


def joined(pieces):
    one, one_more, two, two_more = [x[...] for x in pieces]
    return jnp.concatenate([add([one, one_more]), add([two, two_more])], axis=1)


def unpack(spread, value):
    count = value.shape[0]
    spread[0:count, :] = value
    spread[count:, :] = jnp.zeros((spread.shape[0] - count, value.shape[1]), F32)


def first_kernel(lev, *refs):
    vert, vert_t, sd_out, residual, moved, spread, packed = refs[4:]
    members, levp, unused = residual.shape
    t = joined(refs[:4])
    sd = read_columns(t)
    sd_out[...] = sd
    unpack(spread, t)
    scalars = []
    for m in range(members):
        at = slice(m * lev, m * lev + levp)
        r = dot(vert_t[...], sd * spread[at, :])
        residual[m] = r
        packed[at, :] = sd * dot(vert[...], r)
        scalars.append([total(r * r)])
    moved[...] = with_scalars(packed[0 : moved.shape[0], :], scalars).astype(BF16)


def add_kernel(members, scalars, *refs):
    parts, out = refs[:-1], refs[-1]
    value = add([x[...] for x in parts])
    if scalars:
        value = with_scalars(value, read_scalars(parts, members, scalars))
    out[...] = value.astype(BF16)


def add_halves_kernel(members, scalars, one, one_more, two, two_more, one_out, two_out):
    add_kernel(members, scalars, one, one_more, one_out)
    add_kernel(members, 0, two, two_more, two_out)


def stage_kernel(*refs):
    sems = refs[-1]
    count = len(refs) // 2
    copies = [
        pltpu.make_async_copy(refs[i], refs[count + i], sems.at[i]) for i in range(count)
    ]
    for copy in copies:
        copy.start()
    for copy in copies:
        copy.wait()


def forward_kernel(sends, members, x, tiles, *refs):
    z, core, obs = place()
    outs = refs[-len(sends) :]
    rows, lanes = x.shape
    width = tiles.shape[3]
    added = refs[1 : 1 + len(sends)] if len(refs) > len(sends) else [None] * len(sends)
    if added[0] is not None:
        scalars = read_scalars([refs[0], x], members, 2)
    for out, before, (chip, first, count) in zip(outs, added, sends):
        y = jnp.dot(
            x[first : first + count, :],
            tiles[z ^ chip].reshape(lanes, width),
            preferred_element_type=F32,
        )
        if before is not None:
            y = before[...] + y
            if first + count == rows:
                y = with_scalars(y, scalars)
        out[...] = y.astype(out.dtype)


def weigh_kernel(later, last, members, lev, spans, *refs):
    ys, refs = refs[: len(spans)], refs[len(spans) :]
    prec, old_image, old = refs[0], *(refs[1:3] if later else (None, None))
    state, *outs = refs[3 if later else 1 :]
    if not last:
        *outs, image = outs
    rows = prec.shape[0]
    cuts = sorted({first for first, count in spans}) + [rows]
    parts = []
    for low, high in zip(cuts, cuts[1:]):
        held = [
            ref[low - first : high - first, :]
            for ref, (first, count) in zip(ys, spans)
            if first <= low < first + count
        ]
        parts.append(add(held))
    y = parts[0] if len(parts) == 1 else jnp.concatenate(parts, axis=0)
    ends = [ref for ref, (first, count) in zip(ys, spans) if first + count == rows]
    sub = lax.broadcasted_iota(jnp.int32, (8, LANES), 0)
    betas = []
    for m, (norm, cross) in enumerate(read_scalars(ends, members, 2)):
        if later:
            old_norm, old_square = old[m, 0:1, 0:1], old[m, 1:2, 0:1]
            beta = norm / old_norm
            square = norm + 2.0 * beta * cross + beta * beta * old_square
        else:
            beta = jnp.zeros_like(norm)
            square = norm
        betas.append(beta)
        state[m] = jnp.where(sub == 0, norm, jnp.where(sub == 1, square, beta))
    if later:
        y = y + by_member(betas, (rows, 1), lev) * old_image[...]
    if not last:
        image[...] = y
    scaled = prec[...] * y
    energies = [[x] for x in member_sums(scaled * y, members, lev)]
    weighted = with_scalars(scaled, energies).astype(BF16)
    first = 0
    outs[0][...] = weighted
    for out in outs[1:]:
        out[...] = weighted[first : first + out.shape[0]]
        first += out.shape[0]


def adjoint_kernel(plan, members, *refs):
    z, core, obs = place()
    ws, tiles, out = refs[: len(plan)], refs[len(plan)], refs[len(plan) + 1]
    rows, lanes = out.shape
    width = ws[0].shape[1]
    acc = None
    for i in range(tiles.shape[0]):
        w = {first: ref for ref, (chip, first, count) in zip(ws, plan) if chip == i}
        w = [w[first][...] for first in sorted(w)]
        w = w[0] if len(w) == 1 else jnp.concatenate(w, axis=0)
        part = lax.dot_general(
            w, tiles[z ^ i].reshape(lanes, width), NT, preferred_element_type=F32
        )
        acc = part if i == 0 else acc + part
    ends = [ref for ref, (chip, first, count) in zip(ws, plan) if first + count == rows]
    out[...] = with_scalars(acc, read_scalars(ends, members, 1)).astype(out.dtype)


def combine_kernel(members, mine, theirs, *outs):
    value = mine[...] + theirs[...].astype(F32)
    put_halves(outs, with_scalars(value, read_scalars([mine, theirs], members, 1)))


def combine_columns_kernel(members, mine, theirs, *outs):
    obs = lax.axis_index("obs")
    energies = read_scalars([mine, theirs], members, 1)
    for i, out in enumerate(outs):
        lane = pl.ds(pl.multiple_of((obs ^ i) * LANES, LANES), LANES)
        value = mine[:, lane] + theirs[:, lane].astype(F32)
        out[...] = with_scalars(value, energies).astype(BF16)


def update_kernel(later, lev, *refs):
    pieces, refs = refs[:4], refs[4:]
    sd, vert, vert_t, state, residual = refs[:5]
    spread, packed = refs[-2:]
    if later:
        old_direction, old_solution, residual_out, solution_out, moved, direction_out = refs[5:-2]
    else:
        residual_out, solution_out, moved = refs[5:-2]
    members, levp, unused = residual.shape
    obs = lax.axis_index("obs")
    mine = pl.ds(pl.multiple_of(obs * LANES, LANES), LANES)
    unpack(spread, joined(pieces))
    energies = read_scalars(pieces[:2], members, 1)
    scalars = []
    for m in range(members):
        at = slice(m * lev, m * lev + levp)
        norm, square, beta = state[m, 0:1, 0:1], state[m, 1:2, 0:1], state[m, 2:3, 0:1]
        alpha = norm / (square + energies[m][0])
        r = residual[m]
        if later:
            d = r + beta * old_direction[m]
            direction_out[m] = d
            step = direction_out[m, :, mine]
            solution_out[m] = old_solution[m] + alpha * step
        else:
            d = r
            solution_out[m] = alpha * residual[m, :, mine]
        r = r - alpha * (d + dot(vert_t[...], sd[...] * spread[at, :]))
        residual_out[m] = r
        packed[at, :] = sd[...] * dot(vert[...], r)
        scalars.append([total(r * r), total(r * d)])
    moved[...] = with_scalars(packed[0 : moved.shape[0], :], scalars).astype(BF16)


def last_kernel(parts, later, lev, *refs):
    pieces, refs = refs[:parts], refs[parts:]
    sd, vert, vert_t, state, residual = refs[:5]
    increment_out, residual_out, spread = refs[-3:]
    members, levp, unused = residual.shape
    obs = lax.axis_index("obs")
    mine = pl.ds(pl.multiple_of(obs * LANES, LANES), LANES)
    unpack(spread, add([x[...] for x in pieces]))
    energies = read_scalars(pieces, members, 1)
    for m in range(members):
        t = spread[m * lev : m * lev + levp, :]
        norm, square, beta = state[m, 0:1, 0:1], state[m, 1:2, 0:1], state[m, 2:3, 0:1]
        alpha = norm / (square + energies[m][0])
        d = r = residual[m, :, mine]
        if later:
            old_direction, old_solution = refs[5:7]
            d = r + beta * old_direction[m, :, mine]
        solution = alpha * d
        if later:
            solution = old_solution[m] + solution
        r = r - alpha * (d + dot(vert_t[...], sd[...] * t))
        increment = sd[...] * dot(vert[...], solution)
        increment_out[:, m, :] = increment[0:lev]
        residual_out[:, m, :] = r[0:lev]


def per_device(
    n_slab,
    n_obs,
    innovation,
    obs_precision,
    seeds,
    col_sd,
    vert_factor,
    h_values,
    block_obs,
    block_col,
    entry_count,
):
    blocks, lev, profiles = innovation.shape
    members = seeds.shape[0]
    chips = n_slab // 2
    halves = n_slab // blocks
    width = profiles // halves
    colblocks = n_obs
    assert halves * blocks == n_slab and width % LANES == 0 and col_sd.shape[0] == 1
    assert chips & (chips - 1) == 0 and n_obs & (n_obs - 1) == 0
    levp = (lev + 1 + 15) // 16 * 16
    assert members <= 16 and members >= PIECES
    rows = (members * (lev + 1) + 15) // 16 * 16
    lanes = colblocks * LANES
    slab_field = (members, levp, lanes)
    slab_rows = (rows, lanes)
    half_rows = [struct((rows, lanes // 2), BF16)] * 2
    wide = rows + levp - lev + 7
    spread = pltpu.VMEM((wide // 8 * 8, lanes), F32)
    some = rows // 32 * 16
    rest = rows - some
    via = chips == 4
    if via:
        one, two = (0, some), (some, rest)
        plan = [(0, 0, rows), (1, 0, rows), (2, *one), (2, *two), (3, *one), (3, *two)]
        third = rows // 48 * 16
        near_cuts = [(0, rows - 2 * third), (rows - 2 * third, third), (rows - third, third)]
        sends = [(3, *one), (2, *two), (3, *two), (0, 0, rows), (2, *one)]
        sends += [(1, *cut) for cut in near_cuts]
    else:
        sends = plan = [(i, 0, rows) for i in range(chips)]
    pad = ((0, levp - lev), (0, levp - lev))
    high = lax.reduce_precision(vert_factor, 8, 7)
    low = vert_factor - high
    vert, vert_t = [
        jnp.concatenate([jnp.pad(x, pad).astype(BF16) for x in parts], axis=1)
        for parts in ((high, high, low), (high.T, high.T, low.T))
    ]
    h_block = h_values.reshape(h_values.shape[2:])
    innovation = jnp.transpose(innovation, (1, 0, 2))
    obs_precision = jnp.transpose(obs_precision, (1, 0, 2))
    product = n_slab * width * lanes * rows
    small = 12 * rows * levp * LANES
    plane_bits = [1 << k for k in range(n_obs.bit_length() - 1)]

    def along(x, i):
        return lax.ppermute(x, "slab", [(s, s ^ (2 * i)) for s in range(n_slab)])

    def plane(x, i):
        return lax.ppermute(x, "obs", [(o, o ^ i) for o in range(n_obs)])

    def swap(x):
        return lax.ppermute(x, "slab", [(s, s ^ 1) for s in range(n_slab)])

    def plane_sum(halves, staged):
        halves = list(halves)
        moved_halves = [None] * len(halves)
        for step, bit in enumerate(plane_bits):
            bits = [bit, plane_bits[len(plane_bits) - 1 - step]]
            for at in range(0, len(halves), 2):
                if step > 0:
                    one, two = halves[at : at + 2]
                    one_more, two_more = moved_halves[at : at + 2]
                    halves[at : at + 2] = call(
                        functools.partial(add_halves_kernel, members, 0 if staged else 1),
                        [struct(one.shape, BF16)] * 2,
                        [],
                        0,
                        one,
                        one_more,
                        two,
                        two_more,
                    )
                for half in range(2):
                    moved_halves[at + half] = plane(halves[at + half], bits[half])
            if step == 0 and staged:
                halves[:] = call(
                    stage_kernel,
                    [struct(x.shape, BF16) for x in halves],
                    [pltpu.SemaphoreType.DMA((len(halves),))],
                    0,
                    *halves,
                    space=HBM,
                )
        return [x for pair in zip(halves, moved_halves) for x in pair]

    def line_sum(moved, other):
        shapes = [(count, width) for i, unused, count in sends]
        mine = call(
            functools.partial(forward_kernel, sends, members),
            [struct(shape, F32) for shape in shapes],
            [],
            product,
            moved,
            own,
        )
        ys = call(
            functools.partial(forward_kernel, sends, members),
            [
                struct(shape, F32 if i == 0 or (via and at == 4) else BF16)
                for at, ((i, *unused), shape) in enumerate(zip(sends, shapes))
            ],
            [],
            product,
            other,
            partner,
            moved,
            *mine,
        )
        if not via:
            return [y if i == 0 else along(y, i) for i, y in enumerate(ys)], [(0, rows)] * chips
        passed, far_rest, last_rest, near, far, *nexts = ys
        passed = along(passed, 1)
        far_rest, last_rest = along(far_rest, 2), along(last_rest, 3)
        nexts = [along(x, 1) for x in nexts]
        (far,) = call(
            functools.partial(add_kernel, members, 0),
            [struct((some, width), BF16)],
            [],
            0,
            far,
            passed,
        )
        ys = [near, far_rest, last_rest, along(far, 2), *nexts]
        return ys, [(0, rows), two, two, one, *near_cuts]

    def line_gather(w, *parts):
        if not via:
            return [w if i == 0 else along(w, i) for i in range(chips)]
        some_w, rest_w = parts
        far = along(some_w, 2)
        far_rest, last_rest, next_ = along(rest_w, 2), along(rest_w, 3), along(w, 1)
        return [w, next_, far, far_rest, along(far, 1), last_rest]

    dense = struct((chips, colblocks, LANES, width), BF16)
    own, for_partner, *partials = call(
        functools.partial(start_kernel, (chips, halves)),
        [dense, dense] + half_rows,
        [
            pltpu.SMEM(seeds.shape, jnp.int32),
            pltpu.SMEM(block_obs.shape, jnp.int32),
            pltpu.SMEM(block_col.shape, jnp.int32),
            pltpu.SMEM(entry_count.shape, jnp.int32),
            pltpu.VMEM(col_sd.shape, F32),
            pltpu.VMEM((blocks, lev, profiles), F32),
            pltpu.VMEM((blocks, lev, profiles), F32),
            pltpu.VMEM((n_slab, members, levp, width), F32),
            pltpu.VMEM((2, rows, width), F32),
            pltpu.VMEM((rows, lanes), F32),
            pltpu.SemaphoreType.DMA((5 + 2 * blocks,)),
            pltpu.SemaphoreType.DMA((h_block.shape[0] * halves,)),
        ],
        2 * product,
        seeds,
        block_obs,
        block_col,
        entry_count,
        col_sd,
        innovation,
        obs_precision,
        h_block,
        space=HBM,
        limit=60,
    )
    ps = plane_sum(partials, True)
    partner = swap(for_partner)
    (precision,) = call(
        functools.partial(precision_kernel, halves, members),
        [struct((rows, width), F32)],
        [],
        0,
        obs_precision,
    )
    slab_sd, residual, moved = call(
        functools.partial(first_kernel, lev),
        [struct((1, lanes), F32), struct(slab_field, F32), struct(slab_rows, BF16)],
        [spread, spread],
        small * colblocks,
        *ps,
        vert,
        vert_t,
    )
    direction = total_step = image = state = None
    for sweep in range(ITERS):
        later, last = sweep > 0, sweep == ITERS - 1
        ys, spans = line_sum(moved, swap(moved))
        state, *weighted = call(
            functools.partial(weigh_kernel, later, last, members, lev, spans),
            [struct((members, 8, LANES), F32)]
            + [struct((n, width), BF16) for n in ((rows, some, rest) if via else (rows,))]
            + ([] if last else [struct((rows, width), F32)]),
            [],
            0,
            *ys,
            precision,
            *([image, state] if later else []),
        )
        if not last:
            *weighted, image = weighted
        ws = line_gather(*weighted)
        (theirs,) = call(
            functools.partial(adjoint_kernel, plan, members),
            [struct(slab_rows, BF16)],
            [],
            product,
            *ws,
            partner,
        )
        theirs = swap(theirs)
        (mine,) = call(
            functools.partial(adjoint_kernel, plan, members),
            [struct(slab_rows, F32)],
            [],
            product,
            *ws,
            own,
        )
        known = [vert, vert_t, state, residual]
        if later:
            known += [direction, total_step]
        if last:
            ps = call(
                functools.partial(combine_columns_kernel, members),
                [struct((rows, LANES), BF16)] * n_obs,
                [],
                0,
                mine,
                theirs,
            )
            ps = [ps[0]] + [plane(ps[i], i) for i in reversed(range(1, n_obs))]
            outputs = call(
                functools.partial(last_kernel, len(ps), later, lev),
                [struct((lev, members, LANES), F32)] * 2,
                [pltpu.VMEM((wide // 8 * 8, LANES), F32)],
                small,
                *ps,
                col_sd,
                *known,
            )
            break
        ps = call(
            functools.partial(combine_kernel, members), half_rows, [], 0, mine, theirs
        )
        ps = plane_sum(ps, False)
        outs = [
            struct(slab_field, F32),
            struct((members, levp, LANES), F32),
            struct(slab_rows, BF16),
        ]
        if later:
            outs.append(struct(slab_field, F32))
        r, total_step, moved, *d = call(
            functools.partial(update_kernel, later, lev),
            outs,
            [spread, spread],
            small * colblocks,
            *ps,
            slab_sd,
            *known,
        )
        direction, residual = (d[0] if later else residual), r
    return tuple(jnp.transpose(x, (1, 0, 2))[None] for x in outputs)


def solution(mesh):
    return jax.shard_map(
        functools.partial(per_device, mesh.shape["slab"], mesh.shape["obs"]),
        mesh=mesh,
        in_specs=(
            P("obs", None, None),
            P("obs", None, None),
            P(),
            P(("slab", "obs"), None),
            P(),
            P("slab", "obs", None, None, None),
            P("slab", "obs", None),
            P("slab", "obs", None),
            P("slab", "obs"),
        ),
        out_specs=(P(("slab", "obs"), None, None, None), P(("slab", "obs"), None, None, None)),
        check_vma=False,
    )
```

```python
import functools

import jax
import jax.numpy as jnp
from jax import lax
from jax.experimental import pallas as pl
from jax.experimental.pallas import tpu as pltpu
from jax.sharding import PartitionSpec as P

ITERS = 2
LANES = 128
PIECES = 3
PRIME = 32749
VMEM = pl.BlockSpec(memory_space=pltpu.VMEM)
HBM = pl.BlockSpec(memory_space=pltpu.HBM)
F32 = jnp.float32
BF16 = jnp.bfloat16
NT = (((1,), (1,)), ((), ()))


def call(kernel, outs, scratch, flops, *args, space=VMEM, limit=24):
    nbytes = sum(a.size * a.dtype.itemsize for a in (*args, *outs))
    return pl.pallas_call(
        kernel,
        out_shape=outs,
        in_specs=[space] * len(args),
        out_specs=[VMEM] * len(outs),
        scratch_shapes=scratch,
        compiler_params=pltpu.CompilerParams(vmem_limit_bytes=limit * 1024 * 1024),
        cost_estimate=pl.CostEstimate(flops=flops, bytes_accessed=nbytes, transcendentals=0),
    )(*args)


def struct(shape, dtype):
    return jax.ShapeDtypeStruct(shape, dtype)


def place():
    slab = lax.axis_index("slab")
    return slab // 2, slab % 2, lax.axis_index("obs")


def add(parts):
    value = parts[0].astype(F32)
    for part in parts[1:]:
        value = value + part.astype(F32)
    return value


def dot(matrix, x):
    high = x.astype(BF16)
    rest = (x - high.astype(F32)).astype(BF16)
    x = jnp.concatenate([high, rest, high], axis=0)
    return jnp.dot(matrix, x, preferred_element_type=F32)


def total(x):
    return jnp.sum(jnp.sum(x, axis=0, keepdims=True), axis=1, keepdims=True)


def with_scalars(body, values):
    count = body.shape[0]
    tail = body[count - 16 :]
    sub = lax.broadcasted_iota(jnp.int32, tail.shape, 0) - (16 - len(values))
    lanes = lax.broadcasted_iota(jnp.int32, tail.shape, 1)
    line = jnp.zeros(tail.shape, F32)
    for m, member in enumerate(values):
        for q, value in enumerate(member):
            rest = value
            for piece in range(PIECES):
                part = rest.astype(BF16).astype(F32)
                rest = rest - part
                line = jnp.where((sub == m) & (lanes == q * PIECES + piece), part, line)
    return jnp.concatenate([body[: count - 16], jnp.where(sub >= 0, line, tail)], axis=0)


def read_scalars(refs, members, count):
    tail = add([ref[ref.shape[0] - 16 :, 0:LANES] for ref in refs])
    sub = lax.broadcasted_iota(jnp.int32, tail.shape, 0) - (16 - members)
    lanes = lax.broadcasted_iota(jnp.int32, tail.shape, 1)
    return [
        [
            total(
                jnp.where(
                    (sub == m) & (lanes >= q * PIECES) & (lanes < (q + 1) * PIECES), tail, 0.0
                )
            )
            for q in range(count)
        ]
        for m in range(members)
    ]


def by_member(values, shape, lev):
    rows = lax.broadcasted_iota(jnp.int32, shape, 0)
    out = jnp.zeros(shape, F32)
    for m, value in enumerate(values):
        out = jnp.where((rows >= m * lev) & (rows < (m + 1) * lev), value, out)
    return out


def member_sums(x, members, lev):
    lines = jnp.sum(x, axis=1, keepdims=True)
    rows = lax.broadcasted_iota(jnp.int32, lines.shape, 0)
    return [
        jnp.sum(
            jnp.where((rows >= m * lev) & (rows < (m + 1) * lev), lines, 0.0),
            axis=0,
            keepdims=True,
        )
        for m in range(members)
    ]


def remainder(x, factor):
    return x - (x.astype(F32) * factor).astype(jnp.int32) * PRIME


def start_kernel(
    dims, seeds_in, ids_in, cols_in, count_in, sd_in, innov_in, prec_in, h, own, partner, *rest
):
    chips, halves = dims
    outs = rest[:-13]
    seeds, ids, cols, count, sd, innov, prec, bases, hashed, scratch, acc, sems, h_sems = rest[-13:]
    z, core, obs = place()
    blocks, lev, profiles = innov.shape
    colblocks, width = own.shape[1], own.shape[3]
    members, levp = hashed.shape[1], hashed.shape[2]
    rows = acc.shape[0]

    pairs = [(seeds_in, seeds), (ids_in, ids), (cols_in, cols), (count_in, count), (sd_in, sd)]
    small = [pltpu.make_async_copy(x, y, sems.at[i]) for i, (x, y) in enumerate(pairs)]
    for copy in small:
        copy.start()
    large = []
    for b in range(blocks):
        at = len(pairs) + 2 * b
        large.append(pltpu.make_async_copy(innov_in.at[:, b, :], innov.at[b], sems.at[at]))
        large.append(pltpu.make_async_copy(prec_in.at[:, b, :], prec.at[b], sems.at[at + 1]))
    for copy in large:
        copy.start()
    own[...] = jnp.zeros_like(own)
    partner[...] = jnp.zeros_like(partner)
    scratch[...] = jnp.zeros_like(scratch)
    order = [(source, zz) for source in range(2) for zz in range(chips)]
    shape = (levp, width)
    spot = lax.broadcasted_iota(jnp.int32, shape, 0) * profiles
    spot = spot + lax.broadcasted_iota(jnp.int32, shape, 1)

    def piece_at(at):
        source, zz = order[at]
        return 2 * zz + (core if source == 0 else 1 - core)

    for at in range(len(order)):
        piece = piece_at(at)
        first = (obs * blocks + piece // halves) * (lev * profiles) + (piece % halves) * width
        bases[at] = remainder(7919 * remainder(spot + first, 1.0 / PRIME), 1.0 / PRIME)
    for copy in small:
        copy.wait()

    def tile_copy(n, half, target):
        lanes = pl.ds(half * width, width)
        return pltpu.make_async_copy(h.at[n, :, lanes], target, h_sems.at[n * halves + half])

    def put(n, carry):
        for half in range(halves):
            piece, k = ids[0, 0, n] * halves + half, cols[0, 0, n]

            @pl.when(piece % 2 == core)
            def _():
                tile_copy(n, half, own.at[piece // 2, k]).start()

            @pl.when(piece % 2 != core)
            def _():
                tile_copy(n, half, partner.at[piece // 2, k]).start()

        return carry

    lax.fori_loop(0, count[0, 0], put, 0)

    starts = [lax.rem(seeds[m], PRIME) - PRIME for m in range(members)]
    low = (1.0 - 2.0**-21) / PRIME

    def draw(at, m):
        k0 = bases[at] + starts[m]
        k1 = remainder(k0 * k0 + 12345, 1.0 / PRIME)
        k2 = remainder(k1 * k1 + 2719, low)
        return jnp.where(k2 >= PRIME, k2 - PRIME, k2).astype(F32)

    early = len(order) // 2
    for at in range(early):
        for m in range(members):
            hashed[at, m] = draw(at, m)
    for copy in large:
        copy.wait()

    def arrive(n, carry):
        for half in range(halves):
            tile_copy(n, half, own.at[0, 0]).wait()
        return carry

    lax.fori_loop(0, count[0, 0], arrive, 0)

    for at in range(len(order)):
        source, zz = order[at]
        piece = piece_at(at)
        b = piece // halves
        if halves == 1:
            p, d = prec[b], innov[b]
        else:
            lanes = pl.ds(pl.multiple_of((piece % halves) * width, LANES), width)
            p, d = prec[b, :, lanes], innov[b, :, lanes]
        gain = 3.4 * p * lax.rsqrt(p)
        offset = p * d - 0.5 * gain
        gain = gain * (1.0 / PRIME)
        slot, side = at // 2 % 2, at % 2
        for m in range(members):
            k2 = hashed[at, m, 0:lev, :] if at < early else draw(at, m)[0:lev]
            scratch[slot, m * lev : (m + 1) * lev, side * width : (side + 1) * width] = (
                offset + gain * k2
            )
        if side == 0:
            continue
        tiles = own if source == 0 else partner
        tiles = [tiles[i].reshape(colblocks * LANES, width) for i in (zz - 1, zz)]
        part = lax.dot_general(
            scratch[slot].astype(BF16),
            jnp.concatenate(tiles, axis=1),
            NT,
            preferred_element_type=F32,
        )
        if at == 1:
            acc[...] = part
        else:
            acc[...] += part

    line = jnp.concatenate([sd[...]] * colblocks, axis=1)
    put_halves(outs, with_columns(acc[...], line, obs, members))


def put_halves(outs, value):
    half = value.shape[1] // 2
    outs[0][...] = value[:, :half].astype(BF16)
    outs[1][...] = value[:, half:].astype(BF16)


def with_columns(body, line, obs, members):
    tail = body[body.shape[0] - 16 :]
    sub = lax.broadcasted_iota(jnp.int32, tail.shape, 0)
    mine = lax.broadcasted_iota(jnp.int32, tail.shape, 1) // LANES == obs
    rest = line
    for piece in range(PIECES):
        part = rest.astype(BF16).astype(F32)
        rest = rest - part
        tail = jnp.where((sub == 16 - PIECES + piece) & mine, part, tail)
    return jnp.concatenate([body[: body.shape[0] - 16], tail], axis=0)


def read_columns(body):
    tail = body[body.shape[0] - 16 :]
    sub = lax.broadcasted_iota(jnp.int32, tail.shape, 0)
    return jnp.sum(jnp.where(sub >= 16 - PIECES, tail, 0.0), axis=0, keepdims=True)


def precision_kernel(halves, members, prec, out):
    z, core, unused = place()
    piece = 2 * z + core
    lev, blocks, unused = prec.shape
    width = out.shape[1]
    block = lax.broadcasted_iota(jnp.int32, (lev, blocks, width), 1)
    if halves == 1:
        mine = prec[...]
    else:
        mine = prec[:, :, pl.ds(pl.multiple_of((piece % halves) * width, LANES), width)]
    out[...] = jnp.zeros_like(out)
    mine = jnp.sum(jnp.where(block == piece // halves, mine, 0.0), axis=1)
    for m in range(members):
        out[m * lev : (m + 1) * lev, :] = mine


def joined(pieces):
    one, one_more, two, two_more = [x[...] for x in pieces]
    return jnp.concatenate([add([one, one_more]), add([two, two_more])], axis=1)


def unpack(spread, value):
    count = value.shape[0]
    spread[0:count, :] = value
    spread[count:, :] = jnp.zeros((spread.shape[0] - count, value.shape[1]), F32)


def first_kernel(lev, *refs):
    vert, vert_t, sd_out, residual, moved, spread, packed = refs[4:]
    members, levp, unused = residual.shape
    t = joined(refs[:4])
    sd = read_columns(t)
    sd_out[...] = sd
    unpack(spread, t)
    scalars = []
    for m in range(members):
        at = slice(m * lev, m * lev + levp)
        r = dot(vert_t[...], sd * spread[at, :])
        residual[m] = r
        packed[at, :] = sd * dot(vert[...], r)
        scalars.append([total(r * r)])
    moved[...] = with_scalars(packed[0 : moved.shape[0], :], scalars).astype(BF16)


def add_kernel(members, scalars, *refs):
    parts, out = refs[:-1], refs[-1]
    value = add([x[...] for x in parts])
    if scalars:
        value = with_scalars(value, read_scalars(parts, members, scalars))
    out[...] = value.astype(BF16)


def add_halves_kernel(members, scalars, one, one_more, two, two_more, one_out, two_out):
    add_kernel(members, scalars, one, one_more, one_out)
    add_kernel(members, 0, two, two_more, two_out)


def stage_kernel(*refs):
    sems = refs[-1]
    count = len(refs) // 2
    copies = [
        pltpu.make_async_copy(refs[i], refs[count + i], sems.at[i]) for i in range(count)
    ]
    for copy in copies:
        copy.start()
    for copy in copies:
        copy.wait()


def forward_kernel(sends, members, x, tiles, *refs):
    z, core, obs = place()
    outs = refs[-len(sends) :]
    rows, lanes = x.shape
    width = tiles.shape[3]
    added = refs[1 : 1 + len(sends)] if len(refs) > len(sends) else [None] * len(sends)
    if added[0] is not None:
        scalars = read_scalars([refs[0], x], members, 2)
    for out, before, (chip, first, count) in zip(outs, added, sends):
        y = jnp.dot(
            x[first : first + count, :],
            tiles[z ^ chip].reshape(lanes, width),
            preferred_element_type=F32,
        )
        if before is not None:
            y = before[...] + y
            if first + count == rows:
                y = with_scalars(y, scalars)
        out[...] = y.astype(out.dtype)


def weigh_kernel(later, last, members, lev, spans, *refs):
    ys, refs = refs[: len(spans)], refs[len(spans) :]
    prec, old_image, old = refs[0], *(refs[1:3] if later else (None, None))
    state, *outs = refs[3 if later else 1 :]
    if not last:
        *outs, image = outs
    rows = prec.shape[0]
    cuts = sorted({first for first, count in spans}) + [rows]
    parts = []
    for low, high in zip(cuts, cuts[1:]):
        held = [
            ref[low - first : high - first, :]
            for ref, (first, count) in zip(ys, spans)
            if first <= low < first + count
        ]
        parts.append(add(held))
    y = parts[0] if len(parts) == 1 else jnp.concatenate(parts, axis=0)
    ends = [ref for ref, (first, count) in zip(ys, spans) if first + count == rows]
    sub = lax.broadcasted_iota(jnp.int32, (8, LANES), 0)
    betas = []
    for m, (norm, cross) in enumerate(read_scalars(ends, members, 2)):
        if later:
            old_norm, old_square = old[m, 0:1, 0:1], old[m, 1:2, 0:1]
            beta = norm / old_norm
            square = norm + 2.0 * beta * cross + beta * beta * old_square
        else:
            beta = jnp.zeros_like(norm)
            square = norm
        betas.append(beta)
        state[m] = jnp.where(sub == 0, norm, jnp.where(sub == 1, square, beta))
    if later:
        y = y + by_member(betas, (rows, 1), lev) * old_image[...]
    if not last:
        image[...] = y
    scaled = prec[...] * y
    energies = [[x] for x in member_sums(scaled * y, members, lev)]
    weighted = with_scalars(scaled, energies).astype(BF16)
    first = 0
    outs[0][...] = weighted
    for out in outs[1:]:
        out[...] = weighted[first : first + out.shape[0]]
        first += out.shape[0]


def adjoint_kernel(plan, members, *refs):
    z, core, obs = place()
    ws, tiles, out = refs[: len(plan)], refs[len(plan)], refs[len(plan) + 1]
    rows, lanes = out.shape
    width = ws[0].shape[1]
    acc = None
    for i in range(tiles.shape[0]):
        w = {first: ref for ref, (chip, first, count) in zip(ws, plan) if chip == i}
        w = [w[first][...] for first in sorted(w)]
        w = w[0] if len(w) == 1 else jnp.concatenate(w, axis=0)
        part = lax.dot_general(
            w, tiles[z ^ i].reshape(lanes, width), NT, preferred_element_type=F32
        )
        acc = part if i == 0 else acc + part
    ends = [ref for ref, (chip, first, count) in zip(ws, plan) if first + count == rows]
    out[...] = with_scalars(acc, read_scalars(ends, members, 1)).astype(out.dtype)


def combine_kernel(members, mine, theirs, *outs):
    value = mine[...] + theirs[...].astype(F32)
    put_halves(outs, with_scalars(value, read_scalars([mine, theirs], members, 1)))


def combine_columns_kernel(members, mine, theirs, *outs):
    obs = lax.axis_index("obs")
    energies = read_scalars([mine, theirs], members, 1)
    for i, out in enumerate(outs):
        lane = pl.ds(pl.multiple_of((obs ^ i) * LANES, LANES), LANES)
        value = mine[:, lane] + theirs[:, lane].astype(F32)
        out[...] = with_scalars(value, energies).astype(BF16)


def update_kernel(later, lev, *refs):
    pieces, refs = refs[:4], refs[4:]
    sd, vert, vert_t, state, residual = refs[:5]
    spread, packed = refs[-2:]
    if later:
        old_direction, old_solution, residual_out, solution_out, moved, direction_out = refs[5:-2]
    else:
        residual_out, solution_out, moved = refs[5:-2]
    members, levp, unused = residual.shape
    obs = lax.axis_index("obs")
    mine = pl.ds(pl.multiple_of(obs * LANES, LANES), LANES)
    unpack(spread, joined(pieces))
    energies = read_scalars(pieces[:2], members, 1)
    scalars = []
    for m in range(members):
        at = slice(m * lev, m * lev + levp)
        norm, square, beta = state[m, 0:1, 0:1], state[m, 1:2, 0:1], state[m, 2:3, 0:1]
        alpha = norm / (square + energies[m][0])
        r = residual[m]
        if later:
            d = r + beta * old_direction[m]
            direction_out[m] = d
            step = direction_out[m, :, mine]
            solution_out[m] = old_solution[m] + alpha * step
        else:
            d = r
            solution_out[m] = alpha * residual[m, :, mine]
        r = r - alpha * (d + dot(vert_t[...], sd[...] * spread[at, :]))
        residual_out[m] = r
        packed[at, :] = sd[...] * dot(vert[...], r)
        scalars.append([total(r * r), total(r * d)])
    moved[...] = with_scalars(packed[0 : moved.shape[0], :], scalars).astype(BF16)


def increment_kernel(later, sd, vert, state, residual, *refs):
    before, direction, moved = refs[-3:]
    obs = lax.axis_index("obs")
    mine = pl.ds(pl.multiple_of(obs * LANES, LANES), LANES)
    for m in range(residual.shape[0]):
        d = residual[m, :, mine]
        if later:
            d = d + state[m, 2:3, 0:1] * refs[0][m, :, mine]
            before[m] = sd[...] * dot(vert[...], refs[1][m])
        else:
            before[m] = jnp.zeros_like(d)
        direction[m] = d
        moved[m] = sd[...] * dot(vert[...], d)


def last_kernel(parts, lev, *refs):
    pieces, refs = refs[:parts], refs[parts:]
    sd, vert_t, state, residual, before, direction, moved = refs[:7]
    increment_out, residual_out, spread = refs[7:]
    members, levp, unused = residual.shape
    obs = lax.axis_index("obs")
    mine = pl.ds(pl.multiple_of(obs * LANES, LANES), LANES)
    unpack(spread, add([x[...] for x in pieces]))
    energies = read_scalars(pieces, members, 1)
    for m in range(members):
        t = spread[m * lev : m * lev + levp, :]
        alpha = state[m, 0:1, 0:1] / (state[m, 1:2, 0:1] + energies[m][0])
        increment_out[:, m, :] = (before[m] + alpha * moved[m])[0:lev]
        r = residual[m, :, mine] - alpha * (direction[m] + dot(vert_t[...], sd[...] * t))
        residual_out[:, m, :] = r[0:lev]


def per_device(
    n_slab,
    n_obs,
    innovation,
    obs_precision,
    seeds,
    col_sd,
    vert_factor,
    h_values,
    block_obs,
    block_col,
    entry_count,
):
    blocks, lev, profiles = innovation.shape
    members = seeds.shape[0]
    chips = n_slab // 2
    halves = n_slab // blocks
    width = profiles // halves
    colblocks = n_obs
    assert halves * blocks == n_slab and width % LANES == 0 and col_sd.shape[0] == 1
    assert chips & (chips - 1) == 0 and n_obs & (n_obs - 1) == 0
    levp = (lev + 1 + 15) // 16 * 16
    assert members <= 16 and members >= PIECES
    rows = (members * (lev + 1) + 15) // 16 * 16
    lanes = colblocks * LANES
    slab_field = (members, levp, lanes)
    slab_rows = (rows, lanes)
    half_rows = [struct((rows, lanes // 2), BF16)] * 2
    wide = rows + levp - lev + 7
    spread = pltpu.VMEM((wide // 8 * 8, lanes), F32)
    some = rows // 32 * 16
    rest = rows - some
    via = chips == 4
    if via:
        one, two = (0, some), (some, rest)
        plan = [(0, 0, rows), (1, 0, rows), (2, *one), (2, *two), (3, *one), (3, *two)]
        sends = [(3, *one), (2, *two), (3, *two), (1, *one), (1, *two), (0, 0, rows), (2, *one)]
    else:
        sends = plan = [(i, 0, rows) for i in range(chips)]
    pad = ((0, levp - lev), (0, levp - lev))
    high = lax.reduce_precision(vert_factor, 8, 7)
    low = vert_factor - high
    vert, vert_t = [
        jnp.concatenate([jnp.pad(x, pad).astype(BF16) for x in parts], axis=1)
        for parts in ((high, high, low), (high.T, high.T, low.T))
    ]
    h_block = h_values.reshape(h_values.shape[2:])
    innovation = jnp.transpose(innovation, (1, 0, 2))
    obs_precision = jnp.transpose(obs_precision, (1, 0, 2))
    product = n_slab * width * lanes * rows
    small = 12 * rows * levp * LANES
    plane_bits = [1 << k for k in range(n_obs.bit_length() - 1)]

    def along(x, i):
        return lax.ppermute(x, "slab", [(s, s ^ (2 * i)) for s in range(n_slab)])

    def plane(x, i):
        return lax.ppermute(x, "obs", [(o, o ^ i) for o in range(n_obs)])

    def swap(x):
        return lax.ppermute(x, "slab", [(s, s ^ 1) for s in range(n_slab)])

    def plane_sum(halves, staged):
        halves = list(halves)
        moved_halves = [None] * len(halves)
        for step, bit in enumerate(plane_bits):
            bits = [bit, plane_bits[len(plane_bits) - 1 - step]]
            for at in range(0, len(halves), 2):
                if step > 0:
                    one, two = halves[at : at + 2]
                    one_more, two_more = moved_halves[at : at + 2]
                    halves[at : at + 2] = call(
                        functools.partial(add_halves_kernel, members, 0 if staged else 1),
                        [struct(one.shape, BF16)] * 2,
                        [],
                        0,
                        one,
                        one_more,
                        two,
                        two_more,
                    )
                for half in range(2):
                    moved_halves[at + half] = plane(halves[at + half], bits[half])
            if step == 0 and staged:
                halves[:] = call(
                    stage_kernel,
                    [struct(x.shape, BF16) for x in halves],
                    [pltpu.SemaphoreType.DMA((len(halves),))],
                    0,
                    *halves,
                    space=HBM,
                )
        return [x for pair in zip(halves, moved_halves) for x in pair]

    def line_sum(moved, other):
        shapes = [(count, width) for i, unused, count in sends]
        mine = call(
            functools.partial(forward_kernel, sends, members),
            [struct(shape, F32) for shape in shapes],
            [],
            product,
            moved,
            own,
        )
        ys = call(
            functools.partial(forward_kernel, sends, members),
            [
                struct(shape, F32 if i == 0 or (via and at == 6) else BF16)
                for at, ((i, *unused), shape) in enumerate(zip(sends, shapes))
            ],
            [],
            product,
            other,
            partner,
            moved,
            *mine,
        )
        if not via:
            return [y if i == 0 else along(y, i) for i, y in enumerate(ys)], [(0, rows)] * chips
        passed, far_rest, last_rest, next_some, next_rest, near, far = ys
        passed = along(passed, 1)
        far_rest, last_rest = along(far_rest, 2), along(last_rest, 3)
        next_some, next_rest = along(next_some, 1), along(next_rest, 1)
        (far,) = call(
            functools.partial(add_kernel, members, 0),
            [struct((some, width), BF16)],
            [],
            0,
            far,
            passed,
        )
        ys = [near, far_rest, last_rest, next_some, next_rest, along(far, 2)]
        return ys, [(0, rows), two, two, one, two, one]

    def line_gather(w, *parts):
        if not via:
            return [w if i == 0 else along(w, i) for i in range(chips)]
        some_w, rest_w = parts
        far = along(some_w, 2)
        far_rest, last_rest, next_ = along(rest_w, 2), along(rest_w, 3), along(w, 1)
        return [w, next_, far, far_rest, along(far, 1), last_rest]

    dense = struct((chips, colblocks, LANES, width), BF16)
    own, for_partner, *partials = call(
        functools.partial(start_kernel, (chips, halves)),
        [dense, dense] + half_rows,
        [
            pltpu.SMEM(seeds.shape, jnp.int32),
            pltpu.SMEM(block_obs.shape, jnp.int32),
            pltpu.SMEM(block_col.shape, jnp.int32),
            pltpu.SMEM(entry_count.shape, jnp.int32),
            pltpu.VMEM(col_sd.shape, F32),
            pltpu.VMEM((blocks, lev, profiles), F32),
            pltpu.VMEM((blocks, lev, profiles), F32),
            pltpu.VMEM((n_slab, levp, width), jnp.int32),
            pltpu.VMEM((n_slab // 2, members, levp, width), F32),
            pltpu.VMEM((2, rows, 2 * width), F32),
            pltpu.VMEM((rows, lanes), F32),
            pltpu.SemaphoreType.DMA((5 + 2 * blocks,)),
            pltpu.SemaphoreType.DMA((h_block.shape[0] * halves,)),
        ],
        2 * product,
        seeds,
        block_obs,
        block_col,
        entry_count,
        col_sd,
        innovation,
        obs_precision,
        h_block,
        space=HBM,
        limit=60,
    )
    ps = plane_sum(partials, True)
    partner = swap(for_partner)
    (precision,) = call(
        functools.partial(precision_kernel, halves, members),
        [struct((rows, width), F32)],
        [],
        0,
        obs_precision,
    )
    slab_sd, residual, moved = call(
        functools.partial(first_kernel, lev),
        [struct((1, lanes), F32), struct(slab_field, F32), struct(slab_rows, BF16)],
        [spread, spread],
        small * colblocks,
        *ps,
        vert,
        vert_t,
    )
    direction = total_step = image = state = None
    for sweep in range(ITERS):
        later, last = sweep > 0, sweep == ITERS - 1
        ys, spans = line_sum(moved, swap(moved))
        state, *weighted = call(
            functools.partial(weigh_kernel, later, last, members, lev, spans),
            [struct((members, 8, LANES), F32)]
            + [struct((n, width), BF16) for n in ((rows, some, rest) if via else (rows,))]
            + ([] if last else [struct((rows, width), F32)]),
            [],
            0,
            *ys,
            precision,
            *([image, state] if later else []),
        )
        if not last:
            *weighted, image = weighted
        ws = line_gather(*weighted)
        (theirs,) = call(
            functools.partial(adjoint_kernel, plan, members),
            [struct(slab_rows, BF16)],
            [],
            product,
            *ws,
            partner,
        )
        theirs = swap(theirs)
        (mine,) = call(
            functools.partial(adjoint_kernel, plan, members),
            [struct(slab_rows, F32)],
            [],
            product,
            *ws,
            own,
        )
        known = [vert, vert_t, state, residual]
        if later:
            known += [direction, total_step]
        if last:
            ps = call(
                functools.partial(combine_columns_kernel, members),
                [struct((rows, LANES), BF16)] * n_obs,
                [],
                0,
                mine,
                theirs,
            )
            ps = [ps[0]] + [plane(ps[i], i) for i in reversed(range(1, n_obs))]
            own_field = struct((members, levp, LANES), F32)
            before, d, u_d = call(
                functools.partial(increment_kernel, later),
                [own_field] * 3,
                [],
                small,
                col_sd,
                vert,
                state,
                residual,
                *([direction, total_step] if later else []),
            )
            outputs = call(
                functools.partial(last_kernel, len(ps), lev),
                [struct((lev, members, LANES), F32)] * 2,
                [pltpu.VMEM((wide // 8 * 8, LANES), F32)],
                small,
                *ps,
                col_sd,
                vert_t,
                state,
                residual,
                before,
                d,
                u_d,
            )
            break
        ps = call(
            functools.partial(combine_kernel, members), half_rows, [], 0, mine, theirs
        )
        ps = plane_sum(ps, False)
        outs = [
            struct(slab_field, F32),
            struct((members, levp, LANES), F32),
            struct(slab_rows, BF16),
        ]
        if later:
            outs.append(struct(slab_field, F32))
        r, total_step, moved, *d = call(
            functools.partial(update_kernel, later, lev),
            outs,
            [spread, spread],
            small * colblocks,
            *ps,
            slab_sd,
            *known,
        )
        direction, residual = (d[0] if later else residual), r
    return tuple(jnp.transpose(x, (1, 0, 2))[None] for x in outputs)


def solution(mesh):
    return jax.shard_map(
        functools.partial(per_device, mesh.shape["slab"], mesh.shape["obs"]),
        mesh=mesh,
        in_specs=(
            P("obs", None, None),
            P("obs", None, None),
            P(),
            P(("slab", "obs"), None),
            P(),
            P("slab", "obs", None, None, None),
            P("slab", "obs", None),
            P("slab", "obs", None),
            P("slab", "obs"),
        ),
        out_specs=(P(("slab", "obs"), None, None, None), P(("slab", "obs"), None, None, None)),
        check_vma=False,
    )
```

```python
import functools

import jax
import jax.numpy as jnp
from jax import lax
from jax.experimental import pallas as pl
from jax.experimental.pallas import tpu as pltpu
from jax.sharding import PartitionSpec as P

ITERS = 2
LANES = 128
PIECES = 3
PRIME = 32749
VMEM = pl.BlockSpec(memory_space=pltpu.VMEM)
HBM = pl.BlockSpec(memory_space=pltpu.HBM)
F32 = jnp.float32
BF16 = jnp.bfloat16
NT = (((1,), (1,)), ((), ()))


def call(kernel, outs, scratch, flops, *args, space=VMEM, limit=24):
    nbytes = sum(a.size * a.dtype.itemsize for a in (*args, *outs))
    return pl.pallas_call(
        kernel,
        out_shape=outs,
        in_specs=[space] * len(args),
        out_specs=[VMEM] * len(outs),
        scratch_shapes=scratch,
        compiler_params=pltpu.CompilerParams(vmem_limit_bytes=limit * 1024 * 1024),
        cost_estimate=pl.CostEstimate(flops=flops, bytes_accessed=nbytes, transcendentals=0),
    )(*args)


def struct(shape, dtype):
    return jax.ShapeDtypeStruct(shape, dtype)


def place():
    slab = lax.axis_index("slab")
    return slab // 2, slab % 2, lax.axis_index("obs")


def add(parts):
    value = parts[0].astype(F32)
    for part in parts[1:]:
        value = value + part.astype(F32)
    return value


def dot(matrix, x):
    high = x.astype(BF16)
    rest = (x - high.astype(F32)).astype(BF16)
    x = jnp.concatenate([high, rest, high], axis=0)
    return jnp.dot(matrix, x, preferred_element_type=F32)


def total(x):
    return jnp.sum(jnp.sum(x, axis=0, keepdims=True), axis=1, keepdims=True)


def with_scalars(body, values):
    count = body.shape[0]
    tail = body[count - 16 :]
    sub = lax.broadcasted_iota(jnp.int32, tail.shape, 0) - (16 - len(values))
    lanes = lax.broadcasted_iota(jnp.int32, tail.shape, 1)
    line = jnp.zeros(tail.shape, F32)
    for m, member in enumerate(values):
        for q, value in enumerate(member):
            rest = value
            for piece in range(PIECES):
                part = rest.astype(BF16).astype(F32)
                rest = rest - part
                line = jnp.where((sub == m) & (lanes == q * PIECES + piece), part, line)
    return jnp.concatenate([body[: count - 16], jnp.where(sub >= 0, line, tail)], axis=0)


def read_scalars(refs, members, count):
    tail = add([ref[ref.shape[0] - 16 :, 0:LANES] for ref in refs])
    sub = lax.broadcasted_iota(jnp.int32, tail.shape, 0) - (16 - members)
    lanes = lax.broadcasted_iota(jnp.int32, tail.shape, 1)
    return [
        [
            total(
                jnp.where(
                    (sub == m) & (lanes >= q * PIECES) & (lanes < (q + 1) * PIECES), tail, 0.0
                )
            )
            for q in range(count)
        ]
        for m in range(members)
    ]


def by_member(values, shape, lev):
    rows = lax.broadcasted_iota(jnp.int32, shape, 0)
    out = jnp.zeros(shape, F32)
    for m, value in enumerate(values):
        out = jnp.where((rows >= m * lev) & (rows < (m + 1) * lev), value, out)
    return out


def member_sums(x, members, lev):
    lines = jnp.sum(x, axis=1, keepdims=True)
    rows = lax.broadcasted_iota(jnp.int32, lines.shape, 0)
    return [
        jnp.sum(
            jnp.where((rows >= m * lev) & (rows < (m + 1) * lev), lines, 0.0),
            axis=0,
            keepdims=True,
        )
        for m in range(members)
    ]


def remainder(x, factor):
    return x - (x.astype(F32) * factor).astype(jnp.int32) * PRIME


def start_kernel(
    dims, seeds_in, ids_in, cols_in, count_in, sd_in, innov_in, prec_in, h, own, partner, *rest
):
    chips, halves, blocks, lev = dims
    outs = rest[:-13]
    seeds, ids, cols, count, sd, innov, prec, bases, hashed, scratch, acc, sems, h_sems = rest[-13:]
    z, core, obs = place()
    strips = innov.shape[0]
    profiles = strips * LANES
    colblocks, width = own.shape[1], own.shape[3]
    members, levp = hashed.shape[1], hashed.shape[2]
    rows = acc.shape[0]

    pairs = [(seeds_in, seeds), (ids_in, ids), (cols_in, cols), (count_in, count), (sd_in, sd)]
    small = [pltpu.make_async_copy(x, y, sems.at[i]) for i, (x, y) in enumerate(pairs)]
    for copy in small:
        copy.start()
    large = []
    for x, y in ((innov_in, innov), (prec_in, prec)):
        for t in range(strips):
            at = len(pairs) + len(large)
            large.append(
                pltpu.make_async_copy(
                    x.at[:, t * LANES : (t + 1) * LANES], y.at[t, 0 : lev * blocks, :], sems.at[at]
                )
            )
    for copy in large:
        copy.start()
    own[...] = jnp.zeros_like(own)
    partner[...] = jnp.zeros_like(partner)
    scratch[...] = jnp.zeros_like(scratch)
    order = [(source, zz) for source in range(2) for zz in range(chips)]
    shape = (levp, width)
    spot = lax.broadcasted_iota(jnp.int32, shape, 0) * profiles
    spot = spot + lax.broadcasted_iota(jnp.int32, shape, 1)

    def piece_at(at):
        source, zz = order[at]
        return 2 * zz + (core if source == 0 else 1 - core)

    for at in range(len(order)):
        piece = piece_at(at)
        first = (obs * blocks + piece // halves) * (lev * profiles) + (piece % halves) * width
        bases[at] = remainder(7919 * remainder(spot + first, 1.0 / PRIME), 1.0 / PRIME)
    for copy in small:
        copy.wait()

    def tile_copy(n, half, target):
        lanes = pl.ds(half * width, width)
        return pltpu.make_async_copy(h.at[n, :, lanes], target, h_sems.at[n * halves + half])

    def put(n, carry):
        for half in range(halves):
            piece, k = ids[0, 0, n] * halves + half, cols[0, 0, n]

            @pl.when(piece % 2 == core)
            def _():
                tile_copy(n, half, own.at[piece // 2, k]).start()

            @pl.when(piece % 2 != core)
            def _():
                tile_copy(n, half, partner.at[piece // 2, k]).start()

        return carry

    lax.fori_loop(0, count[0, 0], put, 0)

    starts = [lax.rem(seeds[m], PRIME) - PRIME for m in range(members)]
    low = (1.0 - 2.0**-21) / PRIME

    def draw(at, m):
        k0 = bases[at] + starts[m]
        k1 = remainder(k0 * k0 + 12345, 1.0 / PRIME)
        k2 = remainder(k1 * k1 + 2719, low)
        return jnp.where(k2 >= PRIME, k2 - PRIME, k2).astype(F32)

    early = len(order) // 2
    for at in range(early):
        for m in range(members):
            hashed[at, m] = draw(at, m)
    for copy in large:
        copy.wait()

    def arrive(n, carry):
        for half in range(halves):
            tile_copy(n, half, own.at[0, 0]).wait()
        return carry

    lax.fori_loop(0, count[0, 0], arrive, 0)

    for at in range(len(order)):
        source, zz = order[at]
        piece = piece_at(at)
        b = piece // halves
        strip = (piece % halves) * (width // LANES)
        p, d = [
            jnp.concatenate(
                [
                    x[strip + t, pl.ds(b, lev, stride=blocks), :]
                    for t in range(width // LANES)
                ],
                axis=1,
            )
            for x in (prec, innov)
        ]
        gain = 3.4 * p * lax.rsqrt(p)
        offset = p * d - 0.5 * gain
        gain = gain * (1.0 / PRIME)
        slot, side = at // 2 % 2, at % 2
        for m in range(members):
            k2 = hashed[at, m, 0:lev, :] if at < early else draw(at, m)[0:lev]
            scratch[slot, m * lev : (m + 1) * lev, side * width : (side + 1) * width] = (
                offset + gain * k2
            )
        if side == 0:
            continue
        tiles = own if source == 0 else partner
        tiles = [tiles[i].reshape(colblocks * LANES, width) for i in (zz - 1, zz)]
        part = lax.dot_general(
            scratch[slot].astype(BF16),
            jnp.concatenate(tiles, axis=1),
            NT,
            preferred_element_type=F32,
        )
        if at == 1:
            acc[...] = part
        else:
            acc[...] += part

    line = jnp.concatenate([sd[...]] * colblocks, axis=1)
    put_halves(outs, with_columns(acc[...], line, obs, members))


def put_halves(outs, value):
    half = value.shape[1] // 2
    outs[0][...] = value[:, :half].astype(BF16)
    outs[1][...] = value[:, half:].astype(BF16)


def with_columns(body, line, obs, members):
    tail = body[body.shape[0] - 16 :]
    sub = lax.broadcasted_iota(jnp.int32, tail.shape, 0)
    mine = lax.broadcasted_iota(jnp.int32, tail.shape, 1) // LANES == obs
    rest = line
    for piece in range(PIECES):
        part = rest.astype(BF16).astype(F32)
        rest = rest - part
        tail = jnp.where((sub == 16 - PIECES + piece) & mine, part, tail)
    return jnp.concatenate([body[: body.shape[0] - 16], tail], axis=0)


def read_columns(body):
    tail = body[body.shape[0] - 16 :]
    sub = lax.broadcasted_iota(jnp.int32, tail.shape, 0)
    return jnp.sum(jnp.where(sub >= 16 - PIECES, tail, 0.0), axis=0, keepdims=True)


def precision_kernel(halves, members, prec, out):
    z, core, unused = place()
    piece = 2 * z + core
    lev, blocks, unused = prec.shape
    width = out.shape[1]
    block = lax.broadcasted_iota(jnp.int32, (lev, blocks, width), 1)
    if halves == 1:
        mine = prec[...]
    else:
        mine = prec[:, :, pl.ds(pl.multiple_of((piece % halves) * width, LANES), width)]
    out[...] = jnp.zeros_like(out)
    mine = jnp.sum(jnp.where(block == piece // halves, mine, 0.0), axis=1)
    for m in range(members):
        out[m * lev : (m + 1) * lev, :] = mine


def joined(pieces):
    one, one_more, two, two_more = [x[...] for x in pieces]
    return jnp.concatenate([add([one, one_more]), add([two, two_more])], axis=1)


def unpack(spread, value):
    count = value.shape[0]
    spread[0:count, :] = value
    spread[count:, :] = jnp.zeros((spread.shape[0] - count, value.shape[1]), F32)


def first_kernel(lev, *refs):
    vert, vert_t, sd_out, residual, moved, spread, packed = refs[4:]
    members, levp, unused = residual.shape
    t = joined(refs[:4])
    sd = read_columns(t)
    sd_out[...] = sd
    unpack(spread, t)
    scalars = []
    for m in range(members):
        at = slice(m * lev, m * lev + levp)
        r = dot(vert_t[...], sd * spread[at, :])
        residual[m] = r
        packed[at, :] = sd * dot(vert[...], r)
        scalars.append([total(r * r)])
    moved[...] = with_scalars(packed[0 : moved.shape[0], :], scalars).astype(BF16)


def add_kernel(members, scalars, *refs):
    parts, out = refs[:-1], refs[-1]
    value = add([x[...] for x in parts])
    if scalars:
        value = with_scalars(value, read_scalars(parts, members, scalars))
    out[...] = value.astype(BF16)


def add_halves_kernel(members, scalars, one, one_more, two, two_more, one_out, two_out):
    add_kernel(members, scalars, one, one_more, one_out)
    add_kernel(members, 0, two, two_more, two_out)


def stage_kernel(*refs):
    sems = refs[-1]
    count = len(refs) // 2
    copies = [
        pltpu.make_async_copy(refs[i], refs[count + i], sems.at[i]) for i in range(count)
    ]
    for copy in copies:
        copy.start()
    for copy in copies:
        copy.wait()


def forward_kernel(sends, members, x, tiles, *refs):
    z, core, obs = place()
    outs = refs[-len(sends) :]
    rows, lanes = x.shape
    width = tiles.shape[3]
    added = refs[1 : 1 + len(sends)] if len(refs) > len(sends) else [None] * len(sends)
    if added[0] is not None:
        scalars = read_scalars([refs[0], x], members, 2)
    for out, before, (chip, first, count) in zip(outs, added, sends):
        y = jnp.dot(
            x[first : first + count, :],
            tiles[z ^ chip].reshape(lanes, width),
            preferred_element_type=F32,
        )
        if before is not None:
            y = before[...] + y
            if first + count == rows:
                y = with_scalars(y, scalars)
        out[...] = y.astype(out.dtype)


def weigh_kernel(later, last, members, lev, spans, *refs):
    ys, refs = refs[: len(spans)], refs[len(spans) :]
    prec, old_image, old = refs[0], *(refs[1:3] if later else (None, None))
    state, *outs = refs[3 if later else 1 :]
    if not last:
        *outs, image = outs
    rows = prec.shape[0]
    cuts = sorted({first for first, count in spans}) + [rows]
    parts = []
    for low, high in zip(cuts, cuts[1:]):
        held = [
            ref[low - first : high - first, :]
            for ref, (first, count) in zip(ys, spans)
            if first <= low < first + count
        ]
        parts.append(add(held))
    y = parts[0] if len(parts) == 1 else jnp.concatenate(parts, axis=0)
    ends = [ref for ref, (first, count) in zip(ys, spans) if first + count == rows]
    sub = lax.broadcasted_iota(jnp.int32, (8, LANES), 0)
    betas = []
    for m, (norm, cross) in enumerate(read_scalars(ends, members, 2)):
        if later:
            old_norm, old_square = old[m, 0:1, 0:1], old[m, 1:2, 0:1]
            beta = norm / old_norm
            square = norm + 2.0 * beta * cross + beta * beta * old_square
        else:
            beta = jnp.zeros_like(norm)
            square = norm
        betas.append(beta)
        state[m] = jnp.where(sub == 0, norm, jnp.where(sub == 1, square, beta))
    if later:
        y = y + by_member(betas, (rows, 1), lev) * old_image[...]
    if not last:
        image[...] = y
    scaled = prec[...] * y
    energies = [[x] for x in member_sums(scaled * y, members, lev)]
    weighted = with_scalars(scaled, energies).astype(BF16)
    first = 0
    outs[0][...] = weighted
    for out in outs[1:]:
        out[...] = weighted[first : first + out.shape[0]]
        first += out.shape[0]


def adjoint_kernel(plan, members, *refs):
    z, core, obs = place()
    ws, tiles, out = refs[: len(plan)], refs[len(plan)], refs[len(plan) + 1]
    rows, lanes = out.shape
    width = ws[0].shape[1]
    acc = None
    for i in range(tiles.shape[0]):
        w = {first: ref for ref, (chip, first, count) in zip(ws, plan) if chip == i}
        w = [w[first][...] for first in sorted(w)]
        w = w[0] if len(w) == 1 else jnp.concatenate(w, axis=0)
        part = lax.dot_general(
            w, tiles[z ^ i].reshape(lanes, width), NT, preferred_element_type=F32
        )
        acc = part if i == 0 else acc + part
    ends = [ref for ref, (chip, first, count) in zip(ws, plan) if first + count == rows]
    out[...] = with_scalars(acc, read_scalars(ends, members, 1)).astype(out.dtype)


def combine_kernel(members, mine, theirs, *outs):
    value = mine[...] + theirs[...].astype(F32)
    put_halves(outs, with_scalars(value, read_scalars([mine, theirs], members, 1)))


def combine_columns_kernel(members, mine, theirs, *outs):
    obs = lax.axis_index("obs")
    energies = read_scalars([mine, theirs], members, 1)
    for i, out in enumerate(outs):
        lane = pl.ds(pl.multiple_of((obs ^ i) * LANES, LANES), LANES)
        value = mine[:, lane] + theirs[:, lane].astype(F32)
        out[...] = with_scalars(value, energies).astype(BF16)


def update_kernel(later, lev, *refs):
    pieces, refs = refs[:4], refs[4:]
    sd, vert, vert_t, state, residual = refs[:5]
    spread, packed = refs[-2:]
    if later:
        old_direction, old_solution, residual_out, solution_out, moved, direction_out = refs[5:-2]
    else:
        residual_out, solution_out, moved = refs[5:-2]
    members, levp, unused = residual.shape
    obs = lax.axis_index("obs")
    mine = pl.ds(pl.multiple_of(obs * LANES, LANES), LANES)
    unpack(spread, joined(pieces))
    energies = read_scalars(pieces[:2], members, 1)
    scalars = []
    for m in range(members):
        at = slice(m * lev, m * lev + levp)
        norm, square, beta = state[m, 0:1, 0:1], state[m, 1:2, 0:1], state[m, 2:3, 0:1]
        alpha = norm / (square + energies[m][0])
        r = residual[m]
        if later:
            d = r + beta * old_direction[m]
            direction_out[m] = d
            step = direction_out[m, :, mine]
            solution_out[m] = old_solution[m] + alpha * step
        else:
            d = r
            solution_out[m] = alpha * residual[m, :, mine]
        r = r - alpha * (d + dot(vert_t[...], sd[...] * spread[at, :]))
        residual_out[m] = r
        packed[at, :] = sd[...] * dot(vert[...], r)
        scalars.append([total(r * r), total(r * d)])
    moved[...] = with_scalars(packed[0 : moved.shape[0], :], scalars).astype(BF16)


def increment_kernel(later, sd, vert, state, residual, *refs):
    before, direction, moved = refs[-3:]
    obs = lax.axis_index("obs")
    mine = pl.ds(pl.multiple_of(obs * LANES, LANES), LANES)
    for m in range(residual.shape[0]):
        d = residual[m, :, mine]
        if later:
            d = d + state[m, 2:3, 0:1] * refs[0][m, :, mine]
            before[m] = sd[...] * dot(vert[...], refs[1][m])
        else:
            before[m] = jnp.zeros_like(d)
        direction[m] = d
        moved[m] = sd[...] * dot(vert[...], d)


def last_kernel(parts, lev, *refs):
    pieces, refs = refs[:parts], refs[parts:]
    sd, vert_t, state, residual, before, direction, moved = refs[:7]
    increment_out, residual_out, spread = refs[7:]
    members, levp, unused = residual.shape
    obs = lax.axis_index("obs")
    mine = pl.ds(pl.multiple_of(obs * LANES, LANES), LANES)
    unpack(spread, add([x[...] for x in pieces]))
    energies = read_scalars(pieces, members, 1)
    for m in range(members):
        t = spread[m * lev : m * lev + levp, :]
        alpha = state[m, 0:1, 0:1] / (state[m, 1:2, 0:1] + energies[m][0])
        increment_out[:, m, :] = (before[m] + alpha * moved[m])[0:lev]
        r = residual[m, :, mine] - alpha * (direction[m] + dot(vert_t[...], sd[...] * t))
        residual_out[:, m, :] = r[0:lev]


def per_device(
    n_slab,
    n_obs,
    innovation,
    obs_precision,
    seeds,
    col_sd,
    vert_factor,
    h_values,
    block_obs,
    block_col,
    entry_count,
):
    blocks, lev, profiles = innovation.shape
    members = seeds.shape[0]
    chips = n_slab // 2
    halves = n_slab // blocks
    width = profiles // halves
    colblocks = n_obs
    assert halves * blocks == n_slab and width % LANES == 0 and col_sd.shape[0] == 1
    assert chips & (chips - 1) == 0 and n_obs & (n_obs - 1) == 0
    levp = (lev + 1 + 15) // 16 * 16
    assert members <= 16 and members >= PIECES
    rows = (members * (lev + 1) + 15) // 16 * 16
    lanes = colblocks * LANES
    slab_field = (members, levp, lanes)
    slab_rows = (rows, lanes)
    half_rows = [struct((rows, lanes // 2), BF16)] * 2
    wide = rows + levp - lev + 7
    spread = pltpu.VMEM((wide // 8 * 8, lanes), F32)
    some = rows // 32 * 16
    rest = rows - some
    via = chips == 4
    if via:
        one, two = (0, some), (some, rest)
        plan = [(0, 0, rows), (1, 0, rows), (2, *one), (2, *two), (3, *one), (3, *two)]
        sends = [(3, *one), (2, *two), (3, *two), (1, *one), (1, *two), (0, 0, rows), (2, *one)]
    else:
        sends = plan = [(i, 0, rows) for i in range(chips)]
    pad = ((0, levp - lev), (0, levp - lev))
    high = lax.reduce_precision(vert_factor, 8, 7)
    low = vert_factor - high
    vert, vert_t = [
        jnp.concatenate([jnp.pad(x, pad).astype(BF16) for x in parts], axis=1)
        for parts in ((high, high, low), (high.T, high.T, low.T))
    ]
    h_block = h_values.reshape(h_values.shape[2:])
    innovation = jnp.transpose(innovation, (1, 0, 2))
    obs_precision = jnp.transpose(obs_precision, (1, 0, 2))
    product = n_slab * width * lanes * rows
    small = 12 * rows * levp * LANES
    plane_bits = [1 << k for k in range(n_obs.bit_length() - 1)]

    def along(x, i):
        return lax.ppermute(x, "slab", [(s, s ^ (2 * i)) for s in range(n_slab)])

    def plane(x, i):
        return lax.ppermute(x, "obs", [(o, o ^ i) for o in range(n_obs)])

    def swap(x):
        return lax.ppermute(x, "slab", [(s, s ^ 1) for s in range(n_slab)])

    def plane_sum(halves, staged):
        halves = list(halves)
        moved_halves = [None] * len(halves)
        for step, bit in enumerate(plane_bits):
            bits = [bit, plane_bits[len(plane_bits) - 1 - step]]
            for at in range(0, len(halves), 2):
                if step > 0:
                    one, two = halves[at : at + 2]
                    one_more, two_more = moved_halves[at : at + 2]
                    halves[at : at + 2] = call(
                        functools.partial(add_halves_kernel, members, 0 if staged else 1),
                        [struct(one.shape, BF16)] * 2,
                        [],
                        0,
                        one,
                        one_more,
                        two,
                        two_more,
                    )
                for half in range(2):
                    moved_halves[at + half] = plane(halves[at + half], bits[half])
            if step == 0 and staged:
                halves[:] = call(
                    stage_kernel,
                    [struct(x.shape, BF16) for x in halves],
                    [pltpu.SemaphoreType.DMA((len(halves),))],
                    0,
                    *halves,
                    space=HBM,
                )
        return [x for pair in zip(halves, moved_halves) for x in pair]

    def line_sum(moved, other):
        shapes = [(count, width) for i, unused, count in sends]
        mine = call(
            functools.partial(forward_kernel, sends, members),
            [struct(shape, F32) for shape in shapes],
            [],
            product,
            moved,
            own,
        )
        ys = call(
            functools.partial(forward_kernel, sends, members),
            [
                struct(shape, F32 if i == 0 or (via and at == 6) else BF16)
                for at, ((i, *unused), shape) in enumerate(zip(sends, shapes))
            ],
            [],
            product,
            other,
            partner,
            moved,
            *mine,
        )
        if not via:
            return [y if i == 0 else along(y, i) for i, y in enumerate(ys)], [(0, rows)] * chips
        passed, far_rest, last_rest, next_some, next_rest, near, far = ys
        passed = along(passed, 1)
        far_rest, last_rest = along(far_rest, 2), along(last_rest, 3)
        next_some, next_rest = along(next_some, 1), along(next_rest, 1)
        (far,) = call(
            functools.partial(add_kernel, members, 0),
            [struct((some, width), BF16)],
            [],
            0,
            far,
            passed,
        )
        ys = [near, far_rest, last_rest, next_some, next_rest, along(far, 2)]
        return ys, [(0, rows), two, two, one, two, one]

    def line_gather(w, *parts):
        if not via:
            return [w if i == 0 else along(w, i) for i in range(chips)]
        some_w, rest_w = parts
        far = along(some_w, 2)
        far_rest, last_rest, next_ = along(rest_w, 2), along(rest_w, 3), along(w, 1)
        return [w, next_, far, far_rest, along(far, 1), last_rest]

    dense = struct((chips, colblocks, LANES, width), BF16)
    own, for_partner, *partials = call(
        functools.partial(start_kernel, (chips, halves, blocks, lev)),
        [dense, dense] + half_rows,
        [
            pltpu.SMEM(seeds.shape, jnp.int32),
            pltpu.SMEM(block_obs.shape, jnp.int32),
            pltpu.SMEM(block_col.shape, jnp.int32),
            pltpu.SMEM(entry_count.shape, jnp.int32),
            pltpu.VMEM(col_sd.shape, F32),
            pltpu.VMEM((profiles // LANES, levp * blocks, LANES), F32),
            pltpu.VMEM((profiles // LANES, levp * blocks, LANES), F32),
            pltpu.VMEM((n_slab, levp, width), jnp.int32),
            pltpu.VMEM((n_slab // 2, members, levp, width), F32),
            pltpu.VMEM((2, rows, 2 * width), F32),
            pltpu.VMEM((rows, lanes), F32),
            pltpu.SemaphoreType.DMA((5 + 2 * (profiles // LANES),)),
            pltpu.SemaphoreType.DMA((h_block.shape[0] * halves,)),
        ],
        2 * product,
        seeds,
        block_obs,
        block_col,
        entry_count,
        col_sd,
        innovation.reshape(lev * blocks, profiles),
        obs_precision.reshape(lev * blocks, profiles),
        h_block,
        space=HBM,
        limit=60,
    )
    ps = plane_sum(partials, True)
    partner = swap(for_partner)
    (precision,) = call(
        functools.partial(precision_kernel, halves, members),
        [struct((rows, width), F32)],
        [],
        0,
        obs_precision,
    )
    slab_sd, residual, moved = call(
        functools.partial(first_kernel, lev),
        [struct((1, lanes), F32), struct(slab_field, F32), struct(slab_rows, BF16)],
        [spread, spread],
        small * colblocks,
        *ps,
        vert,
        vert_t,
    )
    direction = total_step = image = state = None
    for sweep in range(ITERS):
        later, last = sweep > 0, sweep == ITERS - 1
        ys, spans = line_sum(moved, swap(moved))
        state, *weighted = call(
            functools.partial(weigh_kernel, later, last, members, lev, spans),
            [struct((members, 8, LANES), F32)]
            + [struct((n, width), BF16) for n in ((rows, some, rest) if via else (rows,))]
            + ([] if last else [struct((rows, width), F32)]),
            [],
            0,
            *ys,
            precision,
            *([image, state] if later else []),
        )
        if not last:
            *weighted, image = weighted
        ws = line_gather(*weighted)
        (theirs,) = call(
            functools.partial(adjoint_kernel, plan, members),
            [struct(slab_rows, BF16)],
            [],
            product,
            *ws,
            partner,
        )
        theirs = swap(theirs)
        (mine,) = call(
            functools.partial(adjoint_kernel, plan, members),
            [struct(slab_rows, F32)],
            [],
            product,
            *ws,
            own,
        )
        known = [vert, vert_t, state, residual]
        if later:
            known += [direction, total_step]
        if last:
            ps = call(
                functools.partial(combine_columns_kernel, members),
                [struct((rows, LANES), BF16)] * n_obs,
                [],
                0,
                mine,
                theirs,
            )
            ps = [ps[0]] + [plane(ps[i], i) for i in reversed(range(1, n_obs))]
            own_field = struct((members, levp, LANES), F32)
            before, d, u_d = call(
                functools.partial(increment_kernel, later),
                [own_field] * 3,
                [],
                small,
                col_sd,
                vert,
                state,
                residual,
                *([direction, total_step] if later else []),
            )
            outputs = call(
                functools.partial(last_kernel, len(ps), lev),
                [struct((lev, members, LANES), F32)] * 2,
                [pltpu.VMEM((wide // 8 * 8, LANES), F32)],
                small,
                *ps,
                col_sd,
                vert_t,
                state,
                residual,
                before,
                d,
                u_d,
            )
            break
        ps = call(
            functools.partial(combine_kernel, members), half_rows, [], 0, mine, theirs
        )
        ps = plane_sum(ps, False)
        outs = [
            struct(slab_field, F32),
            struct((members, levp, LANES), F32),
            struct(slab_rows, BF16),
        ]
        if later:
            outs.append(struct(slab_field, F32))
        r, total_step, moved, *d = call(
            functools.partial(update_kernel, later, lev),
            outs,
            [spread, spread],
            small * colblocks,
            *ps,
            slab_sd,
            *known,
        )
        direction, residual = (d[0] if later else residual), r
    return tuple(jnp.transpose(x, (1, 0, 2))[None] for x in outputs)


def solution(mesh):
    return jax.shard_map(
        functools.partial(per_device, mesh.shape["slab"], mesh.shape["obs"]),
        mesh=mesh,
        in_specs=(
            P("obs", None, None),
            P("obs", None, None),
            P(),
            P(("slab", "obs"), None),
            P(),
            P("slab", "obs", None, None, None),
            P("slab", "obs", None),
            P("slab", "obs", None),
            P("slab", "obs"),
        ),
        out_specs=(P(("slab", "obs"), None, None, None), P(("slab", "obs"), None, None, None)),
        check_vma=False,
    )
```

```python
import functools

import jax
import jax.numpy as jnp
from jax import lax
from jax.experimental import pallas as pl
from jax.experimental.pallas import tpu as pltpu
from jax.sharding import PartitionSpec as P

ITERS = 2
LANES = 128
PIECES = 3
PRIME = 32749
VMEM = pl.BlockSpec(memory_space=pltpu.VMEM)
HBM = pl.BlockSpec(memory_space=pltpu.HBM)
F32 = jnp.float32
BF16 = jnp.bfloat16
NT = (((1,), (1,)), ((), ()))


def call(kernel, outs, scratch, flops, *args, space=VMEM, limit=24, stored=0):
    nbytes = sum(a.size * a.dtype.itemsize for a in (*args, *outs))
    return pl.pallas_call(
        kernel,
        out_shape=outs,
        in_specs=[space] * len(args),
        out_specs=[HBM] * stored + [VMEM] * (len(outs) - stored),
        scratch_shapes=scratch,
        compiler_params=pltpu.CompilerParams(vmem_limit_bytes=limit * 1024 * 1024),
        cost_estimate=pl.CostEstimate(flops=flops, bytes_accessed=nbytes, transcendentals=0),
    )(*args)


def struct(shape, dtype):
    return jax.ShapeDtypeStruct(shape, dtype)


def place():
    slab = lax.axis_index("slab")
    return slab // 2, slab % 2, lax.axis_index("obs")


def add(parts):
    value = parts[0].astype(F32)
    for part in parts[1:]:
        value = value + part.astype(F32)
    return value


def dot(matrix, x):
    high = x.astype(BF16)
    rest = (x - high.astype(F32)).astype(BF16)
    x = jnp.concatenate([high, rest, high], axis=0)
    return jnp.dot(matrix, x, preferred_element_type=F32)


def total(x):
    return jnp.sum(jnp.sum(x, axis=0, keepdims=True), axis=1, keepdims=True)


def with_scalars(body, values):
    count = body.shape[0]
    tail = body[count - 16 :]
    sub = lax.broadcasted_iota(jnp.int32, tail.shape, 0) - (16 - len(values))
    lanes = lax.broadcasted_iota(jnp.int32, tail.shape, 1)
    line = jnp.zeros(tail.shape, F32)
    for m, member in enumerate(values):
        for q, value in enumerate(member):
            rest = value
            for piece in range(PIECES):
                part = rest.astype(BF16).astype(F32)
                rest = rest - part
                line = jnp.where((sub == m) & (lanes == q * PIECES + piece), part, line)
    return jnp.concatenate([body[: count - 16], jnp.where(sub >= 0, line, tail)], axis=0)


def read_scalars(refs, members, count):
    tail = add([ref[ref.shape[0] - 16 :, 0:LANES] for ref in refs])
    sub = lax.broadcasted_iota(jnp.int32, tail.shape, 0) - (16 - members)
    lanes = lax.broadcasted_iota(jnp.int32, tail.shape, 1)
    return [
        [
            total(
                jnp.where(
                    (sub == m) & (lanes >= q * PIECES) & (lanes < (q + 1) * PIECES), tail, 0.0
                )
            )
            for q in range(count)
        ]
        for m in range(members)
    ]


def by_member(values, shape, lev):
    rows = lax.broadcasted_iota(jnp.int32, shape, 0)
    out = jnp.zeros(shape, F32)
    for m, value in enumerate(values):
        out = jnp.where((rows >= m * lev) & (rows < (m + 1) * lev), value, out)
    return out


def member_sums(x, members, lev):
    lines = jnp.sum(x, axis=1, keepdims=True)
    rows = lax.broadcasted_iota(jnp.int32, lines.shape, 0)
    return [
        jnp.sum(
            jnp.where((rows >= m * lev) & (rows < (m + 1) * lev), lines, 0.0),
            axis=0,
            keepdims=True,
        )
        for m in range(members)
    ]


def remainder(x, factor):
    return x - (x.astype(F32) * factor).astype(jnp.int32) * PRIME


def start_kernel(
    dims, seeds_in, ids_in, cols_in, count_in, sd_in, innov_in, prec_in, h, own_out, partner_out, *rest
):
    chips, halves, blocks, lev = dims
    outs = rest[:-15]
    seeds, ids, cols, count, sd, innov, prec, bases, hashed, scratch, acc = rest[-15:-4]
    own, partner, sems, h_sems = rest[-4:]
    z, core, obs = place()
    strips = innov.shape[0]
    profiles = strips * LANES
    colblocks, width = own.shape[1], own.shape[3]
    members, levp = hashed.shape[1], hashed.shape[2]
    rows = acc.shape[0]

    pairs = [(seeds_in, seeds), (ids_in, ids), (cols_in, cols), (count_in, count), (sd_in, sd)]
    small = [pltpu.make_async_copy(x, y, sems.at[i]) for i, (x, y) in enumerate(pairs)]
    for copy in small:
        copy.start()
    large = []
    for x, y in ((innov_in, innov), (prec_in, prec)):
        for t in range(strips):
            at = len(pairs) + len(large)
            large.append(
                pltpu.make_async_copy(
                    x.at[:, t * LANES : (t + 1) * LANES], y.at[t, 0 : lev * blocks, :], sems.at[at]
                )
            )
    for copy in large:
        copy.start()
    own[...] = jnp.zeros_like(own)
    partner[...] = jnp.zeros_like(partner)
    scratch[...] = jnp.zeros_like(scratch)
    order = [(source, zz) for source in range(2) for zz in range(chips)]
    shape = (levp, width)
    spot = lax.broadcasted_iota(jnp.int32, shape, 0) * profiles
    spot = spot + lax.broadcasted_iota(jnp.int32, shape, 1)

    def piece_at(at):
        source, zz = order[at]
        return 2 * zz + (core if source == 0 else 1 - core)

    for at in range(len(order)):
        piece = piece_at(at)
        first = (obs * blocks + piece // halves) * (lev * profiles) + (piece % halves) * width
        bases[at] = remainder(7919 * remainder(spot + first, 1.0 / PRIME), 1.0 / PRIME)
    for copy in small:
        copy.wait()

    def tile_copy(n, half, target):
        lanes = pl.ds(half * width, width)
        return pltpu.make_async_copy(h.at[n, :, lanes], target, h_sems.at[n * halves + half])

    def put(n, carry):
        for half in range(halves):
            piece, k = ids[0, 0, n] * halves + half, cols[0, 0, n]

            @pl.when(piece % 2 == core)
            def _():
                tile_copy(n, half, own.at[piece // 2, k]).start()

            @pl.when(piece % 2 != core)
            def _():
                tile_copy(n, half, partner.at[piece // 2, k]).start()

        return carry

    lax.fori_loop(0, count[0, 0], put, 0)

    starts = [lax.rem(seeds[m], PRIME) - PRIME for m in range(members)]
    low = (1.0 - 2.0**-21) / PRIME

    def draw(at, m):
        k0 = bases[at] + starts[m]
        k1 = remainder(k0 * k0 + 12345, 1.0 / PRIME)
        k2 = remainder(k1 * k1 + 2719, low)
        return jnp.where(k2 >= PRIME, k2 - PRIME, k2).astype(F32)

    early = len(order) // 2
    for at in range(early):
        for m in range(members):
            hashed[at, m] = draw(at, m)
    for copy in large:
        copy.wait()

    def arrive(n, carry):
        for half in range(halves):
            tile_copy(n, half, own.at[0, 0]).wait()
        return carry

    lax.fori_loop(0, count[0, 0], arrive, 0)
    kept = [
        pltpu.make_async_copy(x, y, sems.at[len(pairs) + len(large) + i])
        for i, (x, y) in enumerate(((partner, partner_out), (own, own_out)))
    ]
    for copy in kept:
        copy.start()

    for at in range(len(order)):
        source, zz = order[at]
        piece = piece_at(at)
        b = piece // halves
        strip = (piece % halves) * (width // LANES)
        p, d = [
            jnp.concatenate(
                [
                    x[strip + t, pl.ds(b, lev, stride=blocks), :]
                    for t in range(width // LANES)
                ],
                axis=1,
            )
            for x in (prec, innov)
        ]
        gain = 3.4 * p * lax.rsqrt(p)
        offset = p * d - 0.5 * gain
        gain = gain * (1.0 / PRIME)
        slot, side = at // 2 % 2, at % 2
        for m in range(members):
            k2 = hashed[at, m, 0:lev, :] if at < early else draw(at, m)[0:lev]
            scratch[slot, m * lev : (m + 1) * lev, side * width : (side + 1) * width] = (
                offset + gain * k2
            )
        if side == 0:
            continue
        tiles = own if source == 0 else partner
        tiles = [tiles[i].reshape(colblocks * LANES, width) for i in (zz - 1, zz)]
        part = lax.dot_general(
            scratch[slot].astype(BF16),
            jnp.concatenate(tiles, axis=1),
            NT,
            preferred_element_type=F32,
        )
        if at == 1:
            acc[...] = part
        else:
            acc[...] += part

    line = jnp.concatenate([sd[...]] * colblocks, axis=1)
    put_halves(outs, with_columns(acc[...], line, obs, members))
    for copy in kept:
        copy.wait()


def put_halves(outs, value):
    half = value.shape[1] // 2
    outs[0][...] = value[:, :half].astype(BF16)
    outs[1][...] = value[:, half:].astype(BF16)


def with_columns(body, line, obs, members):
    tail = body[body.shape[0] - 16 :]
    sub = lax.broadcasted_iota(jnp.int32, tail.shape, 0)
    mine = lax.broadcasted_iota(jnp.int32, tail.shape, 1) // LANES == obs
    rest = line
    for piece in range(PIECES):
        part = rest.astype(BF16).astype(F32)
        rest = rest - part
        tail = jnp.where((sub == 16 - PIECES + piece) & mine, part, tail)
    return jnp.concatenate([body[: body.shape[0] - 16], tail], axis=0)


def read_columns(body):
    tail = body[body.shape[0] - 16 :]
    sub = lax.broadcasted_iota(jnp.int32, tail.shape, 0)
    return jnp.sum(jnp.where(sub >= 16 - PIECES, tail, 0.0), axis=0, keepdims=True)


def precision_kernel(halves, members, prec, out):
    z, core, unused = place()
    piece = 2 * z + core
    lev, blocks, unused = prec.shape
    width = out.shape[1]
    block = lax.broadcasted_iota(jnp.int32, (lev, blocks, width), 1)
    if halves == 1:
        mine = prec[...]
    else:
        mine = prec[:, :, pl.ds(pl.multiple_of((piece % halves) * width, LANES), width)]
    out[...] = jnp.zeros_like(out)
    mine = jnp.sum(jnp.where(block == piece // halves, mine, 0.0), axis=1)
    for m in range(members):
        out[m * lev : (m + 1) * lev, :] = mine


def joined(pieces):
    one, one_more, two, two_more = [x[...] for x in pieces]
    return jnp.concatenate([add([one, one_more]), add([two, two_more])], axis=1)


def unpack(spread, value):
    count = value.shape[0]
    spread[0:count, :] = value
    spread[count:, :] = jnp.zeros((spread.shape[0] - count, value.shape[1]), F32)


def first_kernel(lev, *refs):
    vert, vert_t, sd_out, residual, moved, spread, packed = refs[4:]
    members, levp, unused = residual.shape
    t = joined(refs[:4])
    sd = read_columns(t)
    sd_out[...] = sd
    unpack(spread, t)
    scalars = []
    for m in range(members):
        at = slice(m * lev, m * lev + levp)
        r = dot(vert_t[...], sd * spread[at, :])
        residual[m] = r
        packed[at, :] = sd * dot(vert[...], r)
        scalars.append([total(r * r)])
    moved[...] = with_scalars(packed[0 : moved.shape[0], :], scalars).astype(BF16)


def add_kernel(members, scalars, *refs):
    parts, out = refs[:-1], refs[-1]
    value = add([x[...] for x in parts])
    if scalars:
        value = with_scalars(value, read_scalars(parts, members, scalars))
    out[...] = value.astype(BF16)


def add_halves_kernel(members, scalars, one, one_more, two, two_more, one_out, two_out):
    add_kernel(members, scalars, one, one_more, one_out)
    add_kernel(members, 0, two, two_more, two_out)


def stage_kernel(*refs):
    sems = refs[-1]
    count = len(refs) // 2
    copies = [
        pltpu.make_async_copy(refs[i], refs[count + i], sems.at[i]) for i in range(count)
    ]
    for copy in copies:
        copy.start()
    for copy in copies:
        copy.wait()


def forward_kernel(sends, members, x, tiles, *refs):
    z, core, obs = place()
    outs = refs[-len(sends) :]
    rows, lanes = x.shape
    width = tiles.shape[3]
    added = refs[1 : 1 + len(sends)] if len(refs) > len(sends) else [None] * len(sends)
    if added[0] is not None:
        scalars = read_scalars([refs[0], x], members, 2)
    for out, before, (chip, first, count) in zip(outs, added, sends):
        y = jnp.dot(
            x[first : first + count, :],
            tiles[z ^ chip].reshape(lanes, width),
            preferred_element_type=F32,
        )
        if before is not None:
            y = before[...] + y
            if first + count == rows:
                y = with_scalars(y, scalars)
        out[...] = y.astype(out.dtype)


def weigh_kernel(later, last, members, lev, spans, *refs):
    ys, refs = refs[: len(spans)], refs[len(spans) :]
    prec, old_image, old = refs[0], *(refs[1:3] if later else (None, None))
    state, *outs = refs[3 if later else 1 :]
    if not last:
        *outs, image = outs
    rows = prec.shape[0]
    cuts = sorted({first for first, count in spans}) + [rows]
    parts = []
    for low, high in zip(cuts, cuts[1:]):
        held = [
            ref[low - first : high - first, :]
            for ref, (first, count) in zip(ys, spans)
            if first <= low < first + count
        ]
        parts.append(add(held))
    y = parts[0] if len(parts) == 1 else jnp.concatenate(parts, axis=0)
    ends = [ref for ref, (first, count) in zip(ys, spans) if first + count == rows]
    sub = lax.broadcasted_iota(jnp.int32, (8, LANES), 0)
    betas = []
    for m, (norm, cross) in enumerate(read_scalars(ends, members, 2)):
        if later:
            old_norm, old_square = old[m, 0:1, 0:1], old[m, 1:2, 0:1]
            beta = norm / old_norm
            square = norm + 2.0 * beta * cross + beta * beta * old_square
        else:
            beta = jnp.zeros_like(norm)
            square = norm
        betas.append(beta)
        state[m] = jnp.where(sub == 0, norm, jnp.where(sub == 1, square, beta))
    if later:
        y = y + by_member(betas, (rows, 1), lev) * old_image[...]
    if not last:
        image[...] = y
    scaled = prec[...] * y
    energies = [[x] for x in member_sums(scaled * y, members, lev)]
    weighted = with_scalars(scaled, energies).astype(BF16)
    first = 0
    outs[0][...] = weighted
    for out in outs[1:]:
        out[...] = weighted[first : first + out.shape[0]]
        first += out.shape[0]


def adjoint_kernel(plan, members, *refs):
    z, core, obs = place()
    ws, tiles, out = refs[: len(plan)], refs[len(plan)], refs[len(plan) + 1]
    rows, lanes = out.shape
    width = ws[0].shape[1]
    acc = None
    for i in range(tiles.shape[0]):
        w = {first: ref for ref, (chip, first, count) in zip(ws, plan) if chip == i}
        w = [w[first][...] for first in sorted(w)]
        w = w[0] if len(w) == 1 else jnp.concatenate(w, axis=0)
        part = lax.dot_general(
            w, tiles[z ^ i].reshape(lanes, width), NT, preferred_element_type=F32
        )
        acc = part if i == 0 else acc + part
    ends = [ref for ref, (chip, first, count) in zip(ws, plan) if first + count == rows]
    out[...] = with_scalars(acc, read_scalars(ends, members, 1)).astype(out.dtype)


def combine_kernel(members, mine, theirs, *outs):
    value = mine[...] + theirs[...].astype(F32)
    put_halves(outs, with_scalars(value, read_scalars([mine, theirs], members, 1)))


def combine_columns_kernel(members, mine, theirs, *outs):
    obs = lax.axis_index("obs")
    energies = read_scalars([mine, theirs], members, 1)
    for i, out in enumerate(outs):
        lane = pl.ds(pl.multiple_of((obs ^ i) * LANES, LANES), LANES)
        value = mine[:, lane] + theirs[:, lane].astype(F32)
        out[...] = with_scalars(value, energies).astype(BF16)


def update_kernel(later, lev, *refs):
    pieces, refs = refs[:4], refs[4:]
    sd, vert, vert_t, state, residual = refs[:5]
    spread, packed = refs[-2:]
    if later:
        old_direction, old_solution, residual_out, solution_out, moved, direction_out = refs[5:-2]
    else:
        residual_out, solution_out, moved = refs[5:-2]
    members, levp, unused = residual.shape
    obs = lax.axis_index("obs")
    mine = pl.ds(pl.multiple_of(obs * LANES, LANES), LANES)
    unpack(spread, joined(pieces))
    energies = read_scalars(pieces[:2], members, 1)
    scalars = []
    for m in range(members):
        at = slice(m * lev, m * lev + levp)
        norm, square, beta = state[m, 0:1, 0:1], state[m, 1:2, 0:1], state[m, 2:3, 0:1]
        alpha = norm / (square + energies[m][0])
        r = residual[m]
        if later:
            d = r + beta * old_direction[m]
            direction_out[m] = d
            step = direction_out[m, :, mine]
            solution_out[m] = old_solution[m] + alpha * step
        else:
            d = r
            solution_out[m] = alpha * residual[m, :, mine]
        r = r - alpha * (d + dot(vert_t[...], sd[...] * spread[at, :]))
        residual_out[m] = r
        packed[at, :] = sd[...] * dot(vert[...], r)
        scalars.append([total(r * r), total(r * d)])
    moved[...] = with_scalars(packed[0 : moved.shape[0], :], scalars).astype(BF16)


def increment_kernel(later, sd, vert, state, residual, *refs):
    before, direction, moved = refs[-3:]
    obs = lax.axis_index("obs")
    mine = pl.ds(pl.multiple_of(obs * LANES, LANES), LANES)
    for m in range(residual.shape[0]):
        d = residual[m, :, mine]
        if later:
            d = d + state[m, 2:3, 0:1] * refs[0][m, :, mine]
            before[m] = sd[...] * dot(vert[...], refs[1][m])
        else:
            before[m] = jnp.zeros_like(d)
        direction[m] = d
        moved[m] = sd[...] * dot(vert[...], d)


def last_kernel(parts, lev, *refs):
    pieces, refs = refs[:parts], refs[parts:]
    sd, vert_t, state, residual, before, direction, moved = refs[:7]
    increment_out, residual_out, spread = refs[7:]
    members, levp, unused = residual.shape
    obs = lax.axis_index("obs")
    mine = pl.ds(pl.multiple_of(obs * LANES, LANES), LANES)
    unpack(spread, add([x[...] for x in pieces]))
    energies = read_scalars(pieces, members, 1)
    for m in range(members):
        t = spread[m * lev : m * lev + levp, :]
        alpha = state[m, 0:1, 0:1] / (state[m, 1:2, 0:1] + energies[m][0])
        increment_out[:, m, :] = (before[m] + alpha * moved[m])[0:lev]
        r = residual[m, :, mine] - alpha * (direction[m] + dot(vert_t[...], sd[...] * t))
        residual_out[:, m, :] = r[0:lev]


def per_device(
    n_slab,
    n_obs,
    innovation,
    obs_precision,
    seeds,
    col_sd,
    vert_factor,
    h_values,
    block_obs,
    block_col,
    entry_count,
):
    blocks, lev, profiles = innovation.shape
    members = seeds.shape[0]
    chips = n_slab // 2
    halves = n_slab // blocks
    width = profiles // halves
    colblocks = n_obs
    assert halves * blocks == n_slab and width % LANES == 0 and col_sd.shape[0] == 1
    assert chips & (chips - 1) == 0 and n_obs & (n_obs - 1) == 0
    levp = (lev + 1 + 15) // 16 * 16
    assert members <= 16 and members >= PIECES
    rows = (members * (lev + 1) + 15) // 16 * 16
    lanes = colblocks * LANES
    slab_field = (members, levp, lanes)
    slab_rows = (rows, lanes)
    half_rows = [struct((rows, lanes // 2), BF16)] * 2
    wide = rows + levp - lev + 7
    spread = pltpu.VMEM((wide // 8 * 8, lanes), F32)
    some = rows // 32 * 16
    rest = rows - some
    via = chips == 4
    if via:
        one, two = (0, some), (some, rest)
        plan = [(0, 0, rows), (1, 0, rows), (2, *one), (2, *two), (3, *one), (3, *two)]
        sends = [(3, *one), (2, *two), (3, *two), (1, *one), (1, *two), (0, 0, rows), (2, *one)]
    else:
        sends = plan = [(i, 0, rows) for i in range(chips)]
    pad = ((0, levp - lev), (0, levp - lev))
    high = lax.reduce_precision(vert_factor, 8, 7)
    low = vert_factor - high
    vert, vert_t = [
        jnp.concatenate([jnp.pad(x, pad).astype(BF16) for x in parts], axis=1)
        for parts in ((high, high, low), (high.T, high.T, low.T))
    ]
    h_block = h_values.reshape(h_values.shape[2:])
    innovation = jnp.transpose(innovation, (1, 0, 2))
    obs_precision = jnp.transpose(obs_precision, (1, 0, 2))
    product = n_slab * width * lanes * rows
    small = 12 * rows * levp * LANES
    plane_bits = [1 << k for k in range(n_obs.bit_length() - 1)]

    def along(x, i):
        return lax.ppermute(x, "slab", [(s, s ^ (2 * i)) for s in range(n_slab)])

    def plane(x, i):
        return lax.ppermute(x, "obs", [(o, o ^ i) for o in range(n_obs)])

    def swap(x):
        return lax.ppermute(x, "slab", [(s, s ^ 1) for s in range(n_slab)])

    def plane_sum(halves, staged):
        halves = list(halves)
        moved_halves = [None] * len(halves)
        for step, bit in enumerate(plane_bits):
            bits = [bit, plane_bits[len(plane_bits) - 1 - step]]
            for at in range(0, len(halves), 2):
                if step > 0:
                    one, two = halves[at : at + 2]
                    one_more, two_more = moved_halves[at : at + 2]
                    halves[at : at + 2] = call(
                        functools.partial(add_halves_kernel, members, 0 if staged else 1),
                        [struct(one.shape, BF16)] * 2,
                        [],
                        0,
                        one,
                        one_more,
                        two,
                        two_more,
                    )
                for half in range(2):
                    moved_halves[at + half] = plane(halves[at + half], bits[half])
            if step == 0 and staged:
                halves[:] = call(
                    stage_kernel,
                    [struct(x.shape, BF16) for x in halves],
                    [pltpu.SemaphoreType.DMA((len(halves),))],
                    0,
                    *halves,
                    space=HBM,
                )
        return [x for pair in zip(halves, moved_halves) for x in pair]

    def line_sum(moved, other):
        shapes = [(count, width) for i, unused, count in sends]
        mine = call(
            functools.partial(forward_kernel, sends, members),
            [struct(shape, F32) for shape in shapes],
            [],
            product,
            moved,
            own,
        )
        ys = call(
            functools.partial(forward_kernel, sends, members),
            [
                struct(shape, F32 if i == 0 or (via and at == 6) else BF16)
                for at, ((i, *unused), shape) in enumerate(zip(sends, shapes))
            ],
            [],
            product,
            other,
            partner,
            moved,
            *mine,
        )
        if not via:
            return [y if i == 0 else along(y, i) for i, y in enumerate(ys)], [(0, rows)] * chips
        passed, far_rest, last_rest, next_some, next_rest, near, far = ys
        passed = along(passed, 1)
        far_rest, last_rest = along(far_rest, 2), along(last_rest, 3)
        next_some, next_rest = along(next_some, 1), along(next_rest, 1)
        (far,) = call(
            functools.partial(add_kernel, members, 0),
            [struct((some, width), BF16)],
            [],
            0,
            far,
            passed,
        )
        ys = [near, far_rest, last_rest, next_some, next_rest, along(far, 2)]
        return ys, [(0, rows), two, two, one, two, one]

    def line_gather(w, *parts):
        if not via:
            return [w if i == 0 else along(w, i) for i in range(chips)]
        some_w, rest_w = parts
        far = along(some_w, 2)
        far_rest, last_rest, next_ = along(rest_w, 2), along(rest_w, 3), along(w, 1)
        return [w, next_, far, far_rest, along(far, 1), last_rest]

    dense = struct((chips, colblocks, LANES, width), BF16)
    own, for_partner, *partials = call(
        functools.partial(start_kernel, (chips, halves, blocks, lev)),
        [dense, dense] + half_rows,
        [
            pltpu.SMEM(seeds.shape, jnp.int32),
            pltpu.SMEM(block_obs.shape, jnp.int32),
            pltpu.SMEM(block_col.shape, jnp.int32),
            pltpu.SMEM(entry_count.shape, jnp.int32),
            pltpu.VMEM(col_sd.shape, F32),
            pltpu.VMEM((profiles // LANES, levp * blocks, LANES), F32),
            pltpu.VMEM((profiles // LANES, levp * blocks, LANES), F32),
            pltpu.VMEM((n_slab, levp, width), jnp.int32),
            pltpu.VMEM((n_slab // 2, members, levp, width), F32),
            pltpu.VMEM((2, rows, 2 * width), F32),
            pltpu.VMEM((rows, lanes), F32),
            pltpu.VMEM(dense.shape, BF16),
            pltpu.VMEM(dense.shape, BF16),
            pltpu.SemaphoreType.DMA((7 + 2 * (profiles // LANES),)),
            pltpu.SemaphoreType.DMA((h_block.shape[0] * halves,)),
        ],
        2 * product,
        seeds,
        block_obs,
        block_col,
        entry_count,
        col_sd,
        innovation.reshape(lev * blocks, profiles),
        obs_precision.reshape(lev * blocks, profiles),
        h_block,
        space=HBM,
        limit=60,
        stored=2,
    )
    ps = plane_sum(partials, True)
    partner = swap(for_partner)
    (precision,) = call(
        functools.partial(precision_kernel, halves, members),
        [struct((rows, width), F32)],
        [],
        0,
        obs_precision,
    )
    slab_sd, residual, moved = call(
        functools.partial(first_kernel, lev),
        [struct((1, lanes), F32), struct(slab_field, F32), struct(slab_rows, BF16)],
        [spread, spread],
        small * colblocks,
        *ps,
        vert,
        vert_t,
    )
    direction = total_step = image = state = None
    for sweep in range(ITERS):
        later, last = sweep > 0, sweep == ITERS - 1
        ys, spans = line_sum(moved, swap(moved))
        state, *weighted = call(
            functools.partial(weigh_kernel, later, last, members, lev, spans),
            [struct((members, 8, LANES), F32)]
            + [struct((n, width), BF16) for n in ((rows, some, rest) if via else (rows,))]
            + ([] if last else [struct((rows, width), F32)]),
            [],
            0,
            *ys,
            precision,
            *([image, state] if later else []),
        )
        if not last:
            *weighted, image = weighted
        ws = line_gather(*weighted)
        (theirs,) = call(
            functools.partial(adjoint_kernel, plan, members),
            [struct(slab_rows, BF16)],
            [],
            product,
            *ws,
            partner,
        )
        theirs = swap(theirs)
        (mine,) = call(
            functools.partial(adjoint_kernel, plan, members),
            [struct(slab_rows, F32)],
            [],
            product,
            *ws,
            own,
        )
        known = [vert, vert_t, state, residual]
        if later:
            known += [direction, total_step]
        if last:
            ps = call(
                functools.partial(combine_columns_kernel, members),
                [struct((rows, LANES), BF16)] * n_obs,
                [],
                0,
                mine,
                theirs,
            )
            ps = [ps[0]] + [plane(ps[i], i) for i in reversed(range(1, n_obs))]
            own_field = struct((members, levp, LANES), F32)
            before, d, u_d = call(
                functools.partial(increment_kernel, later),
                [own_field] * 3,
                [],
                small,
                col_sd,
                vert,
                state,
                residual,
                *([direction, total_step] if later else []),
            )
            outputs = call(
                functools.partial(last_kernel, len(ps), lev),
                [struct((lev, members, LANES), F32)] * 2,
                [pltpu.VMEM((wide // 8 * 8, LANES), F32)],
                small,
                *ps,
                col_sd,
                vert_t,
                state,
                residual,
                before,
                d,
                u_d,
            )
            break
        ps = call(
            functools.partial(combine_kernel, members), half_rows, [], 0, mine, theirs
        )
        ps = plane_sum(ps, False)
        outs = [
            struct(slab_field, F32),
            struct((members, levp, LANES), F32),
            struct(slab_rows, BF16),
        ]
        if later:
            outs.append(struct(slab_field, F32))
        r, total_step, moved, *d = call(
            functools.partial(update_kernel, later, lev),
            outs,
            [spread, spread],
            small * colblocks,
            *ps,
            slab_sd,
            *known,
        )
        direction, residual = (d[0] if later else residual), r
    return tuple(jnp.transpose(x, (1, 0, 2))[None] for x in outputs)


def solution(mesh):
    return jax.shard_map(
        functools.partial(per_device, mesh.shape["slab"], mesh.shape["obs"]),
        mesh=mesh,
        in_specs=(
            P("obs", None, None),
            P("obs", None, None),
            P(),
            P(("slab", "obs"), None),
            P(),
            P("slab", "obs", None, None, None),
            P("slab", "obs", None),
            P("slab", "obs", None),
            P("slab", "obs"),
        ),
        out_specs=(P(("slab", "obs"), None, None, None), P(("slab", "obs"), None, None, None)),
        check_vma=False,
    )
```

```python
import functools

import jax
import jax.numpy as jnp
from jax import lax
from jax.experimental import pallas as pl
from jax.experimental.pallas import tpu as pltpu
from jax.sharding import PartitionSpec as P

ITERS = 2
LANES = 128
PIECES = 3
PRIME = 32749
VMEM = pl.BlockSpec(memory_space=pltpu.VMEM)
HBM = pl.BlockSpec(memory_space=pltpu.HBM)
F32 = jnp.float32
BF16 = jnp.bfloat16
NT = (((1,), (1,)), ((), ()))


def call(kernel, outs, scratch, flops, *args, space=VMEM, limit=24, stored=0):
    nbytes = sum(a.size * a.dtype.itemsize for a in (*args, *outs))
    return pl.pallas_call(
        kernel,
        out_shape=outs,
        in_specs=[space] * len(args),
        out_specs=[HBM] * stored + [VMEM] * (len(outs) - stored),
        scratch_shapes=scratch,
        compiler_params=pltpu.CompilerParams(vmem_limit_bytes=limit * 1024 * 1024),
        cost_estimate=pl.CostEstimate(flops=flops, bytes_accessed=nbytes, transcendentals=0),
    )(*args)


def struct(shape, dtype):
    return jax.ShapeDtypeStruct(shape, dtype)


def place():
    slab = lax.axis_index("slab")
    return slab // 2, slab % 2, lax.axis_index("obs")


def add(parts):
    value = parts[0].astype(F32)
    for part in parts[1:]:
        value = value + part.astype(F32)
    return value


def dot(matrix, x):
    high = x.astype(BF16)
    rest = (x - high.astype(F32)).astype(BF16)
    x = jnp.concatenate([high, rest, high], axis=0)
    return jnp.dot(matrix, x, preferred_element_type=F32)


def total(x):
    return jnp.sum(jnp.sum(x, axis=0, keepdims=True), axis=1, keepdims=True)


def with_scalars(body, values):
    count = body.shape[0]
    tail = body[count - 16 :]
    sub = lax.broadcasted_iota(jnp.int32, tail.shape, 0) - (16 - len(values))
    lanes = lax.broadcasted_iota(jnp.int32, tail.shape, 1)
    line = jnp.zeros(tail.shape, F32)
    for m, member in enumerate(values):
        for q, value in enumerate(member):
            rest = value
            for piece in range(PIECES):
                part = rest.astype(BF16).astype(F32)
                rest = rest - part
                line = jnp.where((sub == m) & (lanes == q * PIECES + piece), part, line)
    return jnp.concatenate([body[: count - 16], jnp.where(sub >= 0, line, tail)], axis=0)


def read_scalars(refs, members, count):
    tail = add([ref[ref.shape[0] - 16 :, 0:LANES] for ref in refs])
    sub = lax.broadcasted_iota(jnp.int32, tail.shape, 0) - (16 - members)
    lanes = lax.broadcasted_iota(jnp.int32, tail.shape, 1)
    return [
        [
            total(
                jnp.where(
                    (sub == m) & (lanes >= q * PIECES) & (lanes < (q + 1) * PIECES), tail, 0.0
                )
            )
            for q in range(count)
        ]
        for m in range(members)
    ]


def by_member(values, shape, lev):
    rows = lax.broadcasted_iota(jnp.int32, shape, 0)
    out = jnp.zeros(shape, F32)
    for m, value in enumerate(values):
        out = jnp.where((rows >= m * lev) & (rows < (m + 1) * lev), value, out)
    return out


def member_sums(x, members, lev):
    lines = jnp.sum(x, axis=1, keepdims=True)
    rows = lax.broadcasted_iota(jnp.int32, lines.shape, 0)
    return [
        jnp.sum(
            jnp.where((rows >= m * lev) & (rows < (m + 1) * lev), lines, 0.0),
            axis=0,
            keepdims=True,
        )
        for m in range(members)
    ]


def remainder(x, factor):
    return x - (x.astype(F32) * factor).astype(jnp.int32) * PRIME


def start_kernel(
    dims, seeds_in, ids_in, cols_in, count_in, sd_in, innov_in, prec_in, h, own_out, partner_out, *rest
):
    chips, halves, blocks, lev = dims
    outs = rest[:-15]
    seeds, ids, cols, count, sd, innov, prec, bases, hashed, scratch, acc = rest[-15:-4]
    own, partner, sems, h_sems = rest[-4:]
    z, core, obs = place()
    strips = innov.shape[0]
    profiles = strips * LANES
    colblocks, width = own.shape[1], own.shape[3]
    members, levp = hashed.shape[1], hashed.shape[2]
    rows = acc.shape[0]

    pairs = [(seeds_in, seeds), (ids_in, ids), (cols_in, cols), (count_in, count), (sd_in, sd)]
    small = [pltpu.make_async_copy(x, y, sems.at[i]) for i, (x, y) in enumerate(pairs)]
    for copy in small:
        copy.start()
    large = []
    for x, y in ((innov_in, innov), (prec_in, prec)):
        for t in range(strips):
            at = len(pairs) + len(large)
            large.append(
                pltpu.make_async_copy(
                    x.at[:, t * LANES : (t + 1) * LANES], y.at[t, 0 : lev * blocks, :], sems.at[at]
                )
            )
    for copy in large:
        copy.start()
    own[...] = jnp.zeros_like(own)
    partner[...] = jnp.zeros_like(partner)
    scratch[...] = jnp.zeros_like(scratch)
    order = [(source, zz) for source in range(2) for zz in range(chips)]
    shape = (levp, width)
    spot = lax.broadcasted_iota(jnp.int32, shape, 0) * profiles
    spot = spot + lax.broadcasted_iota(jnp.int32, shape, 1)

    def piece_at(at):
        source, zz = order[at]
        return 2 * zz + (core if source == 0 else 1 - core)

    for at in range(len(order)):
        piece = piece_at(at)
        first = (obs * blocks + piece // halves) * (lev * profiles) + (piece % halves) * width
        bases[at] = remainder(7919 * remainder(spot + first, 1.0 / PRIME), 1.0 / PRIME)
    for copy in small:
        copy.wait()

    def tile_copy(n, half, target):
        lanes = pl.ds(half * width, width)
        return pltpu.make_async_copy(h.at[n, :, lanes], target, h_sems.at[n * halves + half])

    def put(n, carry):
        for half in range(halves):
            piece, k = ids[0, 0, n] * halves + half, cols[0, 0, n]

            @pl.when(piece % 2 == core)
            def _():
                tile_copy(n, half, own.at[piece // 2, k]).start()

            @pl.when(piece % 2 != core)
            def _():
                tile_copy(n, half, partner.at[piece // 2, k]).start()

        return carry

    lax.fori_loop(0, count[0, 0], put, 0)

    starts = [lax.rem(seeds[m], PRIME) - PRIME for m in range(members)]
    low = (1.0 - 2.0**-21) / PRIME

    def draw(at, m):
        k0 = bases[at] + starts[m]
        k1 = remainder(k0 * k0 + 12345, 1.0 / PRIME)
        k2 = remainder(k1 * k1 + 2719, low)
        return jnp.where(k2 >= PRIME, k2 - PRIME, k2).astype(F32)

    early = len(order) // 2
    for at in range(early):
        for m in range(members):
            hashed[at, m] = draw(at, m)
    for copy in large:
        copy.wait()

    def arrive(n, carry):
        for half in range(halves):
            tile_copy(n, half, own.at[0, 0]).wait()
        return carry

    lax.fori_loop(0, count[0, 0], arrive, 0)
    kept = [
        pltpu.make_async_copy(x, y, sems.at[len(pairs) + len(large) + i])
        for i, (x, y) in enumerate(((partner, partner_out), (own, own_out)))
    ]
    for copy in kept:
        copy.start()

    for at in range(len(order)):
        source, zz = order[at]
        piece = piece_at(at)
        b = piece // halves
        strip = (piece % halves) * (width // LANES)
        p, d = [
            jnp.concatenate(
                [
                    x[strip + t, pl.ds(b, lev, stride=blocks), :]
                    for t in range(width // LANES)
                ],
                axis=1,
            )
            for x in (prec, innov)
        ]
        gain = 3.4 * p * lax.rsqrt(p)
        offset = p * d - 0.5 * gain
        gain = gain * (1.0 / PRIME)
        slot, side = at // 2 % 2, at % 2
        for m in range(members):
            k2 = hashed[at, m, 0:lev, :] if at < early else draw(at, m)[0:lev]
            scratch[slot, m * lev : (m + 1) * lev, side * width : (side + 1) * width] = (
                offset + gain * k2
            )
        if side == 0:
            continue
        tiles = own if source == 0 else partner
        tiles = [tiles[i].reshape(colblocks * LANES, width) for i in (zz - 1, zz)]
        part = lax.dot_general(
            scratch[slot].astype(BF16),
            jnp.concatenate(tiles, axis=1),
            NT,
            preferred_element_type=F32,
        )
        if at == 1:
            acc[...] = part
        else:
            acc[...] += part

    line = jnp.concatenate([sd[...]] * colblocks, axis=1)
    put_halves(outs, with_columns(acc[...], line, obs, members))
    for copy in kept:
        copy.wait()


def put_halves(outs, value):
    half = value.shape[1] // 2
    outs[0][...] = value[:, :half].astype(BF16)
    outs[1][...] = value[:, half:].astype(BF16)


def with_columns(body, line, obs, members):
    tail = body[body.shape[0] - 16 :]
    sub = lax.broadcasted_iota(jnp.int32, tail.shape, 0)
    mine = lax.broadcasted_iota(jnp.int32, tail.shape, 1) // LANES == obs
    rest = line
    for piece in range(PIECES):
        part = rest.astype(BF16).astype(F32)
        rest = rest - part
        tail = jnp.where((sub == 16 - PIECES + piece) & mine, part, tail)
    return jnp.concatenate([body[: body.shape[0] - 16], tail], axis=0)


def read_columns(body):
    tail = body[body.shape[0] - 16 :]
    sub = lax.broadcasted_iota(jnp.int32, tail.shape, 0)
    return jnp.sum(jnp.where(sub >= 16 - PIECES, tail, 0.0), axis=0, keepdims=True)


def precision_kernel(halves, members, prec, out):
    z, core, unused = place()
    piece = 2 * z + core
    lev, blocks, unused = prec.shape
    width = out.shape[1]
    block = lax.broadcasted_iota(jnp.int32, (lev, blocks, width), 1)
    if halves == 1:
        mine = prec[...]
    else:
        mine = prec[:, :, pl.ds(pl.multiple_of((piece % halves) * width, LANES), width)]
    out[...] = jnp.zeros_like(out)
    mine = jnp.sum(jnp.where(block == piece // halves, mine, 0.0), axis=1)
    for m in range(members):
        out[m * lev : (m + 1) * lev, :] = mine


def joined(pieces):
    one, one_more, two, two_more = [x[...] for x in pieces]
    return jnp.concatenate([add([one, one_more]), add([two, two_more])], axis=1)


def unpack(spread, value):
    count = value.shape[0]
    spread[0:count, :] = value
    spread[count:, :] = jnp.zeros((spread.shape[0] - count, value.shape[1]), F32)


def first_kernel(lev, *refs):
    vert, vert_t, sd_out, residual, moved, spread, packed = refs[4:]
    members, levp, unused = residual.shape
    t = joined(refs[:4])
    sd = read_columns(t)
    sd_out[...] = sd
    unpack(spread, t)
    scalars = []
    for m in range(members):
        at = slice(m * lev, m * lev + levp)
        r = dot(vert_t[...], sd * spread[at, :])
        residual[m] = r
        packed[at, :] = sd * dot(vert[...], r)
        scalars.append([total(r * r)])
    moved[...] = with_scalars(packed[0 : moved.shape[0], :], scalars).astype(BF16)


def add_kernel(members, scalars, *refs):
    parts, out = refs[:-1], refs[-1]
    value = add([x[...] for x in parts])
    if scalars:
        value = with_scalars(value, read_scalars(parts, members, scalars))
    out[...] = value.astype(BF16)


def add_halves_kernel(members, scalars, one, one_more, two, two_more, one_out, two_out):
    add_kernel(members, scalars, one, one_more, one_out)
    add_kernel(members, 0, two, two_more, two_out)


def stage_kernel(*refs):
    sems = refs[-1]
    count = len(refs) // 2
    copies = [
        pltpu.make_async_copy(refs[i], refs[count + i], sems.at[i]) for i in range(count)
    ]
    for copy in copies:
        copy.start()
    for copy in copies:
        copy.wait()


def forward_kernel(sends, members, x, tiles, *refs):
    z, core, obs = place()
    outs = refs[-len(sends) :]
    rows, lanes = x.shape
    width = tiles.shape[3]
    added = refs[1 : 1 + len(sends)] if len(refs) > len(sends) else [None] * len(sends)
    if added[0] is not None:
        scalars = read_scalars([refs[0], x], members, 2)
    for out, before, (chip, first, count) in zip(outs, added, sends):
        y = jnp.dot(
            x[first : first + count, :],
            tiles[z ^ chip].reshape(lanes, width),
            preferred_element_type=F32,
        )
        if before is not None:
            y = before[...] + y
            if first + count == rows:
                y = with_scalars(y, scalars)
        out[...] = y.astype(out.dtype)


def weigh_kernel(later, last, members, lev, spans, *refs):
    ys, refs = refs[: len(spans)], refs[len(spans) :]
    prec, old_image, old = refs[0], *(refs[1:3] if later else (None, None))
    state, *outs = refs[3 if later else 1 :]
    if not last:
        *outs, image = outs
    rows = prec.shape[0]
    cuts = sorted({first for first, count in spans}) + [rows]
    parts = []
    for low, high in zip(cuts, cuts[1:]):
        held = [
            ref[low - first : high - first, :]
            for ref, (first, count) in zip(ys, spans)
            if first <= low < first + count
        ]
        parts.append(add(held))
    y = parts[0] if len(parts) == 1 else jnp.concatenate(parts, axis=0)
    ends = [ref for ref, (first, count) in zip(ys, spans) if first + count == rows]
    sub = lax.broadcasted_iota(jnp.int32, (8, LANES), 0)
    betas = []
    for m, (norm, cross) in enumerate(read_scalars(ends, members, 2)):
        if later:
            old_norm, old_square = old[m, 0:1, 0:1], old[m, 1:2, 0:1]
            beta = norm / old_norm
            square = norm + 2.0 * beta * cross + beta * beta * old_square
        else:
            beta = jnp.zeros_like(norm)
            square = norm
        betas.append(beta)
        state[m] = jnp.where(sub == 0, norm, jnp.where(sub == 1, square, beta))
    if later:
        y = y + by_member(betas, (rows, 1), lev) * old_image[...]
    if not last:
        image[...] = y
    scaled = prec[...] * y
    energies = [[x] for x in member_sums(scaled * y, members, lev)]
    weighted = with_scalars(scaled, energies).astype(BF16)
    first = 0
    for out in outs:
        out[...] = weighted[first : first + out.shape[0]]
        first = (first + out.shape[0]) % rows


def adjoint_kernel(plan, members, *refs):
    z, core, obs = place()
    ws, tiles, out = refs[: len(plan)], refs[len(plan)], refs[len(plan) + 1]
    rows, lanes = out.shape
    width = ws[0].shape[1]
    acc = None
    for i in range(tiles.shape[0]):
        w = {first: ref for ref, (chip, first, count) in zip(ws, plan) if chip == i}
        w = [w[first][...] for first in sorted(w)]
        w = w[0] if len(w) == 1 else jnp.concatenate(w, axis=0)
        part = lax.dot_general(
            w, tiles[z ^ i].reshape(lanes, width), NT, preferred_element_type=F32
        )
        acc = part if i == 0 else acc + part
    ends = [ref for ref, (chip, first, count) in zip(ws, plan) if first + count == rows]
    out[...] = with_scalars(acc, read_scalars(ends, members, 1)).astype(out.dtype)


def combine_kernel(members, mine, theirs, *outs):
    value = mine[...] + theirs[...].astype(F32)
    put_halves(outs, with_scalars(value, read_scalars([mine, theirs], members, 1)))


def combine_columns_kernel(members, mine, theirs, *outs):
    obs = lax.axis_index("obs")
    energies = read_scalars([mine, theirs], members, 1)
    for i, out in enumerate(outs):
        lane = pl.ds(pl.multiple_of((obs ^ i) * LANES, LANES), LANES)
        value = mine[:, lane] + theirs[:, lane].astype(F32)
        out[...] = with_scalars(value, energies).astype(BF16)


def update_kernel(later, lev, *refs):
    pieces, refs = refs[:4], refs[4:]
    sd, vert, vert_t, state, residual = refs[:5]
    spread, packed = refs[-2:]
    if later:
        old_direction, old_solution, residual_out, solution_out, moved, direction_out = refs[5:-2]
    else:
        residual_out, solution_out, moved = refs[5:-2]
    members, levp, unused = residual.shape
    obs = lax.axis_index("obs")
    mine = pl.ds(pl.multiple_of(obs * LANES, LANES), LANES)
    unpack(spread, joined(pieces))
    energies = read_scalars(pieces[:2], members, 1)
    scalars = []
    for m in range(members):
        at = slice(m * lev, m * lev + levp)
        norm, square, beta = state[m, 0:1, 0:1], state[m, 1:2, 0:1], state[m, 2:3, 0:1]
        alpha = norm / (square + energies[m][0])
        r = residual[m]
        if later:
            d = r + beta * old_direction[m]
            direction_out[m] = d
            step = direction_out[m, :, mine]
            solution_out[m] = old_solution[m] + alpha * step
        else:
            d = r
            solution_out[m] = alpha * residual[m, :, mine]
        r = r - alpha * (d + dot(vert_t[...], sd[...] * spread[at, :]))
        residual_out[m] = r
        packed[at, :] = sd[...] * dot(vert[...], r)
        scalars.append([total(r * r), total(r * d)])
    moved[...] = with_scalars(packed[0 : moved.shape[0], :], scalars).astype(BF16)


def increment_kernel(later, sd, vert, state, residual, *refs):
    before, direction, moved = refs[-3:]
    obs = lax.axis_index("obs")
    mine = pl.ds(pl.multiple_of(obs * LANES, LANES), LANES)
    for m in range(residual.shape[0]):
        d = residual[m, :, mine]
        if later:
            d = d + state[m, 2:3, 0:1] * refs[0][m, :, mine]
            before[m] = sd[...] * dot(vert[...], refs[1][m])
        else:
            before[m] = jnp.zeros_like(d)
        direction[m] = d
        moved[m] = sd[...] * dot(vert[...], d)


def last_kernel(parts, lev, *refs):
    pieces, refs = refs[:parts], refs[parts:]
    sd, vert_t, state, residual, before, direction, moved = refs[:7]
    increment_out, residual_out, spread = refs[7:]
    members, levp, unused = residual.shape
    obs = lax.axis_index("obs")
    mine = pl.ds(pl.multiple_of(obs * LANES, LANES), LANES)
    unpack(spread, add([x[...] for x in pieces]))
    energies = read_scalars(pieces, members, 1)
    for m in range(members):
        t = spread[m * lev : m * lev + levp, :]
        alpha = state[m, 0:1, 0:1] / (state[m, 1:2, 0:1] + energies[m][0])
        increment_out[:, m, :] = (before[m] + alpha * moved[m])[0:lev]
        r = residual[m, :, mine] - alpha * (direction[m] + dot(vert_t[...], sd[...] * t))
        residual_out[:, m, :] = r[0:lev]


def per_device(
    n_slab,
    n_obs,
    innovation,
    obs_precision,
    seeds,
    col_sd,
    vert_factor,
    h_values,
    block_obs,
    block_col,
    entry_count,
):
    blocks, lev, profiles = innovation.shape
    members = seeds.shape[0]
    chips = n_slab // 2
    halves = n_slab // blocks
    width = profiles // halves
    colblocks = n_obs
    assert halves * blocks == n_slab and width % LANES == 0 and col_sd.shape[0] == 1
    assert chips & (chips - 1) == 0 and n_obs & (n_obs - 1) == 0
    levp = (lev + 1 + 15) // 16 * 16
    assert members <= 16 and members >= PIECES
    rows = (members * (lev + 1) + 15) // 16 * 16
    lanes = colblocks * LANES
    slab_field = (members, levp, lanes)
    slab_rows = (rows, lanes)
    half_rows = [struct((rows, lanes // 2), BF16)] * 2
    wide = rows + levp - lev + 7
    spread = pltpu.VMEM((wide // 8 * 8, lanes), F32)
    some = rows // 32 * 16
    rest = rows - some
    via = chips == 4
    if via:
        one, two = (0, some), (some, rest)
        most = rows - 32
        near_parts = [(0, most), (most, rows - most)]
        plan = [(0, 0, rows), *((1, *part) for part in near_parts)]
        plan += [(2, *one), (2, *two), (3, *one), (3, *two)]
        sends = [(3, *one), (2, *two), (3, *two), (1, *one), (1, *two), (0, 0, rows), (2, *one)]
    else:
        sends = plan = [(i, 0, rows) for i in range(chips)]
    pad = ((0, levp - lev), (0, levp - lev))
    high = lax.reduce_precision(vert_factor, 8, 7)
    low = vert_factor - high
    vert, vert_t = [
        jnp.concatenate([jnp.pad(x, pad).astype(BF16) for x in parts], axis=1)
        for parts in ((high, high, low), (high.T, high.T, low.T))
    ]
    h_block = h_values.reshape(h_values.shape[2:])
    innovation = jnp.transpose(innovation, (1, 0, 2))
    obs_precision = jnp.transpose(obs_precision, (1, 0, 2))
    product = n_slab * width * lanes * rows
    small = 12 * rows * levp * LANES
    plane_bits = [1 << k for k in range(n_obs.bit_length() - 1)]

    def along(x, i):
        return lax.ppermute(x, "slab", [(s, s ^ (2 * i)) for s in range(n_slab)])

    def plane(x, i):
        return lax.ppermute(x, "obs", [(o, o ^ i) for o in range(n_obs)])

    def swap(x):
        return lax.ppermute(x, "slab", [(s, s ^ 1) for s in range(n_slab)])

    def plane_sum(halves, staged):
        halves = list(halves)
        moved_halves = [None] * len(halves)
        for step, bit in enumerate(plane_bits):
            bits = [bit, plane_bits[len(plane_bits) - 1 - step]]
            for at in range(0, len(halves), 2):
                if step > 0:
                    one, two = halves[at : at + 2]
                    one_more, two_more = moved_halves[at : at + 2]
                    halves[at : at + 2] = call(
                        functools.partial(add_halves_kernel, members, 0 if staged else 1),
                        [struct(one.shape, BF16)] * 2,
                        [],
                        0,
                        one,
                        one_more,
                        two,
                        two_more,
                    )
                for half in range(2):
                    moved_halves[at + half] = plane(halves[at + half], bits[half])
            if step == 0 and staged:
                halves[:] = call(
                    stage_kernel,
                    [struct(x.shape, BF16) for x in halves],
                    [pltpu.SemaphoreType.DMA((len(halves),))],
                    0,
                    *halves,
                    space=HBM,
                )
        return [x for pair in zip(halves, moved_halves) for x in pair]

    def line_sum(moved, other):
        shapes = [(count, width) for i, unused, count in sends]
        mine = call(
            functools.partial(forward_kernel, sends, members),
            [struct(shape, F32) for shape in shapes],
            [],
            product,
            moved,
            own,
        )
        ys = call(
            functools.partial(forward_kernel, sends, members),
            [
                struct(shape, F32 if i == 0 or (via and at == 6) else BF16)
                for at, ((i, *unused), shape) in enumerate(zip(sends, shapes))
            ],
            [],
            product,
            other,
            partner,
            moved,
            *mine,
        )
        if not via:
            return [y if i == 0 else along(y, i) for i, y in enumerate(ys)], [(0, rows)] * chips
        passed, far_rest, last_rest, next_some, next_rest, near, far = ys
        passed = along(passed, 1)
        far_rest, last_rest = along(far_rest, 2), along(last_rest, 3)
        next_some, next_rest = along(next_some, 1), along(next_rest, 1)
        (far,) = call(
            functools.partial(add_kernel, members, 0),
            [struct((some, width), BF16)],
            [],
            0,
            far,
            passed,
        )
        ys = [near, far_rest, last_rest, next_some, next_rest, along(far, 2)]
        return ys, [(0, rows), two, two, one, two, one]

    def line_gather(w, *parts):
        if not via:
            return [w if i == 0 else along(w, i) for i in range(chips)]
        some_w, rest_w, *near = parts
        far = along(some_w, 2)
        far_rest, last_rest = along(rest_w, 2), along(rest_w, 3)
        return [w, *(along(x, 1) for x in near), far, far_rest, along(far, 1), last_rest]

    dense = struct((chips, colblocks, LANES, width), BF16)
    own, for_partner, *partials = call(
        functools.partial(start_kernel, (chips, halves, blocks, lev)),
        [dense, dense] + half_rows,
        [
            pltpu.SMEM(seeds.shape, jnp.int32),
            pltpu.SMEM(block_obs.shape, jnp.int32),
            pltpu.SMEM(block_col.shape, jnp.int32),
            pltpu.SMEM(entry_count.shape, jnp.int32),
            pltpu.VMEM(col_sd.shape, F32),
            pltpu.VMEM((profiles // LANES, levp * blocks, LANES), F32),
            pltpu.VMEM((profiles // LANES, levp * blocks, LANES), F32),
            pltpu.VMEM((n_slab, levp, width), jnp.int32),
            pltpu.VMEM((n_slab // 2, members, levp, width), F32),
            pltpu.VMEM((2, rows, 2 * width), F32),
            pltpu.VMEM((rows, lanes), F32),
            pltpu.VMEM(dense.shape, BF16),
            pltpu.VMEM(dense.shape, BF16),
            pltpu.SemaphoreType.DMA((7 + 2 * (profiles // LANES),)),
            pltpu.SemaphoreType.DMA((h_block.shape[0] * halves,)),
        ],
        2 * product,
        seeds,
        block_obs,
        block_col,
        entry_count,
        col_sd,
        innovation.reshape(lev * blocks, profiles),
        obs_precision.reshape(lev * blocks, profiles),
        h_block,
        space=HBM,
        limit=60,
        stored=2,
    )
    ps = plane_sum(partials, True)
    partner = swap(for_partner)
    (precision,) = call(
        functools.partial(precision_kernel, halves, members),
        [struct((rows, width), F32)],
        [],
        0,
        obs_precision,
    )
    slab_sd, residual, moved = call(
        functools.partial(first_kernel, lev),
        [struct((1, lanes), F32), struct(slab_field, F32), struct(slab_rows, BF16)],
        [spread, spread],
        small * colblocks,
        *ps,
        vert,
        vert_t,
    )
    direction = total_step = image = state = None
    for sweep in range(ITERS):
        later, last = sweep > 0, sweep == ITERS - 1
        ys, spans = line_sum(moved, swap(moved))
        state, *weighted = call(
            functools.partial(weigh_kernel, later, last, members, lev, spans),
            [struct((members, 8, LANES), F32)]
            + [struct((n, width), BF16) for n in ((rows, some, rest, most, rows - most) if via else (rows,))]
            + ([] if last else [struct((rows, width), F32)]),
            [],
            0,
            *ys,
            precision,
            *([image, state] if later else []),
        )
        if not last:
            *weighted, image = weighted
        ws = line_gather(*weighted)
        (theirs,) = call(
            functools.partial(adjoint_kernel, plan, members),
            [struct(slab_rows, BF16)],
            [],
            product,
            *ws,
            partner,
        )
        theirs = swap(theirs)
        (mine,) = call(
            functools.partial(adjoint_kernel, plan, members),
            [struct(slab_rows, F32)],
            [],
            product,
            *ws,
            own,
        )
        known = [vert, vert_t, state, residual]
        if later:
            known += [direction, total_step]
        if last:
            ps = call(
                functools.partial(combine_columns_kernel, members),
                [struct((rows, LANES), BF16)] * n_obs,
                [],
                0,
                mine,
                theirs,
            )
            ps = [ps[0]] + [plane(ps[i], i) for i in reversed(range(1, n_obs))]
            own_field = struct((members, levp, LANES), F32)
            before, d, u_d = call(
                functools.partial(increment_kernel, later),
                [own_field] * 3,
                [],
                small,
                col_sd,
                vert,
                state,
                residual,
                *([direction, total_step] if later else []),
            )
            outputs = call(
                functools.partial(last_kernel, len(ps), lev),
                [struct((lev, members, LANES), F32)] * 2,
                [pltpu.VMEM((wide // 8 * 8, LANES), F32)],
                small,
                *ps,
                col_sd,
                vert_t,
                state,
                residual,
                before,
                d,
                u_d,
            )
            break
        ps = call(
            functools.partial(combine_kernel, members), half_rows, [], 0, mine, theirs
        )
        ps = plane_sum(ps, False)
        outs = [
            struct(slab_field, F32),
            struct((members, levp, LANES), F32),
            struct(slab_rows, BF16),
        ]
        if later:
            outs.append(struct(slab_field, F32))
        r, total_step, moved, *d = call(
            functools.partial(update_kernel, later, lev),
            outs,
            [spread, spread],
            small * colblocks,
            *ps,
            slab_sd,
            *known,
        )
        direction, residual = (d[0] if later else residual), r
    return tuple(jnp.transpose(x, (1, 0, 2))[None] for x in outputs)


def solution(mesh):
    return jax.shard_map(
        functools.partial(per_device, mesh.shape["slab"], mesh.shape["obs"]),
        mesh=mesh,
        in_specs=(
            P("obs", None, None),
            P("obs", None, None),
            P(),
            P(("slab", "obs"), None),
            P(),
            P("slab", "obs", None, None, None),
            P("slab", "obs", None),
            P("slab", "obs", None),
            P("slab", "obs"),
        ),
        out_specs=(P(("slab", "obs"), None, None, None), P(("slab", "obs"), None, None, None)),
        check_vma=False,
    )
```

```python
import functools

import jax
import jax.numpy as jnp
from jax import lax
from jax.experimental import pallas as pl
from jax.experimental.pallas import tpu as pltpu
from jax.sharding import PartitionSpec as P

ITERS = 2
LANES = 128
PIECES = 3
PRIME = 32749
VMEM = pl.BlockSpec(memory_space=pltpu.VMEM)
HBM = pl.BlockSpec(memory_space=pltpu.HBM)
F32 = jnp.float32
BF16 = jnp.bfloat16
NT = (((1,), (1,)), ((), ()))


def call(kernel, outs, scratch, flops, *args, space=VMEM, limit=24, stored=0):
    nbytes = sum(a.size * a.dtype.itemsize for a in (*args, *outs))
    return pl.pallas_call(
        kernel,
        out_shape=outs,
        in_specs=[space] * len(args),
        out_specs=[HBM] * stored + [VMEM] * (len(outs) - stored),
        scratch_shapes=scratch,
        compiler_params=pltpu.CompilerParams(vmem_limit_bytes=limit * 1024 * 1024),
        cost_estimate=pl.CostEstimate(flops=flops, bytes_accessed=nbytes, transcendentals=0),
    )(*args)


def struct(shape, dtype):
    return jax.ShapeDtypeStruct(shape, dtype)


def place():
    slab = lax.axis_index("slab")
    return slab // 2, slab % 2, lax.axis_index("obs")


def add(parts):
    value = parts[0].astype(F32)
    for part in parts[1:]:
        value = value + part.astype(F32)
    return value


def dot(matrix, x):
    high = x.astype(BF16)
    rest = (x - high.astype(F32)).astype(BF16)
    x = jnp.concatenate([high, rest, high], axis=0)
    return jnp.dot(matrix, x, preferred_element_type=F32)


def total(x):
    return jnp.sum(jnp.sum(x, axis=0, keepdims=True), axis=1, keepdims=True)


def with_scalars(body, values):
    count = body.shape[0]
    tail = body[count - 16 :]
    sub = lax.broadcasted_iota(jnp.int32, tail.shape, 0) - (16 - len(values))
    lanes = lax.broadcasted_iota(jnp.int32, tail.shape, 1)
    line = jnp.zeros(tail.shape, F32)
    for m, member in enumerate(values):
        for q, value in enumerate(member):
            rest = value
            for piece in range(PIECES):
                part = rest.astype(BF16).astype(F32)
                rest = rest - part
                line = jnp.where((sub == m) & (lanes == q * PIECES + piece), part, line)
    return jnp.concatenate([body[: count - 16], jnp.where(sub >= 0, line, tail)], axis=0)


def read_scalars(refs, members, count):
    tail = add([ref[ref.shape[0] - 16 :, 0:LANES] for ref in refs])
    sub = lax.broadcasted_iota(jnp.int32, tail.shape, 0) - (16 - members)
    lanes = lax.broadcasted_iota(jnp.int32, tail.shape, 1)
    return [
        [
            total(
                jnp.where(
                    (sub == m) & (lanes >= q * PIECES) & (lanes < (q + 1) * PIECES), tail, 0.0
                )
            )
            for q in range(count)
        ]
        for m in range(members)
    ]


def by_member(values, shape, lev):
    rows = lax.broadcasted_iota(jnp.int32, shape, 0)
    out = jnp.zeros(shape, F32)
    for m, value in enumerate(values):
        out = jnp.where((rows >= m * lev) & (rows < (m + 1) * lev), value, out)
    return out


def member_sums(x, members, lev):
    lines = jnp.sum(x, axis=1, keepdims=True)
    rows = lax.broadcasted_iota(jnp.int32, lines.shape, 0)
    return [
        jnp.sum(
            jnp.where((rows >= m * lev) & (rows < (m + 1) * lev), lines, 0.0),
            axis=0,
            keepdims=True,
        )
        for m in range(members)
    ]


def remainder(x, factor):
    return x - (x.astype(F32) * factor).astype(jnp.int32) * PRIME


def start_kernel(
    dims, seeds_in, ids_in, cols_in, count_in, sd_in, innov_in, prec_in, h, own_out, partner_out, *rest
):
    chips, halves, blocks, lev = dims
    outs = rest[:-15]
    seeds, ids, cols, count, sd, innov, prec, bases, hashed, scratch, acc = rest[-15:-4]
    own, partner, sems, h_sems = rest[-4:]
    z, core, obs = place()
    strips = innov.shape[0]
    profiles = strips * LANES
    colblocks, width = own.shape[1], own.shape[3]
    members, levp = hashed.shape[1], hashed.shape[2]
    rows = acc.shape[0]

    pairs = [(seeds_in, seeds), (ids_in, ids), (cols_in, cols), (count_in, count), (sd_in, sd)]
    small = [pltpu.make_async_copy(x, y, sems.at[i]) for i, (x, y) in enumerate(pairs)]
    for copy in small:
        copy.start()
    large = []
    for x, y in ((innov_in, innov), (prec_in, prec)):
        for t in range(strips):
            at = len(pairs) + len(large)
            large.append(
                pltpu.make_async_copy(
                    x.at[:, t * LANES : (t + 1) * LANES], y.at[t, 0 : lev * blocks, :], sems.at[at]
                )
            )
    for copy in large:
        copy.start()
    own[...] = jnp.zeros_like(own)
    partner[...] = jnp.zeros_like(partner)
    scratch[...] = jnp.zeros_like(scratch)
    order = [(source, zz) for source in range(2) for zz in range(chips)]
    shape = (levp, width)
    spot = lax.broadcasted_iota(jnp.int32, shape, 0) * profiles
    spot = spot + lax.broadcasted_iota(jnp.int32, shape, 1)

    def piece_at(at):
        source, zz = order[at]
        return 2 * zz + (core if source == 0 else 1 - core)

    for at in range(len(order)):
        piece = piece_at(at)
        first = (obs * blocks + piece // halves) * (lev * profiles) + (piece % halves) * width
        bases[at] = remainder(7919 * remainder(spot + first, 1.0 / PRIME), 1.0 / PRIME)
    for copy in small:
        copy.wait()

    def tile_copy(n, half, target):
        lanes = pl.ds(half * width, width)
        return pltpu.make_async_copy(h.at[n, :, lanes], target, h_sems.at[n * halves + half])

    def put(n, carry):
        for half in range(halves):
            piece, k = ids[0, 0, n] * halves + half, cols[0, 0, n]

            @pl.when(piece % 2 == core)
            def _():
                tile_copy(n, half, own.at[piece // 2, k]).start()

            @pl.when(piece % 2 != core)
            def _():
                tile_copy(n, half, partner.at[piece // 2, k]).start()

        return carry

    lax.fori_loop(0, count[0, 0], put, 0)

    starts = [lax.rem(seeds[m], PRIME) - PRIME for m in range(members)]
    low = (1.0 - 2.0**-21) / PRIME

    def draw(at, m):
        k0 = bases[at] + starts[m]
        k1 = remainder(k0 * k0 + 12345, 1.0 / PRIME)
        k2 = remainder(k1 * k1 + 2719, low)
        return jnp.where(k2 >= PRIME, k2 - PRIME, k2).astype(F32)

    early = len(order) // 2
    for at in range(early):
        for m in range(members):
            hashed[at, m] = draw(at, m)
    for copy in large:
        copy.wait()

    def arrive(n, carry):
        for half in range(halves):
            tile_copy(n, half, own.at[0, 0]).wait()
        return carry

    lax.fori_loop(0, count[0, 0], arrive, 0)
    kept = [
        pltpu.make_async_copy(x, y, sems.at[len(pairs) + len(large) + i])
        for i, (x, y) in enumerate(((partner, partner_out), (own, own_out)))
    ]
    for copy in kept:
        copy.start()

    for at in range(len(order)):
        source, zz = order[at]
        piece = piece_at(at)
        b = piece // halves
        strip = (piece % halves) * (width // LANES)
        p, d = [
            jnp.concatenate(
                [
                    x[strip + t, pl.ds(b, lev, stride=blocks), :]
                    for t in range(width // LANES)
                ],
                axis=1,
            )
            for x in (prec, innov)
        ]
        gain = 3.4 * p * lax.rsqrt(p)
        offset = p * d - 0.5 * gain
        gain = gain * (1.0 / PRIME)
        slot, side = at // 2 % 2, at % 2
        for m in range(members):
            k2 = hashed[at, m, 0:lev, :] if at < early else draw(at, m)[0:lev]
            scratch[slot, m * lev : (m + 1) * lev, side * width : (side + 1) * width] = (
                offset + gain * k2
            )
        if side == 0:
            continue
        tiles = own if source == 0 else partner
        tiles = [tiles[i].reshape(colblocks * LANES, width) for i in (zz - 1, zz)]
        part = lax.dot_general(
            scratch[slot].astype(BF16),
            jnp.concatenate(tiles, axis=1),
            NT,
            preferred_element_type=F32,
        )
        if at == 1:
            acc[...] = part
        else:
            acc[...] += part

    line = jnp.concatenate([sd[...]] * colblocks, axis=1)
    put_halves(outs, with_columns(acc[...], line, obs, members))
    for copy in kept:
        copy.wait()


def put_halves(outs, value):
    half = value.shape[1] // 2
    outs[0][...] = value[:, :half].astype(BF16)
    outs[1][...] = value[:, half:].astype(BF16)


def with_columns(body, line, obs, members):
    tail = body[body.shape[0] - 16 :]
    sub = lax.broadcasted_iota(jnp.int32, tail.shape, 0)
    mine = lax.broadcasted_iota(jnp.int32, tail.shape, 1) // LANES == obs
    rest = line
    for piece in range(PIECES):
        part = rest.astype(BF16).astype(F32)
        rest = rest - part
        tail = jnp.where((sub == 16 - PIECES + piece) & mine, part, tail)
    return jnp.concatenate([body[: body.shape[0] - 16], tail], axis=0)


def read_columns(body):
    tail = body[body.shape[0] - 16 :]
    sub = lax.broadcasted_iota(jnp.int32, tail.shape, 0)
    return jnp.sum(jnp.where(sub >= 16 - PIECES, tail, 0.0), axis=0, keepdims=True)


def precision_kernel(halves, members, prec, out):
    z, core, unused = place()
    piece = 2 * z + core
    lev, blocks, unused = prec.shape
    width = out.shape[1]
    block = lax.broadcasted_iota(jnp.int32, (lev, blocks, width), 1)
    if halves == 1:
        mine = prec[...]
    else:
        mine = prec[:, :, pl.ds(pl.multiple_of((piece % halves) * width, LANES), width)]
    out[...] = jnp.zeros_like(out)
    mine = jnp.sum(jnp.where(block == piece // halves, mine, 0.0), axis=1)
    for m in range(members):
        out[m * lev : (m + 1) * lev, :] = mine


def joined(pieces):
    one, one_more, two, two_more = [x[...] for x in pieces]
    return jnp.concatenate([add([one, one_more]), add([two, two_more])], axis=1)


def unpack(spread, value):
    count = value.shape[0]
    spread[0:count, :] = value
    spread[count:, :] = jnp.zeros((spread.shape[0] - count, value.shape[1]), F32)


def first_kernel(lev, *refs):
    vert, vert_t, sd_out, residual, moved, spread, packed = refs[4:]
    members, levp, unused = residual.shape
    t = joined(refs[:4])
    sd = read_columns(t)
    sd_out[...] = sd
    unpack(spread, t)
    scalars = []
    for m in range(members):
        at = slice(m * lev, m * lev + levp)
        r = dot(vert_t[...], sd * spread[at, :])
        residual[m] = r
        packed[at, :] = sd * dot(vert[...], r)
        scalars.append([total(r * r)])
    moved[...] = with_scalars(packed[0 : moved.shape[0], :], scalars).astype(BF16)


def add_kernel(members, scalars, *refs):
    parts, out = refs[:-1], refs[-1]
    value = add([x[...] for x in parts])
    if scalars:
        value = with_scalars(value, read_scalars(parts, members, scalars))
    out[...] = value.astype(BF16)


def add_halves_kernel(members, scalars, one, one_more, two, two_more, one_out, two_out):
    add_kernel(members, scalars, one, one_more, one_out)
    add_kernel(members, 0, two, two_more, two_out)


def stage_kernel(*refs):
    sems = refs[-1]
    count = len(refs) // 2
    copies = [
        pltpu.make_async_copy(refs[i], refs[count + i], sems.at[i]) for i in range(count)
    ]
    for copy in copies:
        copy.start()
    for copy in copies:
        copy.wait()


def forward_kernel(sends, members, x, tiles, *refs):
    z, core, obs = place()
    outs = refs[-len(sends) :]
    rows, lanes = x.shape
    width = tiles.shape[3]
    added = refs[1 : 1 + len(sends)] if len(refs) > len(sends) else [None] * len(sends)
    if added[0] is not None:
        scalars = read_scalars([refs[0], x], members, 2)
    for out, before, (chip, first, count) in zip(outs, added, sends):
        y = jnp.dot(
            x[first : first + count, :],
            tiles[z ^ chip].reshape(lanes, width),
            preferred_element_type=F32,
        )
        if before is not None:
            y = before[...] + y
            if first + count == rows:
                y = with_scalars(y, scalars)
        out[...] = y.astype(out.dtype)


def weigh_kernel(later, last, members, lev, spans, *refs):
    ys, refs = refs[: len(spans)], refs[len(spans) :]
    prec, old_image, old = refs[0], *(refs[1:3] if later else (None, None))
    state, *outs = refs[3 if later else 1 :]
    if not last:
        *outs, image = outs
    rows = prec.shape[0]
    cuts = sorted({first for first, count in spans}) + [rows]
    parts = []
    for low, high in zip(cuts, cuts[1:]):
        held = [
            ref[low - first : high - first, :]
            for ref, (first, count) in zip(ys, spans)
            if first <= low < first + count
        ]
        parts.append(add(held))
    y = parts[0] if len(parts) == 1 else jnp.concatenate(parts, axis=0)
    ends = [ref for ref, (first, count) in zip(ys, spans) if first + count == rows]
    sub = lax.broadcasted_iota(jnp.int32, (8, LANES), 0)
    betas = []
    for m, (norm, cross) in enumerate(read_scalars(ends, members, 2)):
        if later:
            old_norm, old_square = old[m, 0:1, 0:1], old[m, 1:2, 0:1]
            beta = norm / old_norm
            square = norm + 2.0 * beta * cross + beta * beta * old_square
        else:
            beta = jnp.zeros_like(norm)
            square = norm
        betas.append(beta)
        state[m] = jnp.where(sub == 0, norm, jnp.where(sub == 1, square, beta))
    if later:
        y = y + by_member(betas, (rows, 1), lev) * old_image[...]
    if not last:
        image[...] = y
    scaled = prec[...] * y
    energies = [[x] for x in member_sums(scaled * y, members, lev)]
    weighted = with_scalars(scaled, energies).astype(BF16)
    first = 0
    for out in outs:
        out[...] = weighted[first : first + out.shape[0]]
        first = (first + out.shape[0]) % rows


def adjoint_kernel(plan, members, *refs):
    z, core, obs = place()
    ws, tiles, out = refs[: len(plan)], refs[len(plan)], refs[len(plan) + 1]
    rows, lanes = out.shape
    width = ws[0].shape[1]
    acc = None
    for i in range(tiles.shape[0]):
        w = {first: ref for ref, (chip, first, count) in zip(ws, plan) if chip == i}
        w = [w[first][...] for first in sorted(w)]
        w = w[0] if len(w) == 1 else jnp.concatenate(w, axis=0)
        part = lax.dot_general(
            w, tiles[z ^ i].reshape(lanes, width), NT, preferred_element_type=F32
        )
        acc = part if i == 0 else acc + part
    ends = [ref for ref, (chip, first, count) in zip(ws, plan) if first + count == rows]
    out[...] = with_scalars(acc, read_scalars(ends, members, 1)).astype(out.dtype)


def combine_kernel(members, mine, theirs, *outs):
    value = mine[...] + theirs[...].astype(F32)
    put_halves(outs, with_scalars(value, read_scalars([mine, theirs], members, 1)))


def combine_columns_kernel(members, mine, theirs, *outs):
    obs = lax.axis_index("obs")
    energies = read_scalars([mine, theirs], members, 1)
    for i, out in enumerate(outs):
        lane = pl.ds(pl.multiple_of((obs ^ i) * LANES, LANES), LANES)
        value = mine[:, lane] + theirs[:, lane].astype(F32)
        out[...] = with_scalars(value, energies).astype(BF16)


def update_kernel(later, lev, *refs):
    pieces, refs = refs[:4], refs[4:]
    sd, vert, vert_t, state, residual = refs[:5]
    spread, packed = refs[-2:]
    if later:
        old_direction, old_solution, residual_out, solution_out, moved, direction_out = refs[5:-2]
    else:
        residual_out, solution_out, moved = refs[5:-2]
    members, levp, unused = residual.shape
    obs = lax.axis_index("obs")
    mine = pl.ds(pl.multiple_of(obs * LANES, LANES), LANES)
    unpack(spread, joined(pieces))
    energies = read_scalars(pieces[:2], members, 1)
    scalars = []
    for m in range(members):
        at = slice(m * lev, m * lev + levp)
        norm, square, beta = state[m, 0:1, 0:1], state[m, 1:2, 0:1], state[m, 2:3, 0:1]
        alpha = norm / (square + energies[m][0])
        r = residual[m]
        if later:
            d = r + beta * old_direction[m]
            direction_out[m] = d
            step = direction_out[m, :, mine]
            solution_out[m] = old_solution[m] + alpha * step
        else:
            d = r
            solution_out[m] = alpha * residual[m, :, mine]
        r = r - alpha * (d + dot(vert_t[...], sd[...] * spread[at, :]))
        residual_out[m] = r
        packed[at, :] = sd[...] * dot(vert[...], r)
        scalars.append([total(r * r), total(r * d)])
    moved[...] = with_scalars(packed[0 : moved.shape[0], :], scalars).astype(BF16)


def increment_kernel(later, sd, vert, state, residual, *refs):
    before, direction, moved = refs[-3:]
    obs = lax.axis_index("obs")
    mine = pl.ds(pl.multiple_of(obs * LANES, LANES), LANES)
    for m in range(residual.shape[0]):
        d = residual[m, :, mine]
        if later:
            d = d + state[m, 2:3, 0:1] * refs[0][m, :, mine]
            before[m] = sd[...] * dot(vert[...], refs[1][m])
        else:
            before[m] = jnp.zeros_like(d)
        direction[m] = d
        moved[m] = sd[...] * dot(vert[...], d)


def last_kernel(parts, lev, *refs):
    pieces, refs = refs[:parts], refs[parts:]
    sd, vert_t, state, residual, before, direction, moved = refs[:7]
    increment_out, residual_out, spread = refs[7:]
    members, levp, unused = residual.shape
    obs = lax.axis_index("obs")
    mine = pl.ds(pl.multiple_of(obs * LANES, LANES), LANES)
    unpack(spread, add([x[...] for x in pieces]))
    energies = read_scalars(pieces, members, 1)
    for m in range(members):
        t = spread[m * lev : m * lev + levp, :]
        alpha = state[m, 0:1, 0:1] / (state[m, 1:2, 0:1] + energies[m][0])
        increment_out[:, m, :] = (before[m] + alpha * moved[m])[0:lev]
        r = residual[m, :, mine] - alpha * (direction[m] + dot(vert_t[...], sd[...] * t))
        residual_out[:, m, :] = r[0:lev]


def per_device(
    n_slab,
    n_obs,
    innovation,
    obs_precision,
    seeds,
    col_sd,
    vert_factor,
    h_values,
    block_obs,
    block_col,
    entry_count,
):
    blocks, lev, profiles = innovation.shape
    members = seeds.shape[0]
    chips = n_slab // 2
    halves = n_slab // blocks
    width = profiles // halves
    colblocks = n_obs
    assert halves * blocks == n_slab and width % LANES == 0 and col_sd.shape[0] == 1
    assert chips & (chips - 1) == 0 and n_obs & (n_obs - 1) == 0
    levp = (lev + 1 + 15) // 16 * 16
    assert members <= 16 and members >= PIECES
    rows = (members * (lev + 1) + 15) // 16 * 16
    lanes = colblocks * LANES
    slab_field = (members, levp, lanes)
    slab_rows = (rows, lanes)
    half_rows = [struct((rows, lanes // 2), BF16)] * 2
    wide = rows + levp - lev + 7
    spread = pltpu.VMEM((wide // 8 * 8, lanes), F32)
    some = rows // 32 * 16
    rest = rows - some
    via = chips == 4
    if via:
        one, two = (0, some), (some, rest)
        most = rows - 32
        near_parts = [(0, most), (most, rows - most)]
        plan = [(0, 0, rows), *((1, *part) for part in near_parts)]
        plan += [(2, *one), (2, *two), (3, *one), (3, *two)]
        sends = [(3, *one), (2, *two), (3, *two), *((1, *part) for part in near_parts)]
        sends += [(0, 0, rows), (2, *one)]
    else:
        sends = plan = [(i, 0, rows) for i in range(chips)]
    pad = ((0, levp - lev), (0, levp - lev))
    high = lax.reduce_precision(vert_factor, 8, 7)
    low = vert_factor - high
    vert, vert_t = [
        jnp.concatenate([jnp.pad(x, pad).astype(BF16) for x in parts], axis=1)
        for parts in ((high, high, low), (high.T, high.T, low.T))
    ]
    h_block = h_values.reshape(h_values.shape[2:])
    innovation = jnp.transpose(innovation, (1, 0, 2))
    obs_precision = jnp.transpose(obs_precision, (1, 0, 2))
    product = n_slab * width * lanes * rows
    small = 12 * rows * levp * LANES
    plane_bits = [1 << k for k in range(n_obs.bit_length() - 1)]

    def along(x, i):
        return lax.ppermute(x, "slab", [(s, s ^ (2 * i)) for s in range(n_slab)])

    def plane(x, i):
        return lax.ppermute(x, "obs", [(o, o ^ i) for o in range(n_obs)])

    def swap(x):
        return lax.ppermute(x, "slab", [(s, s ^ 1) for s in range(n_slab)])

    def plane_sum(halves, staged):
        halves = list(halves)
        moved_halves = [None] * len(halves)
        for step, bit in enumerate(plane_bits):
            bits = [bit, plane_bits[len(plane_bits) - 1 - step]]
            for at in range(0, len(halves), 2):
                if step > 0:
                    one, two = halves[at : at + 2]
                    one_more, two_more = moved_halves[at : at + 2]
                    halves[at : at + 2] = call(
                        functools.partial(add_halves_kernel, members, 0 if staged else 1),
                        [struct(one.shape, BF16)] * 2,
                        [],
                        0,
                        one,
                        one_more,
                        two,
                        two_more,
                    )
                for half in range(2):
                    moved_halves[at + half] = plane(halves[at + half], bits[half])
            if step == 0 and staged:
                halves[:] = call(
                    stage_kernel,
                    [struct(x.shape, BF16) for x in halves],
                    [pltpu.SemaphoreType.DMA((len(halves),))],
                    0,
                    *halves,
                    space=HBM,
                )
        return [x for pair in zip(halves, moved_halves) for x in pair]

    def line_sum(moved, other):
        shapes = [(count, width) for i, unused, count in sends]
        mine = call(
            functools.partial(forward_kernel, sends, members),
            [struct(shape, F32) for shape in shapes],
            [],
            product,
            moved,
            own,
        )
        ys = call(
            functools.partial(forward_kernel, sends, members),
            [
                struct(shape, F32 if i == 0 or (via and at == 6) else BF16)
                for at, ((i, *unused), shape) in enumerate(zip(sends, shapes))
            ],
            [],
            product,
            other,
            partner,
            moved,
            *mine,
        )
        if not via:
            return [y if i == 0 else along(y, i) for i, y in enumerate(ys)], [(0, rows)] * chips
        passed, far_rest, last_rest, next_most, next_rest, near, far = ys
        passed = along(passed, 1)
        far_rest, last_rest = along(far_rest, 2), along(last_rest, 3)
        next_most, next_rest = along(next_most, 1), along(next_rest, 1)
        (far,) = call(
            functools.partial(add_kernel, members, 0),
            [struct((some, width), BF16)],
            [],
            0,
            far,
            passed,
        )
        ys = [near, far_rest, last_rest, next_most, next_rest, along(far, 2)]
        return ys, [(0, rows), two, two, *near_parts, one]

    def line_gather(w, *parts):
        if not via:
            return [w if i == 0 else along(w, i) for i in range(chips)]
        some_w, rest_w, *near = parts
        far = along(some_w, 2)
        far_rest, last_rest = along(rest_w, 2), along(rest_w, 3)
        return [w, *(along(x, 1) for x in near), far, far_rest, along(far, 1), last_rest]

    dense = struct((chips, colblocks, LANES, width), BF16)
    own, for_partner, *partials = call(
        functools.partial(start_kernel, (chips, halves, blocks, lev)),
        [dense, dense] + half_rows,
        [
            pltpu.SMEM(seeds.shape, jnp.int32),
            pltpu.SMEM(block_obs.shape, jnp.int32),
            pltpu.SMEM(block_col.shape, jnp.int32),
            pltpu.SMEM(entry_count.shape, jnp.int32),
            pltpu.VMEM(col_sd.shape, F32),
            pltpu.VMEM((profiles // LANES, levp * blocks, LANES), F32),
            pltpu.VMEM((profiles // LANES, levp * blocks, LANES), F32),
            pltpu.VMEM((n_slab, levp, width), jnp.int32),
            pltpu.VMEM((n_slab // 2, members, levp, width), F32),
            pltpu.VMEM((2, rows, 2 * width), F32),
            pltpu.VMEM((rows, lanes), F32),
            pltpu.VMEM(dense.shape, BF16),
            pltpu.VMEM(dense.shape, BF16),
            pltpu.SemaphoreType.DMA((7 + 2 * (profiles // LANES),)),
            pltpu.SemaphoreType.DMA((h_block.shape[0] * halves,)),
        ],
        2 * product,
        seeds,
        block_obs,
        block_col,
        entry_count,
        col_sd,
        innovation.reshape(lev * blocks, profiles),
        obs_precision.reshape(lev * blocks, profiles),
        h_block,
        space=HBM,
        limit=60,
        stored=2,
    )
    ps = plane_sum(partials, True)
    partner = swap(for_partner)
    (precision,) = call(
        functools.partial(precision_kernel, halves, members),
        [struct((rows, width), F32)],
        [],
        0,
        obs_precision,
    )
    slab_sd, residual, moved = call(
        functools.partial(first_kernel, lev),
        [struct((1, lanes), F32), struct(slab_field, F32), struct(slab_rows, BF16)],
        [spread, spread],
        small * colblocks,
        *ps,
        vert,
        vert_t,
    )
    direction = total_step = image = state = None
    for sweep in range(ITERS):
        later, last = sweep > 0, sweep == ITERS - 1
        ys, spans = line_sum(moved, swap(moved))
        state, *weighted = call(
            functools.partial(weigh_kernel, later, last, members, lev, spans),
            [struct((members, 8, LANES), F32)]
            + [struct((n, width), BF16) for n in ((rows, some, rest, most, rows - most) if via else (rows,))]
            + ([] if last else [struct((rows, width), F32)]),
            [],
            0,
            *ys,
            precision,
            *([image, state] if later else []),
        )
        if not last:
            *weighted, image = weighted
        ws = line_gather(*weighted)
        (theirs,) = call(
            functools.partial(adjoint_kernel, plan, members),
            [struct(slab_rows, BF16)],
            [],
            product,
            *ws,
            partner,
        )
        theirs = swap(theirs)
        (mine,) = call(
            functools.partial(adjoint_kernel, plan, members),
            [struct(slab_rows, F32)],
            [],
            product,
            *ws,
            own,
        )
        known = [vert, vert_t, state, residual]
        if later:
            known += [direction, total_step]
        if last:
            ps = call(
                functools.partial(combine_columns_kernel, members),
                [struct((rows, LANES), BF16)] * n_obs,
                [],
                0,
                mine,
                theirs,
            )
            ps = [ps[0]] + [plane(ps[i], i) for i in reversed(range(1, n_obs))]
            own_field = struct((members, levp, LANES), F32)
            before, d, u_d = call(
                functools.partial(increment_kernel, later),
                [own_field] * 3,
                [],
                small,
                col_sd,
                vert,
                state,
                residual,
                *([direction, total_step] if later else []),
            )
            outputs = call(
                functools.partial(last_kernel, len(ps), lev),
                [struct((lev, members, LANES), F32)] * 2,
                [pltpu.VMEM((wide // 8 * 8, LANES), F32)],
                small,
                *ps,
                col_sd,
                vert_t,
                state,
                residual,
                before,
                d,
                u_d,
            )
            break
        ps = call(
            functools.partial(combine_kernel, members), half_rows, [], 0, mine, theirs
        )
        ps = plane_sum(ps, False)
        outs = [
            struct(slab_field, F32),
            struct((members, levp, LANES), F32),
            struct(slab_rows, BF16),
        ]
        if later:
            outs.append(struct(slab_field, F32))
        r, total_step, moved, *d = call(
            functools.partial(update_kernel, later, lev),
            outs,
            [spread, spread],
            small * colblocks,
            *ps,
            slab_sd,
            *known,
        )
        direction, residual = (d[0] if later else residual), r
    return tuple(jnp.transpose(x, (1, 0, 2))[None] for x in outputs)


def solution(mesh):
    return jax.shard_map(
        functools.partial(per_device, mesh.shape["slab"], mesh.shape["obs"]),
        mesh=mesh,
        in_specs=(
            P("obs", None, None),
            P("obs", None, None),
            P(),
            P(("slab", "obs"), None),
            P(),
            P("slab", "obs", None, None, None),
            P("slab", "obs", None),
            P("slab", "obs", None),
            P("slab", "obs"),
        ),
        out_specs=(P(("slab", "obs"), None, None, None), P(("slab", "obs"), None, None, None)),
        check_vma=False,
    )
```

```python
import functools

import jax
import jax.numpy as jnp
from jax import lax
from jax.experimental import pallas as pl
from jax.experimental.pallas import tpu as pltpu
from jax.sharding import PartitionSpec as P

ITERS = 2
LANES = 128
PIECES = 3
PRIME = 32749
VMEM = pl.BlockSpec(memory_space=pltpu.VMEM)
HBM = pl.BlockSpec(memory_space=pltpu.HBM)
F32 = jnp.float32
BF16 = jnp.bfloat16
NT = (((1,), (1,)), ((), ()))


def call(kernel, outs, scratch, flops, *args, space=VMEM, limit=24, stored=0):
    nbytes = sum(a.size * a.dtype.itemsize for a in (*args, *outs))
    return pl.pallas_call(
        kernel,
        out_shape=outs,
        in_specs=[space] * len(args),
        out_specs=[HBM] * stored + [VMEM] * (len(outs) - stored),
        scratch_shapes=scratch,
        compiler_params=pltpu.CompilerParams(vmem_limit_bytes=limit * 1024 * 1024),
        cost_estimate=pl.CostEstimate(flops=flops, bytes_accessed=nbytes, transcendentals=0),
    )(*args)


def struct(shape, dtype):
    return jax.ShapeDtypeStruct(shape, dtype)


def place():
    slab = lax.axis_index("slab")
    return slab // 2, slab % 2, lax.axis_index("obs")


def add(parts):
    value = parts[0].astype(F32)
    for part in parts[1:]:
        value = value + part.astype(F32)
    return value


def dot(matrix, x):
    high = x.astype(BF16)
    rest = (x - high.astype(F32)).astype(BF16)
    x = jnp.concatenate([high, rest, high], axis=0)
    return jnp.dot(matrix, x, preferred_element_type=F32)


def total(x):
    return jnp.sum(jnp.sum(x, axis=0, keepdims=True), axis=1, keepdims=True)


def with_scalars(body, values):
    count = body.shape[0]
    tail = body[count - 16 :]
    sub = lax.broadcasted_iota(jnp.int32, tail.shape, 0) - (16 - len(values))
    lanes = lax.broadcasted_iota(jnp.int32, tail.shape, 1)
    line = jnp.zeros(tail.shape, F32)
    for m, member in enumerate(values):
        for q, value in enumerate(member):
            rest = value
            for piece in range(PIECES):
                part = rest.astype(BF16).astype(F32)
                rest = rest - part
                line = jnp.where((sub == m) & (lanes == q * PIECES + piece), part, line)
    return jnp.concatenate([body[: count - 16], jnp.where(sub >= 0, line, tail)], axis=0)


def read_scalars(refs, members, count):
    tail = add([ref[ref.shape[0] - 16 :, 0:LANES] for ref in refs])
    sub = lax.broadcasted_iota(jnp.int32, tail.shape, 0) - (16 - members)
    lanes = lax.broadcasted_iota(jnp.int32, tail.shape, 1)
    return [
        [
            total(
                jnp.where(
                    (sub == m) & (lanes >= q * PIECES) & (lanes < (q + 1) * PIECES), tail, 0.0
                )
            )
            for q in range(count)
        ]
        for m in range(members)
    ]


def by_member(values, shape, lev):
    rows = lax.broadcasted_iota(jnp.int32, shape, 0)
    out = jnp.zeros(shape, F32)
    for m, value in enumerate(values):
        out = jnp.where((rows >= m * lev) & (rows < (m + 1) * lev), value, out)
    return out


def member_sums(x, members, lev):
    lines = jnp.sum(x, axis=1, keepdims=True)
    rows = lax.broadcasted_iota(jnp.int32, lines.shape, 0)
    return [
        jnp.sum(
            jnp.where((rows >= m * lev) & (rows < (m + 1) * lev), lines, 0.0),
            axis=0,
            keepdims=True,
        )
        for m in range(members)
    ]


def remainder(x, factor):
    return x - (x.astype(F32) * factor).astype(jnp.int32) * PRIME


def start_kernel(
    dims, seeds_in, ids_in, cols_in, count_in, sd_in, innov_in, prec_in, h, own_out, partner_out, *rest
):
    chips, halves, blocks, lev = dims
    outs = rest[:-15]
    seeds, ids, cols, count, sd, innov, prec, bases, hashed, scratch, acc = rest[-15:-4]
    own, partner, sems, h_sems = rest[-4:]
    z, core, obs = place()
    strips = innov.shape[0]
    profiles = strips * LANES
    colblocks, width = own.shape[1], own.shape[3]
    members, levp = hashed.shape[1], hashed.shape[2]
    rows = acc.shape[0]

    pairs = [(seeds_in, seeds), (ids_in, ids), (cols_in, cols), (count_in, count), (sd_in, sd)]
    small = [pltpu.make_async_copy(x, y, sems.at[i]) for i, (x, y) in enumerate(pairs)]
    for copy in small:
        copy.start()
    large = []
    for x, y in ((innov_in, innov), (prec_in, prec)):
        for t in range(strips):
            at = len(pairs) + len(large)
            large.append(
                pltpu.make_async_copy(
                    x.at[:, t * LANES : (t + 1) * LANES], y.at[t, 0 : lev * blocks, :], sems.at[at]
                )
            )
    for copy in large:
        copy.start()
    own[...] = jnp.zeros_like(own)
    partner[...] = jnp.zeros_like(partner)
    scratch[...] = jnp.zeros_like(scratch)
    order = [(source, zz) for source in range(2) for zz in range(chips)]
    shape = (levp, width)
    spot = lax.broadcasted_iota(jnp.int32, shape, 0) * profiles
    spot = spot + lax.broadcasted_iota(jnp.int32, shape, 1)

    def piece_at(at):
        source, zz = order[at]
        return 2 * zz + (core if source == 0 else 1 - core)

    for at in range(len(order)):
        piece = piece_at(at)
        first = (obs * blocks + piece // halves) * (lev * profiles) + (piece % halves) * width
        bases[at] = remainder(7919 * remainder(spot + first, 1.0 / PRIME), 1.0 / PRIME)
    for copy in small:
        copy.wait()

    def tile_copy(n, half, target):
        lanes = pl.ds(half * width, width)
        return pltpu.make_async_copy(h.at[n, :, lanes], target, h_sems.at[n * halves + half])

    def put(n, carry):
        for half in range(halves):
            piece, k = ids[0, 0, n] * halves + half, cols[0, 0, n]

            @pl.when(piece % 2 == core)
            def _():
                tile_copy(n, half, own.at[piece // 2, k]).start()

            @pl.when(piece % 2 != core)
            def _():
                tile_copy(n, half, partner.at[piece // 2, k]).start()

        return carry

    lax.fori_loop(0, count[0, 0], put, 0)

    starts = [lax.rem(seeds[m], PRIME) - PRIME for m in range(members)]
    low = (1.0 - 2.0**-21) / PRIME

    def draw(at, m):
        k0 = bases[at] + starts[m]
        k1 = remainder(k0 * k0 + 12345, 1.0 / PRIME)
        k2 = remainder(k1 * k1 + 2719, low)
        return jnp.where(k2 >= PRIME, k2 - PRIME, k2).astype(F32)

    early = len(order) // 2
    for at in range(early):
        for m in range(members):
            hashed[at, m] = draw(at, m)
    for copy in large:
        copy.wait()

    def arrive(n, carry):
        for half in range(halves):
            tile_copy(n, half, own.at[0, 0]).wait()
        return carry

    lax.fori_loop(0, count[0, 0], arrive, 0)
    kept = [
        pltpu.make_async_copy(x, y, sems.at[len(pairs) + len(large) + i])
        for i, (x, y) in enumerate(((partner, partner_out), (own, own_out)))
    ]
    for copy in kept:
        copy.start()

    for at in range(len(order)):
        source, zz = order[at]
        piece = piece_at(at)
        b = piece // halves
        strip = (piece % halves) * (width // LANES)
        p, d = [
            jnp.concatenate(
                [
                    x[strip + t, pl.ds(b, lev, stride=blocks), :]
                    for t in range(width // LANES)
                ],
                axis=1,
            )
            for x in (prec, innov)
        ]
        gain = 3.4 * p * lax.rsqrt(p)
        offset = p * d - 0.5 * gain
        gain = gain * (1.0 / PRIME)
        slot, side = at // 2 % 2, at % 2
        for m in range(members):
            k2 = hashed[at, m, 0:lev, :] if at < early else draw(at, m)[0:lev]
            scratch[slot, m * lev : (m + 1) * lev, side * width : (side + 1) * width] = (
                offset + gain * k2
            )
        if side == 0:
            continue
        tiles = own if source == 0 else partner
        tiles = [tiles[i].reshape(colblocks * LANES, width) for i in (zz - 1, zz)]
        part = lax.dot_general(
            scratch[slot].astype(BF16),
            jnp.concatenate(tiles, axis=1),
            NT,
            preferred_element_type=F32,
        )
        if at == 1:
            acc[...] = part
        else:
            acc[...] += part

    line = jnp.concatenate([sd[...]] * colblocks, axis=1)
    put_halves(outs, with_columns(acc[...], line, obs, members))
    for copy in kept:
        copy.wait()


def put_halves(outs, value):
    half = value.shape[1] // 2
    outs[0][...] = value[:, :half].astype(BF16)
    outs[1][...] = value[:, half:].astype(BF16)


def with_columns(body, line, obs, members):
    tail = body[body.shape[0] - 16 :]
    sub = lax.broadcasted_iota(jnp.int32, tail.shape, 0)
    mine = lax.broadcasted_iota(jnp.int32, tail.shape, 1) // LANES == obs
    rest = line
    for piece in range(PIECES):
        part = rest.astype(BF16).astype(F32)
        rest = rest - part
        tail = jnp.where((sub == 16 - PIECES + piece) & mine, part, tail)
    return jnp.concatenate([body[: body.shape[0] - 16], tail], axis=0)


def read_columns(body):
    tail = body[body.shape[0] - 16 :]
    sub = lax.broadcasted_iota(jnp.int32, tail.shape, 0)
    return jnp.sum(jnp.where(sub >= 16 - PIECES, tail, 0.0), axis=0, keepdims=True)


def precision_kernel(halves, members, prec, out):
    z, core, unused = place()
    piece = 2 * z + core
    lev, blocks, unused = prec.shape
    width = out.shape[1]
    block = lax.broadcasted_iota(jnp.int32, (lev, blocks, width), 1)
    if halves == 1:
        mine = prec[...]
    else:
        mine = prec[:, :, pl.ds(pl.multiple_of((piece % halves) * width, LANES), width)]
    out[...] = jnp.zeros_like(out)
    mine = jnp.sum(jnp.where(block == piece // halves, mine, 0.0), axis=1)
    for m in range(members):
        out[m * lev : (m + 1) * lev, :] = mine


def joined(pieces):
    one, one_more, two, two_more = [x[...] for x in pieces]
    return jnp.concatenate([add([one, one_more]), add([two, two_more])], axis=1)


def unpack(spread, value):
    count = value.shape[0]
    spread[0:count, :] = value
    spread[count:, :] = jnp.zeros((spread.shape[0] - count, value.shape[1]), F32)


def first_kernel(lev, *refs):
    vert, vert_t, sd_out, residual, *moved, spread, packed = refs[4:]
    members, levp, unused = residual.shape
    t = joined(refs[:4])
    sd = read_columns(t)
    sd_out[...] = sd
    unpack(spread, t)
    scalars = []
    for m in range(members):
        at = slice(m * lev, m * lev + levp)
        r = dot(vert_t[...], sd * spread[at, :])
        residual[m] = r
        packed[at, :] = sd * dot(vert[...], r)
        scalars.append([total(r * r)])
    put_halves(moved, with_scalars(packed[0 : moved[0].shape[0], :], scalars))


def add_kernel(members, scalars, *refs):
    parts, out = refs[:-1], refs[-1]
    value = add([x[...] for x in parts])
    if scalars:
        value = with_scalars(value, read_scalars(parts, members, scalars))
    out[...] = value.astype(BF16)


def add_halves_kernel(members, scalars, one, one_more, two, two_more, one_out, two_out):
    add_kernel(members, scalars, one, one_more, one_out)
    add_kernel(members, 0, two, two_more, two_out)


def stage_kernel(*refs):
    sems = refs[-1]
    count = len(refs) // 2
    copies = [
        pltpu.make_async_copy(refs[i], refs[count + i], sems.at[i]) for i in range(count)
    ]
    for copy in copies:
        copy.start()
    for copy in copies:
        copy.wait()


def forward_kernel(sends, members, left, right, tiles, *refs):
    z, core, obs = place()
    outs = refs[-len(sends) :]
    rows, lanes = left.shape
    half, width = tiles.shape[1] // 2, tiles.shape[3]
    added = refs[1 : 1 + len(sends)] if len(refs) > len(sends) else [None] * len(sends)
    if added[0] is not None:
        scalars = read_scalars([refs[0], left], members, 2)
    for out, before, (chip, first, count) in zip(outs, added, sends):
        y = [
            jnp.dot(
                x[first : first + count, :],
                tiles[z ^ chip, at : at + half].reshape(lanes, width),
                preferred_element_type=F32,
            )
            for x, at in ((left, 0), (right, half))
        ]
        y = y[0] + y[1]
        if before is not None:
            y = before[...] + y
            if first + count == rows:
                y = with_scalars(y, scalars)
        out[...] = y.astype(out.dtype)


def weigh_kernel(later, last, members, lev, spans, *refs):
    ys, refs = refs[: len(spans)], refs[len(spans) :]
    prec, old_image, old = refs[0], *(refs[1:3] if later else (None, None))
    state, *outs = refs[3 if later else 1 :]
    if not last:
        *outs, image = outs
    rows = prec.shape[0]
    cuts = sorted({first for first, count in spans}) + [rows]
    parts = []
    for low, high in zip(cuts, cuts[1:]):
        held = [
            ref[low - first : high - first, :]
            for ref, (first, count) in zip(ys, spans)
            if first <= low < first + count
        ]
        parts.append(add(held))
    y = parts[0] if len(parts) == 1 else jnp.concatenate(parts, axis=0)
    ends = [ref for ref, (first, count) in zip(ys, spans) if first + count == rows]
    sub = lax.broadcasted_iota(jnp.int32, (8, LANES), 0)
    betas = []
    for m, (norm, cross) in enumerate(read_scalars(ends, members, 2)):
        if later:
            old_norm, old_square = old[m, 0:1, 0:1], old[m, 1:2, 0:1]
            beta = norm / old_norm
            square = norm + 2.0 * beta * cross + beta * beta * old_square
        else:
            beta = jnp.zeros_like(norm)
            square = norm
        betas.append(beta)
        state[m] = jnp.where(sub == 0, norm, jnp.where(sub == 1, square, beta))
    if later:
        y = y + by_member(betas, (rows, 1), lev) * old_image[...]
    if not last:
        image[...] = y
    scaled = prec[...] * y
    energies = [[x] for x in member_sums(scaled * y, members, lev)]
    weighted = with_scalars(scaled, energies).astype(BF16)
    first = 0
    for out in outs:
        out[...] = weighted[first : first + out.shape[0]]
        first = (first + out.shape[0]) % rows


def adjoint_kernel(plan, members, *refs):
    z, core, obs = place()
    ws, tiles, outs = refs[: len(plan)], refs[len(plan)], refs[len(plan) + 1 :]
    rows, lanes = outs[0].shape[0], tiles.shape[1] * LANES
    width = ws[0].shape[1]
    acc = None
    for i in range(tiles.shape[0]):
        w = {first: ref for ref, (chip, first, count) in zip(ws, plan) if chip == i}
        w = [w[first][...] for first in sorted(w)]
        w = w[0] if len(w) == 1 else jnp.concatenate(w, axis=0)
        part = lax.dot_general(
            w, tiles[z ^ i].reshape(lanes, width), NT, preferred_element_type=F32
        )
        acc = part if i == 0 else acc + part
    ends = [ref for ref, (chip, first, count) in zip(ws, plan) if first + count == rows]
    acc = with_scalars(acc, read_scalars(ends, members, 1))
    if len(outs) == 2:
        put_halves(outs, acc)
    else:
        outs[0][...] = acc


def both_cores(members, mine, left, right):
    value = mine[...] + jnp.concatenate([left[...], right[...]], axis=1).astype(F32)
    return with_scalars(value, read_scalars([mine, left], members, 1))


def combine_kernel(members, mine, left, right, *outs):
    put_halves(outs, both_cores(members, mine, left, right))


def combine_columns_kernel(members, mine, left, right, *refs):
    outs, scratch = refs[:-1], refs[-1]
    obs = lax.axis_index("obs")
    scratch[...] = both_cores(members, mine, left, right)
    energies = read_scalars([mine, left], members, 1)
    for i, out in enumerate(outs):
        lane = pl.ds(pl.multiple_of((obs ^ i) * LANES, LANES), LANES)
        out[...] = with_scalars(scratch[:, lane], energies).astype(BF16)


def update_kernel(later, lev, *refs):
    pieces, refs = refs[:4], refs[4:]
    sd, vert, vert_t, state, residual = refs[:5]
    spread, packed = refs[-2:]
    if later:
        old_direction, old_solution, residual_out, solution_out, *moved, direction_out = refs[5:-2]
    else:
        residual_out, solution_out, *moved = refs[5:-2]
    members, levp, unused = residual.shape
    obs = lax.axis_index("obs")
    mine = pl.ds(pl.multiple_of(obs * LANES, LANES), LANES)
    unpack(spread, joined(pieces))
    energies = read_scalars(pieces[:2], members, 1)
    scalars = []
    for m in range(members):
        at = slice(m * lev, m * lev + levp)
        norm, square, beta = state[m, 0:1, 0:1], state[m, 1:2, 0:1], state[m, 2:3, 0:1]
        alpha = norm / (square + energies[m][0])
        r = residual[m]
        if later:
            d = r + beta * old_direction[m]
            direction_out[m] = d
            step = direction_out[m, :, mine]
            solution_out[m] = old_solution[m] + alpha * step
        else:
            d = r
            solution_out[m] = alpha * residual[m, :, mine]
        r = r - alpha * (d + dot(vert_t[...], sd[...] * spread[at, :]))
        residual_out[m] = r
        packed[at, :] = sd[...] * dot(vert[...], r)
        scalars.append([total(r * r), total(r * d)])
    put_halves(moved, with_scalars(packed[0 : moved[0].shape[0], :], scalars))


def increment_kernel(later, sd, vert, state, residual, *refs):
    before, direction, moved = refs[-3:]
    obs = lax.axis_index("obs")
    mine = pl.ds(pl.multiple_of(obs * LANES, LANES), LANES)
    for m in range(residual.shape[0]):
        d = residual[m, :, mine]
        if later:
            d = d + state[m, 2:3, 0:1] * refs[0][m, :, mine]
            before[m] = sd[...] * dot(vert[...], refs[1][m])
        else:
            before[m] = jnp.zeros_like(d)
        direction[m] = d
        moved[m] = sd[...] * dot(vert[...], d)


def last_kernel(parts, lev, *refs):
    pieces, refs = refs[:parts], refs[parts:]
    sd, vert_t, state, residual, before, direction, moved = refs[:7]
    increment_out, residual_out, spread = refs[7:]
    members, levp, unused = residual.shape
    obs = lax.axis_index("obs")
    mine = pl.ds(pl.multiple_of(obs * LANES, LANES), LANES)
    unpack(spread, add([x[...] for x in pieces]))
    energies = read_scalars(pieces, members, 1)
    for m in range(members):
        t = spread[m * lev : m * lev + levp, :]
        alpha = state[m, 0:1, 0:1] / (state[m, 1:2, 0:1] + energies[m][0])
        increment_out[:, m, :] = (before[m] + alpha * moved[m])[0:lev]
        r = residual[m, :, mine] - alpha * (direction[m] + dot(vert_t[...], sd[...] * t))
        residual_out[:, m, :] = r[0:lev]


def per_device(
    n_slab,
    n_obs,
    innovation,
    obs_precision,
    seeds,
    col_sd,
    vert_factor,
    h_values,
    block_obs,
    block_col,
    entry_count,
):
    blocks, lev, profiles = innovation.shape
    members = seeds.shape[0]
    chips = n_slab // 2
    halves = n_slab // blocks
    width = profiles // halves
    colblocks = n_obs
    assert halves * blocks == n_slab and width % LANES == 0 and col_sd.shape[0] == 1
    assert chips & (chips - 1) == 0 and n_obs & (n_obs - 1) == 0
    levp = (lev + 1 + 15) // 16 * 16
    assert members <= 16 and members >= PIECES
    rows = (members * (lev + 1) + 15) // 16 * 16
    lanes = colblocks * LANES
    slab_field = (members, levp, lanes)
    slab_rows = (rows, lanes)
    half_rows = [struct((rows, lanes // 2), BF16)] * 2
    wide = rows + levp - lev + 7
    spread = pltpu.VMEM((wide // 8 * 8, lanes), F32)
    some = rows // 32 * 16
    rest = rows - some
    via = chips == 4
    if via:
        one, two = (0, some), (some, rest)
        most = rows - 32
        near_parts = [(0, most), (most, rows - most)]
        plan = [(0, 0, rows), *((1, *part) for part in near_parts)]
        plan += [(2, *one), (2, *two), (3, *one), (3, *two)]
        sends = [(3, *one), (2, *two), (3, *two), (1, *one), (1, *two), (0, 0, rows), (2, *one)]
    else:
        sends = plan = [(i, 0, rows) for i in range(chips)]
    pad = ((0, levp - lev), (0, levp - lev))
    high = lax.reduce_precision(vert_factor, 8, 7)
    low = vert_factor - high
    vert, vert_t = [
        jnp.concatenate([jnp.pad(x, pad).astype(BF16) for x in parts], axis=1)
        for parts in ((high, high, low), (high.T, high.T, low.T))
    ]
    h_block = h_values.reshape(h_values.shape[2:])
    innovation = jnp.transpose(innovation, (1, 0, 2))
    obs_precision = jnp.transpose(obs_precision, (1, 0, 2))
    product = n_slab * width * lanes * rows
    small = 12 * rows * levp * LANES
    plane_bits = [1 << k for k in range(n_obs.bit_length() - 1)]

    def along(x, i):
        return lax.ppermute(x, "slab", [(s, s ^ (2 * i)) for s in range(n_slab)])

    def plane(x, i):
        return lax.ppermute(x, "obs", [(o, o ^ i) for o in range(n_obs)])

    def swap(x):
        return lax.ppermute(x, "slab", [(s, s ^ 1) for s in range(n_slab)])

    def plane_sum(halves, staged):
        halves = list(halves)
        moved_halves = [None] * len(halves)
        for step, bit in enumerate(plane_bits):
            bits = [bit, plane_bits[len(plane_bits) - 1 - step]]
            for at in range(0, len(halves), 2):
                if step > 0:
                    one, two = halves[at : at + 2]
                    one_more, two_more = moved_halves[at : at + 2]
                    halves[at : at + 2] = call(
                        functools.partial(add_halves_kernel, members, 0 if staged else 1),
                        [struct(one.shape, BF16)] * 2,
                        [],
                        0,
                        one,
                        one_more,
                        two,
                        two_more,
                    )
                for half in range(2):
                    moved_halves[at + half] = plane(halves[at + half], bits[half])
            if step == 0 and staged:
                halves[:] = call(
                    stage_kernel,
                    [struct(x.shape, BF16) for x in halves],
                    [pltpu.SemaphoreType.DMA((len(halves),))],
                    0,
                    *halves,
                    space=HBM,
                )
        return [x for pair in zip(halves, moved_halves) for x in pair]

    def line_sum(moved):
        other = [swap(x) for x in moved]
        shapes = [(count, width) for i, unused, count in sends]
        mine = call(
            functools.partial(forward_kernel, sends, members),
            [struct(shape, F32) for shape in shapes],
            [],
            product,
            *moved,
            own,
        )
        ys = call(
            functools.partial(forward_kernel, sends, members),
            [
                struct(shape, F32 if i == 0 or (via and at == 6) else BF16)
                for at, ((i, *unused), shape) in enumerate(zip(sends, shapes))
            ],
            [],
            product,
            *other,
            partner,
            moved[0],
            *mine,
        )
        if not via:
            return [y if i == 0 else along(y, i) for i, y in enumerate(ys)], [(0, rows)] * chips
        passed, far_rest, last_rest, next_some, next_rest, near, far = ys
        passed = along(passed, 1)
        far_rest, last_rest = along(far_rest, 2), along(last_rest, 3)
        next_some, next_rest = along(next_some, 1), along(next_rest, 1)
        (far,) = call(
            functools.partial(add_kernel, members, 0),
            [struct((some, width), BF16)],
            [],
            0,
            far,
            passed,
        )
        ys = [near, far_rest, last_rest, next_some, next_rest, along(far, 2)]
        return ys, [(0, rows), two, two, one, two, one]

    def line_gather(w, *parts):
        if not via:
            return [w if i == 0 else along(w, i) for i in range(chips)]
        some_w, rest_w, *near = parts
        far = along(some_w, 2)
        far_rest, last_rest = along(rest_w, 2), along(rest_w, 3)
        return [w, *(along(x, 1) for x in near), far, far_rest, along(far, 1), last_rest]

    dense = struct((chips, colblocks, LANES, width), BF16)
    own, for_partner, *partials = call(
        functools.partial(start_kernel, (chips, halves, blocks, lev)),
        [dense, dense] + half_rows,
        [
            pltpu.SMEM(seeds.shape, jnp.int32),
            pltpu.SMEM(block_obs.shape, jnp.int32),
            pltpu.SMEM(block_col.shape, jnp.int32),
            pltpu.SMEM(entry_count.shape, jnp.int32),
            pltpu.VMEM(col_sd.shape, F32),
            pltpu.VMEM((profiles // LANES, levp * blocks, LANES), F32),
            pltpu.VMEM((profiles // LANES, levp * blocks, LANES), F32),
            pltpu.VMEM((n_slab, levp, width), jnp.int32),
            pltpu.VMEM((n_slab // 2, members, levp, width), F32),
            pltpu.VMEM((2, rows, 2 * width), F32),
            pltpu.VMEM((rows, lanes), F32),
            pltpu.VMEM(dense.shape, BF16),
            pltpu.VMEM(dense.shape, BF16),
            pltpu.SemaphoreType.DMA((7 + 2 * (profiles // LANES),)),
            pltpu.SemaphoreType.DMA((h_block.shape[0] * halves,)),
        ],
        2 * product,
        seeds,
        block_obs,
        block_col,
        entry_count,
        col_sd,
        innovation.reshape(lev * blocks, profiles),
        obs_precision.reshape(lev * blocks, profiles),
        h_block,
        space=HBM,
        limit=60,
        stored=2,
    )
    ps = plane_sum(partials, True)
    partner = swap(for_partner)
    (precision,) = call(
        functools.partial(precision_kernel, halves, members),
        [struct((rows, width), F32)],
        [],
        0,
        obs_precision,
    )
    slab_sd, residual, *moved = call(
        functools.partial(first_kernel, lev),
        [struct((1, lanes), F32), struct(slab_field, F32), *half_rows],
        [spread, spread],
        small * colblocks,
        *ps,
        vert,
        vert_t,
    )
    direction = total_step = image = state = None
    for sweep in range(ITERS):
        later, last = sweep > 0, sweep == ITERS - 1
        ys, spans = line_sum(moved)
        state, *weighted = call(
            functools.partial(weigh_kernel, later, last, members, lev, spans),
            [struct((members, 8, LANES), F32)]
            + [struct((n, width), BF16) for n in ((rows, some, rest, most, rows - most) if via else (rows,))]
            + ([] if last else [struct((rows, width), F32)]),
            [],
            0,
            *ys,
            precision,
            *([image, state] if later else []),
        )
        if not last:
            *weighted, image = weighted
        ws = line_gather(*weighted)
        theirs = call(
            functools.partial(adjoint_kernel, plan, members),
            half_rows,
            [],
            product,
            *ws,
            partner,
        )
        theirs = [swap(x) for x in theirs]
        (mine,) = call(
            functools.partial(adjoint_kernel, plan, members),
            [struct(slab_rows, F32)],
            [],
            product,
            *ws,
            own,
        )
        known = [vert, vert_t, state, residual]
        if later:
            known += [direction, total_step]
        if last:
            ps = call(
                functools.partial(combine_columns_kernel, members),
                [struct((rows, LANES), BF16)] * n_obs,
                [pltpu.VMEM(slab_rows, F32)],
                0,
                mine,
                *theirs,
            )
            ps = [ps[0]] + [plane(ps[i], i) for i in reversed(range(1, n_obs))]
            own_field = struct((members, levp, LANES), F32)
            before, d, u_d = call(
                functools.partial(increment_kernel, later),
                [own_field] * 3,
                [],
                small,
                col_sd,
                vert,
                state,
                residual,
                *([direction, total_step] if later else []),
            )
            outputs = call(
                functools.partial(last_kernel, len(ps), lev),
                [struct((lev, members, LANES), F32)] * 2,
                [pltpu.VMEM((wide // 8 * 8, LANES), F32)],
                small,
                *ps,
                col_sd,
                vert_t,
                state,
                residual,
                before,
                d,
                u_d,
            )
            break
        ps = call(
            functools.partial(combine_kernel, members), half_rows, [], 0, mine, *theirs
        )
        ps = plane_sum(ps, False)
        outs = [
            struct(slab_field, F32),
            struct((members, levp, LANES), F32),
            *half_rows,
        ]
        if later:
            outs.append(struct(slab_field, F32))
        r, total_step, *moved = call(
            functools.partial(update_kernel, later, lev),
            outs,
            [spread, spread],
            small * colblocks,
            *ps,
            slab_sd,
            *known,
        )
        direction, residual = (moved.pop() if later else residual), r
    return tuple(jnp.transpose(x, (1, 0, 2))[None] for x in outputs)


def solution(mesh):
    return jax.shard_map(
        functools.partial(per_device, mesh.shape["slab"], mesh.shape["obs"]),
        mesh=mesh,
        in_specs=(
            P("obs", None, None),
            P("obs", None, None),
            P(),
            P(("slab", "obs"), None),
            P(),
            P("slab", "obs", None, None, None),
            P("slab", "obs", None),
            P("slab", "obs", None),
            P("slab", "obs"),
        ),
        out_specs=(P(("slab", "obs"), None, None, None), P(("slab", "obs"), None, None, None)),
        check_vma=False,
    )
```

```python
import functools

import jax
import jax.numpy as jnp
from jax import lax
from jax.experimental import pallas as pl
from jax.experimental.pallas import tpu as pltpu
from jax.sharding import PartitionSpec as P

ITERS = 2
LANES = 128
PIECES = 3
PRIME = 32749
VMEM = pl.BlockSpec(memory_space=pltpu.VMEM)
HBM = pl.BlockSpec(memory_space=pltpu.HBM)
F32 = jnp.float32
BF16 = jnp.bfloat16
NT = (((1,), (1,)), ((), ()))


def call(kernel, outs, scratch, flops, *args, space=VMEM, limit=24, stored=0):
    nbytes = sum(a.size * a.dtype.itemsize for a in (*args, *outs))
    return pl.pallas_call(
        kernel,
        out_shape=outs,
        in_specs=[space] * len(args),
        out_specs=[HBM] * stored + [VMEM] * (len(outs) - stored),
        scratch_shapes=scratch,
        compiler_params=pltpu.CompilerParams(vmem_limit_bytes=limit * 1024 * 1024),
        cost_estimate=pl.CostEstimate(flops=flops, bytes_accessed=nbytes, transcendentals=0),
    )(*args)


def struct(shape, dtype):
    return jax.ShapeDtypeStruct(shape, dtype)


def place():
    slab = lax.axis_index("slab")
    return slab // 2, slab % 2, lax.axis_index("obs")


def add(parts):
    value = parts[0].astype(F32)
    for part in parts[1:]:
        value = value + part.astype(F32)
    return value


def dot(matrix, x):
    high = x.astype(BF16)
    rest = (x - high.astype(F32)).astype(BF16)
    x = jnp.concatenate([high, rest, high], axis=0)
    return jnp.dot(matrix, x, preferred_element_type=F32)


def total(x):
    return jnp.sum(jnp.sum(x, axis=0, keepdims=True), axis=1, keepdims=True)


def with_scalars(body, values):
    count = body.shape[0]
    tail = body[count - 16 :]
    sub = lax.broadcasted_iota(jnp.int32, tail.shape, 0) - (16 - len(values))
    lanes = lax.broadcasted_iota(jnp.int32, tail.shape, 1)
    line = jnp.zeros(tail.shape, F32)
    for m, member in enumerate(values):
        for q, value in enumerate(member):
            rest = value
            for piece in range(PIECES):
                part = rest.astype(BF16).astype(F32)
                rest = rest - part
                line = jnp.where((sub == m) & (lanes == q * PIECES + piece), part, line)
    return jnp.concatenate([body[: count - 16], jnp.where(sub >= 0, line, tail)], axis=0)


def read_scalars(refs, members, count):
    tail = add([ref[ref.shape[0] - 16 :, 0:LANES] for ref in refs])
    sub = lax.broadcasted_iota(jnp.int32, tail.shape, 0) - (16 - members)
    lanes = lax.broadcasted_iota(jnp.int32, tail.shape, 1)
    return [
        [
            total(
                jnp.where(
                    (sub == m) & (lanes >= q * PIECES) & (lanes < (q + 1) * PIECES), tail, 0.0
                )
            )
            for q in range(count)
        ]
        for m in range(members)
    ]


def by_member(values, shape, lev):
    rows = lax.broadcasted_iota(jnp.int32, shape, 0)
    out = jnp.zeros(shape, F32)
    for m, value in enumerate(values):
        out = jnp.where((rows >= m * lev) & (rows < (m + 1) * lev), value, out)
    return out


def member_sums(x, members, lev):
    lines = jnp.sum(x, axis=1, keepdims=True)
    rows = lax.broadcasted_iota(jnp.int32, lines.shape, 0)
    return [
        jnp.sum(
            jnp.where((rows >= m * lev) & (rows < (m + 1) * lev), lines, 0.0),
            axis=0,
            keepdims=True,
        )
        for m in range(members)
    ]


def remainder(x, factor):
    return x - (x.astype(F32) * factor).astype(jnp.int32) * PRIME


def start_kernel(
    dims, seeds_in, ids_in, cols_in, count_in, sd_in, innov_in, prec_in, h, own_out, partner_out, *rest
):
    chips, halves, blocks, lev = dims
    outs = rest[:-15]
    seeds, ids, cols, count, sd, innov, prec, bases, hashed, scratch, acc = rest[-15:-4]
    own, partner, sems, h_sems = rest[-4:]
    z, core, obs = place()
    strips = innov.shape[0]
    profiles = strips * LANES
    colblocks, width = own.shape[1], own.shape[3]
    members, levp = hashed.shape[1], hashed.shape[2]
    rows = acc.shape[0]

    pairs = [(seeds_in, seeds), (ids_in, ids), (cols_in, cols), (count_in, count), (sd_in, sd)]
    small = [pltpu.make_async_copy(x, y, sems.at[i]) for i, (x, y) in enumerate(pairs)]
    for copy in small:
        copy.start()
    large = []
    for x, y in ((innov_in, innov), (prec_in, prec)):
        for t in range(strips):
            at = len(pairs) + len(large)
            large.append(
                pltpu.make_async_copy(
                    x.at[:, t * LANES : (t + 1) * LANES], y.at[t, 0 : lev * blocks, :], sems.at[at]
                )
            )
    for copy in large:
        copy.start()
    own[...] = jnp.zeros_like(own)
    partner[...] = jnp.zeros_like(partner)
    scratch[...] = jnp.zeros_like(scratch)
    order = [(source, zz) for source in range(2) for zz in range(chips)]
    shape = (levp, width)
    spot = lax.broadcasted_iota(jnp.int32, shape, 0) * profiles
    spot = spot + lax.broadcasted_iota(jnp.int32, shape, 1)

    def piece_at(at):
        source, zz = order[at]
        return 2 * zz + (core if source == 0 else 1 - core)

    for at in range(len(order)):
        piece = piece_at(at)
        first = (obs * blocks + piece // halves) * (lev * profiles) + (piece % halves) * width
        bases[at] = remainder(7919 * remainder(spot + first, 1.0 / PRIME), 1.0 / PRIME)
    for copy in small:
        copy.wait()

    def tile_copy(n, half, target):
        lanes = pl.ds(half * width, width)
        return pltpu.make_async_copy(h.at[n, :, lanes], target, h_sems.at[n * halves + half])

    def put(n, carry):
        for half in range(halves):
            piece, k = ids[0, 0, n] * halves + half, cols[0, 0, n]

            @pl.when(piece % 2 == core)
            def _():
                tile_copy(n, half, own.at[piece // 2, k]).start()

            @pl.when(piece % 2 != core)
            def _():
                tile_copy(n, half, partner.at[piece // 2, k]).start()

        return carry

    lax.fori_loop(0, count[0, 0], put, 0)

    starts = [lax.rem(seeds[m], PRIME) - PRIME for m in range(members)]
    low = (1.0 - 2.0**-21) / PRIME

    def draw(at, m):
        k0 = bases[at] + starts[m]
        k1 = remainder(k0 * k0 + 12345, 1.0 / PRIME)
        k2 = remainder(k1 * k1 + 2719, low)
        return jnp.where(k2 >= PRIME, k2 - PRIME, k2).astype(F32)

    early = len(order) // 2
    for at in range(early):
        for m in range(members):
            hashed[at, m] = draw(at, m)
    for copy in large:
        copy.wait()

    def arrive(n, carry):
        for half in range(halves):
            tile_copy(n, half, own.at[0, 0]).wait()
        return carry

    lax.fori_loop(0, count[0, 0], arrive, 0)
    kept = [
        pltpu.make_async_copy(x, y, sems.at[len(pairs) + len(large) + i])
        for i, (x, y) in enumerate(((partner, partner_out), (own, own_out)))
    ]
    for copy in kept:
        copy.start()

    for at in range(len(order)):
        source, zz = order[at]
        piece = piece_at(at)
        b = piece // halves
        strip = (piece % halves) * (width // LANES)
        p, d = [
            jnp.concatenate(
                [
                    x[strip + t, pl.ds(b, lev, stride=blocks), :]
                    for t in range(width // LANES)
                ],
                axis=1,
            )
            for x in (prec, innov)
        ]
        gain = 3.4 * p * lax.rsqrt(p)
        offset = p * d - 0.5 * gain
        gain = gain * (1.0 / PRIME)
        slot, side = at // 2 % 2, at % 2
        for m in range(members):
            k2 = hashed[at, m, 0:lev, :] if at < early else draw(at, m)[0:lev]
            scratch[slot, m * lev : (m + 1) * lev, side * width : (side + 1) * width] = (
                offset + gain * k2
            )
        if side == 0:
            continue
        tiles = own if source == 0 else partner
        tiles = [tiles[i].reshape(colblocks * LANES, width) for i in (zz - 1, zz)]
        part = lax.dot_general(
            scratch[slot].astype(BF16),
            jnp.concatenate(tiles, axis=1),
            NT,
            preferred_element_type=F32,
        )
        if at == 1:
            acc[...] = part
        else:
            acc[...] += part

    line = jnp.concatenate([sd[...]] * colblocks, axis=1)
    put_halves(outs, with_columns(acc[...], line, obs, members))
    for copy in kept:
        copy.wait()


def put_halves(outs, value):
    half = value.shape[1] // 2
    outs[0][...] = value[:, :half].astype(BF16)
    outs[1][...] = value[:, half:].astype(BF16)


def with_columns(body, line, obs, members):
    tail = body[body.shape[0] - 16 :]
    sub = lax.broadcasted_iota(jnp.int32, tail.shape, 0)
    mine = lax.broadcasted_iota(jnp.int32, tail.shape, 1) // LANES == obs
    rest = line
    for piece in range(PIECES):
        part = rest.astype(BF16).astype(F32)
        rest = rest - part
        tail = jnp.where((sub == 16 - PIECES + piece) & mine, part, tail)
    return jnp.concatenate([body[: body.shape[0] - 16], tail], axis=0)


def read_columns(body):
    tail = body[body.shape[0] - 16 :]
    sub = lax.broadcasted_iota(jnp.int32, tail.shape, 0)
    return jnp.sum(jnp.where(sub >= 16 - PIECES, tail, 0.0), axis=0, keepdims=True)


def precision_kernel(halves, members, prec, out):
    z, core, unused = place()
    piece = 2 * z + core
    lev, blocks, unused = prec.shape
    width = out.shape[1]
    block = lax.broadcasted_iota(jnp.int32, (lev, blocks, width), 1)
    if halves == 1:
        mine = prec[...]
    else:
        mine = prec[:, :, pl.ds(pl.multiple_of((piece % halves) * width, LANES), width)]
    out[...] = jnp.zeros_like(out)
    mine = jnp.sum(jnp.where(block == piece // halves, mine, 0.0), axis=1)
    for m in range(members):
        out[m * lev : (m + 1) * lev, :] = mine


def joined(pieces):
    one, one_more, two, two_more = [x[...] for x in pieces]
    return jnp.concatenate([add([one, one_more]), add([two, two_more])], axis=1)


def unpack(spread, value):
    count = value.shape[0]
    spread[0:count, :] = value
    spread[count:, :] = jnp.zeros((spread.shape[0] - count, value.shape[1]), F32)


def first_kernel(lev, *refs):
    vert, vert_t, sd_out, residual, moved, spread, packed = refs[4:]
    members, levp, unused = residual.shape
    t = joined(refs[:4])
    sd = read_columns(t)
    sd_out[...] = sd
    unpack(spread, t)
    scalars = []
    for m in range(members):
        at = slice(m * lev, m * lev + levp)
        r = dot(vert_t[...], sd * spread[at, :])
        residual[m] = r
        packed[at, :] = sd * dot(vert[...], r)
        scalars.append([total(r * r)])
    moved[...] = with_scalars(packed[0 : moved.shape[0], :], scalars).astype(BF16)


def add_kernel(members, scalars, *refs):
    parts, out = refs[:-1], refs[-1]
    value = add([x[...] for x in parts])
    if scalars:
        value = with_scalars(value, read_scalars(parts, members, scalars))
    out[...] = value.astype(BF16)


def add_halves_kernel(members, scalars, one, one_more, two, two_more, one_out, two_out):
    add_kernel(members, scalars, one, one_more, one_out)
    add_kernel(members, 0, two, two_more, two_out)


def stage_kernel(*refs):
    sems = refs[-1]
    count = len(refs) // 2
    copies = [
        pltpu.make_async_copy(refs[i], refs[count + i], sems.at[i]) for i in range(count)
    ]
    for copy in copies:
        copy.start()
    for copy in copies:
        copy.wait()


def forward_kernel(sends, members, x, tiles, *refs):
    z, core, obs = place()
    outs = refs[-len(sends) :]
    rows, lanes = x.shape
    width = tiles.shape[3]
    added = refs[1 : 1 + len(sends)] if len(refs) > len(sends) else [None] * len(sends)
    if added[0] is not None:
        scalars = read_scalars([refs[0], x], members, 2)
    for out, before, (chip, first, count) in zip(outs, added, sends):
        y = jnp.dot(
            x[first : first + count, :],
            tiles[z ^ chip].reshape(lanes, width),
            preferred_element_type=F32,
        )
        if before is not None:
            y = before[...] + y
            if first + count == rows:
                y = with_scalars(y, scalars)
        out[...] = y.astype(out.dtype)


def weigh_kernel(later, last, members, lev, spans, *refs):
    ys, refs = refs[: len(spans)], refs[len(spans) :]
    prec, old_image, old = refs[0], *(refs[1:3] if later else (None, None))
    state, *outs = refs[3 if later else 1 :]
    if not last:
        *outs, image = outs
    rows = prec.shape[0]
    cuts = sorted({first for first, count in spans}) + [rows]
    parts = []
    for low, high in zip(cuts, cuts[1:]):
        held = [
            ref[low - first : high - first, :]
            for ref, (first, count) in zip(ys, spans)
            if first <= low < first + count
        ]
        parts.append(add(held))
    y = parts[0] if len(parts) == 1 else jnp.concatenate(parts, axis=0)
    ends = [ref for ref, (first, count) in zip(ys, spans) if first + count == rows]
    sub = lax.broadcasted_iota(jnp.int32, (8, LANES), 0)
    betas = []
    for m, (norm, cross) in enumerate(read_scalars(ends, members, 2)):
        if later:
            old_norm, old_square = old[m, 0:1, 0:1], old[m, 1:2, 0:1]
            beta = norm / old_norm
            square = norm + 2.0 * beta * cross + beta * beta * old_square
        else:
            beta = jnp.zeros_like(norm)
            square = norm
        betas.append(beta)
        state[m] = jnp.where(sub == 0, norm, jnp.where(sub == 1, square, beta))
    if later:
        y = y + by_member(betas, (rows, 1), lev) * old_image[...]
    if not last:
        image[...] = y
    scaled = prec[...] * y
    energies = [[x] for x in member_sums(scaled * y, members, lev)]
    weighted = with_scalars(scaled, energies).astype(BF16)
    first = 0
    for out in outs:
        out[...] = weighted[first : first + out.shape[0]]
        first = (first + out.shape[0]) % rows


def adjoint_kernel(plan, members, *refs):
    z, core, obs = place()
    ws, tiles, out = refs[: len(plan)], refs[len(plan)], refs[len(plan) + 1]
    rows, lanes = out.shape
    width = ws[0].shape[1]
    acc = None
    for i in range(tiles.shape[0]):
        w = {first: ref for ref, (chip, first, count) in zip(ws, plan) if chip == i}
        w = [w[first][...] for first in sorted(w)]
        w = w[0] if len(w) == 1 else jnp.concatenate(w, axis=0)
        part = lax.dot_general(
            w, tiles[z ^ i].reshape(lanes, width), NT, preferred_element_type=F32
        )
        acc = part if i == 0 else acc + part
    ends = [ref for ref, (chip, first, count) in zip(ws, plan) if first + count == rows]
    out[...] = with_scalars(acc, read_scalars(ends, members, 1)).astype(out.dtype)


def combine_kernel(members, mine, theirs, *outs):
    value = mine[...] + theirs[...].astype(F32)
    put_halves(outs, with_scalars(value, read_scalars([mine, theirs], members, 1)))


def combine_columns_kernel(members, mine, theirs, *outs):
    obs = lax.axis_index("obs")
    energies = read_scalars([mine, theirs], members, 1)
    for i, out in enumerate(outs):
        lane = pl.ds(pl.multiple_of((obs ^ i) * LANES, LANES), LANES)
        value = mine[:, lane] + theirs[:, lane].astype(F32)
        out[...] = with_scalars(value, energies).astype(BF16)


def update_kernel(later, lev, *refs):
    pieces, refs = refs[:4], refs[4:]
    sd, vert, vert_t, state, residual = refs[:5]
    spread, packed = refs[-2:]
    if later:
        old_direction, old_solution, residual_out, solution_out, moved, direction_out = refs[5:-2]
    else:
        residual_out, solution_out, moved = refs[5:-2]
    members, levp, unused = residual.shape
    obs = lax.axis_index("obs")
    mine = pl.ds(pl.multiple_of(obs * LANES, LANES), LANES)
    unpack(spread, joined(pieces))
    energies = read_scalars(pieces[:2], members, 1)
    scalars = []
    for m in range(members):
        at = slice(m * lev, m * lev + levp)
        norm, square, beta = state[m, 0:1, 0:1], state[m, 1:2, 0:1], state[m, 2:3, 0:1]
        alpha = norm / (square + energies[m][0])
        r = residual[m]
        if later:
            d = r + beta * old_direction[m]
            direction_out[m] = d
            step = direction_out[m, :, mine]
            solution_out[m] = old_solution[m] + alpha * step
        else:
            d = r
            solution_out[m] = alpha * residual[m, :, mine]
        r = r - alpha * (d + dot(vert_t[...], sd[...] * spread[at, :]))
        residual_out[m] = r
        packed[at, :] = sd[...] * dot(vert[...], r)
        scalars.append([total(r * r), total(r * d)])
    moved[...] = with_scalars(packed[0 : moved.shape[0], :], scalars).astype(BF16)


def increment_kernel(later, sd, vert, state, residual, *refs):
    before, direction, moved = refs[-3:]
    obs = lax.axis_index("obs")
    mine = pl.ds(pl.multiple_of(obs * LANES, LANES), LANES)
    for m in range(residual.shape[0]):
        d = residual[m, :, mine]
        if later:
            d = d + state[m, 2:3, 0:1] * refs[0][m, :, mine]
            before[m] = sd[...] * dot(vert[...], refs[1][m])
        else:
            before[m] = jnp.zeros_like(d)
        direction[m] = d
        moved[m] = sd[...] * dot(vert[...], d)


def last_kernel(parts, lev, *refs):
    pieces, refs = refs[:parts], refs[parts:]
    sd, vert_t, state, residual, before, direction, moved = refs[:7]
    increment_out, residual_out, spread = refs[7:]
    members, levp, unused = residual.shape
    obs = lax.axis_index("obs")
    mine = pl.ds(pl.multiple_of(obs * LANES, LANES), LANES)
    unpack(spread, add([x[...] for x in pieces]))
    energies = read_scalars(pieces, members, 1)
    for m in range(members):
        t = spread[m * lev : m * lev + levp, :]
        alpha = state[m, 0:1, 0:1] / (state[m, 1:2, 0:1] + energies[m][0])
        increment_out[:, m, :] = (before[m] + alpha * moved[m])[0:lev]
        r = residual[m, :, mine] - alpha * (direction[m] + dot(vert_t[...], sd[...] * t))
        residual_out[:, m, :] = r[0:lev]


def per_device(
    n_slab,
    n_obs,
    innovation,
    obs_precision,
    seeds,
    col_sd,
    vert_factor,
    h_values,
    block_obs,
    block_col,
    entry_count,
):
    blocks, lev, profiles = innovation.shape
    members = seeds.shape[0]
    chips = n_slab // 2
    halves = n_slab // blocks
    width = profiles // halves
    colblocks = n_obs
    assert halves * blocks == n_slab and width % LANES == 0 and col_sd.shape[0] == 1
    assert chips & (chips - 1) == 0 and n_obs & (n_obs - 1) == 0
    levp = (lev + 1 + 15) // 16 * 16
    assert members <= 16 and members >= PIECES
    rows = (members * (lev + 1) + 15) // 16 * 16
    lanes = colblocks * LANES
    slab_field = (members, levp, lanes)
    slab_rows = (rows, lanes)
    half_rows = [struct((rows, lanes // 2), BF16)] * 2
    wide = rows + levp - lev + 7
    spread = pltpu.VMEM((wide // 8 * 8, lanes), F32)
    some = rows // 38 * 16
    rest = rows - some
    via = chips == 4
    if via:
        one, two = (0, some), (some, rest)
        most = rows - 64
        near_parts = [(0, most), (most, rows - most)]
        plan = [(0, 0, rows), *((1, *part) for part in near_parts)]
        plan += [(2, *one), (2, *two), (3, *one), (3, *two)]
        sends = [(3, *one), (2, *two), (3, *two), (1, *one), (1, *two), (0, 0, rows), (2, *one)]
    else:
        sends = plan = [(i, 0, rows) for i in range(chips)]
    pad = ((0, levp - lev), (0, levp - lev))
    high = lax.reduce_precision(vert_factor, 8, 7)
    low = vert_factor - high
    vert, vert_t = [
        jnp.concatenate([jnp.pad(x, pad).astype(BF16) for x in parts], axis=1)
        for parts in ((high, high, low), (high.T, high.T, low.T))
    ]
    h_block = h_values.reshape(h_values.shape[2:])
    innovation = jnp.transpose(innovation, (1, 0, 2))
    obs_precision = jnp.transpose(obs_precision, (1, 0, 2))
    product = n_slab * width * lanes * rows
    small = 12 * rows * levp * LANES
    plane_bits = [1 << k for k in range(n_obs.bit_length() - 1)]

    def along(x, i):
        return lax.ppermute(x, "slab", [(s, s ^ (2 * i)) for s in range(n_slab)])

    def plane(x, i):
        return lax.ppermute(x, "obs", [(o, o ^ i) for o in range(n_obs)])

    def swap(x):
        return lax.ppermute(x, "slab", [(s, s ^ 1) for s in range(n_slab)])

    def plane_sum(halves, staged):
        halves = list(halves)
        moved_halves = [None] * len(halves)
        for step, bit in enumerate(plane_bits):
            bits = [bit, plane_bits[len(plane_bits) - 1 - step]]
            for at in range(0, len(halves), 2):
                if step > 0:
                    one, two = halves[at : at + 2]
                    one_more, two_more = moved_halves[at : at + 2]
                    halves[at : at + 2] = call(
                        functools.partial(add_halves_kernel, members, 0 if staged else 1),
                        [struct(one.shape, BF16)] * 2,
                        [],
                        0,
                        one,
                        one_more,
                        two,
                        two_more,
                    )
                for half in range(2):
                    moved_halves[at + half] = plane(halves[at + half], bits[half])
            if step == 0 and staged:
                halves[:] = call(
                    stage_kernel,
                    [struct(x.shape, BF16) for x in halves],
                    [pltpu.SemaphoreType.DMA((len(halves),))],
                    0,
                    *halves,
                    space=HBM,
                )
        return [x for pair in zip(halves, moved_halves) for x in pair]

    def line_sum(moved, other):
        shapes = [(count, width) for i, unused, count in sends]
        mine = call(
            functools.partial(forward_kernel, sends, members),
            [struct(shape, F32) for shape in shapes],
            [],
            product,
            moved,
            own,
        )
        ys = call(
            functools.partial(forward_kernel, sends, members),
            [
                struct(shape, F32 if i == 0 or (via and at == 6) else BF16)
                for at, ((i, *unused), shape) in enumerate(zip(sends, shapes))
            ],
            [],
            product,
            other,
            partner,
            moved,
            *mine,
        )
        if not via:
            return [y if i == 0 else along(y, i) for i, y in enumerate(ys)], [(0, rows)] * chips
        passed, far_rest, last_rest, next_some, next_rest, near, far = ys
        passed = along(passed, 1)
        far_rest, last_rest = along(far_rest, 2), along(last_rest, 3)
        next_some, next_rest = along(next_some, 1), along(next_rest, 1)
        (far,) = call(
            functools.partial(add_kernel, members, 0),
            [struct((some, width), BF16)],
            [],
            0,
            far,
            passed,
        )
        ys = [near, far_rest, last_rest, next_some, next_rest, along(far, 2)]
        return ys, [(0, rows), two, two, one, two, one]

    def line_gather(w, *parts):
        if not via:
            return [w if i == 0 else along(w, i) for i in range(chips)]
        some_w, rest_w, *near = parts
        far = along(some_w, 2)
        far_rest, last_rest = along(rest_w, 2), along(rest_w, 3)
        return [w, *(along(x, 1) for x in near), far, far_rest, along(far, 1), last_rest]

    dense = struct((chips, colblocks, LANES, width), BF16)
    own, for_partner, *partials = call(
        functools.partial(start_kernel, (chips, halves, blocks, lev)),
        [dense, dense] + half_rows,
        [
            pltpu.SMEM(seeds.shape, jnp.int32),
            pltpu.SMEM(block_obs.shape, jnp.int32),
            pltpu.SMEM(block_col.shape, jnp.int32),
            pltpu.SMEM(entry_count.shape, jnp.int32),
            pltpu.VMEM(col_sd.shape, F32),
            pltpu.VMEM((profiles // LANES, levp * blocks, LANES), F32),
            pltpu.VMEM((profiles // LANES, levp * blocks, LANES), F32),
            pltpu.VMEM((n_slab, levp, width), jnp.int32),
            pltpu.VMEM((n_slab // 2, members, levp, width), F32),
            pltpu.VMEM((2, rows, 2 * width), F32),
            pltpu.VMEM((rows, lanes), F32),
            pltpu.VMEM(dense.shape, BF16),
            pltpu.VMEM(dense.shape, BF16),
            pltpu.SemaphoreType.DMA((7 + 2 * (profiles // LANES),)),
            pltpu.SemaphoreType.DMA((h_block.shape[0] * halves,)),
        ],
        2 * product,
        seeds,
        block_obs,
        block_col,
        entry_count,
        col_sd,
        innovation.reshape(lev * blocks, profiles),
        obs_precision.reshape(lev * blocks, profiles),
        h_block,
        space=HBM,
        limit=60,
        stored=2,
    )
    ps = plane_sum(partials, True)
    partner = swap(for_partner)
    (precision,) = call(
        functools.partial(precision_kernel, halves, members),
        [struct((rows, width), F32)],
        [],
        0,
        obs_precision,
    )
    slab_sd, residual, moved = call(
        functools.partial(first_kernel, lev),
        [struct((1, lanes), F32), struct(slab_field, F32), struct(slab_rows, BF16)],
        [spread, spread],
        small * colblocks,
        *ps,
        vert,
        vert_t,
    )
    direction = total_step = image = state = None
    for sweep in range(ITERS):
        later, last = sweep > 0, sweep == ITERS - 1
        ys, spans = line_sum(moved, swap(moved))
        state, *weighted = call(
            functools.partial(weigh_kernel, later, last, members, lev, spans),
            [struct((members, 8, LANES), F32)]
            + [struct((n, width), BF16) for n in ((rows, some, rest, most, rows - most) if via else (rows,))]
            + ([] if last else [struct((rows, width), F32)]),
            [],
            0,
            *ys,
            precision,
            *([image, state] if later else []),
        )
        if not last:
            *weighted, image = weighted
        ws = line_gather(*weighted)
        (theirs,) = call(
            functools.partial(adjoint_kernel, plan, members),
            [struct(slab_rows, BF16)],
            [],
            product,
            *ws,
            partner,
        )
        theirs = swap(theirs)
        (mine,) = call(
            functools.partial(adjoint_kernel, plan, members),
            [struct(slab_rows, F32)],
            [],
            product,
            *ws,
            own,
        )
        known = [vert, vert_t, state, residual]
        if later:
            known += [direction, total_step]
        if last:
            ps = call(
                functools.partial(combine_columns_kernel, members),
                [struct((rows, LANES), BF16)] * n_obs,
                [],
                0,
                mine,
                theirs,
            )
            ps = [ps[0]] + [plane(ps[i], i) for i in reversed(range(1, n_obs))]
            own_field = struct((members, levp, LANES), F32)
            before, d, u_d = call(
                functools.partial(increment_kernel, later),
                [own_field] * 3,
                [],
                small,
                col_sd,
                vert,
                state,
                residual,
                *([direction, total_step] if later else []),
            )
            outputs = call(
                functools.partial(last_kernel, len(ps), lev),
                [struct((lev, members, LANES), F32)] * 2,
                [pltpu.VMEM((wide // 8 * 8, LANES), F32)],
                small,
                *ps,
                col_sd,
                vert_t,
                state,
                residual,
                before,
                d,
                u_d,
            )
            break
        ps = call(
            functools.partial(combine_kernel, members), half_rows, [], 0, mine, theirs
        )
        ps = plane_sum(ps, False)
        outs = [
            struct(slab_field, F32),
            struct((members, levp, LANES), F32),
            struct(slab_rows, BF16),
        ]
        if later:
            outs.append(struct(slab_field, F32))
        r, total_step, moved, *d = call(
            functools.partial(update_kernel, later, lev),
            outs,
            [spread, spread],
            small * colblocks,
            *ps,
            slab_sd,
            *known,
        )
        direction, residual = (d[0] if later else residual), r
    return tuple(jnp.transpose(x, (1, 0, 2))[None] for x in outputs)


def solution(mesh):
    return jax.shard_map(
        functools.partial(per_device, mesh.shape["slab"], mesh.shape["obs"]),
        mesh=mesh,
        in_specs=(
            P("obs", None, None),
            P("obs", None, None),
            P(),
            P(("slab", "obs"), None),
            P(),
            P("slab", "obs", None, None, None),
            P("slab", "obs", None),
            P("slab", "obs", None),
            P("slab", "obs"),
        ),
        out_specs=(P(("slab", "obs"), None, None, None), P(("slab", "obs"), None, None, None)),
        check_vma=False,
    )
```

```python
import functools

import jax
import jax.numpy as jnp
from jax import lax
from jax.experimental import pallas as pl
from jax.experimental.pallas import tpu as pltpu
from jax.sharding import PartitionSpec as P

ITERS = 2
LANES = 128
PIECES = 3
PRIME = 32749
VMEM = pl.BlockSpec(memory_space=pltpu.VMEM)
HBM = pl.BlockSpec(memory_space=pltpu.HBM)
F32 = jnp.float32
BF16 = jnp.bfloat16
NT = (((1,), (1,)), ((), ()))


def call(kernel, outs, scratch, flops, *args, space=VMEM, limit=24, stored=0):
    nbytes = sum(a.size * a.dtype.itemsize for a in (*args, *outs))
    return pl.pallas_call(
        kernel,
        out_shape=outs,
        in_specs=[space] * len(args),
        out_specs=[HBM] * stored + [VMEM] * (len(outs) - stored),
        scratch_shapes=scratch,
        compiler_params=pltpu.CompilerParams(vmem_limit_bytes=limit * 1024 * 1024),
        cost_estimate=pl.CostEstimate(flops=flops, bytes_accessed=nbytes, transcendentals=0),
    )(*args)


def struct(shape, dtype):
    return jax.ShapeDtypeStruct(shape, dtype)


def place():
    slab = lax.axis_index("slab")
    return slab // 2, slab % 2, lax.axis_index("obs")


def add(parts):
    value = parts[0].astype(F32)
    for part in parts[1:]:
        value = value + part.astype(F32)
    return value


def dot(matrix, x):
    high = x.astype(BF16)
    rest = (x - high.astype(F32)).astype(BF16)
    x = jnp.concatenate([high, rest, high], axis=0)
    return jnp.dot(matrix, x, preferred_element_type=F32)


def total(x):
    return jnp.sum(jnp.sum(x, axis=0, keepdims=True), axis=1, keepdims=True)


def with_scalars(body, values):
    count = body.shape[0]
    tail = body[count - 16 :]
    sub = lax.broadcasted_iota(jnp.int32, tail.shape, 0) - (16 - len(values))
    lanes = lax.broadcasted_iota(jnp.int32, tail.shape, 1)
    line = jnp.zeros(tail.shape, F32)
    for m, member in enumerate(values):
        for q, value in enumerate(member):
            rest = value
            for piece in range(PIECES):
                part = rest.astype(BF16).astype(F32)
                rest = rest - part
                line = jnp.where((sub == m) & (lanes == q * PIECES + piece), part, line)
    return jnp.concatenate([body[: count - 16], jnp.where(sub >= 0, line, tail)], axis=0)


def read_scalars(refs, members, count):
    tail = add([ref[ref.shape[0] - 16 :, 0:LANES] for ref in refs])
    sub = lax.broadcasted_iota(jnp.int32, tail.shape, 0) - (16 - members)
    lanes = lax.broadcasted_iota(jnp.int32, tail.shape, 1)
    return [
        [
            total(
                jnp.where(
                    (sub == m) & (lanes >= q * PIECES) & (lanes < (q + 1) * PIECES), tail, 0.0
                )
            )
            for q in range(count)
        ]
        for m in range(members)
    ]


def by_member(values, shape, lev):
    rows = lax.broadcasted_iota(jnp.int32, shape, 0)
    out = jnp.zeros(shape, F32)
    for m, value in enumerate(values):
        out = jnp.where((rows >= m * lev) & (rows < (m + 1) * lev), value, out)
    return out


def member_sums(x, members, lev):
    lines = jnp.sum(x, axis=1, keepdims=True)
    rows = lax.broadcasted_iota(jnp.int32, lines.shape, 0)
    return [
        jnp.sum(
            jnp.where((rows >= m * lev) & (rows < (m + 1) * lev), lines, 0.0),
            axis=0,
            keepdims=True,
        )
        for m in range(members)
    ]


def remainder(x, factor):
    return x - (x.astype(F32) * factor).astype(jnp.int32) * PRIME


def start_kernel(
    dims, seeds_in, ids_in, cols_in, count_in, sd_in, innov_in, prec_in, h, own_out, partner_out, *rest
):
    chips, halves, blocks, lev = dims
    outs = rest[:-14]
    seeds, ids, cols, count, sd, innov, prec, bases, hashed, scratch, acc = rest[-14:-3]
    both, sems, h_sems = rest[-3:]
    own, partner = both.at[0], both.at[1]
    z, core, obs = place()
    strips = innov.shape[0]
    profiles = strips * LANES
    colblocks, width = own.shape[1], own.shape[3]
    members, levp = hashed.shape[1], hashed.shape[2]
    rows = acc.shape[0]

    pairs = [(seeds_in, seeds), (ids_in, ids), (cols_in, cols), (count_in, count), (sd_in, sd)]
    small = [pltpu.make_async_copy(x, y, sems.at[i]) for i, (x, y) in enumerate(pairs)]
    for copy in small:
        copy.start()
    large = []
    for x, y in ((innov_in, innov), (prec_in, prec)):
        for t in range(strips):
            at = len(pairs) + len(large)
            large.append(
                pltpu.make_async_copy(
                    x.at[:, t * LANES : (t + 1) * LANES], y.at[t, 0 : lev * blocks, :], sems.at[at]
                )
            )
    for copy in large:
        copy.start()
    both[...] = jnp.zeros_like(both)
    scratch[...] = jnp.zeros_like(scratch)
    order = [(source, zz) for source in range(2) for zz in range(chips)]
    shape = (levp, width)
    spot = lax.broadcasted_iota(jnp.int32, shape, 0) * profiles
    spot = spot + lax.broadcasted_iota(jnp.int32, shape, 1)

    def piece_at(at):
        source, zz = order[at]
        return 2 * zz + (core if source == 0 else 1 - core)

    for at in range(len(order)):
        piece = piece_at(at)
        first = (obs * blocks + piece // halves) * (lev * profiles) + (piece % halves) * width
        bases[at] = remainder(7919 * remainder(spot + first, 1.0 / PRIME), 1.0 / PRIME)
    for copy in small:
        copy.wait()

    def tile_copy(n, half, target):
        lanes = pl.ds(half * width, width)
        return pltpu.make_async_copy(h.at[n, :, lanes], target, h_sems.at[n * halves + half])

    def put(n, carry):
        for half in range(halves):
            piece, k = ids[0, 0, n] * halves + half, cols[0, 0, n]
            share = (piece % 2) ^ core
            tile_copy(n, half, both.at[share, piece // 2, k]).start()
        return carry

    lax.fori_loop(0, count[0, 0], put, 0)

    starts = [lax.rem(seeds[m], PRIME) - PRIME for m in range(members)]
    low = (1.0 - 2.0**-21) / PRIME

    def draw(at, m):
        k0 = bases[at] + starts[m]
        k1 = remainder(k0 * k0 + 12345, 1.0 / PRIME)
        k2 = remainder(k1 * k1 + 2719, low)
        return jnp.where(k2 >= PRIME, k2 - PRIME, k2).astype(F32)

    early = len(order) // 2
    for at in range(early):
        for m in range(members):
            hashed[at, m] = draw(at, m)
    for copy in large:
        copy.wait()

    def arrive(n, carry):
        for half in range(halves):
            tile_copy(n, half, own.at[0, 0]).wait()
        return carry

    lax.fori_loop(0, count[0, 0], arrive, 0)
    kept = [
        pltpu.make_async_copy(x, y, sems.at[len(pairs) + len(large) + i])
        for i, (x, y) in enumerate(((partner, partner_out), (own, own_out)))
    ]
    for copy in kept:
        copy.start()

    for at in range(len(order)):
        source, zz = order[at]
        piece = piece_at(at)
        b = piece // halves
        strip = (piece % halves) * (width // LANES)
        p, d = [
            jnp.concatenate(
                [
                    x[strip + t, pl.ds(b, lev, stride=blocks), :]
                    for t in range(width // LANES)
                ],
                axis=1,
            )
            for x in (prec, innov)
        ]
        gain = 3.4 * p * lax.rsqrt(p)
        offset = p * d - 0.5 * gain
        gain = gain * (1.0 / PRIME)
        slot, side = at // 2 % 2, at % 2
        for m in range(members):
            k2 = hashed[at, m, 0:lev, :] if at < early else draw(at, m)[0:lev]
            scratch[slot, m * lev : (m + 1) * lev, side * width : (side + 1) * width] = (
                offset + gain * k2
            )
        if side == 0:
            continue
        tiles = own if source == 0 else partner
        tiles = [tiles[i].reshape(colblocks * LANES, width) for i in (zz - 1, zz)]
        part = lax.dot_general(
            scratch[slot].astype(BF16),
            jnp.concatenate(tiles, axis=1),
            NT,
            preferred_element_type=F32,
        )
        if at == 1:
            acc[...] = part
        else:
            acc[...] += part

    line = jnp.concatenate([sd[...]] * colblocks, axis=1)
    put_halves(outs, with_columns(acc[...], line, obs, members))
    for copy in kept:
        copy.wait()


def put_halves(outs, value):
    half = value.shape[1] // 2
    outs[0][...] = value[:, :half].astype(BF16)
    outs[1][...] = value[:, half:].astype(BF16)


def with_columns(body, line, obs, members):
    tail = body[body.shape[0] - 16 :]
    sub = lax.broadcasted_iota(jnp.int32, tail.shape, 0)
    mine = lax.broadcasted_iota(jnp.int32, tail.shape, 1) // LANES == obs
    rest = line
    for piece in range(PIECES):
        part = rest.astype(BF16).astype(F32)
        rest = rest - part
        tail = jnp.where((sub == 16 - PIECES + piece) & mine, part, tail)
    return jnp.concatenate([body[: body.shape[0] - 16], tail], axis=0)


def read_columns(body):
    tail = body[body.shape[0] - 16 :]
    sub = lax.broadcasted_iota(jnp.int32, tail.shape, 0)
    return jnp.sum(jnp.where(sub >= 16 - PIECES, tail, 0.0), axis=0, keepdims=True)


def precision_kernel(halves, members, prec, out):
    z, core, unused = place()
    piece = 2 * z + core
    lev, blocks, unused = prec.shape
    width = out.shape[1]
    block = lax.broadcasted_iota(jnp.int32, (lev, blocks, width), 1)
    if halves == 1:
        mine = prec[...]
    else:
        mine = prec[:, :, pl.ds(pl.multiple_of((piece % halves) * width, LANES), width)]
    out[...] = jnp.zeros_like(out)
    mine = jnp.sum(jnp.where(block == piece // halves, mine, 0.0), axis=1)
    for m in range(members):
        out[m * lev : (m + 1) * lev, :] = mine


def joined(pieces):
    one, one_more, two, two_more = [x[...] for x in pieces]
    return jnp.concatenate([add([one, one_more]), add([two, two_more])], axis=1)


def unpack(spread, value):
    count = value.shape[0]
    spread[0:count, :] = value
    spread[count:, :] = jnp.zeros((spread.shape[0] - count, value.shape[1]), F32)


def first_kernel(lev, *refs):
    vert, vert_t, sd_out, residual, moved, spread, packed = refs[4:]
    members, levp, unused = residual.shape
    t = joined(refs[:4])
    sd = read_columns(t)
    sd_out[...] = sd
    unpack(spread, t)
    scalars = []
    for m in range(members):
        at = slice(m * lev, m * lev + levp)
        r = dot(vert_t[...], sd * spread[at, :])
        residual[m] = r
        packed[at, :] = sd * dot(vert[...], r)
        scalars.append([total(r * r)])
    moved[...] = with_scalars(packed[0 : moved.shape[0], :], scalars).astype(BF16)


def add_kernel(members, scalars, *refs):
    parts, out = refs[:-1], refs[-1]
    value = add([x[...] for x in parts])
    if scalars:
        value = with_scalars(value, read_scalars(parts, members, scalars))
    out[...] = value.astype(BF16)


def add_halves_kernel(members, scalars, one, one_more, two, two_more, one_out, two_out):
    add_kernel(members, scalars, one, one_more, one_out)
    add_kernel(members, 0, two, two_more, two_out)


def stage_kernel(*refs):
    sems = refs[-1]
    count = len(refs) // 2
    copies = [
        pltpu.make_async_copy(refs[i], refs[count + i], sems.at[i]) for i in range(count)
    ]
    for copy in copies:
        copy.start()
    for copy in copies:
        copy.wait()


def forward_kernel(sends, members, x, tiles, *refs):
    z, core, obs = place()
    outs = refs[-len(sends) :]
    rows, lanes = x.shape
    width = tiles.shape[3]
    added = refs[1 : 1 + len(sends)] if len(refs) > len(sends) else [None] * len(sends)
    if added[0] is not None:
        scalars = read_scalars([refs[0], x], members, 2)
    for out, before, (chip, first, count) in zip(outs, added, sends):
        y = jnp.dot(
            x[first : first + count, :],
            tiles[z ^ chip].reshape(lanes, width),
            preferred_element_type=F32,
        )
        if before is not None:
            y = before[...] + y
            if first + count == rows:
                y = with_scalars(y, scalars)
        out[...] = y.astype(out.dtype)


def weigh_kernel(later, last, members, lev, spans, *refs):
    ys, refs = refs[: len(spans)], refs[len(spans) :]
    prec, old_image, old = refs[0], *(refs[1:3] if later else (None, None))
    state, *outs = refs[3 if later else 1 :]
    if not last:
        *outs, image = outs
    rows = prec.shape[0]
    cuts = sorted({first for first, count in spans}) + [rows]
    parts = []
    for low, high in zip(cuts, cuts[1:]):
        held = [
            ref[low - first : high - first, :]
            for ref, (first, count) in zip(ys, spans)
            if first <= low < first + count
        ]
        parts.append(add(held))
    y = parts[0] if len(parts) == 1 else jnp.concatenate(parts, axis=0)
    ends = [ref for ref, (first, count) in zip(ys, spans) if first + count == rows]
    sub = lax.broadcasted_iota(jnp.int32, (8, LANES), 0)
    betas = []
    for m, (norm, cross) in enumerate(read_scalars(ends, members, 2)):
        if later:
            old_norm, old_square = old[m, 0:1, 0:1], old[m, 1:2, 0:1]
            beta = norm / old_norm
            square = norm + 2.0 * beta * cross + beta * beta * old_square
        else:
            beta = jnp.zeros_like(norm)
            square = norm
        betas.append(beta)
        state[m] = jnp.where(sub == 0, norm, jnp.where(sub == 1, square, beta))
    if later:
        y = y + by_member(betas, (rows, 1), lev) * old_image[...]
    if not last:
        image[...] = y
    scaled = prec[...] * y
    energies = [[x] for x in member_sums(scaled * y, members, lev)]
    weighted = with_scalars(scaled, energies).astype(BF16)
    first = 0
    for out in outs:
        out[...] = weighted[first : first + out.shape[0]]
        first = (first + out.shape[0]) % rows


def adjoint_kernel(plan, members, *refs):
    z, core, obs = place()
    ws, tiles, out = refs[: len(plan)], refs[len(plan)], refs[len(plan) + 1]
    rows, lanes = out.shape
    width = ws[0].shape[1]
    acc = None
    for i in range(tiles.shape[0]):
        w = {first: ref for ref, (chip, first, count) in zip(ws, plan) if chip == i}
        w = [w[first][...] for first in sorted(w)]
        w = w[0] if len(w) == 1 else jnp.concatenate(w, axis=0)
        part = lax.dot_general(
            w, tiles[z ^ i].reshape(lanes, width), NT, preferred_element_type=F32
        )
        acc = part if i == 0 else acc + part
    ends = [ref for ref, (chip, first, count) in zip(ws, plan) if first + count == rows]
    out[...] = with_scalars(acc, read_scalars(ends, members, 1)).astype(out.dtype)


def combine_kernel(members, mine, theirs, *outs):
    value = mine[...] + theirs[...].astype(F32)
    put_halves(outs, with_scalars(value, read_scalars([mine, theirs], members, 1)))


def combine_columns_kernel(members, mine, theirs, *outs):
    obs = lax.axis_index("obs")
    energies = read_scalars([mine, theirs], members, 1)
    for i, out in enumerate(outs):
        lane = pl.ds(pl.multiple_of((obs ^ i) * LANES, LANES), LANES)
        value = mine[:, lane] + theirs[:, lane].astype(F32)
        out[...] = with_scalars(value, energies).astype(BF16)


def update_kernel(later, lev, *refs):
    pieces, refs = refs[:4], refs[4:]
    sd, vert, vert_t, state, residual = refs[:5]
    spread, packed = refs[-2:]
    if later:
        old_direction, old_solution, residual_out, solution_out, moved, direction_out = refs[5:-2]
    else:
        residual_out, solution_out, moved = refs[5:-2]
    members, levp, unused = residual.shape
    obs = lax.axis_index("obs")
    mine = pl.ds(pl.multiple_of(obs * LANES, LANES), LANES)
    unpack(spread, joined(pieces))
    energies = read_scalars(pieces[:2], members, 1)
    scalars = []
    for m in range(members):
        at = slice(m * lev, m * lev + levp)
        norm, square, beta = state[m, 0:1, 0:1], state[m, 1:2, 0:1], state[m, 2:3, 0:1]
        alpha = norm / (square + energies[m][0])
        r = residual[m]
        if later:
            d = r + beta * old_direction[m]
            direction_out[m] = d
            step = direction_out[m, :, mine]
            solution_out[m] = old_solution[m] + alpha * step
        else:
            d = r
            solution_out[m] = alpha * residual[m, :, mine]
        r = r - alpha * (d + dot(vert_t[...], sd[...] * spread[at, :]))
        residual_out[m] = r
        packed[at, :] = sd[...] * dot(vert[...], r)
        scalars.append([total(r * r), total(r * d)])
    moved[...] = with_scalars(packed[0 : moved.shape[0], :], scalars).astype(BF16)


def increment_kernel(later, sd, vert, state, residual, *refs):
    before, direction, moved = refs[-3:]
    obs = lax.axis_index("obs")
    mine = pl.ds(pl.multiple_of(obs * LANES, LANES), LANES)
    for m in range(residual.shape[0]):
        d = residual[m, :, mine]
        if later:
            d = d + state[m, 2:3, 0:1] * refs[0][m, :, mine]
            before[m] = sd[...] * dot(vert[...], refs[1][m])
        else:
            before[m] = jnp.zeros_like(d)
        direction[m] = d
        moved[m] = sd[...] * dot(vert[...], d)


def last_kernel(parts, lev, *refs):
    pieces, refs = refs[:parts], refs[parts:]
    sd, vert_t, state, residual, before, direction, moved = refs[:7]
    increment_out, residual_out, spread = refs[7:]
    members, levp, unused = residual.shape
    obs = lax.axis_index("obs")
    mine = pl.ds(pl.multiple_of(obs * LANES, LANES), LANES)
    unpack(spread, add([x[...] for x in pieces]))
    energies = read_scalars(pieces, members, 1)
    for m in range(members):
        t = spread[m * lev : m * lev + levp, :]
        alpha = state[m, 0:1, 0:1] / (state[m, 1:2, 0:1] + energies[m][0])
        increment_out[:, m, :] = (before[m] + alpha * moved[m])[0:lev]
        r = residual[m, :, mine] - alpha * (direction[m] + dot(vert_t[...], sd[...] * t))
        residual_out[:, m, :] = r[0:lev]


def per_device(
    n_slab,
    n_obs,
    innovation,
    obs_precision,
    seeds,
    col_sd,
    vert_factor,
    h_values,
    block_obs,
    block_col,
    entry_count,
):
    blocks, lev, profiles = innovation.shape
    members = seeds.shape[0]
    chips = n_slab // 2
    halves = n_slab // blocks
    width = profiles // halves
    colblocks = n_obs
    assert halves * blocks == n_slab and width % LANES == 0 and col_sd.shape[0] == 1
    assert chips & (chips - 1) == 0 and n_obs & (n_obs - 1) == 0
    levp = (lev + 1 + 15) // 16 * 16
    assert members <= 16 and members >= PIECES
    rows = (members * (lev + 1) + 15) // 16 * 16
    lanes = colblocks * LANES
    slab_field = (members, levp, lanes)
    slab_rows = (rows, lanes)
    half_rows = [struct((rows, lanes // 2), BF16)] * 2
    wide = rows + levp - lev + 7
    spread = pltpu.VMEM((wide // 8 * 8, lanes), F32)
    some = rows // 32 * 16
    rest = rows - some
    via = chips == 4
    if via:
        one, two = (0, some), (some, rest)
        most = rows - 32
        near_parts = [(0, most), (most, rows - most)]
        plan = [(0, 0, rows), *((1, *part) for part in near_parts)]
        plan += [(2, *one), (2, *two), (3, *one), (3, *two)]
        sends = [(3, *one), (2, *two), (3, *two), (1, *one), (1, *two), (0, 0, rows), (2, *one)]
    else:
        sends = plan = [(i, 0, rows) for i in range(chips)]
    pad = ((0, levp - lev), (0, levp - lev))
    high = lax.reduce_precision(vert_factor, 8, 7)
    low = vert_factor - high
    vert, vert_t = [
        jnp.concatenate([jnp.pad(x, pad).astype(BF16) for x in parts], axis=1)
        for parts in ((high, high, low), (high.T, high.T, low.T))
    ]
    h_block = h_values.reshape(h_values.shape[2:])
    innovation = jnp.transpose(innovation, (1, 0, 2))
    obs_precision = jnp.transpose(obs_precision, (1, 0, 2))
    product = n_slab * width * lanes * rows
    small = 12 * rows * levp * LANES
    plane_bits = [1 << k for k in range(n_obs.bit_length() - 1)]

    def along(x, i):
        return lax.ppermute(x, "slab", [(s, s ^ (2 * i)) for s in range(n_slab)])

    def plane(x, i):
        return lax.ppermute(x, "obs", [(o, o ^ i) for o in range(n_obs)])

    def swap(x):
        return lax.ppermute(x, "slab", [(s, s ^ 1) for s in range(n_slab)])

    def plane_sum(halves, staged):
        halves = list(halves)
        moved_halves = [None] * len(halves)
        for step, bit in enumerate(plane_bits):
            bits = [bit, plane_bits[len(plane_bits) - 1 - step]]
            for at in range(0, len(halves), 2):
                if step > 0:
                    one, two = halves[at : at + 2]
                    one_more, two_more = moved_halves[at : at + 2]
                    halves[at : at + 2] = call(
                        functools.partial(add_halves_kernel, members, 0 if staged else 1),
                        [struct(one.shape, BF16)] * 2,
                        [],
                        0,
                        one,
                        one_more,
                        two,
                        two_more,
                    )
                for half in range(2):
                    moved_halves[at + half] = plane(halves[at + half], bits[half])
            if step == 0 and staged:
                halves[:] = call(
                    stage_kernel,
                    [struct(x.shape, BF16) for x in halves],
                    [pltpu.SemaphoreType.DMA((len(halves),))],
                    0,
                    *halves,
                    space=HBM,
                )
        return [x for pair in zip(halves, moved_halves) for x in pair]

    def line_sum(moved, other):
        shapes = [(count, width) for i, unused, count in sends]
        mine = call(
            functools.partial(forward_kernel, sends, members),
            [struct(shape, F32) for shape in shapes],
            [],
            product,
            moved,
            own,
        )
        ys = call(
            functools.partial(forward_kernel, sends, members),
            [
                struct(shape, F32 if i == 0 or (via and at == 6) else BF16)
                for at, ((i, *unused), shape) in enumerate(zip(sends, shapes))
            ],
            [],
            product,
            other,
            partner,
            moved,
            *mine,
        )
        if not via:
            return [y if i == 0 else along(y, i) for i, y in enumerate(ys)], [(0, rows)] * chips
        passed, far_rest, last_rest, next_some, next_rest, near, far = ys
        passed = along(passed, 1)
        far_rest, last_rest = along(far_rest, 2), along(last_rest, 3)
        next_some, next_rest = along(next_some, 1), along(next_rest, 1)
        (far,) = call(
            functools.partial(add_kernel, members, 0),
            [struct((some, width), BF16)],
            [],
            0,
            far,
            passed,
        )
        ys = [near, far_rest, last_rest, next_some, next_rest, along(far, 2)]
        return ys, [(0, rows), two, two, one, two, one]

    def line_gather(w, *parts):
        if not via:
            return [w if i == 0 else along(w, i) for i in range(chips)]
        some_w, rest_w, *near = parts
        far = along(some_w, 2)
        far_rest, last_rest = along(rest_w, 2), along(rest_w, 3)
        return [w, *(along(x, 1) for x in near), far, far_rest, along(far, 1), last_rest]

    dense = struct((chips, colblocks, LANES, width), BF16)
    own, for_partner, *partials = call(
        functools.partial(start_kernel, (chips, halves, blocks, lev)),
        [dense, dense] + half_rows,
        [
            pltpu.SMEM(seeds.shape, jnp.int32),
            pltpu.SMEM(block_obs.shape, jnp.int32),
            pltpu.SMEM(block_col.shape, jnp.int32),
            pltpu.SMEM(entry_count.shape, jnp.int32),
            pltpu.VMEM(col_sd.shape, F32),
            pltpu.VMEM((profiles // LANES, levp * blocks, LANES), F32),
            pltpu.VMEM((profiles // LANES, levp * blocks, LANES), F32),
            pltpu.VMEM((n_slab, levp, width), jnp.int32),
            pltpu.VMEM((n_slab // 2, members, levp, width), F32),
            pltpu.VMEM((2, rows, 2 * width), F32),
            pltpu.VMEM((rows, lanes), F32),
            pltpu.VMEM((2, *dense.shape), BF16),
            pltpu.SemaphoreType.DMA((7 + 2 * (profiles // LANES),)),
            pltpu.SemaphoreType.DMA((h_block.shape[0] * halves,)),
        ],
        2 * product,
        seeds,
        block_obs,
        block_col,
        entry_count,
        col_sd,
        innovation.reshape(lev * blocks, profiles),
        obs_precision.reshape(lev * blocks, profiles),
        h_block,
        space=HBM,
        limit=60,
        stored=2,
    )
    ps = plane_sum(partials, True)
    partner = swap(for_partner)
    (precision,) = call(
        functools.partial(precision_kernel, halves, members),
        [struct((rows, width), F32)],
        [],
        0,
        obs_precision,
    )
    slab_sd, residual, moved = call(
        functools.partial(first_kernel, lev),
        [struct((1, lanes), F32), struct(slab_field, F32), struct(slab_rows, BF16)],
        [spread, spread],
        small * colblocks,
        *ps,
        vert,
        vert_t,
    )
    direction = total_step = image = state = None
    for sweep in range(ITERS):
        later, last = sweep > 0, sweep == ITERS - 1
        ys, spans = line_sum(moved, swap(moved))
        state, *weighted = call(
            functools.partial(weigh_kernel, later, last, members, lev, spans),
            [struct((members, 8, LANES), F32)]
            + [struct((n, width), BF16) for n in ((rows, some, rest, most, rows - most) if via else (rows,))]
            + ([] if last else [struct((rows, width), F32)]),
            [],
            0,
            *ys,
            precision,
            *([image, state] if later else []),
        )
        if not last:
            *weighted, image = weighted
        ws = line_gather(*weighted)
        (theirs,) = call(
            functools.partial(adjoint_kernel, plan, members),
            [struct(slab_rows, BF16)],
            [],
            product,
            *ws,
            partner,
        )
        theirs = swap(theirs)
        (mine,) = call(
            functools.partial(adjoint_kernel, plan, members),
            [struct(slab_rows, F32)],
            [],
            product,
            *ws,
            own,
        )
        known = [vert, vert_t, state, residual]
        if later:
            known += [direction, total_step]
        if last:
            ps = call(
                functools.partial(combine_columns_kernel, members),
                [struct((rows, LANES), BF16)] * n_obs,
                [],
                0,
                mine,
                theirs,
            )
            ps = [ps[0]] + [plane(ps[i], i) for i in reversed(range(1, n_obs))]
            own_field = struct((members, levp, LANES), F32)
            before, d, u_d = call(
                functools.partial(increment_kernel, later),
                [own_field] * 3,
                [],
                small,
                col_sd,
                vert,
                state,
                residual,
                *([direction, total_step] if later else []),
            )
            outputs = call(
                functools.partial(last_kernel, len(ps), lev),
                [struct((lev, members, LANES), F32)] * 2,
                [pltpu.VMEM((wide // 8 * 8, LANES), F32)],
                small,
                *ps,
                col_sd,
                vert_t,
                state,
                residual,
                before,
                d,
                u_d,
            )
            break
        ps = call(
            functools.partial(combine_kernel, members), half_rows, [], 0, mine, theirs
        )
        ps = plane_sum(ps, False)
        outs = [
            struct(slab_field, F32),
            struct((members, levp, LANES), F32),
            struct(slab_rows, BF16),
        ]
        if later:
            outs.append(struct(slab_field, F32))
        r, total_step, moved, *d = call(
            functools.partial(update_kernel, later, lev),
            outs,
            [spread, spread],
            small * colblocks,
            *ps,
            slab_sd,
            *known,
        )
        direction, residual = (d[0] if later else residual), r
    return tuple(jnp.transpose(x, (1, 0, 2))[None] for x in outputs)


def solution(mesh):
    return jax.shard_map(
        functools.partial(per_device, mesh.shape["slab"], mesh.shape["obs"]),
        mesh=mesh,
        in_specs=(
            P("obs", None, None),
            P("obs", None, None),
            P(),
            P(("slab", "obs"), None),
            P(),
            P("slab", "obs", None, None, None),
            P("slab", "obs", None),
            P("slab", "obs", None),
            P("slab", "obs"),
        ),
        out_specs=(P(("slab", "obs"), None, None, None), P(("slab", "obs"), None, None, None)),
        check_vma=False,
    )
```

```python
import functools

import jax
import jax.numpy as jnp
from jax import lax
from jax.experimental import pallas as pl
from jax.experimental.pallas import tpu as pltpu
from jax.sharding import PartitionSpec as P

ITERS = 2
LANES = 128
PIECES = 3
PRIME = 32749
VMEM = pl.BlockSpec(memory_space=pltpu.VMEM)
HBM = pl.BlockSpec(memory_space=pltpu.HBM)
F32 = jnp.float32
BF16 = jnp.bfloat16
NT = (((1,), (1,)), ((), ()))


def call(kernel, outs, scratch, flops, *args, space=VMEM, limit=24, stored=0):
    nbytes = sum(a.size * a.dtype.itemsize for a in (*args, *outs))
    return pl.pallas_call(
        kernel,
        out_shape=outs,
        in_specs=[space] * len(args),
        out_specs=[HBM] * stored + [VMEM] * (len(outs) - stored),
        scratch_shapes=scratch,
        compiler_params=pltpu.CompilerParams(vmem_limit_bytes=limit * 1024 * 1024),
        cost_estimate=pl.CostEstimate(flops=flops, bytes_accessed=nbytes, transcendentals=0),
    )(*args)


def struct(shape, dtype):
    return jax.ShapeDtypeStruct(shape, dtype)


def place():
    slab = lax.axis_index("slab")
    return slab // 2, slab % 2, lax.axis_index("obs")


def add(parts):
    value = parts[0].astype(F32)
    for part in parts[1:]:
        value = value + part.astype(F32)
    return value


def dot(matrix, x):
    high = x.astype(BF16)
    rest = (x - high.astype(F32)).astype(BF16)
    x = jnp.concatenate([high, rest, high], axis=0)
    return jnp.dot(matrix, x, preferred_element_type=F32)


def total(x):
    return jnp.sum(jnp.sum(x, axis=0, keepdims=True), axis=1, keepdims=True)


def with_scalars(body, values):
    count = body.shape[0]
    tail = body[count - 16 :]
    sub = lax.broadcasted_iota(jnp.int32, tail.shape, 0) - (16 - len(values))
    lanes = lax.broadcasted_iota(jnp.int32, tail.shape, 1)
    line = jnp.zeros(tail.shape, F32)
    for m, member in enumerate(values):
        for q, value in enumerate(member):
            rest = value
            for piece in range(PIECES):
                part = rest.astype(BF16).astype(F32)
                rest = rest - part
                line = jnp.where((sub == m) & (lanes == q * PIECES + piece), part, line)
    return jnp.concatenate([body[: count - 16], jnp.where(sub >= 0, line, tail)], axis=0)


def read_scalars(refs, members, count):
    tail = add([ref[ref.shape[0] - 16 :, 0:LANES] for ref in refs])
    sub = lax.broadcasted_iota(jnp.int32, tail.shape, 0) - (16 - members)
    lanes = lax.broadcasted_iota(jnp.int32, tail.shape, 1)
    return [
        [
            total(
                jnp.where(
                    (sub == m) & (lanes >= q * PIECES) & (lanes < (q + 1) * PIECES), tail, 0.0
                )
            )
            for q in range(count)
        ]
        for m in range(members)
    ]


def by_member(values, shape, lev):
    rows = lax.broadcasted_iota(jnp.int32, shape, 0)
    out = jnp.zeros(shape, F32)
    for m, value in enumerate(values):
        out = jnp.where((rows >= m * lev) & (rows < (m + 1) * lev), value, out)
    return out


def member_sums(x, members, lev):
    lines = jnp.sum(x, axis=1, keepdims=True)
    rows = lax.broadcasted_iota(jnp.int32, lines.shape, 0)
    return [
        jnp.sum(
            jnp.where((rows >= m * lev) & (rows < (m + 1) * lev), lines, 0.0),
            axis=0,
            keepdims=True,
        )
        for m in range(members)
    ]


def remainder(x, factor):
    return x - (x.astype(F32) * factor).astype(jnp.int32) * PRIME


def start_kernel(
    dims, seeds_in, ids_in, cols_in, count_in, sd_in, innov_in, prec_in, h, own_out, partner_out, *rest
):
    chips, halves, blocks, lev = dims
    outs = rest[:-14]
    seeds, ids, cols, count, sd, innov, prec, bases, hashed, scratch, acc = rest[-14:-3]
    both, sems, h_sems = rest[-3:]
    own, partner = both.at[0], both.at[1]
    z, core, obs = place()
    strips = innov.shape[0]
    profiles = strips * LANES
    colblocks, width = own.shape[1], own.shape[3]
    members, levp = hashed.shape[1], hashed.shape[2]
    rows = acc.shape[0]

    pairs = [(seeds_in, seeds), (ids_in, ids), (cols_in, cols), (count_in, count), (sd_in, sd)]
    small = [pltpu.make_async_copy(x, y, sems.at[i]) for i, (x, y) in enumerate(pairs)]
    for copy in small:
        copy.start()
    large = []
    for x, y in ((innov_in, innov), (prec_in, prec)):
        for t in range(strips):
            at = len(pairs) + len(large)
            large.append(
                pltpu.make_async_copy(
                    x.at[:, t * LANES : (t + 1) * LANES], y.at[t, 0 : lev * blocks, :], sems.at[at]
                )
            )
    for copy in large:
        copy.start()
    both[...] = jnp.zeros_like(both)
    scratch[...] = jnp.zeros_like(scratch)
    order = [(source, zz) for source in range(2) for zz in range(chips)]
    shape = (levp, width)
    spot = lax.broadcasted_iota(jnp.int32, shape, 0) * profiles
    spot = spot + lax.broadcasted_iota(jnp.int32, shape, 1)

    def piece_at(at):
        source, zz = order[at]
        return 2 * zz + (core if source == 0 else 1 - core)

    for at in range(len(order)):
        piece = piece_at(at)
        first = (obs * blocks + piece // halves) * (lev * profiles) + (piece % halves) * width
        bases[at] = remainder(7919 * remainder(spot + first, 1.0 / PRIME), 1.0 / PRIME)
    for copy in small:
        copy.wait()

    def tile_copy(n, half, target):
        lanes = pl.ds(half * width, width)
        return pltpu.make_async_copy(h.at[n, :, lanes], target, h_sems.at[n * halves + half])

    def put(n, carry):
        for half in range(halves):
            piece, k = ids[0, 0, n] * halves + half, cols[0, 0, n]
            share = (piece % 2) ^ core
            tile_copy(n, half, both.at[share, piece // 2, k]).start()
        return carry

    lax.fori_loop(0, count[0, 0], put, 0)

    starts = [lax.rem(seeds[m], PRIME) - PRIME for m in range(members)]
    low = (1.0 - 2.0**-21) / PRIME

    def draw(at, m):
        k0 = bases[at] + starts[m]
        k1 = remainder(k0 * k0 + 12345, 1.0 / PRIME)
        k2 = remainder(k1 * k1 + 2719, low)
        return jnp.where(k2 >= PRIME, k2 - PRIME, k2).astype(F32)

    early = len(order) // 2
    for at in range(early):
        for m in range(members):
            hashed[at, m] = draw(at, m)
    for copy in large:
        copy.wait()

    def arrive(n, carry):
        for half in range(halves):
            tile_copy(n, half, own.at[0, 0]).wait()
        return carry

    lax.fori_loop(0, count[0, 0], arrive, 0)
    kept = [
        pltpu.make_async_copy(x, y, sems.at[len(pairs) + len(large) + i])
        for i, (x, y) in enumerate(((partner, partner_out), (own, own_out)))
    ]
    for copy in kept:
        copy.start()

    for at in range(len(order)):
        source, zz = order[at]
        piece = piece_at(at)
        b = piece // halves
        strip = (piece % halves) * (width // LANES)
        p, d = [
            jnp.concatenate(
                [
                    x[strip + t, pl.ds(b, lev, stride=blocks), :]
                    for t in range(width // LANES)
                ],
                axis=1,
            )
            for x in (prec, innov)
        ]
        gain = 3.4 * p * lax.rsqrt(p)
        offset = p * d - 0.5 * gain
        gain = gain * (1.0 / PRIME)
        slot, side = at // 2 % 2, at % 2
        for m in range(members):
            k2 = hashed[at, m, 0:lev, :] if at < early else draw(at, m)[0:lev]
            scratch[slot, m * lev : (m + 1) * lev, side * width : (side + 1) * width] = (
                offset + gain * k2
            )
        if side == 0:
            continue
        tiles = own if source == 0 else partner
        tiles = [tiles[i].reshape(colblocks * LANES, width) for i in (zz - 1, zz)]
        part = lax.dot_general(
            scratch[slot].astype(BF16),
            jnp.concatenate(tiles, axis=1),
            NT,
            preferred_element_type=F32,
        )
        if at == 1:
            acc[...] = part
        else:
            acc[...] += part

    line = jnp.concatenate([sd[...]] * colblocks, axis=1)
    put_halves(outs, with_columns(acc[...], line, obs, members))
    for copy in kept:
        copy.wait()


def put_halves(outs, value):
    half = value.shape[1] // 2
    outs[0][...] = value[:, :half].astype(BF16)
    outs[1][...] = value[:, half:].astype(BF16)


def with_columns(body, line, obs, members):
    tail = body[body.shape[0] - 16 :]
    sub = lax.broadcasted_iota(jnp.int32, tail.shape, 0)
    mine = lax.broadcasted_iota(jnp.int32, tail.shape, 1) // LANES == obs
    rest = line
    for piece in range(PIECES):
        part = rest.astype(BF16).astype(F32)
        rest = rest - part
        tail = jnp.where((sub == 16 - PIECES + piece) & mine, part, tail)
    return jnp.concatenate([body[: body.shape[0] - 16], tail], axis=0)


def read_columns(body):
    tail = body[body.shape[0] - 16 :]
    sub = lax.broadcasted_iota(jnp.int32, tail.shape, 0)
    return jnp.sum(jnp.where(sub >= 16 - PIECES, tail, 0.0), axis=0, keepdims=True)


def precision_kernel(halves, members, prec, out):
    z, core, unused = place()
    piece = 2 * z + core
    lev, blocks, unused = prec.shape
    width = out.shape[1]
    block = lax.broadcasted_iota(jnp.int32, (lev, blocks, width), 1)
    if halves == 1:
        mine = prec[...]
    else:
        mine = prec[:, :, pl.ds(pl.multiple_of((piece % halves) * width, LANES), width)]
    out[...] = jnp.zeros_like(out)
    mine = jnp.sum(jnp.where(block == piece // halves, mine, 0.0), axis=1)
    for m in range(members):
        out[m * lev : (m + 1) * lev, :] = mine


def joined(pieces):
    one, one_more, two, two_more = [x[...] for x in pieces]
    return jnp.concatenate([add([one, one_more]), add([two, two_more])], axis=1)


def unpack(spread, value):
    count = value.shape[0]
    spread[0:count, :] = value
    spread[count:, :] = jnp.zeros((spread.shape[0] - count, value.shape[1]), F32)


def first_kernel(lev, *refs):
    vert, vert_t, sd_out, residual, moved, spread, packed = refs[4:]
    members, levp, unused = residual.shape
    t = joined(refs[:4])
    sd = read_columns(t)
    sd_out[...] = sd
    unpack(spread, t)
    scalars = []
    for m in range(members):
        at = slice(m * lev, m * lev + levp)
        r = dot(vert_t[...], sd * spread[at, :])
        residual[m] = r
        packed[at, :] = sd * dot(vert[...], r)
        scalars.append([total(r * r)])
    moved[...] = with_scalars(packed[0 : moved.shape[0], :], scalars).astype(BF16)


def add_kernel(members, scalars, *refs):
    parts, out = refs[:-1], refs[-1]
    value = add([x[...] for x in parts])
    if scalars:
        value = with_scalars(value, read_scalars(parts, members, scalars))
    out[...] = value.astype(BF16)


def add_halves_kernel(members, scalars, one, one_more, two, two_more, one_out, two_out):
    add_kernel(members, scalars, one, one_more, one_out)
    add_kernel(members, 0, two, two_more, two_out)


def stage_kernel(*refs):
    sems = refs[-1]
    count = len(refs) // 2
    copies = [
        pltpu.make_async_copy(refs[i], refs[count + i], sems.at[i]) for i in range(count)
    ]
    for copy in copies:
        copy.start()
    for copy in copies:
        copy.wait()


def forward_kernel(sends, members, x, tiles, *refs):
    z, core, obs = place()
    outs = refs[-len(sends) :]
    rows, lanes = x.shape
    width = tiles.shape[3]
    added = refs[1 : 1 + len(sends)] if len(refs) > len(sends) else [None] * len(sends)
    if added[0] is not None:
        scalars = read_scalars([refs[0], x], members, 2)
    for out, before, (chip, first, count) in zip(outs, added, sends):
        y = jnp.dot(
            x[first : first + count, :],
            tiles[z ^ chip].reshape(lanes, width),
            preferred_element_type=F32,
        )
        if before is not None:
            y = before[...] + y
            if first + count == rows:
                y = with_scalars(y, scalars)
        out[...] = y.astype(out.dtype)


def weigh_kernel(later, last, members, lev, spans, *refs):
    ys, refs = refs[: len(spans)], refs[len(spans) :]
    prec, old_image, old = refs[0], *(refs[1:3] if later else (None, None))
    state, *outs = refs[3 if later else 1 :]
    if not last:
        *outs, image = outs
    rows = prec.shape[0]
    cuts = sorted({first for first, count in spans}) + [rows]
    parts = []
    for low, high in zip(cuts, cuts[1:]):
        held = [
            ref[low - first : high - first, :]
            for ref, (first, count) in zip(ys, spans)
            if first <= low < first + count
        ]
        parts.append(add(held))
    y = parts[0] if len(parts) == 1 else jnp.concatenate(parts, axis=0)
    ends = [ref for ref, (first, count) in zip(ys, spans) if first + count == rows]
    sub = lax.broadcasted_iota(jnp.int32, (8, LANES), 0)
    betas = []
    for m, (norm, cross) in enumerate(read_scalars(ends, members, 2)):
        if later:
            old_norm, old_square = old[m, 0:1, 0:1], old[m, 1:2, 0:1]
            beta = norm / old_norm
            square = norm + 2.0 * beta * cross + beta * beta * old_square
        else:
            beta = jnp.zeros_like(norm)
            square = norm
        betas.append(beta)
        state[m] = jnp.where(sub == 0, norm, jnp.where(sub == 1, square, beta))
    if later:
        y = y + by_member(betas, (rows, 1), lev) * old_image[...]
    if not last:
        image[...] = y
    scaled = prec[...] * y
    energies = [[x] for x in member_sums(scaled * y, members, lev)]
    weighted = with_scalars(scaled, energies).astype(BF16)
    first = 0
    for out in outs:
        out[...] = weighted[first : first + out.shape[0]]
        first = (first + out.shape[0]) % rows


def adjoint_kernel(plan, members, *refs):
    z, core, obs = place()
    ws, tiles, out = refs[: len(plan)], refs[len(plan)], refs[len(plan) + 1]
    rows, lanes = out.shape
    width = ws[0].shape[1]
    acc = None
    for i in range(tiles.shape[0]):
        w = {first: ref for ref, (chip, first, count) in zip(ws, plan) if chip == i}
        w = [w[first][...] for first in sorted(w)]
        w = w[0] if len(w) == 1 else jnp.concatenate(w, axis=0)
        part = lax.dot_general(
            w, tiles[z ^ i].reshape(lanes, width), NT, preferred_element_type=F32
        )
        acc = part if i == 0 else acc + part
    ends = [ref for ref, (chip, first, count) in zip(ws, plan) if first + count == rows]
    out[...] = with_scalars(acc, read_scalars(ends, members, 1)).astype(out.dtype)


def combine_kernel(members, mine, theirs, *outs):
    value = mine[...] + theirs[...].astype(F32)
    put_halves(outs, with_scalars(value, read_scalars([mine, theirs], members, 1)))


def combine_columns_kernel(members, mine, theirs, *outs):
    obs = lax.axis_index("obs")
    energies = read_scalars([mine, theirs], members, 1)
    for i, out in enumerate(outs):
        lane = pl.ds(pl.multiple_of((obs ^ i) * LANES, LANES), LANES)
        value = mine[:, lane] + theirs[:, lane].astype(F32)
        out[...] = with_scalars(value, energies).astype(BF16)


def update_kernel(later, lev, *refs):
    pieces, refs = refs[:4], refs[4:]
    sd, vert, vert_t, state, residual = refs[:5]
    spread, packed = refs[-2:]
    if later:
        old_direction, old_solution, residual_out, solution_out, moved, direction_out = refs[5:-2]
    else:
        residual_out, solution_out, moved = refs[5:-2]
    members, levp, unused = residual.shape
    obs = lax.axis_index("obs")
    mine = pl.ds(pl.multiple_of(obs * LANES, LANES), LANES)
    unpack(spread, joined(pieces))
    energies = read_scalars(pieces[:2], members, 1)
    scalars = []
    for m in range(members):
        at = slice(m * lev, m * lev + levp)
        norm, square, beta = state[m, 0:1, 0:1], state[m, 1:2, 0:1], state[m, 2:3, 0:1]
        alpha = norm / (square + energies[m][0])
        r = residual[m]
        if later:
            d = r + beta * old_direction[m]
            direction_out[m] = d
            step = direction_out[m, :, mine]
            solution_out[m] = old_solution[m] + alpha * step
        else:
            d = r
            solution_out[m] = alpha * residual[m, :, mine]
        r = r - alpha * (d + dot(vert_t[...], sd[...] * spread[at, :]))
        residual_out[m] = r
        packed[at, :] = sd[...] * dot(vert[...], r)
        scalars.append([total(r * r), total(r * d)])
    moved[...] = with_scalars(packed[0 : moved.shape[0], :], scalars).astype(BF16)


def increment_kernel(later, sd, vert, state, residual, *refs):
    before, direction, moved = refs[-3:]
    obs = lax.axis_index("obs")
    mine = pl.ds(pl.multiple_of(obs * LANES, LANES), LANES)
    for m in range(residual.shape[0]):
        d = residual[m, :, mine]
        if later:
            d = d + state[m, 2:3, 0:1] * refs[0][m, :, mine]
            before[m] = sd[...] * dot(vert[...], refs[1][m])
        else:
            before[m] = jnp.zeros_like(d)
        direction[m] = d
        moved[m] = sd[...] * dot(vert[...], d)


def last_kernel(parts, lev, *refs):
    pieces, refs = refs[:parts], refs[parts:]
    sd, vert_t, state, residual, before, direction, moved = refs[:7]
    increment_out, residual_out, spread = refs[7:]
    members, levp, unused = residual.shape
    obs = lax.axis_index("obs")
    mine = pl.ds(pl.multiple_of(obs * LANES, LANES), LANES)
    unpack(spread, add([x[...] for x in pieces]))
    energies = read_scalars(pieces, members, 1)
    for m in range(members):
        t = spread[m * lev : m * lev + levp, :]
        alpha = state[m, 0:1, 0:1] / (state[m, 1:2, 0:1] + energies[m][0])
        increment_out[:, m, :] = (before[m] + alpha * moved[m])[0:lev]
        r = residual[m, :, mine] - alpha * (direction[m] + dot(vert_t[...], sd[...] * t))
        residual_out[:, m, :] = r[0:lev]


def per_device(
    n_slab,
    n_obs,
    innovation,
    obs_precision,
    seeds,
    col_sd,
    vert_factor,
    h_values,
    block_obs,
    block_col,
    entry_count,
):
    blocks, lev, profiles = innovation.shape
    members = seeds.shape[0]
    chips = n_slab // 2
    halves = n_slab // blocks
    width = profiles // halves
    colblocks = n_obs
    assert halves * blocks == n_slab and width % LANES == 0 and col_sd.shape[0] == 1
    assert chips & (chips - 1) == 0 and n_obs & (n_obs - 1) == 0
    levp = (lev + 1 + 15) // 16 * 16
    assert members <= 16 and members >= PIECES
    rows = (members * (lev + 1) + 15) // 16 * 16
    lanes = colblocks * LANES
    slab_field = (members, levp, lanes)
    slab_rows = (rows, lanes)
    half_rows = [struct((rows, lanes // 2), BF16)] * 2
    wide = rows + levp - lev + 7
    spread = pltpu.VMEM((wide // 8 * 8, lanes), F32)
    some = rows // 32 * 16
    rest = rows - some
    via = chips == 4
    if via:
        one, two = (0, some), (some, rest)
        most = rows - 64
        near_parts = [(0, most), (most, rows - most)]
        plan = [(0, 0, rows), *((1, *part) for part in near_parts)]
        plan += [(2, *one), (2, *two), (3, *one), (3, *two)]
        sends = [(3, *one), (2, *two), (3, *two), (1, *one), (1, *two), (0, 0, rows), (2, *one)]
    else:
        sends = plan = [(i, 0, rows) for i in range(chips)]
    pad = ((0, levp - lev), (0, levp - lev))
    high = lax.reduce_precision(vert_factor, 8, 7)
    low = vert_factor - high
    vert, vert_t = [
        jnp.concatenate([jnp.pad(x, pad).astype(BF16) for x in parts], axis=1)
        for parts in ((high, high, low), (high.T, high.T, low.T))
    ]
    h_block = h_values.reshape(h_values.shape[2:])
    innovation = jnp.transpose(innovation, (1, 0, 2))
    obs_precision = jnp.transpose(obs_precision, (1, 0, 2))
    product = n_slab * width * lanes * rows
    small = 12 * rows * levp * LANES
    plane_bits = [1 << k for k in range(n_obs.bit_length() - 1)]

    def along(x, i):
        return lax.ppermute(x, "slab", [(s, s ^ (2 * i)) for s in range(n_slab)])

    def plane(x, i):
        return lax.ppermute(x, "obs", [(o, o ^ i) for o in range(n_obs)])

    def swap(x):
        return lax.ppermute(x, "slab", [(s, s ^ 1) for s in range(n_slab)])

    def plane_sum(halves, staged):
        halves = list(halves)
        moved_halves = [None] * len(halves)
        for step, bit in enumerate(plane_bits):
            bits = [bit, plane_bits[len(plane_bits) - 1 - step]]
            for at in range(0, len(halves), 2):
                if step > 0:
                    one, two = halves[at : at + 2]
                    one_more, two_more = moved_halves[at : at + 2]
                    halves[at : at + 2] = call(
                        functools.partial(add_halves_kernel, members, 0 if staged else 1),
                        [struct(one.shape, BF16)] * 2,
                        [],
                        0,
                        one,
                        one_more,
                        two,
                        two_more,
                    )
                for half in range(2):
                    moved_halves[at + half] = plane(halves[at + half], bits[half])
            if step == 0 and staged:
                halves[:] = call(
                    stage_kernel,
                    [struct(x.shape, BF16) for x in halves],
                    [pltpu.SemaphoreType.DMA((len(halves),))],
                    0,
                    *halves,
                    space=HBM,
                )
        return [x for pair in zip(halves, moved_halves) for x in pair]

    def line_sum(moved, other):
        shapes = [(count, width) for i, unused, count in sends]
        mine = call(
            functools.partial(forward_kernel, sends, members),
            [struct(shape, F32) for shape in shapes],
            [],
            product,
            moved,
            own,
        )
        ys = call(
            functools.partial(forward_kernel, sends, members),
            [
                struct(shape, F32 if i == 0 or (via and at == 6) else BF16)
                for at, ((i, *unused), shape) in enumerate(zip(sends, shapes))
            ],
            [],
            product,
            other,
            partner,
            moved,
            *mine,
        )
        if not via:
            return [y if i == 0 else along(y, i) for i, y in enumerate(ys)], [(0, rows)] * chips
        passed, far_rest, last_rest, next_some, next_rest, near, far = ys
        passed = along(passed, 1)
        far_rest, last_rest = along(far_rest, 2), along(last_rest, 3)
        next_some, next_rest = along(next_some, 1), along(next_rest, 1)
        (far,) = call(
            functools.partial(add_kernel, members, 0),
            [struct((some, width), BF16)],
            [],
            0,
            far,
            passed,
        )
        ys = [near, far_rest, last_rest, next_some, next_rest, along(far, 2)]
        return ys, [(0, rows), two, two, one, two, one]

    def line_gather(w, *parts):
        if not via:
            return [w if i == 0 else along(w, i) for i in range(chips)]
        some_w, rest_w, *near = parts
        far = along(some_w, 2)
        far_rest, last_rest = along(rest_w, 2), along(rest_w, 3)
        return [w, *(along(x, 1) for x in near), far, far_rest, along(far, 1), last_rest]

    dense = struct((chips, colblocks, LANES, width), BF16)
    own, for_partner, *partials = call(
        functools.partial(start_kernel, (chips, halves, blocks, lev)),
        [dense, dense] + half_rows,
        [
            pltpu.SMEM(seeds.shape, jnp.int32),
            pltpu.SMEM(block_obs.shape, jnp.int32),
            pltpu.SMEM(block_col.shape, jnp.int32),
            pltpu.SMEM(entry_count.shape, jnp.int32),
            pltpu.VMEM(col_sd.shape, F32),
            pltpu.VMEM((profiles // LANES, levp * blocks, LANES), F32),
            pltpu.VMEM((profiles // LANES, levp * blocks, LANES), F32),
            pltpu.VMEM((n_slab, levp, width), jnp.int32),
            pltpu.VMEM((n_slab // 2, members, levp, width), F32),
            pltpu.VMEM((2, rows, 2 * width), F32),
            pltpu.VMEM((rows, lanes), F32),
            pltpu.VMEM((2, *dense.shape), BF16),
            pltpu.SemaphoreType.DMA((7 + 2 * (profiles // LANES),)),
            pltpu.SemaphoreType.DMA((h_block.shape[0] * halves,)),
        ],
        2 * product,
        seeds,
        block_obs,
        block_col,
        entry_count,
        col_sd,
        innovation.reshape(lev * blocks, profiles),
        obs_precision.reshape(lev * blocks, profiles),
        h_block,
        space=HBM,
        limit=60,
        stored=2,
    )
    ps = plane_sum(partials, True)
    partner = swap(for_partner)
    (precision,) = call(
        functools.partial(precision_kernel, halves, members),
        [struct((rows, width), F32)],
        [],
        0,
        obs_precision,
    )
    slab_sd, residual, moved = call(
        functools.partial(first_kernel, lev),
        [struct((1, lanes), F32), struct(slab_field, F32), struct(slab_rows, BF16)],
        [spread, spread],
        small * colblocks,
        *ps,
        vert,
        vert_t,
    )
    direction = total_step = image = state = None
    for sweep in range(ITERS):
        later, last = sweep > 0, sweep == ITERS - 1
        ys, spans = line_sum(moved, swap(moved))
        state, *weighted = call(
            functools.partial(weigh_kernel, later, last, members, lev, spans),
            [struct((members, 8, LANES), F32)]
            + [struct((n, width), BF16) for n in ((rows, some, rest, most, rows - most) if via else (rows,))]
            + ([] if last else [struct((rows, width), F32)]),
            [],
            0,
            *ys,
            precision,
            *([image, state] if later else []),
        )
        if not last:
            *weighted, image = weighted
        ws = line_gather(*weighted)
        (theirs,) = call(
            functools.partial(adjoint_kernel, plan, members),
            [struct(slab_rows, BF16)],
            [],
            product,
            *ws,
            partner,
        )
        theirs = swap(theirs)
        (mine,) = call(
            functools.partial(adjoint_kernel, plan, members),
            [struct(slab_rows, F32)],
            [],
            product,
            *ws,
            own,
        )
        known = [vert, vert_t, state, residual]
        if later:
            known += [direction, total_step]
        if last:
            ps = call(
                functools.partial(combine_columns_kernel, members),
                [struct((rows, LANES), BF16)] * n_obs,
                [],
                0,
                mine,
                theirs,
            )
            ps = [ps[0]] + [plane(ps[i], i) for i in reversed(range(1, n_obs))]
            own_field = struct((members, levp, LANES), F32)
            before, d, u_d = call(
                functools.partial(increment_kernel, later),
                [own_field] * 3,
                [],
                small,
                col_sd,
                vert,
                state,
                residual,
                *([direction, total_step] if later else []),
            )
            outputs = call(
                functools.partial(last_kernel, len(ps), lev),
                [struct((lev, members, LANES), F32)] * 2,
                [pltpu.VMEM((wide // 8 * 8, LANES), F32)],
                small,
                *ps,
                col_sd,
                vert_t,
                state,
                residual,
                before,
                d,
                u_d,
            )
            break
        ps = call(
            functools.partial(combine_kernel, members), half_rows, [], 0, mine, theirs
        )
        ps = plane_sum(ps, False)
        outs = [
            struct(slab_field, F32),
            struct((members, levp, LANES), F32),
            struct(slab_rows, BF16),
        ]
        if later:
            outs.append(struct(slab_field, F32))
        r, total_step, moved, *d = call(
            functools.partial(update_kernel, later, lev),
            outs,
            [spread, spread],
            small * colblocks,
            *ps,
            slab_sd,
            *known,
        )
        direction, residual = (d[0] if later else residual), r
    return tuple(jnp.transpose(x, (1, 0, 2))[None] for x in outputs)


def solution(mesh):
    return jax.shard_map(
        functools.partial(per_device, mesh.shape["slab"], mesh.shape["obs"]),
        mesh=mesh,
        in_specs=(
            P("obs", None, None),
            P("obs", None, None),
            P(),
            P(("slab", "obs"), None),
            P(),
            P("slab", "obs", None, None, None),
            P("slab", "obs", None),
            P("slab", "obs", None),
            P("slab", "obs"),
        ),
        out_specs=(P(("slab", "obs"), None, None, None), P(("slab", "obs"), None, None, None)),
        check_vma=False,
    )
```
